32 devices in a mesh: dp: 8 (over z, y), mp: 4 (over x, core).
Axes of the slice: x: 2, y: 2, z: 4, core: 2. Of those that a mesh axis runs over, the one named last changes fastest.
Arguments:
- tokens: bfloat16 [16384, 768], P(('dp', 'mp')), may hold values from -6 to 6
- segment_ids: int32 [8, 2048], P('dp'), may hold values from 0 to 7, never falling along the last dimension, each value on 1 to 1024 neighbouring positions
- gene_owner: int32 [16384, 1], P(('dp', 'mp')), may hold values from 0 to 7; in each aligned block of 512 rows (0 to 511, 512 to 1023, ...) at most 80 rows name the same one
- w_qkv: bfloat16 [3, 768, 768], P(None, None, 'mp'), may hold values from -0.21875 to 0.21875
- w_attn_out: bfloat16 [768, 768], P('mp'), may hold values from -3.5 to 3.5
- w_up: bfloat16 [768, 3072], P(None, 'mp'), may hold values from -0.21875 to 0.21875
- w_down: bfloat16 [768, 3072], P(None, 'mp'), may hold values from -0.109375 to 0.109375
- gain_attn: float32 [768], replicated, may hold values from 0.1 to 1.9
- gain_mlp: float32 [768], replicated, may hold values from 0.1 to 1.9
- cotangent: bfloat16 [20480, 768], P(('dp', 'mp')), may hold values from -6 to 6
Outputs:
- relaid: bfloat16 [20480, 768], P(('dp', 'mp'))
- grad_tokens: bfloat16 [16384, 768], P(('dp', 'mp'))
- grad_qkv: float32 [3, 768, 768], P(None, None, 'mp')
- grad_attn_out: float32 [768, 768], P('mp')
- grad_up: float32 [768, 3072], P(None, 'mp')
- grad_down: float32 [768, 3072], P(None, 'mp')
- grad_gain_attn: float32 [768], replicated
- grad_gain_mlp: float32 [768], replicated
The draws below stay inside these ranges and needn't reach their ends.
Inputs may be any that keep to these rules, and one draw needn't show every extreme that they name: `segment_ids`: in each packed row the numbers never fall; a cell holds 1 to 1024 tokens, and some cell of each row holds exactly that many. `gene_owner`: among the tokens of one device (aligned blocks of 512 tokens) at most 80 name the same owner, a bound that some block reaches.
All inputs are finite; a program needn't handle non-finite values.
Results may differ from the reference program's by a relative error of at most 0.015.
Values may be sent and summed in bfloat16 or wider, within the bound.
A program may use at most 192 MiB of HBM per device.

```python
import math
from functools import partial
import jax
import jax.numpy as jnp
import numpy as np
from jax import lax

D = 768
HEADS = 12
HEAD = 64
FF = 3072
ROW_LEN = 2048
CELLS = 8
ROWS = 8
TOK_SHARD = 512
TOKENS = 16384
CAP = 80
SLOTS = 20480
N_DP = 8
N_MP = 4
DEVICES = 32


def level_of(own_key, dims, pieces, least, largest):
    def one(position, parts):
        steps = jax.random.uniform(jax.random.fold_in(jax.random.fold_in(own_key, 6), position), (parts,), jnp.float32, least / len(pieces), largest / len(pieces))
        return jnp.repeat(jnp.exp(steps), dims[position] // parts).reshape((-1,) + (1,) * (len(dims) - position - 1))

    factor_of = one(*pieces[0])
    for cut in pieces[1:]:
        factor_of = factor_of * one(*cut)
    return factor_of


def length_profile(amount, total, limit, lean):
    portions = [(1 << 20) // math.isqrt(rank ** lean) + 1 for rank in range(2, amount + 1)]
    spare, holding = total - limit - (amount - 1), [1] * (amount - 1)
    while spare > 0:
        candidates = [i for i in range(amount - 1) if holding[i] < limit]
        whole, budget = sum([portions[i] for i in candidates]), spare
        for i in candidates:
            extra = min(limit - holding[i], max(1, budget * portions[i] // whole), spare)
            holding[i] = holding[i] + extra
            spare = spare - extra
    return np.array([limit] + holding)


def ragged(own_key, number_of, total, limit, skew):
    if number_of == 2:
        one = jax.random.randint(own_key, (), max(1, total - limit), min(limit, total - 1) + 1)
        return jnp.stack([one, total - one])
    lengths = jnp.asarray(length_profile(number_of, total, limit, skew), jnp.int32)
    pairs = (number_of - 1) // 2
    donor, taker = lengths[1:1 + 2 * pairs:2], lengths[2:2 + 2 * pairs:2]
    margin = jnp.minimum(donor - 1, limit - taker)
    moved = jax.random.randint(jax.random.fold_in(own_key, 1), (pairs,), 0, 1 << 20) % (margin + 1)
    lengths = lengths.at[1:1 + 2 * pairs:2].set(donor - moved).at[2:2 + 2 * pairs:2].set(taker + moved)
    return lengths[jax.random.permutation(jax.random.fold_in(own_key, 2), number_of)]


def deal_out(key, own, number, rows, number_of, top, most, skew):
    order = jax.random.permutation(key, number_of)
    crowded, ordinary = portions_of(number_of, rows * top, most, skew, True), portions_of(number_of, rows * top, most, skew, False)
    places = jnp.arange(number_of)

    def named(tallies, turn):
        used = int((tallies > 0).sum())
        fixed = max(1, used // 4)
        passed = fixed + (places - fixed + turn * (used - fixed)) % max(1, number_of - fixed)
        return jnp.zeros((number_of,), jnp.int32).at[order[jnp.where(places < fixed, places, passed)]].set(jnp.asarray(tallies, jnp.int32))

    tallies = jnp.where(number % 4 == 0, named(crowded, number // 4), named(ordinary, number - number // 4 - 1))
    mixed = jax.random.permutation(jax.random.fold_in(own, 3), number_of)
    source_of, receiver = mixed[0:number_of // 2 * 2:2], mixed[1:number_of // 2 * 2:2]
    slack = jnp.minimum(tallies[source_of] - 1, most - tallies[receiver]) // 2
    slack = jnp.where((source_of == order[0]) | (receiver == order[0]) | (tallies[receiver] == 0), 0, jnp.maximum(slack, 0))
    passed = jax.random.randint(jax.random.fold_in(own, 4), (number_of // 2,), 0, 1 << 20) % (slack + 1)
    tallies = tallies.at[source_of].add(-passed).at[receiver].add(passed)
    labels = jnp.searchsorted(jnp.cumsum(tallies), jnp.arange(rows * top), side="right").astype(jnp.int32)
    listing = labels.reshape(top, rows).T
    listing = listing[jax.random.permutation(jax.random.fold_in(own, 1), rows)]
    turn = jax.random.randint(jax.random.fold_in(own, 2), (rows, 1), 0, top)
    return jnp.take_along_axis(listing, (jnp.arange(top)[None, :] + turn) % top, axis=1)


def portions_of(number_of, total, most, slope, full):
    weights = [(1 << 20) // math.isqrt(standing ** slope) + 1 for standing in range(1, number_of + 1)]
    largest = most if full else min(most, max(-(-total // number_of), total * weights[0] // sum(weights)))
    least = 1 if total - largest >= number_of - 1 else 0
    holding, rest = [largest] + [least] * (number_of - 1), total - largest - least * (number_of - 1)
    while rest > 0:
        movable = [i for i in range(1, number_of) if holding[i] < largest] or [i for i in range(1, number_of) if holding[i] < most]
        pool, budget = sum([weights[i] for i in movable]), rest
        for i in movable:
            extra = min(most - holding[i], max(1, budget * weights[i] // pool), rest)
            holding[i] = holding[i] + extra
            rest = rest - extra
    return np.array(holding)


def scatter_about(rng, dims, deviation, most, shards=(), kind=jnp.bfloat16):
    gain = level_of(rng, dims, shards, -0.22, 0.18) if shards else 1.0
    values = jax.random.normal(rng, dims, jnp.float32) * deviation * gain
    return jnp.minimum(jnp.maximum(values, -most), most).astype(kind)


def setup_inputs(seed: int = 0) -> dict:
    streams_of = jax.random.split(jax.random.key(seed), 11)
    tokens = scatter_about(streams_of[0], (TOKENS, D), 1.0, 6.0, ((0, 32),))
    segment_ids = jax.vmap(lambda own: jnp.searchsorted(jnp.cumsum(ragged(own, CELLS, ROW_LEN, ROW_LEN // 2, 2)), jnp.arange(ROW_LEN), side="right"))(jax.random.split(streams_of[1], ROWS)).reshape((ROWS, ROW_LEN)).astype(jnp.int32)
    gene_owner_keys = jax.random.split(jax.random.fold_in(streams_of[2], 1), TOKENS // TOK_SHARD)
    gene_owner_turns = jax.random.permutation(jax.random.fold_in(streams_of[2], 3), TOKENS // TOK_SHARD)
    gene_owner = jax.vmap(lambda own, number: deal_out(jax.random.fold_in(streams_of[2], 2), own, number, TOK_SHARD, N_DP, 1, CAP, 1))(gene_owner_keys, gene_owner_turns).reshape((TOKENS, 1))
    w_qkv = scatter_about(streams_of[3], (3, D, D), D ** -0.5, 0.21875, ((2, 4),))
    w_attn_out = scatter_about(streams_of[4], (D, D), (max(1, D * 8 // ROW_LEN)) ** -0.5, 3.5, ((0, 4),))
    w_up = scatter_about(streams_of[5], (D, FF), D ** -0.5, 0.21875, ((1, 4),))
    w_down = scatter_about(streams_of[6], (D, FF), FF ** -0.5, 0.109375, ((1, 4),))
    gain_attn = jnp.clip(1.0 + 0.18 * jax.random.normal(streams_of[7], (D,), jnp.float32), 0.1, 1.9)
    gain_mlp = jnp.clip(1.0 + 0.18 * jax.random.normal(streams_of[8], (D,), jnp.float32), 0.1, 1.9)
    cotangent = scatter_about(streams_of[9], (SLOTS, D), 1.0, 6.0, ((0, 32),))
    return dict(tokens=tokens, segment_ids=segment_ids, gene_owner=gene_owner, w_qkv=w_qkv, w_attn_out=w_attn_out, w_up=w_up, w_down=w_down, gain_attn=gain_attn, gain_mlp=gain_mlp, cotangent=cotangent)


@jax.custom_vjp
def low(v):
    return lax.optimization_barrier(v.astype(jnp.bfloat16)).astype(jnp.float32)

@jax.custom_vjp
def low_back(v):
    return v

def low_keep(v):
    return (low(v), None)

def low_pass(kept, grad):
    return (grad,)

def back_keep(v):
    return (v, None)

def back_low(kept, grad):
    return (low(grad),)
low.defvjp(low_keep, low_pass)
low_back.defvjp(back_keep, back_low)
epsilon = 1e-05
highest = lax.Precision.HIGHEST
masked_score = -1e+30

def norm_rows(values, gain_vec):
    average = lax.optimization_barrier(jnp.mean(values, axis=-1, keepdims=True))
    centered = values - average
    variance = lax.optimization_barrier(jnp.mean(centered * centered, axis=-1, keepdims=True))
    return centered * lax.rsqrt(variance + epsilon) * gain_vec

def gelu_exact(values):
    return 0.5 * values * (1.0 + lax.erf(values * 0.7071067811865476))

def row_attention(queries, key_rows, value_rows, row_cells):
    score_scale = queries.shape[-1] ** (-0.5)
    raw_scores = low_back(jnp.einsum('hqd,hkd->hqk', queries, key_rows, precision=highest))
    same_cell = row_cells[:, None] == row_cells[None, :]
    scores = jnp.where(same_cell[None], raw_scores * score_scale, masked_score)
    row_max = lax.optimization_barrier(jnp.max(scores, axis=-1, keepdims=True))
    powers = jnp.exp(scores - row_max)
    probs = powers / lax.optimization_barrier(jnp.sum(powers, axis=-1, keepdims=True))
    return jnp.einsum('hqk,hkd->hqd', low(probs), value_rows, precision=highest)

def token_slots(owners):
    owner_grid = owners.reshape(DEVICES, TOK_SHARD)
    choices_row = jnp.arange(N_DP, dtype=jnp.int32)
    onehot = (owner_grid[:, :, None] == choices_row[None, None, :]).astype(jnp.int32)
    earlier = jnp.cumsum(onehot, axis=1, dtype=jnp.int32) - onehot
    ranking = lax.optimization_barrier(jnp.sum(earlier * onehot, axis=2, dtype=jnp.int32))
    device_id = jnp.arange(DEVICES, dtype=jnp.int32)[:, None]
    source_id = device_id // N_MP
    tensor_lane = device_id % N_MP
    slot_index = ((owner_grid * N_MP + tensor_lane) * N_DP + source_id) * CAP + ranking
    return slot_index.reshape(-1).astype(jnp.int32)

def row_layer(params, row_item):
    qkv_f, attn_f, up_f, down_f, gain_one, gain_two = params
    row_tokens, row_cells = row_item
    normed = low(norm_rows(row_tokens, gain_one))
    projected = [low(low_back(jnp.dot(normed, qkv_f[which], precision=highest))) for which in range(3)]
    head_views = [matrix.reshape(ROW_LEN, HEADS, HEAD).transpose(1, 0, 2) for matrix in projected]
    attended = row_attention(head_views[0], head_views[1], head_views[2], row_cells)
    merged = low(low_back(attended.transpose(1, 0, 2).reshape(ROW_LEN, D)))
    residual = row_tokens + low_back(jnp.dot(merged, attn_f, precision=highest))
    hidden = low(norm_rows(residual, gain_two))
    pre_act = low_back(jnp.dot(hidden, up_f, precision=highest))
    activated = low(gelu_exact(pre_act))
    return low(residual + jnp.dot(activated, down_f.T, precision=highest))

def reference(tokens, segment_ids, gene_owner, w_qkv, w_attn_out, w_up, w_down, gain_attn, gain_mlp, cotangent):
    slot_index = token_slots(gene_owner[:, 0])

    def forward(tokens_f, qkv_f, attn_f, up_f, down_f, gain_one, gain_two):
        params = (qkv_f, attn_f, up_f, down_f, gain_one, gain_two)
        layer_rows = jax.checkpoint(partial(row_layer, params))
        rows_out = lax.map(layer_rows, (tokens_f.reshape(ROWS, ROW_LEN, D), segment_ids))
        return jnp.zeros((SLOTS, D), jnp.float32).at[slot_index].set(rows_out.reshape(TOKENS, D))
    inputs_f = (tokens.astype(jnp.float32), w_qkv.astype(jnp.float32), w_attn_out.astype(jnp.float32), w_up.astype(jnp.float32), w_down.astype(jnp.float32), gain_attn.astype(jnp.float32), gain_mlp.astype(jnp.float32))
    relaid, pullback = jax.vjp(forward, *inputs_f)
    grads = pullback(cotangent.astype(jnp.float32))
    return (relaid.astype(jnp.bfloat16), grads[0].astype(jnp.bfloat16), grads[1], grads[2], grads[3], grads[4], grads[5], grads[6])
```

```python
import functools
import jax
import jax.numpy as jnp
from jax import lax
from jax.experimental import pallas as pl
from jax.experimental.pallas import tpu as pltpu
from jax.sharding import PartitionSpec as P

epsilon = 1e-05


def norm_parts(values, gain_vec):
    average = jnp.mean(values, axis=-1, keepdims=True)
    centered = values - average
    variance = jnp.mean(centered * centered, axis=-1, keepdims=True)
    inverse = lax.rsqrt(variance + epsilon)
    unit_rows = centered * inverse
    return (unit_rows * gain_vec, unit_rows, inverse)


def norm_back(grad_normed, unit_rows, inverse, gain_vec):
    scaled = grad_normed * gain_vec
    first_mean = jnp.mean(scaled, axis=-1, keepdims=True)
    second_mean = jnp.mean(scaled * unit_rows, axis=-1, keepdims=True)
    grad_input = inverse * (scaled - first_mean - unit_rows * second_mean)
    return (grad_input, jnp.sum(grad_normed * unit_rows, axis=0))


def gelu_exact(values):
    return 0.5 * values * (1.0 + lax.erf(values * 0.7071067811865476))


def gelu_slope(values):
    cumulative = 0.5 * (1.0 + lax.erf(values * 0.7071067811865476))
    density = jnp.exp(-0.5 * values * values) * 0.3989422804014327
    return cumulative + values * density


HEAD = 64
TQ = 256
TK = 256
NT = (((1,), (1,)), ((), ()))
NN = (((1,), (0,)), ((), ()))
MASKED = -1e30


def lower_bound(seg, n, value):
    def step(_, c):
        lo, hi = c
        mid = (lo + hi) // 2
        less = seg[jnp.minimum(mid, n - 1)] < value
        go = lo < hi
        return (jnp.where(go & less, mid + 1, lo), jnp.where(go & ~less, mid, hi))
    lo, hi = lax.fori_loop(0, n.bit_length(), step, (jnp.int32(0), jnp.int32(n)))
    return lo


def key_range(seg, n, tile):
    first = lower_bound(seg, n, seg[tile * TQ])
    end = lower_bound(seg, n, seg[tile * TQ + TQ - 1] + 1)
    return first // TK, (end + TK - 1) // TK


def head_masks(width, heads):
    lane = lax.broadcasted_iota(jnp.int32, (1, width), 1)
    return [(lane // HEAD == h) for h in range(heads)]


def seg_columns(segv_ref, cols, n):
    for t in range(n // 128):
        row = segv_ref[0:1, t * 128:(t + 1) * 128].astype(jnp.float32)
        cols[t * 128:(t + 1) * 128, :] = jnp.broadcast_to(row, (128, 128)).T


def fwd_kernel(n, heads, seg, segv_ref, q_ref, k_ref, v_ref, o_ref, lse_ref, vt, cols, scores):
    tile = pl.program_id(0)
    width = heads * HEAD

    @pl.when(tile == 0)
    def _():
        seg_columns(segv_ref, cols, n)
        for t in range(n // TK):
            vt[:, t * TK:(t + 1) * TK] = v_ref[t * TK:(t + 1) * TK, :].astype(jnp.float32).T.astype(jnp.bfloat16)

    lo, hi = key_range(seg, n, tile)
    q0 = pl.multiple_of(tile * TQ, TQ)
    q = q_ref[...] * jnp.bfloat16(HEAD ** -0.5)
    masks = head_masks(width, heads)
    qm = [jnp.where(m, q, jnp.bfloat16(0)) for m in masks]
    seg_row = segv_ref[0:1, pl.ds(q0, TQ)].astype(jnp.float32)

    def first(b, tops):
        k0 = pl.multiple_of(b * TK, TK)
        keys = k_ref[pl.ds(k0, TK), :]
        col = cols[pl.ds(k0, TK), :]
        same = jnp.concatenate([col] * (TQ // 128), axis=1) == seg_row
        out = []
        for h in range(heads):
            s = lax.dot_general(keys, qm[h], NT, preferred_element_type=jnp.float32)
            s = jnp.where(same, s, MASKED)
            scores[h, pl.ds(k0, TK), :] = s
            out.append(jnp.maximum(tops[h], jnp.max(s, axis=0, keepdims=True)))
        return tuple(out)

    tops = lax.fori_loop(lo, hi, first, tuple(jnp.full((1, TQ), MASKED, jnp.float32) for _ in range(heads)))

    def second(b, acc):
        k0 = pl.multiple_of(b * TK, TK)
        out = []
        for h in range(heads):
            p = jnp.exp(scores[h, pl.ds(k0, TK), :] - tops[h])
            total = acc[h][1] + jnp.sum(p, axis=0, keepdims=True)
            part = lax.dot_general(vt[h * HEAD:(h + 1) * HEAD, pl.ds(k0, TK)], p.astype(jnp.bfloat16), NN, preferred_element_type=jnp.float32)
            out.append((acc[h][0] + part, total))
        return tuple(out)

    acc = lax.fori_loop(lo, hi, second, tuple((jnp.zeros((HEAD, TQ), jnp.float32), jnp.zeros((1, TQ), jnp.float32)) for _ in range(heads)))
    ot = jnp.concatenate([acc[h][0] / acc[h][1] for h in range(heads)], axis=0)
    o_ref[...] = ot.T.astype(jnp.bfloat16)
    lse_ref[...] = jnp.concatenate([tops[h] + jnp.log(acc[h][1]) for h in range(heads)] + [jnp.zeros((8 - heads, TQ), jnp.float32)], axis=0)


def attend_forward(seg, q, k, v):
    n, width = q.shape
    heads = width // HEAD
    whole = pl.BlockSpec(memory_space=pltpu.VMEM)
    return pl.pallas_call(
        functools.partial(fwd_kernel, n, heads),
        grid_spec=pltpu.PrefetchScalarGridSpec(
            num_scalar_prefetch=1,
            grid=(n // TQ,),
            in_specs=[whole, pl.BlockSpec((TQ, width), lambda t, s: (t, 0)), whole, whole],
            out_specs=[pl.BlockSpec((TQ, width), lambda t, s: (t, 0)), pl.BlockSpec((8, TQ), lambda t, s: (0, t))],
            scratch_shapes=[pltpu.VMEM((width, n), jnp.bfloat16), pltpu.VMEM((n, 128), jnp.float32), pltpu.VMEM((heads, n, TQ), jnp.float32)],
        ),
        out_shape=[jax.ShapeDtypeStruct((n, width), jnp.bfloat16), jax.ShapeDtypeStruct((8, n), jnp.float32)],
        compiler_params=pltpu.CompilerParams(vmem_limit_bytes=40 << 20),
        cost_estimate=pl.CostEstimate(flops=4 * heads * n * n * HEAD, bytes_accessed=8 * n * width, transcendentals=heads * n * n // 2),
        name="attend_forward",
    )(seg.reshape(-1), seg.reshape(1, -1), q, k, v)


def bwd_kernel(n, heads, seg, segv_ref, q_ref, k_ref, v_ref, o_ref, do_ref, lse_ref, dq_ref, dk_ref, dv_ref, kt, cols, dk_acc, dv_acc):
    tile = pl.program_id(0)
    width = heads * HEAD

    @pl.when(tile == 0)
    def _():
        seg_columns(segv_ref, cols, n)
        for t in range(n // TK):
            kt[:, t * TK:(t + 1) * TK] = k_ref[t * TK:(t + 1) * TK, :].astype(jnp.float32).T.astype(jnp.bfloat16)
        dk_acc[...] = jnp.zeros_like(dk_acc)
        dv_acc[...] = jnp.zeros_like(dv_acc)

    lo, hi = key_range(seg, n, tile)
    q0 = pl.multiple_of(tile * TQ, TQ)
    masks = head_masks(width, heads)
    q = q_ref[...] * jnp.bfloat16(HEAD ** -0.5)
    do = do_ref[...]
    qm = [jnp.where(m, q, jnp.bfloat16(0)) for m in masks]
    dm = [jnp.where(m, do, jnp.bfloat16(0)) for m in masks]
    seg_row = segv_ref[0:1, pl.ds(q0, TQ)].astype(jnp.float32)
    prod = do.astype(jnp.float32) * o_ref[...].astype(jnp.float32)
    high = prod.astype(jnp.bfloat16)
    rest = (prod - high.astype(jnp.float32)).astype(jnp.bfloat16)
    row = lax.broadcasted_iota(jnp.int32, (16, width), 0)
    lane = lax.broadcasted_iota(jnp.int32, (16, width), 1)
    pick = jnp.where(lane // HEAD == row, 1.0, 0.0).astype(jnp.bfloat16)
    delta = lax.dot_general(pick, high, NT, preferred_element_type=jnp.float32) + lax.dot_general(pick, rest, NT, preferred_element_type=jnp.float32)
    lse = lse_ref[...]

    def body(b, acc):
        k0 = pl.multiple_of(b * TK, TK)
        keys = k_ref[pl.ds(k0, TK), :]
        vals = v_ref[pl.ds(k0, TK), :]
        col = cols[pl.ds(k0, TK), :]
        same = jnp.concatenate([col] * (TQ // 128), axis=1) == seg_row
        out = []
        dks = jnp.zeros((TK, width), jnp.float32)
        dvs = jnp.zeros((TK, width), jnp.float32)
        for h in range(heads):
            s = lax.dot_general(keys, qm[h], NT, preferred_element_type=jnp.float32)
            p = jnp.where(same, jnp.exp(s - lse[h:h + 1, :]), 0.0)
            dp = lax.dot_general(vals, dm[h], NT, preferred_element_type=jnp.float32)
            ds = (p * (dp - delta[h:h + 1, :])).astype(jnp.bfloat16)
            dvs = dvs + lax.dot_general(p.astype(jnp.bfloat16), dm[h], NN, preferred_element_type=jnp.float32)
            dks = dks + lax.dot_general(ds, qm[h], NN, preferred_element_type=jnp.float32)
            out.append(acc[h] + lax.dot_general(kt[h * HEAD:(h + 1) * HEAD, pl.ds(k0, TK)], ds, NN, preferred_element_type=jnp.float32))
        dk_acc[pl.ds(k0, TK), :] += dks
        dv_acc[pl.ds(k0, TK), :] += dvs
        return tuple(out)

    acc = lax.fori_loop(lo, hi, body, tuple(jnp.zeros((HEAD, TQ), jnp.float32) for _ in range(heads)))
    dq_ref[...] = (jnp.concatenate(acc, axis=0).T * HEAD ** -0.5).astype(jnp.bfloat16)

    @pl.when(tile == n // TQ - 1)
    def _():
        dk_ref[...] = dk_acc[...].astype(jnp.bfloat16)
        dv_ref[...] = dv_acc[...].astype(jnp.bfloat16)


def attend_backward(seg, q, k, v, o, do, lse):
    n, width = q.shape
    heads = width // HEAD
    whole = pl.BlockSpec(memory_space=pltpu.VMEM)
    rows = pl.BlockSpec((TQ, width), lambda t, s: (t, 0))
    return pl.pallas_call(
        functools.partial(bwd_kernel, n, heads),
        grid_spec=pltpu.PrefetchScalarGridSpec(
            num_scalar_prefetch=1,
            grid=(n // TQ,),
            in_specs=[whole, rows, whole, whole, rows, rows, pl.BlockSpec((8, TQ), lambda t, s: (0, t))],
            out_specs=[rows, whole, whole],
            scratch_shapes=[pltpu.VMEM((width, n), jnp.bfloat16), pltpu.VMEM((n, 128), jnp.float32), pltpu.VMEM((n, width), jnp.float32), pltpu.VMEM((n, width), jnp.float32)],
        ),
        out_shape=[jax.ShapeDtypeStruct((n, width), jnp.bfloat16)] * 3,
        compiler_params=pltpu.CompilerParams(vmem_limit_bytes=40 << 20),
        cost_estimate=pl.CostEstimate(flops=10 * heads * n * n * HEAD, bytes_accessed=16 * n * width, transcendentals=heads * n * n // 2),
        name="attend_backward",
    )(seg.reshape(-1), seg.reshape(1, -1), q, k, v, o, do, lse)


def local(
    tokens, segment_ids, gene_owner, w_qkv, w_attn_out, w_up, w_down, gain_attn, gain_mlp, cotangent
):
    width = tokens.shape[1]
    dp_count = lax.axis_size("dp")
    capacity = cotangent.shape[0] // dp_count
    own_rows = tokens.shape[0]
    contract_last = (((1,), (1,)), ((), ()))
    contract_first = (((0,), (0,)), ((), ()))
    low = jnp.bfloat16

    def scatter_sum(partial):
        return lax.psum_scatter(partial.astype(low), "mp", scatter_dimension=0, tiled=True).astype(jnp.float32)

    returned = lax.all_to_all(
        cotangent.reshape(dp_count, capacity, width), "dp", split_axis=0, concat_axis=0, tiled=True
    ).reshape(dp_count * capacity, width)
    owners = gene_owner[:, 0]
    place = jnp.arange(own_rows, dtype=jnp.int32)
    earlier = (owners[:, None] == owners[None, :]) & (place[None, :] < place[:, None])
    slots = owners * capacity + jnp.sum(earlier.astype(jnp.int32), axis=1)
    onehot = (slots[:, None] == jnp.arange(dp_count * capacity, dtype=jnp.int32)[None, :]).astype(low)

    tokens_f = tokens.astype(jnp.float32)
    normed_one, unit_one, inverse_one = norm_parts(tokens_f, gain_attn)
    attn_in = lax.all_gather(normed_one.astype(low), "mp", axis=0, tiled=True)
    projected = [jnp.dot(attn_in, w_qkv[p], preferred_element_type=jnp.float32).astype(low) for p in range(3)]
    merged, log_sums = attend_forward(segment_ids, *projected)
    residual = tokens_f + scatter_sum(jnp.dot(merged, w_attn_out, preferred_element_type=jnp.float32))
    normed_two, unit_two, inverse_two = norm_parts(residual, gain_mlp)
    mlp_rows = lax.all_gather(normed_two.astype(low), "mp", axis=0, tiled=True)
    grad_block = jnp.dot(onehot, returned, preferred_element_type=jnp.float32).astype(low)
    grad_rows = lax.all_gather(grad_block, "mp", axis=0, tiled=True)
    pre_act = jnp.dot(mlp_rows, w_up, preferred_element_type=jnp.float32)
    activated = gelu_exact(pre_act).astype(low)
    grad_act = jnp.dot(grad_rows, w_down, preferred_element_type=jnp.float32)
    grad_pre = (grad_act * gelu_slope(pre_act)).astype(low)
    grad_mlp_in = scatter_sum(
        lax.dot_general(grad_pre, w_up, contract_last, preferred_element_type=jnp.float32)
    )
    grad_down_local = lax.dot_general(
        grad_rows, activated, contract_first, preferred_element_type=jnp.float32
    ).astype(low)
    grad_up_local = lax.dot_general(
        mlp_rows, grad_pre, contract_first, preferred_element_type=jnp.float32
    ).astype(low)
    norm_two_grad, gain_mlp_grad = norm_back(grad_mlp_in, unit_two, inverse_two, gain_mlp)
    up_sum, down_sum = lax.psum((grad_up_local, grad_down_local), "dp")
    output = residual + scatter_sum(
        lax.dot_general(activated, w_down, contract_last, preferred_element_type=jnp.float32)
    )
    outgoing = lax.dot_general(
        onehot, output.astype(low), contract_first, preferred_element_type=jnp.float32
    ).astype(low)
    relaid = lax.all_to_all(
        outgoing.reshape(dp_count, capacity, width), "dp", split_axis=0, concat_axis=0, tiled=True
    ).reshape(dp_count * capacity, width)
    grad_residual = grad_block.astype(jnp.float32) + norm_two_grad
    residual_rows = lax.all_gather(grad_residual.astype(low), "mp", axis=0, tiled=True)
    grad_attn_local = lax.dot_general(
        merged, residual_rows, contract_first, preferred_element_type=jnp.float32
    ).astype(low)
    grad_merged = lax.dot_general(
        residual_rows, w_attn_out, contract_last, preferred_element_type=jnp.float32
    ).astype(low)
    grad_proj = attend_backward(segment_ids, *projected, merged, grad_merged, log_sums)
    grad_attn_in = scatter_sum(
        sum(
            lax.dot_general(grad_proj[p], w_qkv[p], contract_last, preferred_element_type=jnp.float32)
            for p in range(3)
        )
    )
    grad_qkv_local = jnp.stack(
        [
            lax.dot_general(attn_in, grad_proj[p], contract_first, preferred_element_type=jnp.float32).astype(low)
            for p in range(3)
        ]
    )
    grad_qkv_local, up_sum, down_sum = lax.optimization_barrier((grad_qkv_local, up_sum, down_sum))
    qkv_sum, attn_sum = lax.psum((grad_qkv_local, grad_attn_local), "dp")
    norm_one_grad, gain_attn_grad = norm_back(grad_attn_in, unit_one, inverse_one, gain_attn)
    grad_tokens = (grad_residual + norm_one_grad).astype(low)
    gain_attn_sum, gain_mlp_sum = lax.psum((gain_attn_grad, gain_mlp_grad), ("dp", "mp"))
    full = jnp.float32
    return (
        relaid,
        grad_tokens,
        qkv_sum.astype(full),
        attn_sum.astype(full),
        up_sum.astype(full),
        down_sum.astype(full),
        gain_attn_sum,
        gain_mlp_sum,
    )


def solution(mesh):
    placed = (
        P(("dp", "mp"), None),
        P("dp", None),
        P(("dp", "mp"), None),
        P(None, None, "mp"),
        P("mp", None),
        P(None, "mp"),
        P(None, "mp"),
        P(),
        P(),
        P(("dp", "mp"), None),
    )
    return jax.shard_map(
        local,
        mesh=mesh,
        in_specs=placed,
        out_specs=(
            P(("dp", "mp"), None),
            P(("dp", "mp"), None),
            P(None, None, "mp"),
            P("mp", None),
            P(None, "mp"),
            P(None, "mp"),
            P(),
            P(),
        ),
        check_vma=False,
    )
```

```python
import functools
import jax
import jax.numpy as jnp
from jax import lax
from jax.experimental import pallas as pl
from jax.experimental.pallas import tpu as pltpu
from jax.sharding import PartitionSpec as P

epsilon = 1e-05


def norm_parts(values, gain_vec):
    average = jnp.mean(values, axis=-1, keepdims=True)
    centered = values - average
    variance = jnp.mean(centered * centered, axis=-1, keepdims=True)
    inverse = lax.rsqrt(variance + epsilon)
    unit_rows = centered * inverse
    return (unit_rows * gain_vec, unit_rows, inverse)


def norm_back(grad_normed, unit_rows, inverse, gain_vec):
    scaled = grad_normed * gain_vec
    first_mean = jnp.mean(scaled, axis=-1, keepdims=True)
    second_mean = jnp.mean(scaled * unit_rows, axis=-1, keepdims=True)
    grad_input = inverse * (scaled - first_mean - unit_rows * second_mean)
    return (grad_input, jnp.sum(grad_normed * unit_rows, axis=0))


def gelu_exact(values):
    return 0.5 * values * (1.0 + lax.erf(values * 0.7071067811865476))


def gelu_slope(values):
    cumulative = 0.5 * (1.0 + lax.erf(values * 0.7071067811865476))
    density = jnp.exp(-0.5 * values * values) * 0.3989422804014327
    return cumulative + values * density


HEAD = 64
TQ = 256
TK = 256
NT = (((1,), (1,)), ((), ()))
NN = (((1,), (0,)), ((), ()))
MASKED = -1e30


def lower_bound(seg, n, value):
    def step(_, c):
        lo, hi = c
        mid = (lo + hi) // 2
        less = seg[jnp.minimum(mid, n - 1)] < value
        go = lo < hi
        return (jnp.where(go & less, mid + 1, lo), jnp.where(go & ~less, mid, hi))
    lo, hi = lax.fori_loop(0, n.bit_length(), step, (jnp.int32(0), jnp.int32(n)))
    return lo


def key_range(seg, n, tile):
    first = lower_bound(seg, n, seg[tile * TQ])
    end = lower_bound(seg, n, seg[tile * TQ + TQ - 1] + 1)
    return first // TK, (end + TK - 1) // TK


def head_masks(width, heads):
    lane = lax.broadcasted_iota(jnp.int32, (1, width), 1)
    return [(lane // HEAD == h) for h in range(heads)]


def seg_columns(segv_ref, cols, n):
    for t in range(n // 128):
        row = segv_ref[0:1, t * 128:(t + 1) * 128].astype(jnp.float32)
        cols[t * 128:(t + 1) * 128, :] = jnp.broadcast_to(row, (128, 128)).T


def fwd_kernel(n, heads, seg, segv_ref, q_ref, k_ref, v_ref, o_ref, lse_ref, vt, cols, scores):
    tile = pl.program_id(0)
    width = heads * HEAD

    @pl.when(tile == 0)
    def _():
        seg_columns(segv_ref, cols, n)
        for t in range(n // TK):
            vt[:, t * TK:(t + 1) * TK] = v_ref[t * TK:(t + 1) * TK, :].astype(jnp.float32).T.astype(jnp.bfloat16)

    lo, hi = key_range(seg, n, tile)
    q0 = pl.multiple_of(tile * TQ, TQ)
    q = q_ref[...] * jnp.bfloat16(HEAD ** -0.5)
    masks = head_masks(width, heads)
    qm = [jnp.where(m, q, jnp.bfloat16(0)) for m in masks]
    seg_row = segv_ref[0:1, pl.ds(q0, TQ)].astype(jnp.float32)

    def first(b, tops):
        k0 = pl.multiple_of(b * TK, TK)
        keys = k_ref[pl.ds(k0, TK), :]
        col = cols[pl.ds(k0, TK), :]
        same = jnp.concatenate([col] * (TQ // 128), axis=1) == seg_row
        out = []
        for h in range(heads):
            s = lax.dot_general(keys, qm[h], NT, preferred_element_type=jnp.float32)
            s = jnp.where(same, s, MASKED)
            scores[h, pl.ds(k0, TK), :] = s
            out.append(jnp.maximum(tops[h], jnp.max(s, axis=0, keepdims=True)))
        return tuple(out)

    tops = lax.fori_loop(lo, hi, first, tuple(jnp.full((1, TQ), MASKED, jnp.float32) for _ in range(heads)))

    def second(b, acc):
        k0 = pl.multiple_of(b * TK, TK)
        out = []
        for h in range(heads):
            p = jnp.exp(scores[h, pl.ds(k0, TK), :] - tops[h])
            total = acc[h][1] + jnp.sum(p, axis=0, keepdims=True)
            part = lax.dot_general(vt[h * HEAD:(h + 1) * HEAD, pl.ds(k0, TK)], p.astype(jnp.bfloat16), NN, preferred_element_type=jnp.float32)
            out.append((acc[h][0] + part, total))
        return tuple(out)

    acc = lax.fori_loop(lo, hi, second, tuple((jnp.zeros((HEAD, TQ), jnp.float32), jnp.zeros((1, TQ), jnp.float32)) for _ in range(heads)))
    ot = jnp.concatenate([acc[h][0] / acc[h][1] for h in range(heads)], axis=0)
    o_ref[...] = ot.T.astype(jnp.bfloat16)
    lse_ref[...] = jnp.concatenate([tops[h] + jnp.log(acc[h][1]) for h in range(heads)] + [jnp.zeros((8 - heads, TQ), jnp.float32)], axis=0)


def attend_forward(seg, q, k, v):
    n, width = q.shape
    heads = width // HEAD
    whole = pl.BlockSpec(memory_space=pltpu.VMEM)
    return pl.pallas_call(
        functools.partial(fwd_kernel, n, heads),
        grid_spec=pltpu.PrefetchScalarGridSpec(
            num_scalar_prefetch=1,
            grid=(n // TQ,),
            in_specs=[whole, pl.BlockSpec((TQ, width), lambda t, s: (t, 0)), whole, whole],
            out_specs=[pl.BlockSpec((TQ, width), lambda t, s: (t, 0)), pl.BlockSpec((8, TQ), lambda t, s: (0, t))],
            scratch_shapes=[pltpu.VMEM((width, n), jnp.bfloat16), pltpu.VMEM((n, 128), jnp.float32), pltpu.VMEM((heads, n, TQ), jnp.float32)],
        ),
        out_shape=[jax.ShapeDtypeStruct((n, width), jnp.bfloat16), jax.ShapeDtypeStruct((8, n), jnp.float32)],
        compiler_params=pltpu.CompilerParams(vmem_limit_bytes=40 << 20),
        cost_estimate=pl.CostEstimate(flops=4 * heads * n * n * HEAD, bytes_accessed=8 * n * width, transcendentals=heads * n * n // 2),
        name="attend_forward",
    )(seg.reshape(-1), seg.reshape(1, -1), q, k, v)


def bwd_kernel(n, heads, seg, segv_ref, q_ref, k_ref, v_ref, o_ref, do_ref, lse_ref, dq_ref, dk_ref, dv_ref, kt, cols, dk_acc, dv_acc):
    tile = pl.program_id(0)
    width = heads * HEAD

    @pl.when(tile == 0)
    def _():
        seg_columns(segv_ref, cols, n)
        for t in range(n // TK):
            kt[:, t * TK:(t + 1) * TK] = k_ref[t * TK:(t + 1) * TK, :].astype(jnp.float32).T.astype(jnp.bfloat16)
        dk_acc[...] = jnp.zeros_like(dk_acc)
        dv_acc[...] = jnp.zeros_like(dv_acc)

    lo, hi = key_range(seg, n, tile)
    q0 = pl.multiple_of(tile * TQ, TQ)
    masks = head_masks(width, heads)
    q = q_ref[...] * jnp.bfloat16(HEAD ** -0.5)
    do = do_ref[...]
    qm = [jnp.where(m, q, jnp.bfloat16(0)) for m in masks]
    dm = [jnp.where(m, do, jnp.bfloat16(0)) for m in masks]
    seg_row = segv_ref[0:1, pl.ds(q0, TQ)].astype(jnp.float32)
    prod = do.astype(jnp.float32) * o_ref[...].astype(jnp.float32)
    high = prod.astype(jnp.bfloat16)
    rest = (prod - high.astype(jnp.float32)).astype(jnp.bfloat16)
    row = lax.broadcasted_iota(jnp.int32, (16, width), 0)
    lane = lax.broadcasted_iota(jnp.int32, (16, width), 1)
    pick = jnp.where(lane // HEAD == row, 1.0, 0.0).astype(jnp.bfloat16)
    delta = lax.dot_general(pick, high, NT, preferred_element_type=jnp.float32) + lax.dot_general(pick, rest, NT, preferred_element_type=jnp.float32)
    lse = lse_ref[...]

    def body(b, acc):
        k0 = pl.multiple_of(b * TK, TK)
        keys = k_ref[pl.ds(k0, TK), :]
        vals = v_ref[pl.ds(k0, TK), :]
        col = cols[pl.ds(k0, TK), :]
        same = jnp.concatenate([col] * (TQ // 128), axis=1) == seg_row
        out = []
        dks = jnp.zeros((TK, width), jnp.float32)
        dvs = jnp.zeros((TK, width), jnp.float32)
        for h in range(heads):
            s = lax.dot_general(keys, qm[h], NT, preferred_element_type=jnp.float32)
            p = jnp.where(same, jnp.exp(s - lse[h:h + 1, :]), 0.0)
            dp = lax.dot_general(vals, dm[h], NT, preferred_element_type=jnp.float32)
            ds = (p * (dp - delta[h:h + 1, :])).astype(jnp.bfloat16)
            dvs = dvs + lax.dot_general(p.astype(jnp.bfloat16), dm[h], NN, preferred_element_type=jnp.float32)
            dks = dks + lax.dot_general(ds, qm[h], NN, preferred_element_type=jnp.float32)
            out.append(acc[h] + lax.dot_general(kt[h * HEAD:(h + 1) * HEAD, pl.ds(k0, TK)], ds, NN, preferred_element_type=jnp.float32))
        dk_acc[pl.ds(k0, TK), :] += dks
        dv_acc[pl.ds(k0, TK), :] += dvs
        return tuple(out)

    acc = lax.fori_loop(lo, hi, body, tuple(jnp.zeros((HEAD, TQ), jnp.float32) for _ in range(heads)))
    dq_ref[...] = (jnp.concatenate(acc, axis=0).T * HEAD ** -0.5).astype(jnp.bfloat16)

    @pl.when(tile == n // TQ - 1)
    def _():
        dk_ref[...] = dk_acc[...].astype(jnp.bfloat16)
        dv_ref[...] = dv_acc[...].astype(jnp.bfloat16)


def attend_backward(seg, q, k, v, o, do, lse):
    n, width = q.shape
    heads = width // HEAD
    whole = pl.BlockSpec(memory_space=pltpu.VMEM)
    rows = pl.BlockSpec((TQ, width), lambda t, s: (t, 0))
    return pl.pallas_call(
        functools.partial(bwd_kernel, n, heads),
        grid_spec=pltpu.PrefetchScalarGridSpec(
            num_scalar_prefetch=1,
            grid=(n // TQ,),
            in_specs=[whole, rows, whole, whole, rows, rows, pl.BlockSpec((8, TQ), lambda t, s: (0, t))],
            out_specs=[rows, whole, whole],
            scratch_shapes=[pltpu.VMEM((width, n), jnp.bfloat16), pltpu.VMEM((n, 128), jnp.float32), pltpu.VMEM((n, width), jnp.float32), pltpu.VMEM((n, width), jnp.float32)],
        ),
        out_shape=[jax.ShapeDtypeStruct((n, width), jnp.bfloat16)] * 3,
        compiler_params=pltpu.CompilerParams(vmem_limit_bytes=40 << 20),
        cost_estimate=pl.CostEstimate(flops=10 * heads * n * n * HEAD, bytes_accessed=16 * n * width, transcendentals=heads * n * n // 2),
        name="attend_backward",
    )(seg.reshape(-1), seg.reshape(1, -1), q, k, v, o, do, lse)


MESH_ID = pl.DeviceIdType.MESH
PARTS = 4


def remote(src, dst, send, recv, device):
    return pltpu.make_async_remote_copy(
        src_ref=src, dst_ref=dst, send_sem=send, recv_sem=recv, device_id=device, device_id_type=MESH_ID
    )


def greet(devices):
    barrier = pltpu.get_barrier_semaphore()
    for device in devices:
        pl.semaphore_signal(barrier, inc=1, device_id=device, device_id_type=MESH_ID)
    pl.semaphore_wait(barrier, len(devices))


def norm_unit(values):
    average = jnp.mean(values, axis=-1, keepdims=True)
    centered = values - average
    variance = jnp.mean(centered * centered, axis=-1, keepdims=True)
    inverse = lax.rsqrt(variance + epsilon)
    return centered * inverse, inverse


def project_kernel(
    dp_count, tokens_ref, gain_ref, w_ref, cot_ref, rows_ref, q_ref, k_ref, v_ref, returned_ref,
    across_send, across_recv, pair_send, pair_recv, pass_send, pass_recv, slot_send, slot_recv, self_sem,
):
    dp, mp = lax.axis_index("dp"), lax.axis_index("mp")
    pair, across, far = mp ^ 1, mp ^ 2, mp ^ 3
    own = tokens_ref.shape[0]
    part = own // PARTS
    greet([(dp, pair), (dp, across)] + [(lax.rem(dp + k, dp_count), mp) for k in range(1, dp_count)])

    def spot(owner, c, size):
        return pl.ds(pl.multiple_of(owner * own + c * size, size), size)

    def gather_copy(c, owner, device, send, recv):
        rows = rows_ref.at[spot(owner, c, part)]
        return remote(rows, rows, send.at[c], recv.at[c], device)

    def slot_copy(k):
        other = lax.rem(dp + k, dp_count)
        return remote(cot_ref.at[other], returned_ref.at[dp], slot_send.at[k], slot_recv.at[k], (other, mp))

    for c in range(PARTS):
        values = tokens_ref[c * part:(c + 1) * part, :].astype(jnp.float32)
        unit, _ = norm_unit(values)
        rows_ref[spot(mp, c, part), :] = (unit * gain_ref[...]).astype(jnp.bfloat16)
        gather_copy(c, mp, (dp, across), across_send, across_recv).start()
        gather_copy(c, mp, (dp, pair), pair_send, pair_recv).start()
    for k in range(1, dp_count):
        slot_copy(k).start()
    self_copy = pltpu.make_async_copy(cot_ref.at[dp], returned_ref.at[dp], self_sem)
    self_copy.start()

    def product(owner, half):
        where = spot(owner, half, own // 2)
        rows = rows_ref[where, :]
        for p, out in enumerate((q_ref, k_ref, v_ref)):
            out[where, :] = jnp.dot(rows, w_ref[p], preferred_element_type=jnp.float32).astype(jnp.bfloat16)

    def both(owner):
        def step(half, _):
            product(owner, half)
            return 0
        lax.fori_loop(0, 2, step, 0)

    both(mp)
    for c in range(PARTS):
        gather_copy(c, pair, (dp, pair), pair_send, pair_recv).wait_recv()
    both(pair)
    for half in range(2):
        for c in range(half * PARTS // 2, (half + 1) * PARTS // 2):
            gather_copy(c, across, (dp, across), across_send, across_recv).wait_recv()
            gather_copy(c, across, (dp, pair), pass_send, pass_recv).start()
        product(across, half)
    for half in range(2):
        for c in range(half * PARTS // 2, (half + 1) * PARTS // 2):
            gather_copy(c, far, (dp, pair), pass_send, pass_recv).wait_recv()
        product(far, half)
    for c in range(PARTS):
        gather_copy(c, mp, (dp, across), across_send, across_recv).wait_send()
        gather_copy(c, mp, (dp, pair), pair_send, pair_recv).wait_send()
        gather_copy(c, across, (dp, pair), pass_send, pass_recv).wait_send()
    self_copy.wait()
    for k in range(1, dp_count):
        slot_copy(k).wait_send()
        other = lax.rem(dp + dp_count - k, dp_count)
        remote(cot_ref.at[dp], returned_ref.at[other], slot_send.at[k], slot_recv.at[k], (other, mp)).wait_recv()


def project(tokens, gain, w_qkv, cot):
    own, width = tokens.shape
    dp_count = cot.shape[0]
    total = own * 4
    cols = w_qkv.shape[2]
    vmem = pl.BlockSpec(memory_space=pltpu.VMEM)
    hbm = pl.BlockSpec(memory_space=pl.ANY)
    dma = pltpu.SemaphoreType.DMA
    return pl.pallas_call(
        functools.partial(project_kernel, dp_count),
        out_shape=[jax.ShapeDtypeStruct((total, width), jnp.bfloat16)]
        + [jax.ShapeDtypeStruct((total, cols), jnp.bfloat16)] * 3
        + [jax.ShapeDtypeStruct(cot.shape, cot.dtype)],
        in_specs=[vmem, vmem, vmem, hbm],
        out_specs=[vmem] * 4 + [hbm],
        scratch_shapes=[dma((PARTS,))] * 6 + [dma((dp_count,))] * 2 + [dma],
        compiler_params=pltpu.CompilerParams(collective_id=1, has_side_effects=True, vmem_limit_bytes=40 << 20),
        cost_estimate=pl.CostEstimate(flops=6 * total * width * cols, bytes_accessed=10 * total * width, transcendentals=0),
        name="project",
    )(tokens, gain, w_qkv, cot)


def local(
    tokens, segment_ids, gene_owner, w_qkv, w_attn_out, w_up, w_down, gain_attn, gain_mlp, cotangent
):
    width = tokens.shape[1]
    dp_count = lax.axis_size("dp")
    capacity = cotangent.shape[0] // dp_count
    own_rows = tokens.shape[0]
    contract_last = (((1,), (1,)), ((), ()))
    contract_first = (((0,), (0,)), ((), ()))
    low = jnp.bfloat16

    def scatter_sum(partial):
        return lax.psum_scatter(partial.astype(low), "mp", scatter_dimension=0, tiled=True).astype(jnp.float32)

    owners = gene_owner[:, 0]
    place = jnp.arange(own_rows, dtype=jnp.int32)
    earlier = (owners[:, None] == owners[None, :]) & (place[None, :] < place[:, None])
    slots = owners * capacity + jnp.sum(earlier.astype(jnp.int32), axis=1)
    onehot = (slots[:, None] == jnp.arange(dp_count * capacity, dtype=jnp.int32)[None, :]).astype(low)

    tokens_f = tokens.astype(jnp.float32)
    normed_one, unit_one, inverse_one = norm_parts(tokens_f, gain_attn)
    attn_in, *projected, returned = project(
        tokens, gain_attn.reshape(1, -1), w_qkv, cotangent.reshape(dp_count, capacity, width)
    )
    returned = returned.reshape(dp_count * capacity, width)
    merged, log_sums = attend_forward(segment_ids, *projected)
    residual = tokens_f + scatter_sum(jnp.dot(merged, w_attn_out, preferred_element_type=jnp.float32))
    normed_two, unit_two, inverse_two = norm_parts(residual, gain_mlp)
    mlp_rows = lax.all_gather(normed_two.astype(low), "mp", axis=0, tiled=True)
    grad_block = jnp.dot(onehot, returned, preferred_element_type=jnp.float32).astype(low)
    grad_rows = lax.all_gather(grad_block, "mp", axis=0, tiled=True)
    pre_act = jnp.dot(mlp_rows, w_up, preferred_element_type=jnp.float32)
    activated = gelu_exact(pre_act).astype(low)
    grad_act = jnp.dot(grad_rows, w_down, preferred_element_type=jnp.float32)
    grad_pre = (grad_act * gelu_slope(pre_act)).astype(low)
    grad_mlp_in = scatter_sum(
        lax.dot_general(grad_pre, w_up, contract_last, preferred_element_type=jnp.float32)
    )
    grad_down_local = lax.dot_general(
        grad_rows, activated, contract_first, preferred_element_type=jnp.float32
    ).astype(low)
    grad_up_local = lax.dot_general(
        mlp_rows, grad_pre, contract_first, preferred_element_type=jnp.float32
    ).astype(low)
    norm_two_grad, gain_mlp_grad = norm_back(grad_mlp_in, unit_two, inverse_two, gain_mlp)
    up_sum, down_sum = lax.psum((grad_up_local, grad_down_local), "dp")
    output = residual + scatter_sum(
        lax.dot_general(activated, w_down, contract_last, preferred_element_type=jnp.float32)
    )
    outgoing = lax.dot_general(
        onehot, output.astype(low), contract_first, preferred_element_type=jnp.float32
    ).astype(low)
    relaid = lax.all_to_all(
        outgoing.reshape(dp_count, capacity, width), "dp", split_axis=0, concat_axis=0, tiled=True
    ).reshape(dp_count * capacity, width)
    grad_residual = grad_block.astype(jnp.float32) + norm_two_grad
    residual_rows = lax.all_gather(grad_residual.astype(low), "mp", axis=0, tiled=True)
    grad_attn_local = lax.dot_general(
        merged, residual_rows, contract_first, preferred_element_type=jnp.float32
    ).astype(low)
    grad_merged = lax.dot_general(
        residual_rows, w_attn_out, contract_last, preferred_element_type=jnp.float32
    ).astype(low)
    grad_proj = attend_backward(segment_ids, *projected, merged, grad_merged, log_sums)
    grad_attn_in = scatter_sum(
        sum(
            lax.dot_general(grad_proj[p], w_qkv[p], contract_last, preferred_element_type=jnp.float32)
            for p in range(3)
        )
    )
    grad_qkv_local = jnp.stack(
        [
            lax.dot_general(attn_in, grad_proj[p], contract_first, preferred_element_type=jnp.float32).astype(low)
            for p in range(3)
        ]
    )
    grad_qkv_local, up_sum, down_sum = lax.optimization_barrier((grad_qkv_local, up_sum, down_sum))
    qkv_sum, attn_sum = lax.psum((grad_qkv_local, grad_attn_local), "dp")
    norm_one_grad, gain_attn_grad = norm_back(grad_attn_in, unit_one, inverse_one, gain_attn)
    grad_tokens = (grad_residual + norm_one_grad).astype(low)
    gain_attn_sum, gain_mlp_sum = lax.psum((gain_attn_grad, gain_mlp_grad), ("dp", "mp"))
    full = jnp.float32
    return (
        relaid,
        grad_tokens,
        qkv_sum.astype(full),
        attn_sum.astype(full),
        up_sum.astype(full),
        down_sum.astype(full),
        gain_attn_sum,
        gain_mlp_sum,
    )


def solution(mesh):
    placed = (
        P(("dp", "mp"), None),
        P("dp", None),
        P(("dp", "mp"), None),
        P(None, None, "mp"),
        P("mp", None),
        P(None, "mp"),
        P(None, "mp"),
        P(),
        P(),
        P(("dp", "mp"), None),
    )
    return jax.shard_map(
        local,
        mesh=mesh,
        in_specs=placed,
        out_specs=(
            P(("dp", "mp"), None),
            P(("dp", "mp"), None),
            P(None, None, "mp"),
            P("mp", None),
            P(None, "mp"),
            P(None, "mp"),
            P(),
            P(),
        ),
        check_vma=False,
    )
```

```python
import functools
import jax
import jax.numpy as jnp
from jax import lax
from jax.experimental import pallas as pl
from jax.experimental.pallas import tpu as pltpu
from jax.sharding import PartitionSpec as P

epsilon = 1e-05


def norm_parts(values, gain_vec):
    average = jnp.mean(values, axis=-1, keepdims=True)
    centered = values - average
    variance = jnp.mean(centered * centered, axis=-1, keepdims=True)
    inverse = lax.rsqrt(variance + epsilon)
    unit_rows = centered * inverse
    return (unit_rows * gain_vec, unit_rows, inverse)


def norm_back(grad_normed, unit_rows, inverse, gain_vec):
    scaled = grad_normed * gain_vec
    first_mean = jnp.mean(scaled, axis=-1, keepdims=True)
    second_mean = jnp.mean(scaled * unit_rows, axis=-1, keepdims=True)
    grad_input = inverse * (scaled - first_mean - unit_rows * second_mean)
    return (grad_input, jnp.sum(grad_normed * unit_rows, axis=0))


def gelu_exact(values):
    return 0.5 * values * (1.0 + lax.erf(values * 0.7071067811865476))


def gelu_slope(values):
    cumulative = 0.5 * (1.0 + lax.erf(values * 0.7071067811865476))
    density = jnp.exp(-0.5 * values * values) * 0.3989422804014327
    return cumulative + values * density


HEAD = 64
TQ = 256
TK = 256
NT = (((1,), (1,)), ((), ()))
NN = (((1,), (0,)), ((), ()))
TN = (((0,), (0,)), ((), ()))
MASKED = -1e30


def lower_bound(seg, n, value):
    def step(_, c):
        lo, hi = c
        mid = (lo + hi) // 2
        less = seg[jnp.minimum(mid, n - 1)] < value
        go = lo < hi
        return (jnp.where(go & less, mid + 1, lo), jnp.where(go & ~less, mid, hi))
    lo, hi = lax.fori_loop(0, n.bit_length(), step, (jnp.int32(0), jnp.int32(n)))
    return lo


def key_range(seg, n, tile):
    first = lower_bound(seg, n, seg[tile * TQ])
    end = lower_bound(seg, n, seg[tile * TQ + TQ - 1] + 1)
    return first // TK, (end + TK - 1) // TK


def head_masks(width, heads):
    lane = lax.broadcasted_iota(jnp.int32, (1, width), 1)
    return [(lane // HEAD == h) for h in range(heads)]


def seg_columns(segv_ref, cols, n):
    for t in range(n // 128):
        row = segv_ref[0:1, t * 128:(t + 1) * 128].astype(jnp.float32)
        cols[t * 128:(t + 1) * 128, :] = jnp.broadcast_to(row, (128, 128)).T


def fwd_kernel(n, heads, seg, segv_ref, q_ref, k_ref, v_ref, o_ref, lse_ref, vt, cols, scores):
    tile = pl.program_id(0)
    width = heads * HEAD

    @pl.when(tile == 0)
    def _():
        seg_columns(segv_ref, cols, n)
        for t in range(n // TK):
            vt[:, t * TK:(t + 1) * TK] = v_ref[t * TK:(t + 1) * TK, :].astype(jnp.float32).T.astype(jnp.bfloat16)

    lo, hi = key_range(seg, n, tile)
    q0 = pl.multiple_of(tile * TQ, TQ)
    q = q_ref[...] * jnp.bfloat16(HEAD ** -0.5)
    masks = head_masks(width, heads)
    qm = [jnp.where(m, q, jnp.bfloat16(0)) for m in masks]
    seg_row = segv_ref[0:1, pl.ds(q0, TQ)].astype(jnp.float32)

    def first(b, tops):
        k0 = pl.multiple_of(b * TK, TK)
        keys = k_ref[pl.ds(k0, TK), :]
        col = cols[pl.ds(k0, TK), :]
        same = jnp.concatenate([col] * (TQ // 128), axis=1) == seg_row
        out = []
        for h in range(heads):
            s = lax.dot_general(keys, qm[h], NT, preferred_element_type=jnp.float32)
            s = jnp.where(same, s, MASKED)
            scores[h, pl.ds(k0, TK), :] = s
            out.append(jnp.maximum(tops[h], jnp.max(s, axis=0, keepdims=True)))
        return tuple(out)

    tops = lax.fori_loop(lo, hi, first, tuple(jnp.full((1, TQ), MASKED, jnp.float32) for _ in range(heads)))

    def second(b, acc):
        k0 = pl.multiple_of(b * TK, TK)
        out = []
        for h in range(heads):
            p = jnp.exp(scores[h, pl.ds(k0, TK), :] - tops[h])
            total = acc[h][1] + jnp.sum(p, axis=0, keepdims=True)
            part = lax.dot_general(vt[h * HEAD:(h + 1) * HEAD, pl.ds(k0, TK)], p.astype(jnp.bfloat16), NN, preferred_element_type=jnp.float32)
            out.append((acc[h][0] + part, total))
        return tuple(out)

    acc = lax.fori_loop(lo, hi, second, tuple((jnp.zeros((HEAD, TQ), jnp.float32), jnp.zeros((1, TQ), jnp.float32)) for _ in range(heads)))
    ot = jnp.concatenate([acc[h][0] / acc[h][1] for h in range(heads)], axis=0)
    o_ref[...] = ot.T.astype(jnp.bfloat16)
    lse_ref[...] = jnp.concatenate([tops[h] + jnp.log(acc[h][1]) for h in range(heads)] + [jnp.zeros((8 - heads, TQ), jnp.float32)], axis=0)


def attend_forward(seg, q, k, v):
    n, width = q.shape
    heads = width // HEAD
    whole = pl.BlockSpec(memory_space=pltpu.VMEM)
    return pl.pallas_call(
        functools.partial(fwd_kernel, n, heads),
        grid_spec=pltpu.PrefetchScalarGridSpec(
            num_scalar_prefetch=1,
            grid=(n // TQ,),
            in_specs=[whole, pl.BlockSpec((TQ, width), lambda t, s: (t, 0)), whole, whole],
            out_specs=[pl.BlockSpec((TQ, width), lambda t, s: (t, 0)), pl.BlockSpec((8, TQ), lambda t, s: (0, t))],
            scratch_shapes=[pltpu.VMEM((width, n), jnp.bfloat16), pltpu.VMEM((n, 128), jnp.float32), pltpu.VMEM((heads, n, TQ), jnp.float32)],
        ),
        out_shape=[jax.ShapeDtypeStruct((n, width), jnp.bfloat16), jax.ShapeDtypeStruct((8, n), jnp.float32)],
        compiler_params=pltpu.CompilerParams(vmem_limit_bytes=40 << 20),
        cost_estimate=pl.CostEstimate(flops=4 * heads * n * n * HEAD, bytes_accessed=8 * n * width, transcendentals=heads * n * n // 2),
        name="attend_forward",
    )(seg.reshape(-1), seg.reshape(1, -1), q, k, v)


def bwd_kernel(n, heads, seg, segv_ref, q_ref, k_ref, v_ref, o_ref, do_ref, lse_ref, dq_ref, dk_ref, dv_ref, kt, cols, dk_acc, dv_acc):
    tile = pl.program_id(0)
    width = heads * HEAD

    @pl.when(tile == 0)
    def _():
        seg_columns(segv_ref, cols, n)
        for t in range(n // TK):
            kt[:, t * TK:(t + 1) * TK] = k_ref[t * TK:(t + 1) * TK, :].astype(jnp.float32).T.astype(jnp.bfloat16)
        dk_acc[...] = jnp.zeros_like(dk_acc)
        dv_acc[...] = jnp.zeros_like(dv_acc)

    lo, hi = key_range(seg, n, tile)
    q0 = pl.multiple_of(tile * TQ, TQ)
    masks = head_masks(width, heads)
    q = q_ref[...] * jnp.bfloat16(HEAD ** -0.5)
    do = do_ref[...]
    qm = [jnp.where(m, q, jnp.bfloat16(0)) for m in masks]
    dm = [jnp.where(m, do, jnp.bfloat16(0)) for m in masks]
    seg_row = segv_ref[0:1, pl.ds(q0, TQ)].astype(jnp.float32)
    prod = do.astype(jnp.float32) * o_ref[...].astype(jnp.float32)
    high = prod.astype(jnp.bfloat16)
    rest = (prod - high.astype(jnp.float32)).astype(jnp.bfloat16)
    row = lax.broadcasted_iota(jnp.int32, (16, width), 0)
    lane = lax.broadcasted_iota(jnp.int32, (16, width), 1)
    pick = jnp.where(lane // HEAD == row, 1.0, 0.0).astype(jnp.bfloat16)
    delta = lax.dot_general(pick, high, NT, preferred_element_type=jnp.float32) + lax.dot_general(pick, rest, NT, preferred_element_type=jnp.float32)
    lse = lse_ref[...]

    def body(b, acc):
        k0 = pl.multiple_of(b * TK, TK)
        keys = k_ref[pl.ds(k0, TK), :]
        vals = v_ref[pl.ds(k0, TK), :]
        col = cols[pl.ds(k0, TK), :]
        same = jnp.concatenate([col] * (TQ // 128), axis=1) == seg_row
        out = []
        dks = jnp.zeros((TK, width), jnp.float32)
        dvs = jnp.zeros((TK, width), jnp.float32)
        for h in range(heads):
            s = lax.dot_general(keys, qm[h], NT, preferred_element_type=jnp.float32)
            p = jnp.where(same, jnp.exp(s - lse[h:h + 1, :]), 0.0)
            dp = lax.dot_general(vals, dm[h], NT, preferred_element_type=jnp.float32)
            ds = (p * (dp - delta[h:h + 1, :])).astype(jnp.bfloat16)
            dvs = dvs + lax.dot_general(p.astype(jnp.bfloat16), dm[h], NN, preferred_element_type=jnp.float32)
            dks = dks + lax.dot_general(ds, qm[h], NN, preferred_element_type=jnp.float32)
            out.append(acc[h] + lax.dot_general(kt[h * HEAD:(h + 1) * HEAD, pl.ds(k0, TK)], ds, NN, preferred_element_type=jnp.float32))
        dk_acc[pl.ds(k0, TK), :] += dks
        dv_acc[pl.ds(k0, TK), :] += dvs
        return tuple(out)

    acc = lax.fori_loop(lo, hi, body, tuple(jnp.zeros((HEAD, TQ), jnp.float32) for _ in range(heads)))
    dq_ref[...] = (jnp.concatenate(acc, axis=0).T * HEAD ** -0.5).astype(jnp.bfloat16)

    @pl.when(tile == n // TQ - 1)
    def _():
        dk_ref[...] = dk_acc[...].astype(jnp.bfloat16)
        dv_ref[...] = dv_acc[...].astype(jnp.bfloat16)


def attend_backward(seg, q, k, v, o, do, lse):
    n, width = q.shape
    heads = width // HEAD
    whole = pl.BlockSpec(memory_space=pltpu.VMEM)
    rows = pl.BlockSpec((TQ, width), lambda t, s: (t, 0))
    return pl.pallas_call(
        functools.partial(bwd_kernel, n, heads),
        grid_spec=pltpu.PrefetchScalarGridSpec(
            num_scalar_prefetch=1,
            grid=(n // TQ,),
            in_specs=[whole, rows, whole, whole, rows, rows, pl.BlockSpec((8, TQ), lambda t, s: (0, t))],
            out_specs=[rows, whole, whole],
            scratch_shapes=[pltpu.VMEM((width, n), jnp.bfloat16), pltpu.VMEM((n, 128), jnp.float32), pltpu.VMEM((n, width), jnp.float32), pltpu.VMEM((n, width), jnp.float32)],
        ),
        out_shape=[jax.ShapeDtypeStruct((n, width), jnp.bfloat16)] * 3,
        compiler_params=pltpu.CompilerParams(vmem_limit_bytes=40 << 20),
        cost_estimate=pl.CostEstimate(flops=10 * heads * n * n * HEAD, bytes_accessed=16 * n * width, transcendentals=heads * n * n // 2),
        name="attend_backward",
    )(seg.reshape(-1), seg.reshape(1, -1), q, k, v, o, do, lse)


MESH_ID = pl.DeviceIdType.MESH
PARTS = 4


def remote(src, dst, send, recv, device):
    return pltpu.make_async_remote_copy(
        src_ref=src, dst_ref=dst, send_sem=send, recv_sem=recv, device_id=device, device_id_type=MESH_ID
    )


def greet(devices):
    barrier = pltpu.get_barrier_semaphore()
    for device in devices:
        pl.semaphore_signal(barrier, inc=1, device_id=device, device_id_type=MESH_ID)
    pl.semaphore_wait(barrier, len(devices))


def norm_unit(values):
    average = jnp.mean(values, axis=-1, keepdims=True)
    centered = values - average
    variance = jnp.mean(centered * centered, axis=-1, keepdims=True)
    inverse = lax.rsqrt(variance + epsilon)
    return centered * inverse, inverse


def project_kernel(
    dp_count, tokens_ref, gain_ref, w_ref, cot_ref, rows_ref, q_ref, k_ref, v_ref, returned_ref,
    across_send, across_recv, pair_send, pair_recv, pass_send, pass_recv, slot_send, slot_recv, self_sem,
):
    dp, mp = lax.axis_index("dp"), lax.axis_index("mp")
    pair, across, far = mp ^ 1, mp ^ 2, mp ^ 3
    own = tokens_ref.shape[0]
    part = own // PARTS
    greet([(dp, pair), (dp, across)] + [(lax.rem(dp + k, dp_count), mp) for k in range(1, dp_count)])

    def spot(owner, c, size):
        return pl.ds(pl.multiple_of(owner * own + c * size, size), size)

    def gather_copy(c, owner, device, send, recv):
        rows = rows_ref.at[spot(owner, c, part)]
        return remote(rows, rows, send.at[c], recv.at[c], device)

    def slot_copy(k):
        other = lax.rem(dp + k, dp_count)
        return remote(cot_ref.at[other], returned_ref.at[dp], slot_send.at[k], slot_recv.at[k], (other, mp))

    for c in range(PARTS):
        values = tokens_ref[c * part:(c + 1) * part, :].astype(jnp.float32)
        unit, _ = norm_unit(values)
        rows_ref[spot(mp, c, part), :] = (unit * gain_ref[...]).astype(jnp.bfloat16)
        gather_copy(c, mp, (dp, across), across_send, across_recv).start()
        gather_copy(c, mp, (dp, pair), pair_send, pair_recv).start()
    for k in range(1, dp_count):
        slot_copy(k).start()
    self_copy = pltpu.make_async_copy(cot_ref.at[dp], returned_ref.at[dp], self_sem)
    self_copy.start()

    def product(owner, half):
        where = spot(owner, half, own // 2)
        rows = rows_ref[where, :]
        for p, out in enumerate((q_ref, k_ref, v_ref)):
            out[where, :] = jnp.dot(rows, w_ref[p], preferred_element_type=jnp.float32).astype(jnp.bfloat16)

    def both(owner):
        def step(half, _):
            product(owner, half)
            return 0
        lax.fori_loop(0, 2, step, 0)

    both(mp)
    for c in range(PARTS):
        gather_copy(c, pair, (dp, pair), pair_send, pair_recv).wait_recv()
    both(pair)
    for half in range(2):
        for c in range(half * PARTS // 2, (half + 1) * PARTS // 2):
            gather_copy(c, across, (dp, across), across_send, across_recv).wait_recv()
            gather_copy(c, across, (dp, pair), pass_send, pass_recv).start()
        product(across, half)
    for half in range(2):
        for c in range(half * PARTS // 2, (half + 1) * PARTS // 2):
            gather_copy(c, far, (dp, pair), pass_send, pass_recv).wait_recv()
        product(far, half)
    for c in range(PARTS):
        gather_copy(c, mp, (dp, across), across_send, across_recv).wait_send()
        gather_copy(c, mp, (dp, pair), pair_send, pair_recv).wait_send()
        gather_copy(c, across, (dp, pair), pass_send, pass_recv).wait_send()
    self_copy.wait()
    for k in range(1, dp_count):
        slot_copy(k).wait_send()
        other = lax.rem(dp + dp_count - k, dp_count)
        remote(cot_ref.at[dp], returned_ref.at[other], slot_send.at[k], slot_recv.at[k], (other, mp)).wait_recv()


def project(tokens, gain, w_qkv, cot):
    own, width = tokens.shape
    dp_count = cot.shape[0]
    total = own * 4
    cols = w_qkv.shape[2]
    vmem = pl.BlockSpec(memory_space=pltpu.VMEM)
    hbm = pl.BlockSpec(memory_space=pl.ANY)
    dma = pltpu.SemaphoreType.DMA
    return pl.pallas_call(
        functools.partial(project_kernel, dp_count),
        out_shape=[jax.ShapeDtypeStruct((total, width), jnp.bfloat16)]
        + [jax.ShapeDtypeStruct((total, cols), jnp.bfloat16)] * 3
        + [jax.ShapeDtypeStruct(cot.shape, cot.dtype)],
        in_specs=[vmem, vmem, vmem, hbm],
        out_specs=[vmem] * 4 + [hbm],
        scratch_shapes=[dma((PARTS,))] * 6 + [dma((dp_count,))] * 2 + [dma],
        compiler_params=pltpu.CompilerParams(collective_id=1, has_side_effects=True, vmem_limit_bytes=40 << 20),
        cost_estimate=pl.CostEstimate(flops=6 * total * width * cols, bytes_accessed=10 * total * width, transcendentals=0),
        name="project",
    )(tokens, gain, w_qkv, cot)


def gelu_and_slope(values):
    cumulative = 0.5 * (1.0 + lax.erf(values * 0.7071067811865476))
    density = jnp.exp(-0.5 * values * values) * 0.3989422804014327
    return values * cumulative, cumulative + values * density


def middle_kernel(
    merged_ref, w_out_ref, tokens_ref, gain_ref, w_up_ref, w_down_ref, grad_own_ref, grad_across_ref,
    back_rows_ref, grad_merged_ref, grad_residual_ref, output_ref, d_up_ref, d_down_ref, d_out_ref,
    mlp_rows, grad_rows, active, grad_pre, residual, mine, bufs,
    sum_send, sum_recv, row_send, row_recv, grad_send, grad_recv, self_sem,
):
    low, full = jnp.bfloat16, jnp.float32
    dp, mp = lax.axis_index("dp"), lax.axis_index("mp")
    pair, across, far = mp ^ 1, mp ^ 2, mp ^ 3
    own, width = tokens_ref.shape
    part = own // PARTS
    to_pair, to_across = (dp, pair), (dp, across)
    greet([to_pair, to_across])

    def spot(owner, c=None):
        if c is None:
            return pl.ds(pl.multiple_of(owner * own, own), own)
        return pl.ds(pl.multiple_of(owner * own + c * part, part), part)

    def piece(c):
        return pl.ds(pl.multiple_of(c * part, part), part)

    def grad_copy(i, owner, src):
        return remote(src, grad_rows.at[spot(owner)], grad_send.at[i], grad_recv.at[i], to_pair)

    local_copies = [
        pltpu.make_async_copy(grad_own_ref, grad_rows.at[spot(mp)], self_sem.at[0]),
        pltpu.make_async_copy(grad_across_ref, grad_rows.at[spot(across)], self_sem.at[1]),
    ]

    FAR, ACROSS, PAIR = 0, 1, 2

    def sum_copy(which, kind, c):
        src, dst = bufs.at[which, 0, kind, piece(c)], bufs.at[which, 1, kind, piece(c)]
        return remote(src, dst, sum_send.at[which, kind, c], sum_recv.at[which, kind, c], to_across if kind == ACROSS else to_pair)

    def arrived(which, kind, c):
        sum_copy(which, kind, c).wait_recv()
        return bufs[which, 1, kind, piece(c), :].astype(full)

    def ship(which, kind, c, values):
        bufs[which, 0, kind, piece(c), :] = values.astype(low)
        sum_copy(which, kind, c).start()

    def row_copy(which, kind, c, owner, ref):
        rows = ref.at[spot(owner, c)]
        return remote(rows, rows, row_send.at[which, kind, c], row_recv.at[which, kind, c], to_across if kind == 0 else to_pair)

    def each(count, body):
        def step(i, _):
            body(i)
            return 0
        lax.fori_loop(0, count, step, 0)

    def out_part(owner):
        return jnp.dot(merged_ref[spot(owner), :], w_out_ref[...], preferred_element_type=full)

    bufs[0, 0, FAR] = out_part(far).astype(low)
    each(PARTS, lambda c: sum_copy(0, FAR, c).start())
    mine[0] = out_part(across)

    def pass_across(c):
        ship(0, ACROSS, c, mine[0, piece(c), :] + arrived(0, FAR, c))
    each(PARTS, pass_across)
    bufs[0, 0, PAIR] = out_part(pair).astype(low)
    each(PARTS, lambda c: sum_copy(0, PAIR, c).start())
    for copy in local_copies:
        copy.start()
    grad_copy(0, mp, grad_own_ref).start()
    grad_copy(1, across, grad_across_ref).start()
    mine[0] = out_part(mp) + tokens_ref[...].astype(full)
    for copy in local_copies:
        copy.wait()
    grad_copy(0, pair, grad_own_ref).wait_recv()
    grad_copy(1, far, grad_across_ref).wait_recv()

    blocks = w_up_ref.shape[1] // 256
    both = 2 * part

    def mlp(first, second, c):
        rows = jnp.concatenate([mlp_rows[spot(first, c), :], mlp_rows[spot(second, c), :]], axis=0)
        grads = jnp.concatenate([grad_rows[spot(first, c), :], grad_rows[spot(second, c), :]], axis=0)

        def block(b):
            cols = pl.ds(pl.multiple_of(b * 256, 256), 256)
            pre = jnp.dot(rows, w_up_ref[:, cols], preferred_element_type=full)
            value, slope = gelu_and_slope(pre)
            value = value.astype(low)
            active[spot(first, c), cols] = value[:part]
            active[spot(second, c), cols] = value[part:]
            back = (jnp.dot(grads, w_down_ref[:, cols], preferred_element_type=full) * slope).astype(low)
            grad_pre[spot(first, c), cols] = back[:part]
            grad_pre[spot(second, c), cols] = back[part:]
        each(blocks, block)
        back = jnp.concatenate([grad_pre[spot(first, c), :], grad_pre[spot(second, c), :]], axis=0)
        return lax.dot_general(back, w_up_ref[...], NT, preferred_element_type=full)

    def near(c):
        values = mine[0, piece(c), :] + arrived(0, PAIR, c) + arrived(0, ACROSS, c)
        residual[piece(c), :] = values
        unit, _ = norm_unit(values)
        mlp_rows[spot(mp, c), :] = (unit * gain_ref[...]).astype(low)
        row_copy(0, 0, c, mp, mlp_rows).start()
        row_copy(0, 1, c, mp, mlp_rows).start()
        row_copy(0, 1, c, pair, mlp_rows).wait_recv()
        got = mlp(mp, pair, c)
        mine[1, piece(c), :] = got[:part]
        ship(1, PAIR, c, got[part:])
    each(PARTS, near)

    def distant(c):
        row_copy(0, 0, c, across, mlp_rows).wait_recv()
        row_copy(0, 2, c, across, mlp_rows).start()
        row_copy(0, 2, c, far, mlp_rows).wait_recv()
        got = mlp(far, across, c)
        ship(1, FAR, c, got[:part])
        ship(1, ACROSS, c, got[part:] + arrived(1, FAR, c))
    each(PARTS, distant)

    def weight_block(b):
        cols = pl.ds(pl.multiple_of(b * 256, 256), 256)
        d_down_ref[cols, :] = lax.dot_general(grad_rows[:, cols], active[...], TN, preferred_element_type=full).astype(low)
        d_up_ref[cols, :] = lax.dot_general(mlp_rows[:, cols], grad_pre[...], TN, preferred_element_type=full).astype(low)
    each(width // 256, weight_block)

    def down_part(owner):
        return lax.dot_general(active[spot(owner), :], w_down_ref[...], NT, preferred_element_type=full)

    bufs[2, 0, FAR] = down_part(far).astype(low)
    each(PARTS, lambda c: sum_copy(2, FAR, c).start())
    bufs[2, 0, PAIR] = down_part(pair).astype(low)
    each(PARTS, lambda c: sum_copy(2, PAIR, c).start())

    def back_norm(c):
        grad = mine[1, piece(c), :] + arrived(1, PAIR, c) + arrived(1, ACROSS, c)
        unit, inverse = norm_unit(residual[piece(c), :])
        scaled = grad * gain_ref[...]
        first_mean = jnp.mean(scaled, axis=-1, keepdims=True)
        second_mean = jnp.mean(scaled * unit, axis=-1, keepdims=True)
        total = inverse * (scaled - first_mean - unit * second_mean) + grad_own_ref[piece(c), :].astype(full)
        grad_residual_ref[piece(c), :] = total
        back_rows_ref[spot(mp, c), :] = total.astype(low)
        row_copy(1, 0, c, mp, back_rows_ref).start()
        row_copy(1, 1, c, mp, back_rows_ref).start()
    each(PARTS, back_norm)

    mine[1] = down_part(across)

    def pass_output(c):
        ship(2, ACROSS, c, mine[1, piece(c), :] + arrived(2, FAR, c))
    each(PARTS, pass_output)
    mine[0] = residual[...] + down_part(mp)

    def merged_part(owner):
        grad_merged_ref[spot(owner), :] = lax.dot_general(
            back_rows_ref[spot(owner), :], w_out_ref[...], NT, preferred_element_type=full
        ).astype(low)

    merged_part(mp)
    each(PARTS, lambda c: row_copy(1, 1, c, pair, back_rows_ref).wait_recv())
    merged_part(pair)

    def hand_on(c):
        row_copy(1, 0, c, across, back_rows_ref).wait_recv()
        row_copy(1, 2, c, across, back_rows_ref).start()
    each(PARTS, hand_on)
    merged_part(across)
    each(PARTS, lambda c: row_copy(1, 2, c, far, back_rows_ref).wait_recv())
    merged_part(far)
    d_out_ref[...] = lax.dot_general(merged_ref[...], back_rows_ref[...], TN, preferred_element_type=full).astype(low)

    def finish(c):
        output_ref[piece(c), :] = (mine[0, piece(c), :] + arrived(2, PAIR, c) + arrived(2, ACROSS, c)).astype(low)
    each(PARTS, finish)

    def drain(c):
        for which in range(3):
            for kind in range(3):
                sum_copy(which, kind, c).wait_send()
        for which, ref in ((0, mlp_rows), (1, back_rows_ref)):
            row_copy(which, 0, c, mp, ref).wait_send()
            row_copy(which, 1, c, mp, ref).wait_send()
            row_copy(which, 2, c, across, ref).wait_send()
    each(PARTS, drain)
    grad_copy(0, mp, grad_own_ref).wait_send()
    grad_copy(1, across, grad_across_ref).wait_send()


def middle(merged, w_out, tokens, gain, w_up, w_down, grad_own, grad_across):
    total, cols = merged.shape
    own, width = tokens.shape
    hidden = w_up.shape[1]
    low, full = jnp.bfloat16, jnp.float32
    vmem = pl.BlockSpec(memory_space=pltpu.VMEM)
    dma = pltpu.SemaphoreType.DMA
    shape = jax.ShapeDtypeStruct
    return pl.pallas_call(
        middle_kernel,
        out_shape=[
            shape((total, width), low), shape((total, cols), low), shape((own, width), full), shape((own, width), low),
            shape((width, hidden), low), shape((width, hidden), low), shape((cols, width), low),
        ],
        in_specs=[vmem] * 8,
        out_specs=[vmem] * 7,
        scratch_shapes=[
            pltpu.VMEM((total, width), low), pltpu.VMEM((total, width), low),
            pltpu.VMEM((total, hidden), low), pltpu.VMEM((total, hidden), low),
            pltpu.VMEM((own, width), full), pltpu.VMEM((2, own, width), full),
            pltpu.VMEM((3, 2, 3, own, width), low),
            dma((3, 3, PARTS)), dma((3, 3, PARTS)), dma((2, 3, PARTS)), dma((2, 3, PARTS)), dma((2,)), dma((2,)), dma((2,)),
        ],
        compiler_params=pltpu.CompilerParams(collective_id=2, has_side_effects=True, vmem_limit_bytes=56 << 20),
        cost_estimate=pl.CostEstimate(flops=16 * total * width * hidden, bytes_accessed=20 * total * width, transcendentals=0),
        name="middle",
    )(merged, w_out, tokens, gain, w_up, w_down, grad_own, grad_across)


def local(
    tokens, segment_ids, gene_owner, w_qkv, w_attn_out, w_up, w_down, gain_attn, gain_mlp, cotangent
):
    width = tokens.shape[1]
    dp_count = lax.axis_size("dp")
    capacity = cotangent.shape[0] // dp_count
    own_rows = tokens.shape[0]
    contract_last = (((1,), (1,)), ((), ()))
    contract_first = (((0,), (0,)), ((), ()))
    low = jnp.bfloat16

    def scatter_sum(partial):
        return lax.psum_scatter(partial.astype(low), "mp", scatter_dimension=0, tiled=True).astype(jnp.float32)

    owners = gene_owner[:, 0]
    place = jnp.arange(own_rows, dtype=jnp.int32)
    earlier = (owners[:, None] == owners[None, :]) & (place[None, :] < place[:, None])
    slots = owners * capacity + jnp.sum(earlier.astype(jnp.int32), axis=1)
    onehot = (slots[:, None] == jnp.arange(dp_count * capacity, dtype=jnp.int32)[None, :]).astype(low)

    tokens_f = tokens.astype(jnp.float32)
    normed_one, unit_one, inverse_one = norm_parts(tokens_f, gain_attn)
    attn_in, *projected, returned = project(
        tokens, gain_attn.reshape(1, -1), w_qkv, cotangent.reshape(dp_count, capacity, width)
    )
    returned = returned.reshape(dp_count * capacity, width)
    grad_block = jnp.dot(onehot, returned, preferred_element_type=jnp.float32).astype(low)
    grad_across = lax.ppermute(grad_block, "mp", [(i, i ^ 2) for i in range(lax.axis_size("mp"))])
    merged, log_sums = attend_forward(segment_ids, *projected)
    residual_rows, grad_merged, grad_residual, output, grad_up_local, grad_down_local, grad_attn_local = middle(
        merged, w_attn_out, tokens, gain_mlp.reshape(1, -1), w_up, w_down, grad_block, grad_across
    )
    up_sum, down_sum = lax.psum((grad_up_local, grad_down_local), "dp")
    outgoing = lax.dot_general(onehot, output, contract_first, preferred_element_type=jnp.float32).astype(low)
    relaid = lax.all_to_all(
        outgoing.reshape(dp_count, capacity, width), "dp", split_axis=0, concat_axis=0, tiled=True
    ).reshape(dp_count * capacity, width)
    grad_proj = attend_backward(segment_ids, *projected, merged, grad_merged, log_sums)
    grad_attn_in = scatter_sum(
        sum(
            lax.dot_general(grad_proj[p], w_qkv[p], contract_last, preferred_element_type=jnp.float32)
            for p in range(3)
        )
    )
    grad_qkv_local = jnp.stack(
        [
            lax.dot_general(attn_in, grad_proj[p], contract_first, preferred_element_type=jnp.float32).astype(low)
            for p in range(3)
        ]
    )
    grad_qkv_local, up_sum, down_sum = lax.optimization_barrier((grad_qkv_local, up_sum, down_sum))
    qkv_sum, attn_sum = lax.psum((grad_qkv_local, grad_attn_local), "dp")
    norm_one_grad, gain_attn_grad = norm_back(grad_attn_in, unit_one, inverse_one, gain_attn)
    grad_tokens = (grad_residual + norm_one_grad).astype(low)
    gain_mlp_grad = jnp.sum(w_up.astype(jnp.float32) * up_sum.astype(jnp.float32), axis=1) / gain_mlp
    gain_attn_sum, gain_mlp_sum = lax.psum((gain_attn_grad, gain_mlp_grad / dp_count), ("dp", "mp"))
    full = jnp.float32
    return (
        relaid,
        grad_tokens,
        qkv_sum.astype(full),
        attn_sum.astype(full),
        up_sum.astype(full),
        down_sum.astype(full),
        gain_attn_sum,
        gain_mlp_sum,
    )


def solution(mesh):
    placed = (
        P(("dp", "mp"), None),
        P("dp", None),
        P(("dp", "mp"), None),
        P(None, None, "mp"),
        P("mp", None),
        P(None, "mp"),
        P(None, "mp"),
        P(),
        P(),
        P(("dp", "mp"), None),
    )
    return jax.shard_map(
        local,
        mesh=mesh,
        in_specs=placed,
        out_specs=(
            P(("dp", "mp"), None),
            P(("dp", "mp"), None),
            P(None, None, "mp"),
            P("mp", None),
            P(None, "mp"),
            P(None, "mp"),
            P(),
            P(),
        ),
        check_vma=False,
    )
```

```python
import functools
import jax
import jax.numpy as jnp
from jax import lax
from jax.experimental import pallas as pl
from jax.experimental.pallas import tpu as pltpu
from jax.sharding import PartitionSpec as P

HEAD = 64
TQ = 256
TK = 256
NT = (((1,), (1,)), ((), ()))
NN = (((1,), (0,)), ((), ()))
TN = (((0,), (0,)), ((), ()))
MASKED = -1e30
epsilon = 1e-05


def lower_bound(seg, n, value):
    def step(_, c):
        lo, hi = c
        mid = (lo + hi) // 2
        less = seg[jnp.minimum(mid, n - 1)] < value
        go = lo < hi
        return (jnp.where(go & less, mid + 1, lo), jnp.where(go & ~less, mid, hi))
    lo, hi = lax.fori_loop(0, n.bit_length(), step, (jnp.int32(0), jnp.int32(n)))
    return lo


def key_range(seg, n, tile):
    first = lower_bound(seg, n, seg[tile * TQ])
    end = lower_bound(seg, n, seg[tile * TQ + TQ - 1] + 1)
    return first // TK, (end + TK - 1) // TK


def head_masks(width, heads):
    lane = lax.broadcasted_iota(jnp.int32, (1, width), 1)
    return [(lane // HEAD == h) for h in range(heads)]


def seg_columns(segv_ref, cols, n):
    for t in range(n // 128):
        row = segv_ref[0:1, t * 128:(t + 1) * 128].astype(jnp.float32)
        cols[t * 128:(t + 1) * 128, :] = jnp.broadcast_to(row, (128, 128)).T


def fwd_kernel(n, heads, seg, segv_ref, q_ref, k_ref, v_ref, o_ref, lse_ref, vt, cols, scores):
    tile = pl.program_id(0)
    width = heads * HEAD

    @pl.when(tile == 0)
    def _():
        seg_columns(segv_ref, cols, n)
        for t in range(n // TK):
            vt[:, t * TK:(t + 1) * TK] = v_ref[t * TK:(t + 1) * TK, :].astype(jnp.float32).T.astype(jnp.bfloat16)

    lo, hi = key_range(seg, n, tile)
    q0 = pl.multiple_of(tile * TQ, TQ)
    q = q_ref[...] * jnp.bfloat16(HEAD ** -0.5)
    masks = head_masks(width, heads)
    qm = [jnp.where(m, q, jnp.bfloat16(0)) for m in masks]
    seg_row = segv_ref[0:1, pl.ds(q0, TQ)].astype(jnp.float32)

    def first(b, tops):
        k0 = pl.multiple_of(b * TK, TK)
        keys = k_ref[pl.ds(k0, TK), :]
        col = cols[pl.ds(k0, TK), :]
        same = jnp.concatenate([col] * (TQ // 128), axis=1) == seg_row
        out = []
        for h in range(heads):
            s = lax.dot_general(keys, qm[h], NT, preferred_element_type=jnp.float32)
            s = jnp.where(same, s, MASKED)
            scores[h, pl.ds(k0, TK), :] = s
            out.append(jnp.maximum(tops[h], jnp.max(s, axis=0, keepdims=True)))
        return tuple(out)

    tops = lax.fori_loop(lo, hi, first, tuple(jnp.full((1, TQ), MASKED, jnp.float32) for _ in range(heads)))

    def second(b, acc):
        k0 = pl.multiple_of(b * TK, TK)
        out = []
        for h in range(heads):
            p = jnp.exp(scores[h, pl.ds(k0, TK), :] - tops[h])
            total = acc[h][1] + jnp.sum(p, axis=0, keepdims=True)
            part = lax.dot_general(vt[h * HEAD:(h + 1) * HEAD, pl.ds(k0, TK)], p.astype(jnp.bfloat16), NN, preferred_element_type=jnp.float32)
            out.append((acc[h][0] + part, total))
        return tuple(out)

    acc = lax.fori_loop(lo, hi, second, tuple((jnp.zeros((HEAD, TQ), jnp.float32), jnp.zeros((1, TQ), jnp.float32)) for _ in range(heads)))
    ot = jnp.concatenate([acc[h][0] / acc[h][1] for h in range(heads)], axis=0)
    o_ref[...] = ot.T.astype(jnp.bfloat16)
    lse_ref[...] = jnp.concatenate([tops[h] + jnp.log(acc[h][1]) for h in range(heads)] + [jnp.zeros((8 - heads, TQ), jnp.float32)], axis=0)


def attend_forward(seg, q, k, v):
    n, width = q.shape
    heads = width // HEAD
    whole = pl.BlockSpec(memory_space=pltpu.VMEM)
    return pl.pallas_call(
        functools.partial(fwd_kernel, n, heads),
        grid_spec=pltpu.PrefetchScalarGridSpec(
            num_scalar_prefetch=1,
            grid=(n // TQ,),
            in_specs=[whole, pl.BlockSpec((TQ, width), lambda t, s: (t, 0)), whole, whole],
            out_specs=[pl.BlockSpec((TQ, width), lambda t, s: (t, 0)), pl.BlockSpec((8, TQ), lambda t, s: (0, t))],
            scratch_shapes=[pltpu.VMEM((width, n), jnp.bfloat16), pltpu.VMEM((n, 128), jnp.float32), pltpu.VMEM((heads, n, TQ), jnp.float32)],
        ),
        out_shape=[jax.ShapeDtypeStruct((n, width), jnp.bfloat16), jax.ShapeDtypeStruct((8, n), jnp.float32)],
        compiler_params=pltpu.CompilerParams(vmem_limit_bytes=40 << 20),
        cost_estimate=pl.CostEstimate(flops=4 * heads * n * n * HEAD, bytes_accessed=8 * n * width, transcendentals=heads * n * n // 2),
        name="attend_forward",
    )(seg.reshape(-1), seg.reshape(1, -1), q, k, v)


def bwd_kernel(n, heads, seg, segv_ref, q_ref, k_ref, v_ref, o_ref, do_ref, lse_ref, dq_ref, dk_ref, dv_ref, kt, cols, dk_acc, dv_acc):
    tile = pl.program_id(0)
    width = heads * HEAD

    @pl.when(tile == 0)
    def _():
        seg_columns(segv_ref, cols, n)
        for t in range(n // TK):
            kt[:, t * TK:(t + 1) * TK] = k_ref[t * TK:(t + 1) * TK, :].astype(jnp.float32).T.astype(jnp.bfloat16)
        dk_acc[...] = jnp.zeros_like(dk_acc)
        dv_acc[...] = jnp.zeros_like(dv_acc)

    lo, hi = key_range(seg, n, tile)
    q0 = pl.multiple_of(tile * TQ, TQ)
    masks = head_masks(width, heads)
    q = q_ref[...] * jnp.bfloat16(HEAD ** -0.5)
    do = do_ref[...]
    qm = [jnp.where(m, q, jnp.bfloat16(0)) for m in masks]
    dm = [jnp.where(m, do, jnp.bfloat16(0)) for m in masks]
    seg_row = segv_ref[0:1, pl.ds(q0, TQ)].astype(jnp.float32)
    prod = do.astype(jnp.float32) * o_ref[...].astype(jnp.float32)
    high = prod.astype(jnp.bfloat16)
    rest = (prod - high.astype(jnp.float32)).astype(jnp.bfloat16)
    row = lax.broadcasted_iota(jnp.int32, (16, width), 0)
    lane = lax.broadcasted_iota(jnp.int32, (16, width), 1)
    pick = jnp.where(lane // HEAD == row, 1.0, 0.0).astype(jnp.bfloat16)
    delta = lax.dot_general(pick, high, NT, preferred_element_type=jnp.float32) + lax.dot_general(pick, rest, NT, preferred_element_type=jnp.float32)
    lse = lse_ref[...]

    def body(b, acc):
        k0 = pl.multiple_of(b * TK, TK)
        keys = k_ref[pl.ds(k0, TK), :]
        vals = v_ref[pl.ds(k0, TK), :]
        col = cols[pl.ds(k0, TK), :]
        same = jnp.concatenate([col] * (TQ // 128), axis=1) == seg_row
        out = []
        dks = jnp.zeros((TK, width), jnp.float32)
        dvs = jnp.zeros((TK, width), jnp.float32)
        for h in range(heads):
            s = lax.dot_general(keys, qm[h], NT, preferred_element_type=jnp.float32)
            p = jnp.where(same, jnp.exp(s - lse[h:h + 1, :]), 0.0)
            dp = lax.dot_general(vals, dm[h], NT, preferred_element_type=jnp.float32)
            ds = (p * (dp - delta[h:h + 1, :])).astype(jnp.bfloat16)
            dvs = dvs + lax.dot_general(p.astype(jnp.bfloat16), dm[h], NN, preferred_element_type=jnp.float32)
            dks = dks + lax.dot_general(ds, qm[h], NN, preferred_element_type=jnp.float32)
            out.append(acc[h] + lax.dot_general(kt[h * HEAD:(h + 1) * HEAD, pl.ds(k0, TK)], ds, NN, preferred_element_type=jnp.float32))
        dk_acc[pl.ds(k0, TK), :] += dks
        dv_acc[pl.ds(k0, TK), :] += dvs
        return tuple(out)

    acc = lax.fori_loop(lo, hi, body, tuple(jnp.zeros((HEAD, TQ), jnp.float32) for _ in range(heads)))
    dq_ref[...] = (jnp.concatenate(acc, axis=0).T * HEAD ** -0.5).astype(jnp.bfloat16)

    @pl.when(tile == n // TQ - 1)
    def _():
        dk_ref[...] = dk_acc[...].astype(jnp.bfloat16)
        dv_ref[...] = dv_acc[...].astype(jnp.bfloat16)


def attend_backward(seg, q, k, v, o, do, lse):
    n, width = q.shape
    heads = width // HEAD
    whole = pl.BlockSpec(memory_space=pltpu.VMEM)
    rows = pl.BlockSpec((TQ, width), lambda t, s: (t, 0))
    return pl.pallas_call(
        functools.partial(bwd_kernel, n, heads),
        grid_spec=pltpu.PrefetchScalarGridSpec(
            num_scalar_prefetch=1,
            grid=(n // TQ,),
            in_specs=[whole, rows, whole, whole, rows, rows, pl.BlockSpec((8, TQ), lambda t, s: (0, t))],
            out_specs=[rows, whole, whole],
            scratch_shapes=[pltpu.VMEM((width, n), jnp.bfloat16), pltpu.VMEM((n, 128), jnp.float32), pltpu.VMEM((n, width), jnp.float32), pltpu.VMEM((n, width), jnp.float32)],
        ),
        out_shape=[jax.ShapeDtypeStruct((n, width), jnp.bfloat16)] * 3,
        compiler_params=pltpu.CompilerParams(vmem_limit_bytes=40 << 20),
        cost_estimate=pl.CostEstimate(flops=10 * heads * n * n * HEAD, bytes_accessed=16 * n * width, transcendentals=heads * n * n // 2),
        name="attend_backward",
    )(seg.reshape(-1), seg.reshape(1, -1), q, k, v, o, do, lse)


MESH_ID = pl.DeviceIdType.MESH
PARTS = 4
MLP_CHUNKS = 3
QKV_CHUNKS = 3


def remote(src, dst, send, recv, device):
    return pltpu.make_async_remote_copy(
        src_ref=src, dst_ref=dst, send_sem=send, recv_sem=recv, device_id=device, device_id_type=MESH_ID
    )


def greet(devices):
    barrier = pltpu.get_barrier_semaphore()
    for device in devices:
        pl.semaphore_signal(barrier, inc=1, device_id=device, device_id_type=MESH_ID)
    pl.semaphore_wait(barrier, len(devices))


def norm_unit(values):
    average = jnp.mean(values, axis=-1, keepdims=True)
    centered = values - average
    variance = jnp.mean(centered * centered, axis=-1, keepdims=True)
    inverse = lax.rsqrt(variance + epsilon)
    return centered * inverse, inverse


def sum_stages(rows, chunks, dp_count):
    stages = dp_count.bit_length() - 1
    return stages if dp_count == 1 << stages and rows % (16 * chunks * dp_count) == 0 else 0


def sum_scratch(rows, width, chunks, stages):
    dma = pltpu.SemaphoreType.DMA
    return [
        pltpu.VMEM((rows, width), jnp.bfloat16), pltpu.VMEM((rows, width), jnp.bfloat16),
        dma((chunks, max(1, 2 * stages))), dma((chunks, max(1, 2 * stages))),
    ]


def sum_steps(stages, chunks, acc, came, send, recv, out):
    dp, mp = lax.axis_index("dp"), lax.axis_index("mp")
    chunk = acc.shape[0] // chunks

    def bit(s):
        return lax.rem(dp // (1 << s), 2)

    def held(k, s):
        start = k * chunk
        for j in range(s):
            start = start + bit(j) * (chunk >> (j + 1))
        return start

    def span(start, size):
        return pl.ds(pl.multiple_of(start, 16), size)

    def halve(k, s):
        size = chunk >> (s + 1)
        return remote(
            acc.at[span(held(k, s) + (1 - bit(s)) * size, size)],
            came.at[span(k * chunk + chunk - (chunk >> s), size)],
            send.at[k, s], recv.at[k, s], (dp ^ (1 << s), mp),
        )

    def double(k, s, mine=True):
        size = chunk >> (s + 1)
        rows = out.at[span(held(k, s + 1) if mine else held(k, s) + (1 - bit(s)) * size, size)]
        return remote(rows, rows, send.at[k, stages + s], recv.at[k, stages + s], (dp ^ (1 << s), mp))

    def step(k, i):
        if i == 0:
            halve(k, 0).start()
        elif i <= stages:
            halve(k, i - 1).wait_recv()
            size = chunk >> i
            rows = span(held(k, i), size)
            total = acc[rows, :].astype(jnp.float32) + came[span(k * chunk + chunk - (chunk >> (i - 1)), size), :].astype(jnp.float32)
            if i < stages:
                acc[rows, :] = total.astype(jnp.bfloat16)
                halve(k, i).start()
            else:
                out[rows, :] = total.astype(jnp.bfloat16)
                double(k, stages - 1).start()
        else:
            s = 2 * stages - i
            double(k, s, False).wait_recv()
            if s > 0:
                double(k, s - 1).start()

    def drain():
        for k in range(chunks):
            for s in range(stages):
                halve(k, s).wait_send()
                double(k, s).wait_send()

    return step, drain


def project_kernel(
    dp_count, tokens_ref, gain_ref, w_ref, cot_ref, rows_ref, q_ref, k_ref, v_ref, returned_ref,
    across_send, across_recv, pair_send, pair_recv, pass_send, pass_recv, slot_send, slot_recv, self_sem,
):
    dp, mp = lax.axis_index("dp"), lax.axis_index("mp")
    pair, across, far = mp ^ 1, mp ^ 2, mp ^ 3
    own = tokens_ref.shape[0]
    part = own // PARTS
    greet([(dp, pair), (dp, across)] + [(lax.rem(dp + k, dp_count), mp) for k in range(1, dp_count)])

    def spot(owner, c, size):
        return pl.ds(pl.multiple_of(owner * own + c * size, size), size)

    def gather_copy(c, owner, device, send, recv):
        rows = rows_ref.at[spot(owner, c, part)]
        return remote(rows, rows, send.at[c], recv.at[c], device)

    def slot_copy(k):
        other = lax.rem(dp + k, dp_count)
        return remote(cot_ref.at[other], returned_ref.at[dp], slot_send.at[k], slot_recv.at[k], (other, mp))

    for c in range(PARTS):
        values = tokens_ref[c * part:(c + 1) * part, :].astype(jnp.float32)
        unit, _ = norm_unit(values)
        rows_ref[spot(mp, c, part), :] = (unit * gain_ref[...]).astype(jnp.bfloat16)
        gather_copy(c, mp, (dp, across), across_send, across_recv).start()
        gather_copy(c, mp, (dp, pair), pair_send, pair_recv).start()
    for k in range(1, dp_count):
        slot_copy(k).start()
    self_copy = pltpu.make_async_copy(cot_ref.at[dp], returned_ref.at[dp], self_sem)
    self_copy.start()

    def product(owner, half):
        where = spot(owner, half, own // 2)
        rows = rows_ref[where, :]
        for p, out in enumerate((q_ref, k_ref, v_ref)):
            out[where, :] = lax.dot_general(rows, w_ref[p], NT, preferred_element_type=jnp.float32).astype(jnp.bfloat16)

    def both(owner):
        def step(half, _):
            product(owner, half)
            return 0
        lax.fori_loop(0, 2, step, 0)

    both(mp)
    for c in range(PARTS):
        gather_copy(c, pair, (dp, pair), pair_send, pair_recv).wait_recv()
    both(pair)
    for half in range(2):
        for c in range(half * PARTS // 2, (half + 1) * PARTS // 2):
            gather_copy(c, across, (dp, across), across_send, across_recv).wait_recv()
            gather_copy(c, across, (dp, pair), pass_send, pass_recv).start()
        product(across, half)
    for half in range(2):
        for c in range(half * PARTS // 2, (half + 1) * PARTS // 2):
            gather_copy(c, far, (dp, pair), pass_send, pass_recv).wait_recv()
        product(far, half)
    for c in range(PARTS):
        gather_copy(c, mp, (dp, across), across_send, across_recv).wait_send()
        gather_copy(c, mp, (dp, pair), pair_send, pair_recv).wait_send()
        gather_copy(c, across, (dp, pair), pass_send, pass_recv).wait_send()
    self_copy.wait()
    for k in range(1, dp_count):
        slot_copy(k).wait_send()
        other = lax.rem(dp + dp_count - k, dp_count)
        remote(cot_ref.at[dp], returned_ref.at[other], slot_send.at[k], slot_recv.at[k], (other, mp)).wait_recv()


def project(tokens, gain, w_qkv, cot):
    own, width = tokens.shape
    dp_count = cot.shape[0]
    total = own * 4
    cols = w_qkv.shape[1]
    vmem = pl.BlockSpec(memory_space=pltpu.VMEM)
    hbm = pl.BlockSpec(memory_space=pl.ANY)
    dma = pltpu.SemaphoreType.DMA
    return pl.pallas_call(
        functools.partial(project_kernel, dp_count),
        out_shape=[jax.ShapeDtypeStruct((total, width), jnp.bfloat16)]
        + [jax.ShapeDtypeStruct((total, cols), jnp.bfloat16)] * 3
        + [jax.ShapeDtypeStruct(cot.shape, cot.dtype)],
        in_specs=[vmem, vmem, vmem, hbm],
        out_specs=[vmem] * 4 + [hbm],
        scratch_shapes=[dma((PARTS,))] * 6 + [dma((dp_count,))] * 2 + [dma],
        compiler_params=pltpu.CompilerParams(collective_id=1, has_side_effects=True, vmem_limit_bytes=40 << 20),
        cost_estimate=pl.CostEstimate(flops=6 * total * width * cols, bytes_accessed=10 * total * width, transcendentals=0),
        name="project",
    )(tokens, gain, w_qkv, cot)


def gelu_and_slope(values):
    cumulative = 0.5 * (1.0 + lax.erf(values * 0.7071067811865476))
    density = jnp.exp(-0.5 * values * values) * 0.3989422804014327
    return values * cumulative, cumulative + values * density


def middle_kernel(
    stages, merged_ref, w_out_ref, tokens_ref, gain_ref, w_up_ref, w_down_ref, grad_own_ref, grad_across_ref,
    back_rows_ref, grad_merged_ref, grad_residual_ref, output_ref, d_mlp_ref, d_out_ref,
    mlp_rows, grad_rows, active, grad_pre, residual, mine, bufs,
    sum_send, sum_recv, row_send, row_recv, grad_send, grad_recv, self_sem, acc, came, dp_send, dp_recv,
):
    low, full = jnp.bfloat16, jnp.float32
    dp, mp = lax.axis_index("dp"), lax.axis_index("mp")
    pair, across, far = mp ^ 1, mp ^ 2, mp ^ 3
    own, width = tokens_ref.shape
    part = own // PARTS
    to_pair, to_across = (dp, pair), (dp, across)
    greet([to_pair, to_across] + [(dp ^ (1 << j), mp) for j in range(stages)])
    add_step, add_drain = sum_steps(stages, MLP_CHUNKS, acc, came, dp_send, dp_recv, d_mlp_ref)

    def spot(owner, c=None):
        if c is None:
            return pl.ds(pl.multiple_of(owner * own, own), own)
        return pl.ds(pl.multiple_of(owner * own + c * part, part), part)

    def piece(c):
        return pl.ds(pl.multiple_of(c * part, part), part)

    def grad_copy(i, owner, src):
        return remote(src, grad_rows.at[spot(owner)], grad_send.at[i], grad_recv.at[i], to_pair)

    local_copies = [
        pltpu.make_async_copy(grad_own_ref, grad_rows.at[spot(mp)], self_sem.at[0]),
        pltpu.make_async_copy(grad_across_ref, grad_rows.at[spot(across)], self_sem.at[1]),
    ]

    FAR, ACROSS, PAIR = 0, 1, 2

    def sum_copy(which, kind, c):
        src, dst = bufs.at[which, 0, kind, piece(c)], bufs.at[which, 1, kind, piece(c)]
        return remote(src, dst, sum_send.at[which, kind, c], sum_recv.at[which, kind, c], to_across if kind == ACROSS else to_pair)

    def arrived(which, kind, c):
        sum_copy(which, kind, c).wait_recv()
        return bufs[which, 1, kind, piece(c), :].astype(full)

    def ship(which, kind, c, values):
        bufs[which, 0, kind, piece(c), :] = values.astype(low)
        sum_copy(which, kind, c).start()

    def row_copy(which, kind, c, owner, ref):
        rows = ref.at[spot(owner, c)]
        return remote(rows, rows, row_send.at[which, kind, c], row_recv.at[which, kind, c], to_across if kind == 0 else to_pair)

    def each(count, body):
        def step(i, _):
            body(i)
            return 0
        lax.fori_loop(0, count, step, 0)

    def out_part(owner):
        return jnp.dot(merged_ref[spot(owner), :], w_out_ref[...], preferred_element_type=full)

    bufs[0, 0, FAR] = out_part(far).astype(low)
    each(PARTS, lambda c: sum_copy(0, FAR, c).start())
    mine[0] = out_part(across)

    def pass_across(c):
        ship(0, ACROSS, c, mine[0, piece(c), :] + arrived(0, FAR, c))
    each(PARTS, pass_across)
    bufs[0, 0, PAIR] = out_part(pair).astype(low)
    each(PARTS, lambda c: sum_copy(0, PAIR, c).start())
    for copy in local_copies:
        copy.start()
    grad_copy(0, mp, grad_own_ref).start()
    grad_copy(1, across, grad_across_ref).start()
    mine[0] = out_part(mp) + tokens_ref[...].astype(full)
    for copy in local_copies:
        copy.wait()
    grad_copy(0, pair, grad_own_ref).wait_recv()
    grad_copy(1, far, grad_across_ref).wait_recv()

    blocks = w_up_ref.shape[1] // 256
    both = 2 * part

    def mlp(first, second, c):
        rows = jnp.concatenate([mlp_rows[spot(first, c), :], mlp_rows[spot(second, c), :]], axis=0)
        grads = jnp.concatenate([grad_rows[spot(first, c), :], grad_rows[spot(second, c), :]], axis=0)

        def block(b):
            cols = pl.ds(pl.multiple_of(b * 256, 256), 256)
            pre = jnp.dot(rows, w_up_ref[:, cols], preferred_element_type=full)
            value, slope = gelu_and_slope(pre)
            value = value.astype(low)
            active[spot(first, c), cols] = value[:part]
            active[spot(second, c), cols] = value[part:]
            back = (jnp.dot(grads, w_down_ref[:, cols], preferred_element_type=full) * slope).astype(low)
            grad_pre[spot(first, c), cols] = back[:part]
            grad_pre[spot(second, c), cols] = back[part:]
        each(blocks, block)
        back = jnp.concatenate([grad_pre[spot(first, c), :], grad_pre[spot(second, c), :]], axis=0)
        return lax.dot_general(back, w_up_ref[...], NT, preferred_element_type=full)

    def near(c):
        values = mine[0, piece(c), :] + arrived(0, PAIR, c) + arrived(0, ACROSS, c)
        residual[piece(c), :] = values
        unit, _ = norm_unit(values)
        mlp_rows[spot(mp, c), :] = (unit * gain_ref[...]).astype(low)
        row_copy(0, 0, c, mp, mlp_rows).start()
        row_copy(0, 1, c, mp, mlp_rows).start()
        row_copy(0, 1, c, pair, mlp_rows).wait_recv()
        got = mlp(mp, pair, c)
        mine[1, piece(c), :] = got[:part]
        ship(1, PAIR, c, got[part:])
    each(PARTS, near)

    def distant(c):
        row_copy(0, 0, c, across, mlp_rows).wait_recv()
        row_copy(0, 2, c, across, mlp_rows).start()
        row_copy(0, 2, c, far, mlp_rows).wait_recv()
        got = mlp(far, across, c)
        ship(1, FAR, c, got[:part])
        ship(1, ACROSS, c, got[part:] + arrived(1, FAR, c))
    each(PARTS, distant)

    for b in range(MLP_CHUNKS):
        cols = slice(b * 256, (b + 1) * 256)
        target = acc if stages else d_mlp_ref
        target[b * 512:b * 512 + 256, :] = lax.dot_general(
            mlp_rows[:, cols], grad_pre[...], TN, preferred_element_type=full
        ).astype(low)
        target[b * 512 + 256:b * 512 + 512, :] = lax.dot_general(
            grad_rows[:, cols], active[...], TN, preferred_element_type=full
        ).astype(low)
        if stages:
            add_step(b, 0)

    def add(*steps):
        if stages:
            for k, i in steps:
                add_step(k, i)

    def down_part(owner):
        return lax.dot_general(active[spot(owner), :], w_down_ref[...], NT, preferred_element_type=full)

    bufs[2, 0, FAR] = down_part(far).astype(low)
    each(PARTS, lambda c: sum_copy(2, FAR, c).start())
    bufs[2, 0, PAIR] = down_part(pair).astype(low)
    each(PARTS, lambda c: sum_copy(2, PAIR, c).start())

    def back_norm(c):
        grad = mine[1, piece(c), :] + arrived(1, PAIR, c) + arrived(1, ACROSS, c)
        unit, inverse = norm_unit(residual[piece(c), :])
        scaled = grad * gain_ref[...]
        first_mean = jnp.mean(scaled, axis=-1, keepdims=True)
        second_mean = jnp.mean(scaled * unit, axis=-1, keepdims=True)
        total = inverse * (scaled - first_mean - unit * second_mean) + grad_own_ref[piece(c), :].astype(full)
        grad_residual_ref[piece(c), :] = total
        back_rows_ref[spot(mp, c), :] = total.astype(low)
        row_copy(1, 0, c, mp, back_rows_ref).start()
        row_copy(1, 1, c, mp, back_rows_ref).start()
    each(2, back_norm)
    add((0, 1))
    each(2, lambda c: back_norm(c + 2))

    mine[1] = down_part(across)

    def pass_output(c):
        ship(2, ACROSS, c, mine[1, piece(c), :] + arrived(2, FAR, c))
    each(PARTS, pass_output)
    add((0, 2), (1, 1))
    mine[0] = residual[...] + down_part(mp)

    def merged_part(owner):
        grad_merged_ref[spot(owner), :] = lax.dot_general(
            back_rows_ref[spot(owner), :], w_out_ref[...], NT, preferred_element_type=full
        ).astype(low)

    merged_part(mp)
    each(PARTS, lambda c: row_copy(1, 1, c, pair, back_rows_ref).wait_recv())
    merged_part(pair)

    def hand_on(c):
        row_copy(1, 0, c, across, back_rows_ref).wait_recv()
        row_copy(1, 2, c, across, back_rows_ref).start()
    each(2, hand_on)
    add((0, 3), (1, 2))
    each(1, lambda c: hand_on(c + 2))
    add((2, 1))
    each(1, lambda c: hand_on(c + 3))
    add((0, 4), (1, 3), (2, 2))
    merged_part(across)
    each(PARTS, lambda c: row_copy(1, 2, c, far, back_rows_ref).wait_recv())
    merged_part(far)
    d_out_ref[...] = lax.dot_general(merged_ref[...], back_rows_ref[...], TN, preferred_element_type=full).astype(low)
    add((0, 5), (1, 4), (2, 3))

    def finish(c):
        output_ref[piece(c), :] = (mine[0, piece(c), :] + arrived(2, PAIR, c) + arrived(2, ACROSS, c)).astype(low)
    each(2, finish)
    add((1, 5), (2, 4))
    each(2, lambda c: finish(c + 2))
    add((2, 5), (0, 6), (1, 6), (2, 6))
    if stages:
        add_drain()

    def drain(c):
        for which in range(3):
            for kind in range(3):
                sum_copy(which, kind, c).wait_send()
        for which, ref in ((0, mlp_rows), (1, back_rows_ref)):
            row_copy(which, 0, c, mp, ref).wait_send()
            row_copy(which, 1, c, mp, ref).wait_send()
            row_copy(which, 2, c, across, ref).wait_send()
    each(PARTS, drain)
    grad_copy(0, mp, grad_own_ref).wait_send()
    grad_copy(1, across, grad_across_ref).wait_send()


def middle(dp_count, merged, w_out, tokens, gain, w_up, w_down, grad_own, grad_across):
    stages = sum_stages(2 * w_up.shape[0], MLP_CHUNKS, dp_count)
    total, cols = merged.shape
    own, width = tokens.shape
    hidden = w_up.shape[1]
    low, full = jnp.bfloat16, jnp.float32
    vmem = pl.BlockSpec(memory_space=pltpu.VMEM)
    dma = pltpu.SemaphoreType.DMA
    shape = jax.ShapeDtypeStruct
    return pl.pallas_call(
        functools.partial(middle_kernel, stages),
        out_shape=[
            shape((total, width), low), shape((total, cols), low), shape((own, width), full), shape((own, width), low),
            shape((2 * width, hidden), low), shape((cols, width), low),
        ],
        in_specs=[vmem] * 8,
        out_specs=[vmem] * 6,
        scratch_shapes=[
            pltpu.VMEM((total, width), low), pltpu.VMEM((total, width), low),
            pltpu.VMEM((total, hidden), low), pltpu.VMEM((total, hidden), low),
            pltpu.VMEM((own, width), full), pltpu.VMEM((2, own, width), full),
            pltpu.VMEM((3, 2, 3, own, width), low),
            dma((3, 3, PARTS)), dma((3, 3, PARTS)), dma((2, 3, PARTS)), dma((2, 3, PARTS)), dma((2,)), dma((2,)), dma((2,)),
        ]
        + sum_scratch(2 * width, hidden, MLP_CHUNKS, stages),
        compiler_params=pltpu.CompilerParams(collective_id=2, has_side_effects=True, vmem_limit_bytes=56 << 20),
        cost_estimate=pl.CostEstimate(flops=16 * total * width * hidden, bytes_accessed=20 * total * width, transcendentals=0),
        name="middle",
    )(merged, w_out, tokens, gain, w_up, w_down, grad_own, grad_across)


def last_kernel(
    stages, dq_ref, dk_ref, dv_ref, w_ref, rows_ref, grad_residual_ref, tokens_ref, gain_ref, d_out_ref, gain_part_ref,
    grad_tokens_ref, d_sum_ref, gains_ref,
    mine, bufs, gain_all, sum_send, sum_recv, gain_send, gain_recv, acc, came, dp_send, dp_recv,
):
    low, full = jnp.bfloat16, jnp.float32
    dp, mp = lax.axis_index("dp"), lax.axis_index("mp")
    pair, across, far = mp ^ 1, mp ^ 2, mp ^ 3
    own, width = tokens_ref.shape
    part = own // PARTS
    cols = dq_ref.shape[1]
    to_pair, to_across = (dp, pair), (dp, across)
    greet([to_pair, to_across, (dp, far)] + [(dp ^ (1 << j), mp) for j in range(stages)])
    add_step, add_drain = sum_steps(stages, QKV_CHUNKS, acc, came, dp_send, dp_recv, d_sum_ref)
    target = acc if stages else d_sum_ref
    chunk = target.shape[0] // QKV_CHUNKS
    FAR, ACROSS, PAIR = 0, 1, 2

    def add(*steps):
        if stages:
            for k, i in steps:
                add_step(k, i)

    def piece(c):
        return pl.ds(pl.multiple_of(c * part, part), part)

    def each(count, body):
        def step(i, _):
            body(i)
            return 0
        lax.fori_loop(0, count, step, 0)

    def sum_copy(kind, c):
        src, dst = bufs.at[0, kind, piece(c)], bufs.at[1, kind, piece(c)]
        return remote(src, dst, sum_send.at[kind, c], sum_recv.at[kind, c], to_across if kind == ACROSS else to_pair)

    def arrived(kind, c):
        sum_copy(kind, c).wait_recv()
        return bufs[1, kind, piece(c), :].astype(full)

    target[0:cols, :] = d_out_ref[...]
    started = 0
    for p, ref in enumerate((dq_ref, dk_ref, dv_ref)):
        target[(p + 1) * cols:(p + 2) * cols, :] = lax.dot_general(
            ref[...], rows_ref[...], TN, preferred_element_type=full
        ).astype(low)
        while started < QKV_CHUNKS and (started + 1) * chunk <= (p + 2) * cols:
            add((started, 0))
            started += 1

    def in_part(owner):
        where = pl.ds(pl.multiple_of(owner * own, own), own)
        total = jnp.dot(dq_ref[where, :], w_ref[0], preferred_element_type=full)
        total = total + jnp.dot(dk_ref[where, :], w_ref[1], preferred_element_type=full)
        return total + jnp.dot(dv_ref[where, :], w_ref[2], preferred_element_type=full)

    bufs[0, FAR] = in_part(far).astype(low)
    each(PARTS, lambda c: sum_copy(FAR, c).start())
    mine[...] = in_part(across)

    def pass_across(c):
        bufs[0, ACROSS, piece(c), :] = (mine[piece(c), :] + arrived(FAR, c)).astype(low)
        sum_copy(ACROSS, c).start()
    each(PARTS, pass_across)
    bufs[0, PAIR] = in_part(pair).astype(low)
    each(PARTS, lambda c: sum_copy(PAIR, c).start())
    mine[...] = in_part(mp)
    add((0, 1))

    def back_norm(c):
        grad = mine[piece(c), :] + arrived(PAIR, c) + arrived(ACROSS, c)
        unit, inverse = norm_unit(tokens_ref[piece(c), :].astype(full))
        scaled = grad * gain_ref[...]
        first_mean = jnp.mean(scaled, axis=-1, keepdims=True)
        second_mean = jnp.mean(scaled * unit, axis=-1, keepdims=True)
        total = inverse * (scaled - first_mean - unit * second_mean) + grad_residual_ref[piece(c), :]
        grad_tokens_ref[piece(c), :] = total.astype(low)

    each(1, back_norm)
    add((0, 2), (1, 1))
    each(1, lambda c: back_norm(c + 1))
    add((0, 3), (1, 2), (2, 1))
    each(1, lambda c: back_norm(c + 2))
    add((0, 4), (1, 3), (2, 2))
    each(1, lambda c: back_norm(c + 3))
    add((0, 5), (1, 4), (2, 3), (1, 5), (2, 4), (2, 5), (0, 6), (1, 6), (2, 6))
    if stages:
        add_drain()

    total = jnp.zeros((1, width), full)
    for p in range(3):
        prod = w_ref[p].astype(full) * d_sum_ref[(p + 1) * cols:(p + 2) * cols, :].astype(full)
        total = total + jnp.sum(prod, axis=0, keepdims=True)
    row = lax.broadcasted_iota(jnp.int32, (8, width), 0)
    gain_all[mp] = jnp.where(row == 0, gain_part_ref[...], jnp.where(row == 1, total / gain_ref[...], 0.0))

    def gain_copy(i, owner, other):
        return remote(gain_all.at[owner], gain_all.at[owner], gain_send.at[i], gain_recv.at[i], (dp, other))

    others = (pair, across, far)
    for i, other in enumerate(others):
        gain_copy(i, mp, other).start()
    for i, other in enumerate(others):
        gain_copy(i, other, other).wait_recv()
    gains_ref[...] = (gain_all[0] + gain_all[1]) + (gain_all[2] + gain_all[3])
    for i, other in enumerate(others):
        gain_copy(i, mp, other).wait_send()

    def drain(c):
        for kind in range(3):
            sum_copy(kind, c).wait_send()
    each(PARTS, drain)


def last(dp_count, dq, dk, dv, w_qkv, rows, grad_residual, tokens, gain, d_out, gain_part):
    own, width = tokens.shape
    cols = dq.shape[1]
    stages = sum_stages(4 * cols, QKV_CHUNKS, dp_count)
    low, full = jnp.bfloat16, jnp.float32
    vmem = pl.BlockSpec(memory_space=pltpu.VMEM)
    dma = pltpu.SemaphoreType.DMA
    shape = jax.ShapeDtypeStruct
    return pl.pallas_call(
        functools.partial(last_kernel, stages),
        out_shape=[shape((own, width), low), shape((4 * cols, width), low), shape((8, width), full)],
        in_specs=[vmem] * 10,
        out_specs=[vmem] * 3,
        scratch_shapes=[
            pltpu.VMEM((own, width), full), pltpu.VMEM((2, 3, own, width), low), pltpu.VMEM((4, 8, width), full),
            dma((3, PARTS)), dma((3, PARTS)), dma((3,)), dma((3,)),
        ]
        + sum_scratch(4 * cols, width, QKV_CHUNKS, stages),
        compiler_params=pltpu.CompilerParams(collective_id=3, has_side_effects=True, vmem_limit_bytes=48 << 20),
        cost_estimate=pl.CostEstimate(flops=12 * 4 * own * width * cols, bytes_accessed=20 * own * width, transcendentals=0),
        name="last",
    )(dq, dk, dv, w_qkv, rows, grad_residual, tokens, gain, d_out, gain_part)


def local(
    tokens, segment_ids, gene_owner, w_qkv, w_attn_out, w_up, w_down, gain_attn, gain_mlp, cotangent
):
    width = tokens.shape[1]
    dp_count = lax.axis_size("dp")
    capacity = cotangent.shape[0] // dp_count
    own_rows = tokens.shape[0]
    contract_first = (((0,), (0,)), ((), ()))
    low = jnp.bfloat16

    owners = gene_owner[:, 0]
    place = jnp.arange(own_rows, dtype=jnp.int32)
    earlier = (owners[:, None] == owners[None, :]) & (place[None, :] < place[:, None])
    slots = owners * capacity + jnp.sum(earlier.astype(jnp.int32), axis=1)
    onehot = (slots[:, None] == jnp.arange(dp_count * capacity, dtype=jnp.int32)[None, :]).astype(low)

    w_rows = jnp.swapaxes(w_qkv, 1, 2)
    gain_one = gain_attn.reshape(1, -1)
    attn_in, *projected, returned = project(tokens, gain_one, w_rows, cotangent.reshape(dp_count, capacity, width))
    returned = returned.reshape(dp_count * capacity, width)
    grad_block = jnp.dot(onehot, returned, preferred_element_type=jnp.float32).astype(low)
    grad_across = lax.ppermute(grad_block, "mp", [(i, i ^ 2) for i in range(lax.axis_size("mp"))])
    merged, log_sums = attend_forward(segment_ids, *projected)
    residual_rows, grad_merged, grad_residual, output, mlp_sum, d_out = middle(
        dp_count, merged, w_attn_out, tokens, gain_mlp.reshape(1, -1), w_up, w_down, grad_block, grad_across
    )
    if not sum_stages(2 * width, MLP_CHUNKS, dp_count):
        mlp_sum = lax.psum(mlp_sum, "dp")
    mlp_sum = mlp_sum.reshape(MLP_CHUNKS, 2, width // MLP_CHUNKS, w_up.shape[1]).astype(jnp.float32)
    up_sum, down_sum = (mlp_sum[:, i].reshape(w_up.shape) for i in range(2))
    gain_part = (jnp.sum(w_up.astype(jnp.float32) * up_sum, axis=1) / gain_mlp).reshape(1, -1)
    outgoing = lax.dot_general(onehot, output, contract_first, preferred_element_type=jnp.float32).astype(low)
    relaid = lax.all_to_all(
        outgoing.reshape(dp_count, capacity, width), "dp", split_axis=0, concat_axis=0, tiled=True
    ).reshape(dp_count * capacity, width)
    grad_proj = attend_backward(segment_ids, *projected, merged, grad_merged, log_sums)
    grad_tokens, weight_sum, gains = last(
        dp_count, *grad_proj, w_rows, attn_in, grad_residual, tokens, gain_one, d_out, gain_part
    )
    cols = w_qkv.shape[2]
    if not sum_stages(4 * cols, QKV_CHUNKS, dp_count):
        weight_sum = lax.psum(weight_sum, "dp")
        products = w_rows.astype(jnp.float32) * weight_sum[cols:].reshape(w_rows.shape).astype(jnp.float32)
        gains = gains.at[1].set(lax.psum(jnp.sum(products, axis=(0, 1)) / gain_attn, "mp"))
    weight_sum = weight_sum.astype(jnp.float32)
    return (
        relaid,
        grad_tokens,
        jnp.swapaxes(weight_sum[cols:].reshape(3, cols, width), 1, 2),
        weight_sum[:cols],
        up_sum,
        down_sum,
        gains[1],
        gains[0],
    )


def solution(mesh):
    placed = (
        P(("dp", "mp"), None),
        P("dp", None),
        P(("dp", "mp"), None),
        P(None, None, "mp"),
        P("mp", None),
        P(None, "mp"),
        P(None, "mp"),
        P(),
        P(),
        P(("dp", "mp"), None),
    )
    return jax.shard_map(
        local,
        mesh=mesh,
        in_specs=placed,
        out_specs=(
            P(("dp", "mp"), None),
            P(("dp", "mp"), None),
            P(None, None, "mp"),
            P("mp", None),
            P(None, "mp"),
            P(None, "mp"),
            P(),
            P(),
        ),
        check_vma=False,
    )
```

```python
import functools
import jax
import jax.numpy as jnp
from jax import lax
from jax.experimental import pallas as pl
from jax.experimental.pallas import tpu as pltpu
from jax.sharding import PartitionSpec as P

HEAD = 64
TQ = 256
TK = 512
NT = (((1,), (1,)), ((), ()))
NN = (((1,), (0,)), ((), ()))
TN = (((0,), (0,)), ((), ()))
MASKED = -1e30
epsilon = 1e-05


def lower_bound(seg, n, value):
    def step(_, c):
        lo, hi = c
        mid = (lo + hi) // 2
        less = seg[jnp.minimum(mid, n - 1)] < value
        go = lo < hi
        return (jnp.where(go & less, mid + 1, lo), jnp.where(go & ~less, mid, hi))
    lo, hi = lax.fori_loop(0, n.bit_length(), step, (jnp.int32(0), jnp.int32(n)))
    return lo


def key_range(seg, n, tile):
    first = lower_bound(seg, n, seg[tile * TQ])
    end = lower_bound(seg, n, seg[tile * TQ + TQ - 1] + 1)
    return first // TK, (end + TK - 1) // TK


def head_masks(width, heads):
    lane = lax.broadcasted_iota(jnp.int32, (1, width), 1)
    return [(lane // HEAD == h) for h in range(heads)]


def seg_columns(segv_ref, cols, n):
    for t in range(n // 128):
        row = segv_ref[0:1, t * 128:(t + 1) * 128].astype(jnp.float32)
        cols[t * 128:(t + 1) * 128, :] = jnp.broadcast_to(row, (128, 128)).T


def fwd_kernel(n, heads, seg, segv_ref, q_ref, k_ref, v_ref, o_ref, lse_ref, vt, cols, scores):
    tile = pl.program_id(0)
    width = heads * HEAD

    @pl.when(tile == 0)
    def _():
        seg_columns(segv_ref, cols, n)
        for t in range(n // TK):
            vt[:, t * TK:(t + 1) * TK] = v_ref[t * TK:(t + 1) * TK, :].astype(jnp.float32).T.astype(jnp.bfloat16)

    lo, hi = key_range(seg, n, tile)
    q0 = pl.multiple_of(tile * TQ, TQ)
    q = q_ref[...] * jnp.bfloat16(HEAD ** -0.5)
    masks = head_masks(width, heads)
    qm = [jnp.where(m, q, jnp.bfloat16(0)) for m in masks]
    seg_row = segv_ref[0:1, pl.ds(q0, TQ)].astype(jnp.float32)

    def first(b, tops):
        k0 = pl.multiple_of(b * TK, TK)
        keys = k_ref[pl.ds(k0, TK), :]
        col = cols[pl.ds(k0, TK), :]
        same = jnp.concatenate([col] * (TQ // 128), axis=1) == seg_row
        out = []
        for h in range(heads):
            s = lax.dot_general(keys, qm[h], NT, preferred_element_type=jnp.float32)
            s = jnp.where(same, s, MASKED)
            scores[h, pl.ds(k0, TK), :] = s
            out.append(jnp.maximum(tops[h], jnp.max(s, axis=0, keepdims=True)))
        return tuple(out)

    tops = lax.fori_loop(lo, hi, first, tuple(jnp.full((1, TQ), MASKED, jnp.float32) for _ in range(heads)))

    def second(b, acc):
        k0 = pl.multiple_of(b * TK, TK)
        out = []
        for h in range(heads):
            p = jnp.exp(scores[h, pl.ds(k0, TK), :] - tops[h])
            total = acc[h][1] + jnp.sum(p, axis=0, keepdims=True)
            part = lax.dot_general(vt[h * HEAD:(h + 1) * HEAD, pl.ds(k0, TK)], p.astype(jnp.bfloat16), NN, preferred_element_type=jnp.float32)
            out.append((acc[h][0] + part, total))
        return tuple(out)

    acc = lax.fori_loop(lo, hi, second, tuple((jnp.zeros((HEAD, TQ), jnp.float32), jnp.zeros((1, TQ), jnp.float32)) for _ in range(heads)))
    ot = jnp.concatenate([acc[h][0] / acc[h][1] for h in range(heads)], axis=0)
    o_ref[...] = ot.T.astype(jnp.bfloat16)
    lse_ref[...] = jnp.concatenate([tops[h] + jnp.log(acc[h][1]) for h in range(heads)] + [jnp.zeros((8 - heads, TQ), jnp.float32)], axis=0)


def attend_forward(seg, q, k, v):
    n, width = q.shape
    heads = width // HEAD
    whole = pl.BlockSpec(memory_space=pltpu.VMEM)
    return pl.pallas_call(
        functools.partial(fwd_kernel, n, heads),
        grid_spec=pltpu.PrefetchScalarGridSpec(
            num_scalar_prefetch=1,
            grid=(n // TQ,),
            in_specs=[whole, pl.BlockSpec((TQ, width), lambda t, s: (t, 0)), whole, whole],
            out_specs=[pl.BlockSpec((TQ, width), lambda t, s: (t, 0)), pl.BlockSpec((8, TQ), lambda t, s: (0, t))],
            scratch_shapes=[pltpu.VMEM((width, n), jnp.bfloat16), pltpu.VMEM((n, 128), jnp.float32), pltpu.VMEM((heads, n, TQ), jnp.float32)],
        ),
        out_shape=[jax.ShapeDtypeStruct((n, width), jnp.bfloat16), jax.ShapeDtypeStruct((8, n), jnp.float32)],
        compiler_params=pltpu.CompilerParams(vmem_limit_bytes=VMEM_BYTES),
        cost_estimate=pl.CostEstimate(flops=4 * heads * n * n * HEAD, bytes_accessed=8 * n * width, transcendentals=heads * n * n // 2),
        name="attend_forward",
    )(seg.reshape(-1), seg.reshape(1, -1), q, k, v)


def bwd_kernel(n, heads, seg, segv_ref, q_ref, k_ref, v_ref, o_ref, do_ref, lse_ref, dq_ref, dk_ref, dv_ref, kt, cols, dk_acc, dv_acc):
    tile = pl.program_id(0)
    width = heads * HEAD

    @pl.when(tile == 0)
    def _():
        seg_columns(segv_ref, cols, n)
        for t in range(n // TK):
            kt[:, t * TK:(t + 1) * TK] = k_ref[t * TK:(t + 1) * TK, :].astype(jnp.float32).T.astype(jnp.bfloat16)
        dk_acc[...] = jnp.zeros_like(dk_acc)
        dv_acc[...] = jnp.zeros_like(dv_acc)

    lo, hi = key_range(seg, n, tile)
    q0 = pl.multiple_of(tile * TQ, TQ)
    masks = head_masks(width, heads)
    q = q_ref[...] * jnp.bfloat16(HEAD ** -0.5)
    do = do_ref[...]
    qm = [jnp.where(m, q, jnp.bfloat16(0)) for m in masks]
    dm = [jnp.where(m, do, jnp.bfloat16(0)) for m in masks]
    seg_row = segv_ref[0:1, pl.ds(q0, TQ)].astype(jnp.float32)
    prod = do.astype(jnp.float32) * o_ref[...].astype(jnp.float32)
    high = prod.astype(jnp.bfloat16)
    rest = (prod - high.astype(jnp.float32)).astype(jnp.bfloat16)
    row = lax.broadcasted_iota(jnp.int32, (16, width), 0)
    lane = lax.broadcasted_iota(jnp.int32, (16, width), 1)
    pick = jnp.where(lane // HEAD == row, 1.0, 0.0).astype(jnp.bfloat16)
    delta = lax.dot_general(pick, high, NT, preferred_element_type=jnp.float32) + lax.dot_general(pick, rest, NT, preferred_element_type=jnp.float32)
    lse = lse_ref[...]

    def body(b, acc):
        k0 = pl.multiple_of(b * TK, TK)
        keys = k_ref[pl.ds(k0, TK), :]
        vals = v_ref[pl.ds(k0, TK), :]
        col = cols[pl.ds(k0, TK), :]
        same = jnp.concatenate([col] * (TQ // 128), axis=1) == seg_row
        out = []
        dks = jnp.zeros((TK, width), jnp.float32)
        dvs = jnp.zeros((TK, width), jnp.float32)
        for h in range(heads):
            s = lax.dot_general(keys, qm[h], NT, preferred_element_type=jnp.float32)
            p = jnp.where(same, jnp.exp(s - lse[h:h + 1, :]), 0.0)
            dp = lax.dot_general(vals, dm[h], NT, preferred_element_type=jnp.float32)
            ds = (p * (dp - delta[h:h + 1, :])).astype(jnp.bfloat16)
            dvs = dvs + lax.dot_general(p.astype(jnp.bfloat16), dm[h], NN, preferred_element_type=jnp.float32)
            dks = dks + lax.dot_general(ds, qm[h], NN, preferred_element_type=jnp.float32)
            out.append(acc[h] + lax.dot_general(kt[h * HEAD:(h + 1) * HEAD, pl.ds(k0, TK)], ds, NN, preferred_element_type=jnp.float32))
        dk_acc[pl.ds(k0, TK), :] += dks
        dv_acc[pl.ds(k0, TK), :] += dvs
        return tuple(out)

    acc = lax.fori_loop(lo, hi, body, tuple(jnp.zeros((HEAD, TQ), jnp.float32) for _ in range(heads)))
    dq_ref[...] = (jnp.concatenate(acc, axis=0).T * HEAD ** -0.5).astype(jnp.bfloat16)

    @pl.when(tile == n // TQ - 1)
    def _():
        dk_ref[...] = dk_acc[...].astype(jnp.bfloat16)
        dv_ref[...] = dv_acc[...].astype(jnp.bfloat16)


def attend_backward(seg, q, k, v, o, do, lse):
    n, width = q.shape
    heads = width // HEAD
    whole = pl.BlockSpec(memory_space=pltpu.VMEM)
    rows = pl.BlockSpec((TQ, width), lambda t, s: (t, 0))
    return pl.pallas_call(
        functools.partial(bwd_kernel, n, heads),
        grid_spec=pltpu.PrefetchScalarGridSpec(
            num_scalar_prefetch=1,
            grid=(n // TQ,),
            in_specs=[whole, rows, whole, whole, rows, rows, pl.BlockSpec((8, TQ), lambda t, s: (0, t))],
            out_specs=[rows, whole, whole],
            scratch_shapes=[pltpu.VMEM((width, n), jnp.bfloat16), pltpu.VMEM((n, 128), jnp.float32), pltpu.VMEM((n, width), jnp.float32), pltpu.VMEM((n, width), jnp.float32)],
        ),
        out_shape=[jax.ShapeDtypeStruct((n, width), jnp.bfloat16)] * 3,
        compiler_params=pltpu.CompilerParams(vmem_limit_bytes=VMEM_BYTES),
        cost_estimate=pl.CostEstimate(flops=10 * heads * n * n * HEAD, bytes_accessed=16 * n * width, transcendentals=heads * n * n // 2),
        name="attend_backward",
    )(seg.reshape(-1), seg.reshape(1, -1), q, k, v, o, do, lse)


MESH_ID = pl.DeviceIdType.MESH
PARTS = 4
VMEM_BYTES = 60 << 20
MLP_CHUNKS = 6
QKV_CHUNKS = 6
NORM_TICKS = (5, 7, 9, 10)


def remote(src, dst, send, recv, device):
    return pltpu.make_async_remote_copy(
        src_ref=src, dst_ref=dst, send_sem=send, recv_sem=recv, device_id=device, device_id_type=MESH_ID
    )


def greet(devices):
    barrier = pltpu.get_barrier_semaphore()
    for device in devices:
        pl.semaphore_signal(barrier, inc=1, device_id=device, device_id_type=MESH_ID)
    pl.semaphore_wait(barrier, len(devices))


def norm_unit(values):
    average = jnp.mean(values, axis=-1, keepdims=True)
    centered = values - average
    variance = jnp.mean(centered * centered, axis=-1, keepdims=True)
    inverse = lax.rsqrt(variance + epsilon)
    return centered * inverse, inverse


def sum_stages(rows, chunks, dp_count):
    stages = dp_count.bit_length() - 1
    return stages if dp_count == 1 << stages and rows % (16 * chunks * dp_count) == 0 else 0


def sum_scratch(rows, width, chunks, stages):
    dma = pltpu.SemaphoreType.DMA
    return [
        pltpu.VMEM((rows, width), jnp.bfloat16), pltpu.VMEM((rows, width), jnp.bfloat16),
        dma((chunks, max(1, 2 * stages))), dma((chunks, max(1, 2 * stages))),
    ]


def left_bit(k, chunks):
    return 0 if 2 * k < chunks else 1


def sum_steps(stages, chunks, acc, came, send, recv, out, half=False):
    dp, mp = lax.axis_index("dp"), lax.axis_index("mp")
    chunk = acc.shape[0] // chunks

    def bit(s):
        return lax.rem(dp // (1 << s), 2)

    def held(k, s):
        start = k * chunk
        for j in range(s):
            start = start + bit(j) * (chunk >> (j + 1))
        return start

    def span(start, size):
        return pl.ds(pl.multiple_of(start, 16), size)

    def placed(k, start):
        if not half:
            return start
        return k * (chunk // 2) + bit(1 - left_bit(k, chunks)) * (chunk // 4) + start - held(k, 2)

    def halve(k, s):
        size = chunk >> (s + 1)
        return remote(
            acc.at[span(held(k, s) + (1 - bit(s)) * size, size)],
            came.at[span(k * chunk + chunk - (chunk >> s), size)],
            send.at[k, s], recv.at[k, s], (dp ^ (1 << s), mp),
        )

    def double(k, s, mine=True):
        if half and s == 1:
            s = 1 - left_bit(k, chunks)
            place = bit(s) if mine else 1 - bit(s)
            rows = out.at[span(k * (chunk // 2) + place * (chunk // 4), chunk // 4)]
            return remote(rows, rows, send.at[k, stages + 1], recv.at[k, stages + 1], (dp ^ (1 << s), mp))
        size = chunk >> (s + 1)
        start = held(k, s + 1) if mine else held(k, s) + (1 - bit(s)) * size
        rows = out.at[span(placed(k, start), size)]
        return remote(rows, rows, send.at[k, stages + s], recv.at[k, stages + s], (dp ^ (1 << s), mp))

    final = 1 if half else 0

    def step(k, i):
        if i == 0:
            halve(k, 0).start()
        elif i <= stages:
            halve(k, i - 1).wait_recv()
            size = chunk >> i
            rows = span(held(k, i), size)
            total = acc[rows, :].astype(jnp.float32) + came[span(k * chunk + chunk - (chunk >> (i - 1)), size), :].astype(jnp.float32)
            if i < stages:
                acc[rows, :] = total.astype(jnp.bfloat16)
                halve(k, i).start()
            else:
                out[span(placed(k, held(k, i)), size), :] = total.astype(jnp.bfloat16)
                double(k, stages - 1).start()
        elif 2 * stages - i >= final:
            s = 2 * stages - i
            double(k, s, False).wait_recv()
            if s > final:
                double(k, s - 1).start()

    def drain():
        for k in range(chunks):
            for s in range(stages):
                halve(k, s).wait_send()
                if s >= final:
                    double(k, s).wait_send()

    return step, drain


def columns_of(row):
    return jnp.concatenate(
        [jnp.broadcast_to(row[:, t * 128:(t + 1) * 128], (128, 128)).T for t in range(row.shape[1] // 128)], axis=0
    )


def project_kernel(
    dp_count, tokens_hbm, gain_ref, w_hbm, cot_ref, owner_ref, rows_hbm, q_ref, k_ref, v_ref, grad_ref, place_ref,
    tokens_ref, w_ref, rows_ref, load_sem, store_sem, returned_ref, across_send, across_recv, pair_send, pair_recv, pass_send, pass_recv, slot_send, slot_recv, self_sem,
):
    load_tokens = pltpu.make_async_copy(tokens_hbm, tokens_ref, load_sem.at[0])
    load_w = pltpu.make_async_copy(w_hbm, w_ref, load_sem.at[1])
    load_tokens.start()
    load_w.start()
    dp, mp = lax.axis_index("dp"), lax.axis_index("mp")
    pair, across, far = mp ^ 1, mp ^ 2, mp ^ 3
    own = tokens_ref.shape[0]
    part = own // PARTS
    greet([(dp, pair), (dp, across)] + [(lax.rem(dp + k, dp_count), mp) for k in range(1, dp_count)])

    def spot(owner, c, size):
        return pl.ds(pl.multiple_of(owner * own + c * size, size), size)

    def gather_copy(c, owner, device, send, recv):
        rows = rows_ref.at[spot(owner, c, part)]
        return remote(rows, rows, send.at[c], recv.at[c], device)

    def slot_copy(k):
        other = lax.rem(dp + k, dp_count)
        return remote(cot_ref.at[other], returned_ref.at[dp], slot_send.at[k], slot_recv.at[k], (other, mp))

    def store(i, owner):
        rows = pl.ds(pl.multiple_of(owner * own, own), own)
        return pltpu.make_async_copy(rows_ref.at[rows], rows_hbm.at[rows], store_sem.at[i])

    load_tokens.wait()
    for c in range(PARTS):
        values = tokens_ref[c * part:(c + 1) * part, :].astype(jnp.float32)
        unit, _ = norm_unit(values)
        rows_ref[spot(mp, c, part), :] = (unit * gain_ref[0:1, :]).astype(jnp.bfloat16)
        gather_copy(c, mp, (dp, across), across_send, across_recv).start()
        gather_copy(c, mp, (dp, pair), pair_send, pair_recv).start()
    for k in range(1, dp_count):
        slot_copy(k).start()
    self_copy = pltpu.make_async_copy(cot_ref.at[dp], returned_ref.at[dp], self_sem)
    self_copy.start()

    def product(owner, half):
        where = spot(owner, half, own // 2)
        rows = rows_ref[where, :]
        for p, out in enumerate((q_ref, k_ref, v_ref)):
            out[where, :] = lax.dot_general(rows, w_ref[p], NT, preferred_element_type=jnp.float32).astype(jnp.bfloat16)

    def both(owner):
        def step(half, _):
            product(owner, half)
            return 0
        lax.fori_loop(0, 2, step, 0)

    load_w.wait()
    both(mp)
    store(0, mp).start()
    capacity = cot_ref.shape[1]
    owner_row = owner_ref[...].astype(jnp.float32)
    owner_col = columns_of(owner_row)
    earlier = lax.broadcasted_iota(jnp.int32, (own, own), 0) < lax.broadcasted_iota(jnp.int32, (own, own), 1)
    same = jnp.concatenate([owner_col] * (own // 128), axis=1) == owner_row
    rank_row = jnp.sum(jnp.where(same & earlier, 1.0, 0.0), axis=0, keepdims=True)
    slot_row = owner_row * capacity + rank_row
    slots = place_ref.shape[0]
    place_ref[...] = jnp.where(
        lax.broadcasted_iota(jnp.int32, (slots, own), 0).astype(jnp.float32) == slot_row, 1.0, 0.0
    ).astype(jnp.bfloat16)
    for c in range(PARTS):
        gather_copy(c, pair, (dp, pair), pair_send, pair_recv).wait_recv()
    both(pair)
    store(1, pair).start()
    for half in range(2):
        for c in range(half * PARTS // 2, (half + 1) * PARTS // 2):
            gather_copy(c, across, (dp, across), across_send, across_recv).wait_recv()
            gather_copy(c, across, (dp, pair), pass_send, pass_recv).start()
        product(across, half)
    store(2, across).start()
    for half in range(2):
        for c in range(half * PARTS // 2, (half + 1) * PARTS // 2):
            gather_copy(c, far, (dp, pair), pass_send, pass_recv).wait_recv()
        product(far, half)
    store(3, far).start()
    for c in range(PARTS):
        gather_copy(c, mp, (dp, across), across_send, across_recv).wait_send()
        gather_copy(c, mp, (dp, pair), pair_send, pair_recv).wait_send()
        gather_copy(c, across, (dp, pair), pass_send, pass_recv).wait_send()
    self_copy.wait()
    for k in range(1, dp_count):
        slot_copy(k).wait_send()
        other = lax.rem(dp + dp_count - k, dp_count)
        remote(cot_ref.at[dp], returned_ref.at[other], slot_send.at[k], slot_recv.at[k], (other, mp)).wait_recv()
    for i, owner in enumerate((mp, pair, across, far)):
        store(i, owner).wait()
    if capacity % 16 == 0:
        back = returned_ref[...].reshape(slots, cot_ref.shape[2])
        grad_ref[...] = lax.dot_general(place_ref[...], back, TN, preferred_element_type=jnp.float32).astype(jnp.bfloat16)
    else:
        rank_col = columns_of(rank_row)[:, :capacity]
        lane = lax.broadcasted_iota(jnp.int32, (own, capacity), 1).astype(jnp.float32)

        def take(d, total):
            pick = (owner_col[:, :capacity] == d.astype(jnp.float32)) & (rank_col == lane)
            pick = jnp.where(pick, 1.0, 0.0).astype(jnp.bfloat16)
            return total + jnp.dot(pick, returned_ref[d], preferred_element_type=jnp.float32)
        grad_ref[...] = lax.fori_loop(0, dp_count, take, jnp.zeros(grad_ref.shape, jnp.float32)).astype(jnp.bfloat16)


def project(tokens, gain, w_qkv, cot, owners):
    own, width = tokens.shape
    dp_count = cot.shape[0]
    total = own * 4
    cols = w_qkv.shape[1]
    vmem = pl.BlockSpec(memory_space=pltpu.VMEM)
    hbm = pl.BlockSpec(memory_space=pltpu.HBM)
    dma = pltpu.SemaphoreType.DMA
    return pl.pallas_call(
        functools.partial(project_kernel, dp_count),
        out_shape=[jax.ShapeDtypeStruct((total, width), jnp.bfloat16)]
        + [jax.ShapeDtypeStruct((total, cols), jnp.bfloat16)] * 3
        + [jax.ShapeDtypeStruct((own, width), jnp.bfloat16), jax.ShapeDtypeStruct((dp_count * cot.shape[1], own), jnp.bfloat16)],
        in_specs=[hbm, vmem, hbm, hbm, vmem],
        out_specs=[hbm] + [vmem] * 5,
        scratch_shapes=[
            pltpu.VMEM(tokens.shape, tokens.dtype), pltpu.VMEM(w_qkv.shape, w_qkv.dtype),
            pltpu.VMEM((total, width), jnp.bfloat16), dma((2,)), dma((4,)), pltpu.VMEM(cot.shape, cot.dtype),
        ] + [dma((PARTS,))] * 6 + [dma((dp_count,))] * 2 + [dma],
        compiler_params=pltpu.CompilerParams(collective_id=1, has_side_effects=True, vmem_limit_bytes=VMEM_BYTES),
        cost_estimate=pl.CostEstimate(flops=6 * total * width * cols, bytes_accessed=10 * total * width, transcendentals=0),
        name="project",
    )(tokens, gain, w_qkv, cot, owners)


def gelu_and_slope(values):
    cumulative = 0.5 * (1.0 + lax.erf(values * 0.7071067811865476))
    density = jnp.exp(-0.5 * values * values) * 0.3989422804014327
    return values * cumulative, cumulative + values * density


def middle_kernel(
    stages, merged_hbm, w_out_hbm, tokens_hbm, gain_ref, w_up_hbm, w_down_hbm, grad_own_hbm, grad_across_hbm, place_hbm,
    back_rows_hbm, grad_merged_hbm, grad_residual_hbm, outgoing_hbm, first_hbm, second_hbm, gain_part_ref, d_out_ref,
    merged_ref, w_out_ref, tokens_ref, w_up_ref, w_down_ref, grad_own_ref, grad_across_ref, place_ref,
    back_rows_ref, grad_merged_ref, grad_residual_ref, outgoing_ref, d_mlp_ref, load_sem, store_sem,
    mlp_rows, grad_rows, active, grad_pre, residual, mine, bufs,
    sum_send, sum_recv, row_send, row_recv, grad_send, grad_recv, self_sem, acc, came, dp_send, dp_recv,
):
    first_rows = first_hbm.shape[0]
    loads = [
        pltpu.make_async_copy(src, dst, load_sem.at[i])
        for i, (src, dst) in enumerate((
            (merged_hbm, merged_ref), (w_out_hbm, w_out_ref), (tokens_hbm, tokens_ref), (grad_own_hbm, grad_own_ref),
            (grad_across_hbm, grad_across_ref), (w_up_hbm, w_up_ref), (w_down_hbm, w_down_ref), (place_hbm, place_ref),
        ))
    ]
    for load in loads:
        load.start()
    stores = [
        pltpu.make_async_copy(src, dst, store_sem.at[i])
        for i, (src, dst) in enumerate((
            (back_rows_ref, back_rows_hbm), (grad_merged_ref, grad_merged_hbm), (grad_residual_ref, grad_residual_hbm),
            (outgoing_ref, outgoing_hbm), (d_mlp_ref.at[0:first_rows], first_hbm), (d_mlp_ref.at[first_rows:], second_hbm),
        ))
    ]
    low, full = jnp.bfloat16, jnp.float32
    dp, mp = lax.axis_index("dp"), lax.axis_index("mp")
    pair, across, far = mp ^ 1, mp ^ 2, mp ^ 3
    own, width = tokens_ref.shape
    part = own // PARTS
    to_pair, to_across = (dp, pair), (dp, across)
    greet([to_pair, to_across] + [(dp ^ (1 << j), mp) for j in range(stages)])
    add_step, add_drain = sum_steps(stages, MLP_CHUNKS, acc, came, dp_send, dp_recv, d_mlp_ref, half=True)
    target = acc if stages else d_mlp_ref

    def spot(owner, c=None):
        if c is None:
            return pl.ds(pl.multiple_of(owner * own, own), own)
        return pl.ds(pl.multiple_of(owner * own + c * part, part), part)

    def piece(c):
        return pl.ds(pl.multiple_of(c * part, part), part)

    def grad_copy(i, owner, src):
        return remote(src, grad_rows.at[spot(owner)], grad_send.at[i], grad_recv.at[i], to_pair)

    local_copies = [
        pltpu.make_async_copy(grad_own_ref, grad_rows.at[spot(mp)], self_sem.at[0]),
        pltpu.make_async_copy(grad_across_ref, grad_rows.at[spot(across)], self_sem.at[1]),
    ]

    FAR, ACROSS, PAIR = 0, 1, 2

    def sum_copy(which, kind, c):
        src, dst = bufs.at[which, 0, kind, piece(c)], bufs.at[which, 1, kind, piece(c)]
        return remote(src, dst, sum_send.at[which, kind, c], sum_recv.at[which, kind, c], to_across if kind == ACROSS else to_pair)

    def arrived(which, kind, c):
        sum_copy(which, kind, c).wait_recv()
        return bufs[which, 1, kind, piece(c), :].astype(full)

    def ship(which, kind, c, values):
        bufs[which, 0, kind, piece(c), :] = values.astype(low)
        sum_copy(which, kind, c).start()

    def row_copy(which, kind, c, owner, ref):
        rows = ref.at[spot(owner, c)]
        return remote(rows, rows, row_send.at[which, kind, c], row_recv.at[which, kind, c], to_across if kind == 0 else to_pair)

    def each(count, body):
        def step(i, _):
            body(i)
            return 0
        lax.fori_loop(0, count, step, 0)

    def out_part(owner):
        return jnp.dot(merged_ref[spot(owner), :], w_out_ref[...], preferred_element_type=full)

    loads[0].wait()
    loads[1].wait()
    bufs[0, 0, FAR] = out_part(far).astype(low)
    each(PARTS, lambda c: sum_copy(0, FAR, c).start())
    mine[0] = out_part(across)

    def pass_across(c):
        ship(0, ACROSS, c, mine[0, piece(c), :] + arrived(0, FAR, c))
    each(PARTS, pass_across)
    bufs[0, 0, PAIR] = out_part(pair).astype(low)
    each(PARTS, lambda c: sum_copy(0, PAIR, c).start())
    for load in loads[2:5]:
        load.wait()
    for copy in local_copies:
        copy.start()
    grad_copy(0, mp, grad_own_ref).start()
    grad_copy(1, across, grad_across_ref).start()
    mine[0] = out_part(mp) + tokens_ref[...].astype(full)
    for copy in local_copies:
        copy.wait()
    grad_copy(0, pair, grad_own_ref).wait_recv()
    grad_copy(1, far, grad_across_ref).wait_recv()

    for load in loads[5:8]:
        load.wait()
    blocks = w_up_ref.shape[1] // 256
    both = 2 * part

    def mlp(first, second, c):
        rows = jnp.concatenate([mlp_rows[spot(first, c), :], mlp_rows[spot(second, c), :]], axis=0)
        grads = jnp.concatenate([grad_rows[spot(first, c), :], grad_rows[spot(second, c), :]], axis=0)

        def block(b):
            cols = pl.ds(pl.multiple_of(b * 256, 256), 256)
            pre = jnp.dot(rows, w_up_ref[:, cols], preferred_element_type=full)
            value, slope = gelu_and_slope(pre)
            value = value.astype(low)
            active[spot(first, c), cols] = value[:part]
            active[spot(second, c), cols] = value[part:]
            back = (jnp.dot(grads, w_down_ref[:, cols], preferred_element_type=full) * slope).astype(low)
            grad_pre[spot(first, c), cols] = back[:part]
            grad_pre[spot(second, c), cols] = back[part:]
        each(blocks, block)
        back = jnp.concatenate([grad_pre[spot(first, c), :], grad_pre[spot(second, c), :]], axis=0)
        return lax.dot_general(back, w_up_ref[...], NT, preferred_element_type=full)

    def near(c):
        values = mine[0, piece(c), :] + arrived(0, PAIR, c) + arrived(0, ACROSS, c)
        residual[piece(c), :] = values
        unit, _ = norm_unit(values)
        mlp_rows[spot(mp, c), :] = (unit * gain_ref[1:2, :]).astype(low)
        row_copy(0, 0, c, mp, mlp_rows).start()
        row_copy(0, 1, c, mp, mlp_rows).start()
        row_copy(0, 1, c, pair, mlp_rows).wait_recv()
        got = mlp(mp, pair, c)
        mine[1, piece(c), :] = got[:part]
        ship(1, PAIR, c, got[part:])
    each(PARTS, near)

    def distant(c):
        row_copy(0, 0, c, across, mlp_rows).wait_recv()
        row_copy(0, 2, c, across, mlp_rows).start()
        row_copy(0, 2, c, far, mlp_rows).wait_recv()
        got = mlp(far, across, c)
        ship(1, FAR, c, got[:part])
        ship(1, ACROSS, c, got[part:] + arrived(1, FAR, c))
    each(PARTS, distant)

    size = width // MLP_CHUNKS
    for b in range(3):
        cols = slice(b * 256, (b + 1) * 256)
        up = lax.dot_general(mlp_rows[:, cols], grad_pre[...], TN, preferred_element_type=full)
        gain_col = jnp.sum(up * w_up_ref[cols, :].astype(full), axis=1, keepdims=True)
        gain_part_ref[:, cols] = jnp.broadcast_to(gain_col, (256, 128)).T[0:8] / gain_ref[1:2, cols]
        up = up.astype(low)
        down = lax.dot_general(grad_rows[:, cols], active[...], TN, preferred_element_type=full).astype(low)
        for j in range(256 // size):
            k = b * (256 // size) + j
            target[2 * k * size:(2 * k + 1) * size, :] = up[j * size:(j + 1) * size]
            target[(2 * k + 1) * size:(2 * k + 2) * size, :] = down[j * size:(j + 1) * size]
            if stages:
                add_step(k, 0)

    def add(*steps):
        if stages:
            for k, i in steps:
                add_step(k, i)

    def down_part(owner):
        return lax.dot_general(active[spot(owner), :], w_down_ref[...], NT, preferred_element_type=full)

    bufs[2, 0, FAR] = down_part(far).astype(low)
    each(PARTS, lambda c: sum_copy(2, FAR, c).start())
    bufs[2, 0, PAIR] = down_part(pair).astype(low)
    each(PARTS, lambda c: sum_copy(2, PAIR, c).start())

    def back_norm(c):
        grad = mine[1, piece(c), :] + arrived(1, PAIR, c) + arrived(1, ACROSS, c)
        unit, inverse = norm_unit(residual[piece(c), :])
        scaled = grad * gain_ref[1:2, :]
        first_mean = jnp.mean(scaled, axis=-1, keepdims=True)
        second_mean = jnp.mean(scaled * unit, axis=-1, keepdims=True)
        total = inverse * (scaled - first_mean - unit * second_mean) + grad_own_ref[piece(c), :].astype(full)
        grad_residual_ref[piece(c), :] = total
        back_rows_ref[spot(mp, c), :] = total.astype(low)
        row_copy(1, 0, c, mp, back_rows_ref).start()
        row_copy(1, 1, c, mp, back_rows_ref).start()
    def tick(t):
        add(*[(t - i, i) for i in range(2 * stages, 0, -1) if 0 <= t - i < MLP_CHUNKS])

    each(2, back_norm)
    tick(1)
    each(1, lambda c: back_norm(c + 2))
    tick(2)
    each(1, lambda c: back_norm(c + 3))

    mine[1] = down_part(across)

    def pass_output(c):
        ship(2, ACROSS, c, mine[1, piece(c), :] + arrived(2, FAR, c))
    each(PARTS, pass_output)
    tick(3)
    mine[0] = residual[...] + down_part(mp)

    def merged_part(owner):
        grad_merged_ref[spot(owner), :] = lax.dot_general(
            back_rows_ref[spot(owner), :], w_out_ref[...], NT, preferred_element_type=full
        ).astype(low)

    merged_part(mp)
    each(PARTS, lambda c: row_copy(1, 1, c, pair, back_rows_ref).wait_recv())
    merged_part(pair)

    def hand_on(c):
        row_copy(1, 0, c, across, back_rows_ref).wait_recv()
        row_copy(1, 2, c, across, back_rows_ref).start()
    for c in range(PARTS):
        each(1, lambda i: hand_on(i + c))
        tick(4 + c)
    merged_part(across)
    each(PARTS, lambda c: row_copy(1, 2, c, far, back_rows_ref).wait_recv())
    merged_part(far)
    stores[0].start()
    stores[1].start()
    stores[2].start()
    d_out_ref[...] = lax.dot_general(merged_ref[...], back_rows_ref[...], TN, preferred_element_type=full).astype(low)

    def finish(c):
        mine[0, piece(c), :] = mine[0, piece(c), :] + arrived(2, PAIR, c) + arrived(2, ACROSS, c)
    for c in range(PARTS):
        each(1, lambda i: finish(i + c))
        tick(8 + c)
    stores[4].start()
    stores[5].start()
    outgoing_ref[...] = jnp.dot(place_ref[...], mine[0].astype(low), preferred_element_type=full).astype(low)
    stores[3].start()
    if stages:
        add_drain()
    for store in stores:
        store.wait()

    def drain(c):
        for which in range(3):
            for kind in range(3):
                sum_copy(which, kind, c).wait_send()
        for which, ref in ((0, mlp_rows), (1, back_rows_ref)):
            row_copy(which, 0, c, mp, ref).wait_send()
            row_copy(which, 1, c, mp, ref).wait_send()
            row_copy(which, 2, c, across, ref).wait_send()
    each(PARTS, drain)
    grad_copy(0, mp, grad_own_ref).wait_send()
    grad_copy(1, across, grad_across_ref).wait_send()


def middle(dp_count, merged, w_out, tokens, gain, w_up, w_down, grad_own, grad_across, place):
    stages = sum_stages(2 * w_up.shape[0], MLP_CHUNKS, dp_count)
    d_rows = w_up.shape[0] * (1 if stages else 2)
    total, cols = merged.shape
    own, width = tokens.shape
    hidden = w_up.shape[1]
    slots = place.shape[0]
    low, full = jnp.bfloat16, jnp.float32
    vmem = pl.BlockSpec(memory_space=pltpu.VMEM)
    hbm = pl.BlockSpec(memory_space=pl.ANY)
    dma = pltpu.SemaphoreType.DMA
    shape, room = jax.ShapeDtypeStruct, pltpu.VMEM
    return pl.pallas_call(
        functools.partial(middle_kernel, stages),
        out_shape=[
            shape((total, width), low), shape((total, cols), low), shape((own, width), full), shape((slots, width), low),
            shape((d_rows // 2, hidden), low), shape((d_rows // 2, hidden), low), shape((8, width), full), shape((cols, width), low),
        ],
        in_specs=[hbm] * 3 + [vmem] + [hbm] * 5,
        out_specs=[hbm] * 6 + [vmem] * 2,
        scratch_shapes=[
            room((total, cols), low), room(w_out.shape, low), room((own, width), low), room(w_up.shape, low),
            room(w_down.shape, low), room((own, width), low), room((own, width), low), room(place.shape, low),
            room((total, width), low), room((total, cols), low), room((own, width), full), room((slots, width), low),
            room((d_rows, hidden), low), dma((8,)), dma((6,)),
            room((total, width), low), room((total, width), low),
            room((total, hidden), low), room((total, hidden), low),
            room((own, width), full), room((2, own, width), full),
            room((3, 2, 3, own, width), low),
            dma((3, 3, PARTS)), dma((3, 3, PARTS)), dma((2, 3, PARTS)), dma((2, 3, PARTS)), dma((2,)), dma((2,)), dma((2,)),
        ]
        + sum_scratch(2 * width, hidden, MLP_CHUNKS, stages),
        compiler_params=pltpu.CompilerParams(collective_id=2, has_side_effects=True, vmem_limit_bytes=VMEM_BYTES),
        cost_estimate=pl.CostEstimate(flops=16 * total * width * hidden, bytes_accessed=20 * total * width, transcendentals=0),
        name="middle",
    )(merged, w_out, tokens, gain, w_up, w_down, grad_own, grad_across, place)


def last_kernel(
    dp_count, stages, dq_ref, dk_ref, dv_ref, w_hbm, rows_hbm, grad_residual_hbm, tokens_hbm, gain_ref, gain_part_ref, d_out_ref,
    grad_tokens_ref, d_sum_ref, gains_ref,
    w_ref, rows_ref, grad_residual_ref, tokens_ref, load_sem, mine, bufs, gain_mine, gain_came, sum_send, sum_recv, gain_send, gain_recv, acc, came, dp_send, dp_recv,
):
    load_w = pltpu.make_async_copy(w_hbm, w_ref, load_sem.at[0])
    load_rows = pltpu.make_async_copy(rows_hbm, rows_ref, load_sem.at[1])
    load_residual = pltpu.make_async_copy(grad_residual_hbm, grad_residual_ref, load_sem.at[2])
    load_tokens = pltpu.make_async_copy(tokens_hbm, tokens_ref, load_sem.at[3])
    for load in (load_w, load_rows, load_residual, load_tokens):
        load.start()
    low, full = jnp.bfloat16, jnp.float32
    dp, mp = lax.axis_index("dp"), lax.axis_index("mp")
    pair, across, far = mp ^ 1, mp ^ 2, mp ^ 3
    own, width = tokens_ref.shape
    part = own // PARTS
    cols = dq_ref.shape[1]
    to_pair, to_across = (dp, pair), (dp, across)
    links = [to_pair, to_across] + [(dp ^ (1 << j), mp) for j in range(dp_count.bit_length() - 1)]
    greet(links)
    add_step, add_drain = sum_steps(stages, QKV_CHUNKS, acc, came, dp_send, dp_recv, d_sum_ref)
    target = acc if stages else d_sum_ref
    chunk = target.shape[0] // QKV_CHUNKS
    FAR, ACROSS, PAIR = 0, 1, 2

    def add(*steps):
        if stages:
            for k, i in steps:
                if 0 <= k < QKV_CHUNKS:
                    add_step(k, i)

    def tick(t):
        add(*[(t - i, i) for i in range(2 * stages, 0, -1)])

    def piece(c):
        return pl.ds(pl.multiple_of(c * part, part), part)

    def each(count, body):
        def step(i, _):
            body(i)
            return 0
        lax.fori_loop(0, count, step, 0)

    def sum_copy(kind, c):
        src, dst = bufs.at[0, kind, piece(c)], bufs.at[1, kind, piece(c)]
        return remote(src, dst, sum_send.at[kind, c], sum_recv.at[kind, c], to_across if kind == ACROSS else to_pair)

    def arrived(kind, c):
        sum_copy(kind, c).wait_recv()
        return bufs[1, kind, piece(c), :].astype(full)

    def in_part(owner):
        where = pl.ds(pl.multiple_of(owner * own, own), own)
        total = jnp.dot(dq_ref[where, :], w_ref[0], preferred_element_type=full)
        total = total + jnp.dot(dk_ref[where, :], w_ref[1], preferred_element_type=full)
        return total + jnp.dot(dv_ref[where, :], w_ref[2], preferred_element_type=full)

    def ready(low_row, high_row):
        add(*[(k, 0) for k in range(QKV_CHUNKS) if low_row < (k + 1) * chunk <= high_row])

    target[0:cols, :] = d_out_ref[...]
    ready(0, cols)

    def weight_grad(p, ref, gain_row):
        grad = lax.dot_general(ref[...], rows_ref[...], TN, preferred_element_type=full)
        target[(p + 1) * cols:(p + 2) * cols, :] = grad.astype(low)
        ready((p + 1) * cols, (p + 2) * cols)
        return gain_row + jnp.sum(grad * w_ref[p].astype(full), axis=0, keepdims=True)

    load_w.wait()
    bufs[0, FAR] = in_part(far).astype(low)
    each(PARTS, lambda c: sum_copy(FAR, c).start())
    load_rows.wait()
    gain_row = weight_grad(0, dq_ref, jnp.zeros((1, width), full))
    mine[...] = in_part(across)

    def pass_across(c):
        bufs[0, ACROSS, piece(c), :] = (mine[piece(c), :] + arrived(FAR, c)).astype(low)
        sum_copy(ACROSS, c).start()
    each(PARTS, pass_across)
    gain_row = weight_grad(1, dk_ref, gain_row)
    gain_row = weight_grad(2, dv_ref, gain_row)
    bufs[0, PAIR] = in_part(pair).astype(low)
    each(PARTS, lambda c: sum_copy(PAIR, c).start())

    def gain_copy(i):
        return remote(gain_mine.at[i], gain_came.at[i], gain_send.at[i], gain_recv.at[i], links[i])

    def gain_step(i):
        gain_copy(i).wait_recv()
        gain_mine[i + 1] = gain_mine[i] + gain_came[i]
        if i + 1 < len(links):
            gain_copy(i + 1).start()

    row = lax.broadcasted_iota(jnp.int32, (8, width), 0)
    gain_mine[0] = jnp.where(row == 0, gain_part_ref[...], jnp.where(row == 1, gain_row / gain_ref[0:1, :], 0.0))
    gain_copy(0).start()
    mine[...] = in_part(mp)
    load_residual.wait()
    load_tokens.wait()

    def back_norm(c):
        grad = mine[piece(c), :] + arrived(PAIR, c) + arrived(ACROSS, c)
        unit, inverse = norm_unit(tokens_ref[piece(c), :].astype(full))
        scaled = grad * gain_ref[0:1, :]
        first_mean = jnp.mean(scaled, axis=-1, keepdims=True)
        second_mean = jnp.mean(scaled * unit, axis=-1, keepdims=True)
        total = inverse * (scaled - first_mean - unit * second_mean) + grad_residual_ref[piece(c), :]
        grad_tokens_ref[piece(c), :] = total.astype(low)

    for t in range(1, QKV_CHUNKS + 2 * stages if stages else 1):
        tick(t)
        for c, when in enumerate(NORM_TICKS):
            if t == when:
                each(1, lambda i: back_norm(i + c))
        if 2 <= t < 2 + len(links):
            gain_step(t - 2)
    if not stages:
        each(PARTS, back_norm)
        for i in range(len(links)):
            gain_step(i)
    gains_ref[...] = gain_mine[len(links)]
    if stages:
        add_drain()
    for i in range(len(links)):
        gain_copy(i).wait_send()

    def drain(c):
        for kind in range(3):
            sum_copy(kind, c).wait_send()
    each(PARTS, drain)


def last(dp_count, dq, dk, dv, w_qkv, rows, grad_residual, tokens, gain, gain_part, d_out):
    own, width = tokens.shape
    cols = dq.shape[1]
    d_rows = 4 * cols
    stages = sum_stages(d_rows, QKV_CHUNKS, dp_count)
    low, full = jnp.bfloat16, jnp.float32
    count = 2 + dp_count.bit_length() - 1
    hbm = pl.BlockSpec(memory_space=pltpu.HBM)
    vmem = pl.BlockSpec(memory_space=pltpu.VMEM)
    dma = pltpu.SemaphoreType.DMA
    shape = jax.ShapeDtypeStruct
    grad_tokens, d_sum, gains = pl.pallas_call(
        functools.partial(last_kernel, dp_count, stages),
        out_shape=[shape((own, width), low), shape((d_rows, width), low), shape((8, width), full)],
        in_specs=[vmem] * 3 + [hbm] * 4 + [vmem] * 3,
        out_specs=[vmem] * 3,
        scratch_shapes=[
            pltpu.VMEM(w_qkv.shape, low), pltpu.VMEM(rows.shape, low), pltpu.VMEM((own, width), full),
            pltpu.VMEM((own, width), low), dma((4,)),
            pltpu.VMEM((own, width), full), pltpu.VMEM((2, 3, own, width), low),
            pltpu.VMEM((count + 1, 8, width), full), pltpu.VMEM((count, 8, width), full),
            dma((3, PARTS)), dma((3, PARTS)), dma((count,)), dma((count,)),
        ]
        + sum_scratch(d_rows, width, QKV_CHUNKS, stages),
        compiler_params=pltpu.CompilerParams(collective_id=3, has_side_effects=True, vmem_limit_bytes=VMEM_BYTES),
        cost_estimate=pl.CostEstimate(flops=12 * 4 * own * width * cols, bytes_accessed=20 * own * width, transcendentals=0),
        name="last",
    )(dq, dk, dv, w_qkv, rows, grad_residual, tokens, gain, gain_part, d_out)
    return grad_tokens, d_sum if stages else lax.psum(d_sum, "dp"), gains


def local(
    tokens, segment_ids, gene_owner, w_qkv, w_attn_out, w_up, w_down, gain_attn, gain_mlp, cotangent
):
    width = tokens.shape[1]
    dp_count = lax.axis_size("dp")
    capacity = cotangent.shape[0] // dp_count
    low, full = jnp.bfloat16, jnp.float32
    w_rows = jnp.swapaxes(w_qkv, 1, 2)
    gains_in = jnp.stack([gain_attn, gain_mlp])
    attn_in, *projected, grad_block, place = project(
        tokens, gains_in, w_rows, cotangent.reshape(dp_count, capacity, width), gene_owner.reshape(1, -1)
    )
    grad_across = lax.ppermute(grad_block, "mp", [(i, i ^ 2) for i in range(lax.axis_size("mp"))])
    merged, log_sums = attend_forward(segment_ids, *projected)
    residual_rows, grad_merged, grad_residual, outgoing, first, second, gain_part, d_out = middle(
        dp_count, merged, w_attn_out, tokens, gains_in, w_up, w_down, grad_block, grad_across, place
    )
    cols = w_qkv.shape[2]
    if sum_stages(2 * width, MLP_CHUNKS, dp_count):
        size = width // MLP_CHUNKS
        place_y = lax.rem(lax.axis_index("dp"), 2) == 0
        place_z = lax.rem(lax.axis_index("dp") // 2, 2) == 0
        count = sum(left_bit(k, MLP_CHUNKS) == 0 for k in range(MLP_CHUNKS))
        first_came = lax.ppermute(first, "dp", [(i, i ^ 1) for i in range(dp_count)])
        second_came = lax.ppermute(second, "dp", [(i, i ^ 2) for i in range(dp_count)])
        gain_part, first_came, second_came = lax.optimization_barrier((gain_part, first_came, second_came))
        first = [jnp.where(place_y, first, first_came), jnp.where(place_y, first_came, first)]
        second = jnp.stack(
            [
                one.reshape(MLP_CHUNKS - count, 2, size // 2, width)
                for one in (jnp.where(place_z, second, second_came), jnp.where(place_z, second_came, second))
            ],
            axis=2,
        )
        up_sum, down_sum = (
            jnp.concatenate([first[i], second[:, i].reshape(-1, width)]).astype(full) for i in range(2)
        )
    else:
        d_sum = lax.psum(jnp.concatenate([first, second]), "dp").reshape(MLP_CHUNKS, 2, -1, width).astype(full)
        up_sum, down_sum = (d_sum[:, i].reshape(-1, width) for i in range(2))
    relaid = lax.all_to_all(
        outgoing.reshape(dp_count, capacity, width), "dp", split_axis=0, concat_axis=0, tiled=True
    ).reshape(dp_count * capacity, width)
    grad_proj = attend_backward(segment_ids, *projected, merged, grad_merged, log_sums)
    grad_tokens, weight_sum, gains = last(
        dp_count, *grad_proj, w_rows, attn_in, grad_residual, tokens, gains_in, gain_part, d_out
    )
    qkv_sum = weight_sum[cols:].reshape(3, cols, width).astype(full)
    attn_sum = weight_sum[:cols].astype(full)
    return (
        relaid,
        grad_tokens,
        jnp.swapaxes(qkv_sum, 1, 2),
        attn_sum,
        up_sum,
        down_sum,
        gains[1],
        gains[0],
    )


def solution(mesh):
    placed = (
        P(("dp", "mp"), None),
        P("dp", None),
        P(("dp", "mp"), None),
        P(None, None, "mp"),
        P("mp", None),
        P(None, "mp"),
        P(None, "mp"),
        P(),
        P(),
        P(("dp", "mp"), None),
    )
    return jax.shard_map(
        local,
        mesh=mesh,
        in_specs=placed,
        out_specs=(
            P(("dp", "mp"), None),
            P(("dp", "mp"), None),
            P(None, None, "mp"),
            P("mp", None),
            P(None, "mp"),
            P(None, "mp"),
            P(),
            P(),
        ),
        check_vma=False,
    )
```

```python
import functools
import jax
import jax.numpy as jnp
from jax import lax
from jax.experimental import pallas as pl
from jax.experimental.pallas import tpu as pltpu
from jax.sharding import PartitionSpec as P

HEAD = 64
TQ = 256
TK = 512
NT = (((1,), (1,)), ((), ()))
NN = (((1,), (0,)), ((), ()))
TN = (((0,), (0,)), ((), ()))
MASKED = -1e30
epsilon = 1e-05


def local_copies(pairs, sems):
    return [pltpu.make_async_copy(src, dst, sems.at[i]) for i, (src, dst) in enumerate(pairs)]


def lower_bound(seg, n, value):
    def step(_, c):
        lo, hi = c
        mid = (lo + hi) // 2
        less = seg[jnp.minimum(mid, n - 1)] < value
        go = lo < hi
        return (jnp.where(go & less, mid + 1, lo), jnp.where(go & ~less, mid, hi))
    lo, hi = lax.fori_loop(0, n.bit_length(), step, (jnp.int32(0), jnp.int32(n)))
    return lo


def key_range(seg, n, tile):
    first = lower_bound(seg, n, seg[tile * TQ])
    end = lower_bound(seg, n, seg[tile * TQ + TQ - 1] + 1)
    return first // TK, (end + TK - 1) // TK


def head_masks(width, heads):
    lane = lax.broadcasted_iota(jnp.int32, (1, width), 1)
    return [(lane // HEAD == h) for h in range(heads)]


def seg_columns(segv_ref, cols, n):
    for t in range(n // 128):
        row = segv_ref[0:1, t * 128:(t + 1) * 128].astype(jnp.float32)
        cols[t * 128:(t + 1) * 128, :] = jnp.broadcast_to(row, (128, 128)).T


def fwd_kernel(n, heads, seg, segv_ref, q_ref, k_ref, v_ref, o_ref, lse_ref, vt, cols, scores):
    tile = pl.program_id(0)
    width = heads * HEAD

    @pl.when(tile == 0)
    def _():
        seg_columns(segv_ref, cols, n)
        for t in range(n // TK):
            vt[:, t * TK:(t + 1) * TK] = v_ref[t * TK:(t + 1) * TK, :].astype(jnp.float32).T.astype(jnp.bfloat16)

    lo, hi = key_range(seg, n, tile)
    q0 = pl.multiple_of(tile * TQ, TQ)
    q = q_ref[...] * jnp.bfloat16(HEAD ** -0.5)
    masks = head_masks(width, heads)
    qm = [jnp.where(m, q, jnp.bfloat16(0)) for m in masks]
    seg_row = segv_ref[0:1, pl.ds(q0, TQ)].astype(jnp.float32)

    def first(b, tops):
        k0 = pl.multiple_of(b * TK, TK)
        keys = k_ref[pl.ds(k0, TK), :]
        col = cols[pl.ds(k0, TK), :]
        same = jnp.concatenate([col] * (TQ // 128), axis=1) == seg_row
        out = []
        for h in range(heads):
            s = lax.dot_general(keys, qm[h], NT, preferred_element_type=jnp.float32)
            s = jnp.where(same, s, MASKED)
            scores[h, pl.ds(k0, TK), :] = s
            out.append(jnp.maximum(tops[h], jnp.max(s, axis=0, keepdims=True)))
        return tuple(out)

    tops = lax.fori_loop(lo, hi, first, tuple(jnp.full((1, TQ), MASKED, jnp.float32) for _ in range(heads)))

    def second(b, acc):
        k0 = pl.multiple_of(b * TK, TK)
        out = []
        for h in range(heads):
            p = jnp.exp(scores[h, pl.ds(k0, TK), :] - tops[h])
            total = acc[h][1] + jnp.sum(p, axis=0, keepdims=True)
            part = lax.dot_general(vt[h * HEAD:(h + 1) * HEAD, pl.ds(k0, TK)], p.astype(jnp.bfloat16), NN, preferred_element_type=jnp.float32)
            out.append((acc[h][0] + part, total))
        return tuple(out)

    acc = lax.fori_loop(lo, hi, second, tuple((jnp.zeros((HEAD, TQ), jnp.float32), jnp.zeros((1, TQ), jnp.float32)) for _ in range(heads)))
    ot = jnp.concatenate([acc[h][0] / acc[h][1] for h in range(heads)], axis=0)
    o_ref[...] = ot.T.astype(jnp.bfloat16)
    lse_ref[...] = jnp.concatenate([tops[h] + jnp.log(acc[h][1]) for h in range(heads)] + [jnp.zeros((8 - heads, TQ), jnp.float32)], axis=0)


def attend_forward(seg, q, k, v):
    n, width = q.shape
    heads = width // HEAD
    whole = pl.BlockSpec(memory_space=pltpu.VMEM)
    return pl.pallas_call(
        functools.partial(fwd_kernel, n, heads),
        grid_spec=pltpu.PrefetchScalarGridSpec(
            num_scalar_prefetch=1,
            grid=(n // TQ,),
            in_specs=[whole, pl.BlockSpec((TQ, width), lambda t, s: (t, 0)), whole, whole],
            out_specs=[pl.BlockSpec((TQ, width), lambda t, s: (t, 0)), pl.BlockSpec((8, TQ), lambda t, s: (0, t))],
            scratch_shapes=[pltpu.VMEM((width, n), jnp.bfloat16), pltpu.VMEM((n, 128), jnp.float32), pltpu.VMEM((heads, n, TQ), jnp.float32)],
        ),
        out_shape=[jax.ShapeDtypeStruct((n, width), jnp.bfloat16), jax.ShapeDtypeStruct((8, n), jnp.float32)],
        compiler_params=pltpu.CompilerParams(vmem_limit_bytes=VMEM_BYTES),
        cost_estimate=pl.CostEstimate(flops=4 * heads * n * n * HEAD, bytes_accessed=8 * n * width, transcendentals=heads * n * n // 2),
        name="attend_forward",
    )(seg.reshape(-1), seg.reshape(1, -1), q, k, v)


def bwd_kernel(n, heads, seg, segv_ref, q_ref, k_ref, v_ref, o_ref, do_ref, lse_ref, dq_ref, dk_ref, dv_ref, kt, cols, dk_acc, dv_acc):
    tile = pl.program_id(0)
    width = heads * HEAD

    @pl.when(tile == 0)
    def _():
        seg_columns(segv_ref, cols, n)
        for t in range(n // TK):
            kt[:, t * TK:(t + 1) * TK] = k_ref[t * TK:(t + 1) * TK, :].astype(jnp.float32).T.astype(jnp.bfloat16)
        dk_acc[...] = jnp.zeros_like(dk_acc)
        dv_acc[...] = jnp.zeros_like(dv_acc)

    lo, hi = key_range(seg, n, tile)
    q0 = pl.multiple_of(tile * TQ, TQ)
    masks = head_masks(width, heads)
    q = q_ref[...] * jnp.bfloat16(HEAD ** -0.5)
    do = do_ref[...]
    qm = [jnp.where(m, q, jnp.bfloat16(0)) for m in masks]
    dm = [jnp.where(m, do, jnp.bfloat16(0)) for m in masks]
    seg_row = segv_ref[0:1, pl.ds(q0, TQ)].astype(jnp.float32)
    prod = do.astype(jnp.float32) * o_ref[...].astype(jnp.float32)
    high = prod.astype(jnp.bfloat16)
    rest = (prod - high.astype(jnp.float32)).astype(jnp.bfloat16)
    row = lax.broadcasted_iota(jnp.int32, (16, width), 0)
    lane = lax.broadcasted_iota(jnp.int32, (16, width), 1)
    pick = jnp.where(lane // HEAD == row, 1.0, 0.0).astype(jnp.bfloat16)
    delta = lax.dot_general(pick, high, NT, preferred_element_type=jnp.float32) + lax.dot_general(pick, rest, NT, preferred_element_type=jnp.float32)
    lse = lse_ref[...]

    def body(b, acc):
        k0 = pl.multiple_of(b * TK, TK)
        keys = k_ref[pl.ds(k0, TK), :]
        vals = v_ref[pl.ds(k0, TK), :]
        col = cols[pl.ds(k0, TK), :]
        same = jnp.concatenate([col] * (TQ // 128), axis=1) == seg_row
        out = []
        dks = jnp.zeros((TK, width), jnp.float32)
        dvs = jnp.zeros((TK, width), jnp.float32)
        for h in range(heads):
            s = lax.dot_general(keys, qm[h], NT, preferred_element_type=jnp.float32)
            p = jnp.where(same, jnp.exp(s - lse[h:h + 1, :]), 0.0)
            dp = lax.dot_general(vals, dm[h], NT, preferred_element_type=jnp.float32)
            ds = (p * (dp - delta[h:h + 1, :])).astype(jnp.bfloat16)
            dvs = dvs + lax.dot_general(p.astype(jnp.bfloat16), dm[h], NN, preferred_element_type=jnp.float32)
            dks = dks + lax.dot_general(ds, qm[h], NN, preferred_element_type=jnp.float32)
            out.append(acc[h] + lax.dot_general(kt[h * HEAD:(h + 1) * HEAD, pl.ds(k0, TK)], ds, NN, preferred_element_type=jnp.float32))
        dk_acc[pl.ds(k0, TK), :] += dks
        dv_acc[pl.ds(k0, TK), :] += dvs
        return tuple(out)

    acc = lax.fori_loop(lo, hi, body, tuple(jnp.zeros((HEAD, TQ), jnp.float32) for _ in range(heads)))
    dq_ref[...] = (jnp.concatenate(acc, axis=0).T * HEAD ** -0.5).astype(jnp.bfloat16)

    @pl.when(tile == n // TQ - 1)
    def _():
        dk_ref[...] = dk_acc[...].astype(jnp.bfloat16)
        dv_ref[...] = dv_acc[...].astype(jnp.bfloat16)


def attend_backward(seg, q, k, v, o, do, lse):
    n, width = q.shape
    heads = width // HEAD
    whole = pl.BlockSpec(memory_space=pltpu.VMEM)
    rows = pl.BlockSpec((TQ, width), lambda t, s: (t, 0))
    return pl.pallas_call(
        functools.partial(bwd_kernel, n, heads),
        grid_spec=pltpu.PrefetchScalarGridSpec(
            num_scalar_prefetch=1,
            grid=(n // TQ,),
            in_specs=[whole, rows, whole, whole, rows, rows, pl.BlockSpec((8, TQ), lambda t, s: (0, t))],
            out_specs=[rows, whole, whole],
            scratch_shapes=[pltpu.VMEM((width, n), jnp.bfloat16), pltpu.VMEM((n, 128), jnp.float32), pltpu.VMEM((n, width), jnp.float32), pltpu.VMEM((n, width), jnp.float32)],
        ),
        out_shape=[jax.ShapeDtypeStruct((n, width), jnp.bfloat16)] * 3,
        compiler_params=pltpu.CompilerParams(vmem_limit_bytes=VMEM_BYTES),
        cost_estimate=pl.CostEstimate(flops=10 * heads * n * n * HEAD, bytes_accessed=16 * n * width, transcendentals=heads * n * n // 2),
        name="attend_backward",
    )(seg.reshape(-1), seg.reshape(1, -1), q, k, v, o, do, lse)


MESH_ID = pl.DeviceIdType.MESH
PARTS = 4
VMEM_BYTES = 60 << 20
MLP_CHUNKS = 6
QKV_CHUNKS = 3


def remote(src, dst, send, recv, device):
    return pltpu.make_async_remote_copy(
        src_ref=src, dst_ref=dst, send_sem=send, recv_sem=recv, device_id=device, device_id_type=MESH_ID
    )


def greet(devices):
    barrier = pltpu.get_barrier_semaphore()
    for device in devices:
        pl.semaphore_signal(barrier, inc=1, device_id=device, device_id_type=MESH_ID)
    pl.semaphore_wait(barrier, len(devices))


def norm_unit(values):
    average = jnp.mean(values, axis=-1, keepdims=True)
    centered = values - average
    variance = jnp.mean(centered * centered, axis=-1, keepdims=True)
    inverse = lax.rsqrt(variance + epsilon)
    return centered * inverse, inverse


def sum_stages(rows, chunks, dp_count):
    stages = dp_count.bit_length() - 1
    return stages if dp_count == 1 << stages and rows % (16 * chunks * dp_count) == 0 else 0


def sum_scratch(rows, width, chunks, stages):
    dma = pltpu.SemaphoreType.DMA
    return [
        pltpu.VMEM((rows, width), jnp.bfloat16), pltpu.VMEM((rows, width), jnp.bfloat16),
        dma((chunks, max(1, 2 * stages))), dma((chunks, max(1, 2 * stages))),
    ]


def left_bit(k):
    return k % 2


def packed(k, chunks):
    return k // 2 if k % 2 == 0 else (chunks + 1) // 2 + k // 2


def sum_steps(stages, chunks, acc, came, send, recv, out, half=False):
    dp, mp = lax.axis_index("dp"), lax.axis_index("mp")
    chunk = acc.shape[0] // chunks

    def bit(s):
        return lax.rem(dp // (1 << s), 2)

    def held(k, s):
        start = k * chunk
        for j in range(s):
            start = start + bit(j) * (chunk >> (j + 1))
        return start

    def span(start, size):
        return pl.ds(pl.multiple_of(start, 16), size)

    def placed(k, start):
        if not half:
            return start
        return packed(k, chunks) * (chunk // 2) + bit(1 - left_bit(k)) * (chunk // 4) + start - held(k, 2)

    def halve(k, s):
        size = chunk >> (s + 1)
        return remote(
            acc.at[span(held(k, s) + (1 - bit(s)) * size, size)],
            came.at[span(k * chunk + chunk - (chunk >> s), size)],
            send.at[k, s], recv.at[k, s], (dp ^ (1 << s), mp),
        )

    def double(k, s, mine=True):
        if half and s == 1:
            s = 1 - left_bit(k)
            place = bit(s) if mine else 1 - bit(s)
            rows = out.at[span(packed(k, chunks) * (chunk // 2) + place * (chunk // 4), chunk // 4)]
            return remote(rows, rows, send.at[k, stages + 1], recv.at[k, stages + 1], (dp ^ (1 << s), mp))
        size = chunk >> (s + 1)
        start = held(k, s + 1) if mine else held(k, s) + (1 - bit(s)) * size
        rows = out.at[span(placed(k, start), size)]
        return remote(rows, rows, send.at[k, stages + s], recv.at[k, stages + s], (dp ^ (1 << s), mp))

    final = 1 if half else 0

    def step(k, i):
        if i == 0:
            halve(k, 0).start()
        elif i <= stages:
            halve(k, i - 1).wait_recv()
            size = chunk >> i
            rows = span(held(k, i), size)
            total = acc[rows, :].astype(jnp.float32) + came[span(k * chunk + chunk - (chunk >> (i - 1)), size), :].astype(jnp.float32)
            if i < stages:
                acc[rows, :] = total.astype(jnp.bfloat16)
                halve(k, i).start()
            else:
                out[span(placed(k, held(k, i)), size), :] = total.astype(jnp.bfloat16)
                double(k, stages - 1).start()
        elif 2 * stages - i >= final:
            s = 2 * stages - i
            double(k, s, False).wait_recv()
            if s > final:
                double(k, s - 1).start()

    def drain():
        for k in range(chunks):
            for s in range(stages):
                halve(k, s).wait_send()
                if s >= final:
                    double(k, s).wait_send()

    return step, drain


def columns_of(row):
    return jnp.concatenate(
        [jnp.broadcast_to(row[:, t * 128:(t + 1) * 128], (128, 128)).T for t in range(row.shape[1] // 128)], axis=0
    )


def project_kernel(
    dp_count, tokens_hbm, gain_hbm, w_hbm, cot_ref, owner_hbm, rows_hbm, q_hbm, k_hbm, v_hbm, grad_hbm, place_hbm,
    tokens_ref, gain_ref, w_ref, owner_ref, rows_ref, q_ref, k_ref, v_ref, grad_ref, place_ref, load_sem, store_sem, out_sem, returned_ref, across_send, across_recv, pair_send, pair_recv, pass_send, pass_recv, slot_send, slot_recv, self_sem,
):
    load_tokens, load_gain, load_w, load_owner = loads = local_copies(
        ((tokens_hbm, tokens_ref), (gain_hbm, gain_ref), (w_hbm, w_ref), (owner_hbm, owner_ref)), load_sem
    )
    for load in loads:
        load.start()
    stores = local_copies(
        ((q_ref, q_hbm), (k_ref, k_hbm), (v_ref, v_hbm), (place_ref, place_hbm), (grad_ref, grad_hbm)), out_sem
    )
    dp, mp = lax.axis_index("dp"), lax.axis_index("mp")
    pair, across, far = mp ^ 1, mp ^ 2, mp ^ 3
    own = tokens_ref.shape[0]
    part = own // PARTS
    greet([(dp, pair), (dp, across)] + [(lax.rem(dp + k, dp_count), mp) for k in range(1, dp_count)])

    def spot(owner, c, size):
        return pl.ds(pl.multiple_of(owner * own + c * size, size), size)

    def gather_copy(c, owner, device, send, recv):
        rows = rows_ref.at[spot(owner, c, part)]
        return remote(rows, rows, send.at[c], recv.at[c], device)

    def slot_copy(k):
        other = lax.rem(dp + k, dp_count)
        return remote(cot_ref.at[other], returned_ref.at[dp], slot_send.at[k], slot_recv.at[k], (other, mp))

    def store(i, owner):
        rows = pl.ds(pl.multiple_of(owner * own, own), own)
        return pltpu.make_async_copy(rows_ref.at[rows], rows_hbm.at[rows], store_sem.at[i])

    for k in range(1, dp_count):
        slot_copy(k).start()
    self_copy = pltpu.make_async_copy(cot_ref.at[dp], returned_ref.at[dp], self_sem)
    self_copy.start()
    load_tokens.wait()
    load_gain.wait()
    for c in range(PARTS):
        values = tokens_ref[c * part:(c + 1) * part, :].astype(jnp.float32)
        unit, _ = norm_unit(values)
        rows_ref[spot(mp, c, part), :] = (unit * gain_ref[0:1, :]).astype(jnp.bfloat16)
        gather_copy(c, mp, (dp, across), across_send, across_recv).start()
        gather_copy(c, mp, (dp, pair), pair_send, pair_recv).start()
    def product(owner, half):
        where = spot(owner, half, own // 2)
        rows = rows_ref[where, :]
        for p, out in enumerate((q_ref, k_ref, v_ref)):
            out[where, :] = lax.dot_general(rows, w_ref[p], NT, preferred_element_type=jnp.float32).astype(jnp.bfloat16)

    def both(owner):
        def step(half, _):
            product(owner, half)
            return 0
        lax.fori_loop(0, 2, step, 0)

    load_w.wait()
    load_owner.wait()
    both(mp)
    store(0, mp).start()
    capacity = cot_ref.shape[1]
    owner_row = owner_ref[...].astype(jnp.float32)
    owner_col = columns_of(owner_row)
    earlier = lax.broadcasted_iota(jnp.int32, (own, own), 0) < lax.broadcasted_iota(jnp.int32, (own, own), 1)
    same = jnp.concatenate([owner_col] * (own // 128), axis=1) == owner_row
    rank_row = jnp.sum(jnp.where(same & earlier, 1.0, 0.0), axis=0, keepdims=True)
    slot_row = owner_row * capacity + rank_row
    slots = place_ref.shape[0]
    place_ref[...] = jnp.where(
        lax.broadcasted_iota(jnp.int32, (slots, own), 0).astype(jnp.float32) == slot_row, 1.0, 0.0
    ).astype(jnp.bfloat16)
    stores[3].start()
    for c in range(PARTS):
        gather_copy(c, pair, (dp, pair), pair_send, pair_recv).wait_recv()
    both(pair)
    store(1, pair).start()
    for half in range(2):
        for c in range(half * PARTS // 2, (half + 1) * PARTS // 2):
            gather_copy(c, across, (dp, across), across_send, across_recv).wait_recv()
            gather_copy(c, across, (dp, pair), pass_send, pass_recv).start()
        product(across, half)
    store(2, across).start()
    for half in range(2):
        for c in range(half * PARTS // 2, (half + 1) * PARTS // 2):
            gather_copy(c, far, (dp, pair), pass_send, pass_recv).wait_recv()
        product(far, half)
    store(3, far).start()
    for out in stores[:3]:
        out.start()
    for c in range(PARTS):
        gather_copy(c, mp, (dp, across), across_send, across_recv).wait_send()
        gather_copy(c, mp, (dp, pair), pair_send, pair_recv).wait_send()
        gather_copy(c, across, (dp, pair), pass_send, pass_recv).wait_send()
    self_copy.wait()
    for k in range(1, dp_count):
        slot_copy(k).wait_send()
        other = lax.rem(dp + dp_count - k, dp_count)
        remote(cot_ref.at[dp], returned_ref.at[other], slot_send.at[k], slot_recv.at[k], (other, mp)).wait_recv()
    for i, owner in enumerate((mp, pair, across, far)):
        store(i, owner).wait()
    if capacity % 16 == 0:
        back = returned_ref[...].reshape(slots, cot_ref.shape[2])
        grad_ref[...] = lax.dot_general(place_ref[...], back, TN, preferred_element_type=jnp.float32).astype(jnp.bfloat16)
    else:
        rank_col = columns_of(rank_row)[:, :capacity]
        lane = lax.broadcasted_iota(jnp.int32, (own, capacity), 1).astype(jnp.float32)

        def take(d, total):
            pick = (owner_col[:, :capacity] == d.astype(jnp.float32)) & (rank_col == lane)
            pick = jnp.where(pick, 1.0, 0.0).astype(jnp.bfloat16)
            return total + jnp.dot(pick, returned_ref[d], preferred_element_type=jnp.float32)
        grad_ref[...] = lax.fori_loop(0, dp_count, take, jnp.zeros(grad_ref.shape, jnp.float32)).astype(jnp.bfloat16)
    stores[4].start()
    for out in stores:
        out.wait()


def project(tokens, gain, w_qkv, cot, owners):
    own, width = tokens.shape
    dp_count = cot.shape[0]
    total = own * 4
    cols = w_qkv.shape[1]
    vmem = pl.BlockSpec(memory_space=pltpu.VMEM)
    hbm = pl.BlockSpec(memory_space=pltpu.HBM)
    dma = pltpu.SemaphoreType.DMA
    return pl.pallas_call(
        functools.partial(project_kernel, dp_count),
        out_shape=[jax.ShapeDtypeStruct((total, width), jnp.bfloat16)]
        + [jax.ShapeDtypeStruct((total, cols), jnp.bfloat16)] * 3
        + [jax.ShapeDtypeStruct((own, width), jnp.bfloat16), jax.ShapeDtypeStruct((dp_count * cot.shape[1], own), jnp.bfloat16)],
        in_specs=[hbm] * 5,
        out_specs=[hbm] * 6,
        scratch_shapes=[pltpu.VMEM(one.shape, one.dtype) for one in (tokens, gain, w_qkv, owners)]
        + [pltpu.VMEM((total, width), jnp.bfloat16)] + [pltpu.VMEM((total, cols), jnp.bfloat16)] * 3
        + [pltpu.VMEM((own, width), jnp.bfloat16), pltpu.VMEM((dp_count * cot.shape[1], own), jnp.bfloat16)]
        + [dma((4,)), dma((4,)), dma((5,)), pltpu.VMEM(cot.shape, cot.dtype)] + [dma((PARTS,))] * 6 + [dma((dp_count,))] * 2 + [dma],
        compiler_params=pltpu.CompilerParams(collective_id=1, has_side_effects=True, vmem_limit_bytes=VMEM_BYTES),
        cost_estimate=pl.CostEstimate(flops=6 * total * width * cols, bytes_accessed=10 * total * width, transcendentals=0),
        name="project",
    )(tokens, gain, w_qkv, cot, owners)


def gelu_and_slope(values):
    cumulative = 0.5 * (1.0 + lax.erf(values * 0.7071067811865476))
    density = jnp.exp(-0.5 * values * values) * 0.3989422804014327
    return values * cumulative, cumulative + values * density


def middle_kernel(
    stages, merged_hbm, w_out_hbm, tokens_hbm, gain_hbm, w_up_hbm, w_down_hbm, grad_own_hbm, grad_across_hbm, place_hbm,
    back_rows_hbm, grad_merged_hbm, grad_residual_hbm, outgoing_hbm, first_hbm, second_hbm, gain_part_hbm, d_out_hbm,
    merged_ref, w_out_ref, tokens_ref, gain_ref, gain_part_ref, d_out_ref, w_up_ref, w_down_ref, grad_own_ref, grad_across_ref, place_ref,
    back_rows_ref, grad_merged_ref, grad_residual_ref, outgoing_ref, d_mlp_ref, load_sem, store_sem,
    mlp_rows, grad_rows, active, grad_pre, residual, mine, bufs,
    sum_send, sum_recv, row_send, row_recv, grad_send, grad_recv, self_sem, acc, came, dp_send, dp_recv,
):
    first_rows = first_hbm.shape[0]
    loads = local_copies(
        (
            (merged_hbm, merged_ref), (w_out_hbm, w_out_ref), (tokens_hbm, tokens_ref), (grad_own_hbm, grad_own_ref),
            (grad_across_hbm, grad_across_ref), (w_up_hbm, w_up_ref), (w_down_hbm, w_down_ref), (place_hbm, place_ref),
            (gain_hbm, gain_ref),
        ),
        load_sem,
    )
    for load in loads:
        load.start()
    stores = local_copies(
        (
            (back_rows_ref, back_rows_hbm), (grad_merged_ref, grad_merged_hbm), (grad_residual_ref, grad_residual_hbm),
            (outgoing_ref, outgoing_hbm), (d_mlp_ref.at[0:first_rows], first_hbm), (d_mlp_ref.at[first_rows:], second_hbm),
            (gain_part_ref, gain_part_hbm), (d_out_ref, d_out_hbm),
        ),
        store_sem,
    )
    low, full = jnp.bfloat16, jnp.float32
    dp, mp = lax.axis_index("dp"), lax.axis_index("mp")
    pair, across, far = mp ^ 1, mp ^ 2, mp ^ 3
    own, width = tokens_ref.shape
    part = own // PARTS
    to_pair, to_across = (dp, pair), (dp, across)
    greet([to_pair, to_across] + [(dp ^ (1 << j), mp) for j in range(stages)])
    add_step, add_drain = sum_steps(stages, MLP_CHUNKS, acc, came, dp_send, dp_recv, d_mlp_ref, half=True)
    target = acc if stages else d_mlp_ref

    def spot(owner, c=None):
        if c is None:
            return pl.ds(pl.multiple_of(owner * own, own), own)
        return pl.ds(pl.multiple_of(owner * own + c * part, part), part)

    def piece(c):
        return pl.ds(pl.multiple_of(c * part, part), part)

    def grad_copy(i, owner, src):
        return remote(src, grad_rows.at[spot(owner)], grad_send.at[i], grad_recv.at[i], to_pair)

    grad_loads = [
        pltpu.make_async_copy(grad_own_ref, grad_rows.at[spot(mp)], self_sem.at[0]),
        pltpu.make_async_copy(grad_across_ref, grad_rows.at[spot(across)], self_sem.at[1]),
    ]

    FAR, ACROSS, PAIR = 0, 1, 2

    def sum_copy(which, kind, c):
        src, dst = bufs.at[which, 0, kind, piece(c)], bufs.at[which, 1, kind, piece(c)]
        return remote(src, dst, sum_send.at[which, kind, c], sum_recv.at[which, kind, c], to_across if kind == ACROSS else to_pair)

    def arrived(which, kind, c):
        sum_copy(which, kind, c).wait_recv()
        return bufs[which, 1, kind, piece(c), :].astype(full)

    def ship(which, kind, c, values):
        bufs[which, 0, kind, piece(c), :] = values.astype(low)
        sum_copy(which, kind, c).start()

    def row_copy(which, kind, c, owner, ref):
        rows = ref.at[spot(owner, c)]
        return remote(rows, rows, row_send.at[which, kind, c], row_recv.at[which, kind, c], to_across if kind == 0 else to_pair)

    def each(count, body):
        def step(i, _):
            body(i)
            return 0
        lax.fori_loop(0, count, step, 0)

    def out_part(owner):
        return jnp.dot(merged_ref[spot(owner), :], w_out_ref[...], preferred_element_type=full)

    loads[0].wait()
    loads[1].wait()
    bufs[0, 0, FAR] = out_part(far).astype(low)
    each(PARTS, lambda c: sum_copy(0, FAR, c).start())
    mine[0] = out_part(across)

    def pass_across(c):
        ship(0, ACROSS, c, mine[0, piece(c), :] + arrived(0, FAR, c))
    each(PARTS, pass_across)
    bufs[0, 0, PAIR] = out_part(pair).astype(low)
    each(PARTS, lambda c: sum_copy(0, PAIR, c).start())
    for load in loads[2:5]:
        load.wait()
    for copy in grad_loads:
        copy.start()
    grad_copy(0, mp, grad_own_ref).start()
    grad_copy(1, across, grad_across_ref).start()
    mine[0] = out_part(mp) + tokens_ref[...].astype(full)
    for copy in grad_loads:
        copy.wait()
    grad_copy(0, pair, grad_own_ref).wait_recv()
    grad_copy(1, far, grad_across_ref).wait_recv()

    for load in loads[5:]:
        load.wait()
    blocks = w_up_ref.shape[1] // 256
    both = 2 * part

    def mlp(first, second, c):
        rows = jnp.concatenate([mlp_rows[spot(first, c), :], mlp_rows[spot(second, c), :]], axis=0)
        grads = jnp.concatenate([grad_rows[spot(first, c), :], grad_rows[spot(second, c), :]], axis=0)

        def block(b):
            cols = pl.ds(pl.multiple_of(b * 256, 256), 256)
            pre = jnp.dot(rows, w_up_ref[:, cols], preferred_element_type=full)
            value, slope = gelu_and_slope(pre)
            value = value.astype(low)
            active[spot(first, c), cols] = value[:part]
            active[spot(second, c), cols] = value[part:]
            back = (jnp.dot(grads, w_down_ref[:, cols], preferred_element_type=full) * slope).astype(low)
            grad_pre[spot(first, c), cols] = back[:part]
            grad_pre[spot(second, c), cols] = back[part:]
        each(blocks, block)
        back = jnp.concatenate([grad_pre[spot(first, c), :], grad_pre[spot(second, c), :]], axis=0)
        return lax.dot_general(back, w_up_ref[...], NT, preferred_element_type=full)

    def near(c):
        values = mine[0, piece(c), :] + arrived(0, PAIR, c) + arrived(0, ACROSS, c)
        residual[piece(c), :] = values
        unit, _ = norm_unit(values)
        mlp_rows[spot(mp, c), :] = (unit * gain_ref[1:2, :]).astype(low)
        row_copy(0, 0, c, mp, mlp_rows).start()
        row_copy(0, 1, c, mp, mlp_rows).start()
        row_copy(0, 1, c, pair, mlp_rows).wait_recv()
        got = mlp(mp, pair, c)
        mine[1, piece(c), :] = got[:part]
        ship(1, PAIR, c, got[part:])
    each(PARTS, near)

    def distant(c):
        row_copy(0, 0, c, across, mlp_rows).wait_recv()
        row_copy(0, 2, c, across, mlp_rows).start()
        row_copy(0, 2, c, far, mlp_rows).wait_recv()
        got = mlp(far, across, c)
        ship(1, FAR, c, got[:part])
        ship(1, ACROSS, c, got[part:] + arrived(1, FAR, c))
    each(PARTS, distant)

    size = width // MLP_CHUNKS
    for b in range(3):
        cols = slice(b * 256, (b + 1) * 256)
        up = lax.dot_general(mlp_rows[:, cols], grad_pre[...], TN, preferred_element_type=full)
        gain_col = jnp.sum(up * w_up_ref[cols, :].astype(full), axis=1, keepdims=True)
        gain_part_ref[:, cols] = jnp.broadcast_to(gain_col, (256, 128)).T[0:8] / gain_ref[1:2, cols]
        up = up.astype(low)
        down = lax.dot_general(grad_rows[:, cols], active[...], TN, preferred_element_type=full).astype(low)
        for j in range(256 // size):
            k = b * (256 // size) + j
            target[2 * k * size:(2 * k + 1) * size, :] = up[j * size:(j + 1) * size]
            target[(2 * k + 1) * size:(2 * k + 2) * size, :] = down[j * size:(j + 1) * size]
            if stages:
                add_step(k, 0)

    def add(*steps):
        if stages:
            for k, i in steps:
                add_step(k, i)

    def down_part(owner):
        return lax.dot_general(active[spot(owner), :], w_down_ref[...], NT, preferred_element_type=full)

    bufs[2, 0, FAR] = down_part(far).astype(low)
    each(PARTS, lambda c: sum_copy(2, FAR, c).start())
    bufs[2, 0, PAIR] = down_part(pair).astype(low)
    each(PARTS, lambda c: sum_copy(2, PAIR, c).start())

    def back_norm(c):
        grad = mine[1, piece(c), :] + arrived(1, PAIR, c) + arrived(1, ACROSS, c)
        unit, inverse = norm_unit(residual[piece(c), :])
        scaled = grad * gain_ref[1:2, :]
        first_mean = jnp.mean(scaled, axis=-1, keepdims=True)
        second_mean = jnp.mean(scaled * unit, axis=-1, keepdims=True)
        total = inverse * (scaled - first_mean - unit * second_mean) + grad_own_ref[piece(c), :].astype(full)
        grad_residual_ref[piece(c), :] = total
        back_rows_ref[spot(mp, c), :] = total.astype(low)
        row_copy(1, 0, c, mp, back_rows_ref).start()
        row_copy(1, 1, c, mp, back_rows_ref).start()
    def tick(t):
        add(*[(t - i, i) for i in range(1, 2 * stages + 1) if 0 <= t - i < MLP_CHUNKS])

    each(2, back_norm)
    tick(1)
    each(1, lambda c: back_norm(c + 2))
    tick(2)
    each(1, lambda c: back_norm(c + 3))

    mine[1] = down_part(across)

    def pass_output(c):
        ship(2, ACROSS, c, mine[1, piece(c), :] + arrived(2, FAR, c))
    each(PARTS, pass_output)
    tick(3)
    mine[0] = residual[...] + down_part(mp)

    def merged_part(owner):
        grad_merged_ref[spot(owner), :] = lax.dot_general(
            back_rows_ref[spot(owner), :], w_out_ref[...], NT, preferred_element_type=full
        ).astype(low)

    merged_part(mp)
    each(PARTS, lambda c: row_copy(1, 1, c, pair, back_rows_ref).wait_recv())
    merged_part(pair)

    def hand_on(c):
        row_copy(1, 0, c, across, back_rows_ref).wait_recv()
        row_copy(1, 2, c, across, back_rows_ref).start()
    for c in range(PARTS):
        each(1, lambda i: hand_on(i + c))
        tick(4 + c)
    tick(8)
    merged_part(across)
    each(PARTS, lambda c: row_copy(1, 2, c, far, back_rows_ref).wait_recv())
    tick(9)
    merged_part(far)
    stores[0].start()
    stores[1].start()
    stores[2].start()
    d_out_ref[...] = lax.dot_general(merged_ref[...], back_rows_ref[...], TN, preferred_element_type=full).astype(low)
    stores[6].start()
    stores[7].start()

    tick(10)

    def finish(c):
        mine[0, piece(c), :] = mine[0, piece(c), :] + arrived(2, PAIR, c) + arrived(2, ACROSS, c)
    for c in range(PARTS):
        each(1, lambda i: finish(i + c))
    stores[4].start()
    stores[5].start()
    outgoing_ref[...] = jnp.dot(place_ref[...], mine[0].astype(low), preferred_element_type=full).astype(low)
    stores[3].start()
    if stages:
        add_drain()
    for store in stores:
        store.wait()

    def drain(c):
        for which in range(3):
            for kind in range(3):
                sum_copy(which, kind, c).wait_send()
        for which, ref in ((0, mlp_rows), (1, back_rows_ref)):
            row_copy(which, 0, c, mp, ref).wait_send()
            row_copy(which, 1, c, mp, ref).wait_send()
            row_copy(which, 2, c, across, ref).wait_send()
    each(PARTS, drain)
    grad_copy(0, mp, grad_own_ref).wait_send()
    grad_copy(1, across, grad_across_ref).wait_send()


def middle(dp_count, merged, w_out, tokens, gain, w_up, w_down, grad_own, grad_across, place):
    stages = sum_stages(2 * w_up.shape[0], MLP_CHUNKS, dp_count)
    d_rows = w_up.shape[0] * (1 if stages else 2)
    total, cols = merged.shape
    own, width = tokens.shape
    hidden = w_up.shape[1]
    slots = place.shape[0]
    low, full = jnp.bfloat16, jnp.float32
    vmem = pl.BlockSpec(memory_space=pltpu.VMEM)
    hbm = pl.BlockSpec(memory_space=pl.ANY)
    dma = pltpu.SemaphoreType.DMA
    shape, room = jax.ShapeDtypeStruct, pltpu.VMEM
    return pl.pallas_call(
        functools.partial(middle_kernel, stages),
        out_shape=[
            shape((total, width), low), shape((total, cols), low), shape((own, width), full), shape((slots, width), low),
            shape((d_rows // 2, hidden), low), shape((d_rows // 2, hidden), low), shape((8, width), full), shape((cols, width), low),
        ],
        in_specs=[hbm] * 9,
        out_specs=[hbm] * 8,
        scratch_shapes=[
            room((total, cols), low), room(w_out.shape, low), room((own, width), low), room(gain.shape, full),
            room((8, width), full), room((cols, width), low), room(w_up.shape, low),
            room(w_down.shape, low), room((own, width), low), room((own, width), low), room(place.shape, low),
            room((total, width), low), room((total, cols), low), room((own, width), full), room((slots, width), low),
            room((d_rows, hidden), low), dma((9,)), dma((8,)),
            room((total, width), low), room((total, width), low),
            room((total, hidden), low), room((total, hidden), low),
            room((own, width), full), room((2, own, width), full),
            room((3, 2, 3, own, width), low),
            dma((3, 3, PARTS)), dma((3, 3, PARTS)), dma((2, 3, PARTS)), dma((2, 3, PARTS)), dma((2,)), dma((2,)), dma((2,)),
        ]
        + sum_scratch(2 * width, hidden, MLP_CHUNKS, stages),
        compiler_params=pltpu.CompilerParams(collective_id=2, has_side_effects=True, vmem_limit_bytes=VMEM_BYTES),
        cost_estimate=pl.CostEstimate(flops=16 * total * width * hidden, bytes_accessed=20 * total * width, transcendentals=0),
        name="middle",
    )(merged, w_out, tokens, gain, w_up, w_down, grad_own, grad_across, place)


def direct_fits(rows, chunks, dp_count):
    return dp_count % 2 == 0 and rows % (16 * chunks * dp_count) == 0


def direct_steps(dp_count, chunks, acc, came, send, recv, out, out_hbm, keep_sem):
    dp, mp = lax.axis_index("dp"), lax.axis_index("mp")
    chunk = acc.shape[0] // chunks
    group = dp_count // 2
    half, slot = chunk // 2, chunk // dp_count
    y, z = lax.rem(dp, 2), dp // 2
    beside = (dp + 1 - 2 * y, mp)
    others = sorted(range(1, group), key=lambda j: -min(j, group - j))

    def span(start, size):
        return pl.ds(pl.multiple_of(start, 16), size)

    def low(k, side, g=0):
        return k * chunk + side * half + g * slot

    def member(j):
        return lax.rem(z + j, group)

    def slot_of(k, j):
        return span(k * chunk + half + (j - 1) * slot, slot)

    def halve(k):
        return remote(acc.at[span(low(k, 1 - y), half)], came.at[span(k * chunk, half)], send.at[k, 0], recv.at[k, 0], beside)

    def scatter(k, j):
        piece = acc.at[span(low(k, y, member(j)), slot)]
        return remote(piece, came.at[slot_of(k, j)], send.at[k, j], recv.at[k, j], (y + 2 * member(j), mp))

    def gather(k, j, mine=True):
        rows = out.at[span(low(k, y, z if mine else member(group - j)), slot)]
        return remote(rows, rows, send.at[k, group + j - 1], recv.at[k, group + j - 1], (y + 2 * member(j), mp))

    def double(k, mine=True):
        rows = span(low(k, y if mine else 1 - y), half)
        return remote(out.at[rows], out_hbm.at[rows], send.at[k, 2 * group - 1], recv.at[k, 2 * group - 1], beside)

    def keep(k):
        rows = span(low(k, y), half)
        return pltpu.make_async_copy(out.at[rows], out_hbm.at[rows], keep_sem.at[k])

    def step(k, i):
        if i == 0:
            halve(k).start()
        elif i == 1:
            halve(k).wait_recv()
            rows = span(low(k, y), half)
            total = acc[rows, :].astype(jnp.float32) + came[span(k * chunk, half), :].astype(jnp.float32)
            acc[rows, :] = total.astype(jnp.bfloat16)
            for j in others:
                scatter(k, j).start()
        elif i == 2:
            rows = span(low(k, y, z), slot)
            total = acc[rows, :].astype(jnp.float32)
            for j in others:
                scatter(k, j).wait_recv()
                total = total + came[slot_of(k, j), :].astype(jnp.float32)
            out[rows, :] = total.astype(jnp.bfloat16)
            for j in others:
                gather(k, j).start()
        elif i == 3:
            for j in others:
                gather(k, j, False).wait_recv()
            double(k).start()
            keep(k).start()
        else:
            double(k, False).wait_recv()

    def drain():
        for k in range(chunks):
            halve(k).wait_send()
            for j in others:
                scatter(k, j).wait_send()
                gather(k, j).wait_send()
            double(k).wait_send()
            keep(k).wait()

    return step, drain


def last_kernel(
    dp_count, fits, dq_hbm, dk_hbm, dv_hbm, w_hbm, rows_hbm, grad_residual_hbm, tokens_hbm, gain_hbm, gain_part_hbm, d_out_hbm,
    grad_tokens_hbm, d_sum_hbm, gains_hbm,
    dq_ref, dk_ref, dv_ref, w_ref, rows_ref, grad_residual_ref, tokens_ref, gain_ref, gain_part_ref, d_out_ref,
    grad_tokens_ref, gains_ref, load_sem, store_sem, mine, bufs, gain_dp, gain_mp,
    sum_send, sum_recv, dp_gain_send, dp_gain_recv, mp_gain_send, mp_gain_recv, acc, came, out, dp_send, dp_recv, keep_sem,
):
    loads = local_copies(
        (
            (dq_hbm, dq_ref), (rows_hbm, rows_ref), (w_hbm, w_ref), (d_out_hbm, d_out_ref), (dk_hbm, dk_ref), (dv_hbm, dv_ref),
            (gain_hbm, gain_ref), (gain_part_hbm, gain_part_ref), (grad_residual_hbm, grad_residual_ref), (tokens_hbm, tokens_ref),
        ),
        load_sem,
    )
    for load in loads:
        load.start()
    store_tokens, store_gains = local_copies(((grad_tokens_ref, grad_tokens_hbm), (gains_ref, gains_hbm)), store_sem)
    low, full = jnp.bfloat16, jnp.float32
    dp, mp = lax.axis_index("dp"), lax.axis_index("mp")
    pair, across, far = mp ^ 1, mp ^ 2, mp ^ 3
    own, width = tokens_ref.shape
    part = own // PARTS
    cols = dq_ref.shape[1]
    to_pair, to_across = (dp, pair), (dp, across)
    greet([to_pair, to_across, (dp, far)] + [(lax.rem(dp + k, dp_count), mp) for k in range(1, dp_count)])
    add_step, add_drain = direct_steps(dp_count, QKV_CHUNKS, acc, came, dp_send, dp_recv, out, d_sum_hbm, keep_sem)
    FAR, ACROSS, PAIR = 0, 1, 2

    def add(*steps):
        if fits:
            for k, i in steps:
                add_step(k, i)

    def piece(c):
        return pl.ds(pl.multiple_of(c * part, part), part)

    def each(count, body):
        def step(i, _):
            body(i)
            return 0
        lax.fori_loop(0, count, step, 0)

    def sum_copy(kind, c):
        src, dst = bufs.at[0, kind, piece(c)], bufs.at[1, kind, piece(c)]
        return remote(src, dst, sum_send.at[kind, c], sum_recv.at[kind, c], to_across if kind == ACROSS else to_pair)

    def arrived(kind, c):
        sum_copy(kind, c).wait_recv()
        return bufs[1, kind, piece(c), :].astype(full)

    def in_part(owner):
        where = pl.ds(pl.multiple_of(owner * own, own), own)
        total = jnp.dot(dq_ref[where, :], w_ref[0], preferred_element_type=full)
        total = total + jnp.dot(dk_ref[where, :], w_ref[1], preferred_element_type=full)
        return total + jnp.dot(dv_ref[where, :], w_ref[2], preferred_element_type=full)

    def weight_grad(p, ref):
        grad = lax.dot_general(ref[...], rows_ref[...], TN, preferred_element_type=full)
        acc[(p + 1) * cols:(p + 2) * cols, :] = grad.astype(low)
        return jnp.sum(grad * w_ref[p].astype(full), axis=0, keepdims=True)

    for load in loads[:4]:
        load.wait()
    acc[0:cols, :] = d_out_ref[...]
    gain_row = weight_grad(0, dq_ref)
    add((0, 0))
    for load in loads[4:]:
        load.wait()
    bufs[0, FAR] = in_part(far).astype(low)
    each(PARTS, lambda c: sum_copy(FAR, c).start())
    gain_row = gain_row + weight_grad(1, dk_ref)
    add((1, 0))
    mine[...] = in_part(across)

    def pass_across(c):
        bufs[0, ACROSS, piece(c), :] = (mine[piece(c), :] + arrived(FAR, c)).astype(low)
        sum_copy(ACROSS, c).start()
    each(PARTS, pass_across)
    gain_row = gain_row + weight_grad(2, dv_ref)
    add((2, 0))

    row = lax.broadcasted_iota(jnp.int32, (8, width), 0)
    gain_dp[dp] = jnp.where(row == 0, gain_part_ref[...], jnp.where(row == 1, gain_row / gain_ref[0:1, :], 0.0))

    def gain_over_dp(k, owner):
        return remote(gain_dp.at[owner], gain_dp.at[owner], dp_gain_send.at[k], dp_gain_recv.at[k], (lax.rem(dp + k, dp_count), mp))

    def gain_over_mp(i, owner):
        other = (pair, across, far)[i]
        return remote(gain_mp.at[owner], gain_mp.at[owner], mp_gain_send.at[i], mp_gain_recv.at[i], (dp, other))

    for k in range(1, dp_count):
        gain_over_dp(k, dp).start()

    def turn_gains():
        for k in range(1, dp_count):
            gain_over_dp(k, lax.rem(dp + dp_count - k, dp_count)).wait_recv()
        total = gain_dp[0]
        for k in range(1, dp_count):
            total = total + gain_dp[k]
        gain_mp[mp] = total
        for i in range(3):
            gain_over_mp(i, mp).start()

    def end_gains():
        for i, owner in enumerate((pair, across, far)):
            gain_over_mp(i, owner).wait_recv()
        gains_ref[...] = (gain_mp[0] + gain_mp[1]) + (gain_mp[2] + gain_mp[3])
        store_gains.start()

    bufs[0, PAIR] = in_part(pair).astype(low)
    each(PARTS, lambda c: sum_copy(PAIR, c).start())
    mine[...] = in_part(mp)

    def back_norm(c):
        grad = mine[piece(c), :] + arrived(PAIR, c) + arrived(ACROSS, c)
        unit, inverse = norm_unit(tokens_ref[piece(c), :].astype(full))
        scaled = grad * gain_ref[0:1, :]
        first_mean = jnp.mean(scaled, axis=-1, keepdims=True)
        second_mean = jnp.mean(scaled * unit, axis=-1, keepdims=True)
        total = inverse * (scaled - first_mean - unit * second_mean) + grad_residual_ref[piece(c), :]
        grad_tokens_ref[piece(c), :] = total.astype(low)

    def norm(c):
        each(1, lambda i: back_norm(i + c))

    add((0, 1))
    norm(0)
    add((1, 1), (0, 2))
    norm(1)
    add((2, 1), (1, 2), (0, 3))
    norm(2)
    turn_gains()
    add((2, 2), (1, 3))
    norm(3)
    store_tokens.start()
    add((0, 4), (2, 3))
    end_gains()
    add((1, 4), (2, 4))
    if fits:
        add_drain()
    else:
        whole = pltpu.make_async_copy(acc, d_sum_hbm, keep_sem.at[0])
        whole.start()
        whole.wait()
    for k in range(1, dp_count):
        gain_over_dp(k, dp).wait_send()
    for i in range(3):
        gain_over_mp(i, mp).wait_send()

    def drain(c):
        for kind in range(3):
            sum_copy(kind, c).wait_send()
    each(PARTS, drain)
    store_tokens.wait()
    store_gains.wait()


def last(dp_count, dq, dk, dv, w_qkv, rows, grad_residual, tokens, gain, gain_part, d_out):
    own, width = tokens.shape
    cols = dq.shape[1]
    d_rows = 4 * cols
    fits = direct_fits(d_rows, QKV_CHUNKS, dp_count)
    low, full = jnp.bfloat16, jnp.float32
    hbm = pl.BlockSpec(memory_space=pl.ANY)
    dma = pltpu.SemaphoreType.DMA
    shape, room = jax.ShapeDtypeStruct, pltpu.VMEM
    operands = (dq, dk, dv, w_qkv, rows, grad_residual, tokens, gain, gain_part, d_out)
    grad_tokens, d_sum, gains = pl.pallas_call(
        functools.partial(last_kernel, dp_count, fits),
        out_shape=[shape((own, width), low), shape((d_rows, width), low), shape((8, width), full)],
        in_specs=[hbm] * 10,
        out_specs=[hbm] * 3,
        scratch_shapes=[room(one.shape, one.dtype) for one in operands]
        + [
            room((own, width), low), room((8, width), full), dma((10,)), dma((2,)),
            room((own, width), full), room((2, 3, own, width), low), room((dp_count, 8, width), full), room((4, 8, width), full),
            dma((3, PARTS)), dma((3, PARTS)), dma((dp_count,)), dma((dp_count,)), dma((3,)), dma((3,)),
            room((d_rows, width), low), room((d_rows, width), low), room((d_rows, width), low),
            dma((QKV_CHUNKS, dp_count)), dma((QKV_CHUNKS, dp_count)), dma((QKV_CHUNKS,)),
        ],
        compiler_params=pltpu.CompilerParams(collective_id=3, has_side_effects=True, vmem_limit_bytes=VMEM_BYTES),
        cost_estimate=pl.CostEstimate(flops=12 * 4 * own * width * cols, bytes_accessed=20 * own * width, transcendentals=0),
        name="last",
    )(*operands)
    return grad_tokens, d_sum if fits else lax.psum(d_sum, "dp"), gains


def local(
    tokens, segment_ids, gene_owner, w_qkv, w_attn_out, w_up, w_down, gain_attn, gain_mlp, cotangent
):
    width = tokens.shape[1]
    dp_count = lax.axis_size("dp")
    capacity = cotangent.shape[0] // dp_count
    low, full = jnp.bfloat16, jnp.float32
    w_rows = jnp.swapaxes(w_qkv, 1, 2)
    gains_in = jnp.stack([gain_attn, gain_mlp])
    attn_in, *projected, grad_block, place = project(
        tokens, gains_in, w_rows, cotangent.reshape(dp_count, capacity, width), gene_owner.reshape(1, -1)
    )
    grad_across = lax.ppermute(grad_block, "mp", [(i, i ^ 2) for i in range(lax.axis_size("mp"))])
    merged, log_sums = attend_forward(segment_ids, *projected)
    residual_rows, grad_merged, grad_residual, outgoing, first, second, gain_part, d_out = middle(
        dp_count, merged, w_attn_out, tokens, gains_in, w_up, w_down, grad_block, grad_across, place
    )
    cols = w_qkv.shape[2]
    if sum_stages(2 * width, MLP_CHUNKS, dp_count):
        size = width // MLP_CHUNKS
        place_y = lax.rem(lax.axis_index("dp"), 2) == 0
        place_z = lax.rem(lax.axis_index("dp") // 2, 2) == 0
        first_came = lax.ppermute(first, "dp", [(i, i ^ 1) for i in range(dp_count)])
        second_came = lax.ppermute(second, "dp", [(i, i ^ 2) for i in range(dp_count)])
        gain_part, first_came, second_came = lax.optimization_barrier((gain_part, first_came, second_came))
        first = [
            one.reshape(-1, size, width)
            for one in (jnp.where(place_y, first, first_came), jnp.where(place_y, first_came, first))
        ]
        second = jnp.stack(
            [
                one.reshape(-1, 2, size // 2, width)
                for one in (jnp.where(place_z, second, second_came), jnp.where(place_z, second_came, second))
            ],
            axis=2,
        )
        up_sum, down_sum = (
            jnp.stack([first[i], second[:, i].reshape(-1, size, width)], axis=1).reshape(-1, width).astype(full)
            for i in range(2)
        )
    else:
        d_sum = lax.psum(jnp.concatenate([first, second]), "dp").reshape(MLP_CHUNKS, 2, -1, width).astype(full)
        up_sum, down_sum = (d_sum[:, i].reshape(-1, width) for i in range(2))
    relaid = lax.all_to_all(
        outgoing.reshape(dp_count, capacity, width), "dp", split_axis=0, concat_axis=0, tiled=True
    ).reshape(dp_count * capacity, width)
    grad_proj = attend_backward(segment_ids, *projected, merged, grad_merged, log_sums)
    grad_tokens, weight_sum, gains = last(
        dp_count, *grad_proj, w_rows, attn_in, grad_residual, tokens, gains_in, gain_part, d_out
    )
    qkv_sum = weight_sum[cols:].reshape(3, cols, width).astype(full)
    attn_sum = weight_sum[:cols].astype(full)
    return (
        relaid,
        grad_tokens,
        jnp.swapaxes(qkv_sum, 1, 2),
        attn_sum,
        up_sum,
        down_sum,
        gains[1],
        gains[0],
    )


def solution(mesh):
    placed = (
        P(("dp", "mp"), None),
        P("dp", None),
        P(("dp", "mp"), None),
        P(None, None, "mp"),
        P("mp", None),
        P(None, "mp"),
        P(None, "mp"),
        P(),
        P(),
        P(("dp", "mp"), None),
    )
    return jax.shard_map(
        local,
        mesh=mesh,
        in_specs=placed,
        out_specs=(
            P(("dp", "mp"), None),
            P(("dp", "mp"), None),
            P(None, None, "mp"),
            P("mp", None),
            P(None, "mp"),
            P(None, "mp"),
            P(),
            P(),
        ),
        check_vma=False,
    )
```

```python
import functools
import jax
import jax.numpy as jnp
from jax import lax
from jax.experimental import pallas as pl
from jax.experimental.pallas import tpu as pltpu
from jax.sharding import PartitionSpec as P

HEAD = 64
TQ = 256
TK = 256
NT = (((1,), (1,)), ((), ()))
NN = (((1,), (0,)), ((), ()))
TN = (((0,), (0,)), ((), ()))
MASKED = -1e30
epsilon = 1e-05


def local_copies(pairs, sems):
    return [pltpu.make_async_copy(src, dst, sems.at[i]) for i, (src, dst) in enumerate(pairs)]


def key_ranges(seg, tiles):
    n = seg.shape[1]
    lane = lax.broadcasted_iota(jnp.int32, (tiles, n), 1)
    row = lax.broadcasted_iota(jnp.int32, (tiles, n), 0)
    ids = jnp.broadcast_to(seg.astype(jnp.float32), (tiles, n))

    def total(mask, values):
        return jnp.sum(jnp.where(mask, values, 0.0), axis=1, keepdims=True)

    first = total(lane == row * TQ, ids)
    last = total(lane == row * TQ + TQ - 1, ids)
    start = jnp.floor(total(ids < first, 1.0) * (1.0 / TK))
    end = jnp.floor((total(ids <= last, 1.0) + (TK - 1.0)) * (1.0 / TK))
    lane = lax.broadcasted_iota(jnp.int32, (tiles, 128), 1)
    return jnp.where(lane == 0, start, jnp.where(lane == 1, end, 0.0)).astype(jnp.int32)


def over_blocks(ranges, tile, body, state):
    lo, hi = ranges[tile, 0], ranges[tile, 1]
    pairs = (hi - lo) // 2
    state = lax.fori_loop(
        0, pairs, lambda i, one: body(pl.multiple_of((lo + 2 * i) * TK, TK), 2 * TK, one), state
    )
    return lax.fori_loop(lo + 2 * pairs, hi, lambda i, one: body(pl.multiple_of(i * TK, TK), TK, one), state)


def head_masks(width, heads):
    lane = lax.broadcasted_iota(jnp.int32, (1, width), 1)
    return [(lane // HEAD == h) for h in range(heads)]


def seg_columns(segv_ref, cols, n):
    for t in range(n // 128):
        row = segv_ref[0:1, t * 128:(t + 1) * 128].astype(jnp.float32)
        cols[t * 128:(t + 1) * 128, :] = jnp.broadcast_to(row, (128, 128)).T


def fwd_kernel(n, heads, ranges, segv_ref, q_ref, k_ref, v_ref, o_ref, lse_ref, vt, cols, scores):
    tile = pl.program_id(0)
    width = heads * HEAD

    @pl.when(tile == 0)
    def _():
        seg_columns(segv_ref, cols, n)
        for t in range(n // TK):
            vt[:, t * TK:(t + 1) * TK] = v_ref[t * TK:(t + 1) * TK, :].astype(jnp.float32).T.astype(jnp.bfloat16)

    q0 = pl.multiple_of(tile * TQ, TQ)
    q = q_ref[...] * jnp.bfloat16(HEAD ** -0.5)
    masks = head_masks(width, heads)
    qm = [jnp.where(m, q, jnp.bfloat16(0)) for m in masks]
    seg_row = segv_ref[0:1, pl.ds(q0, TQ)].astype(jnp.float32)

    def first(k0, size, tops):
        keys = k_ref[pl.ds(k0, size), :]
        col = cols[pl.ds(k0, size), :]
        same = jnp.concatenate([col] * (TQ // 128), axis=1) == seg_row
        out = []
        for h in range(heads):
            s = lax.dot_general(keys, qm[h], NT, preferred_element_type=jnp.float32)
            s = jnp.where(same, s, MASKED)
            scores[h, pl.ds(k0, size), :] = s
            out.append(jnp.maximum(tops[h], jnp.max(s, axis=0, keepdims=True)))
        return tuple(out)

    tops = over_blocks(ranges, tile, first, tuple(jnp.full((1, TQ), MASKED, jnp.float32) for _ in range(heads)))

    def second(k0, size, acc):
        out = []
        for h in range(heads):
            p = jnp.exp(scores[h, pl.ds(k0, size), :] - tops[h])
            total = acc[h][1] + jnp.sum(p, axis=0, keepdims=True)
            part = lax.dot_general(vt[h * HEAD:(h + 1) * HEAD, pl.ds(k0, size)], p.astype(jnp.bfloat16), NN, preferred_element_type=jnp.float32)
            out.append((acc[h][0] + part, total))
        return tuple(out)

    acc = over_blocks(ranges, tile, second, tuple((jnp.zeros((HEAD, TQ), jnp.float32), jnp.zeros((1, TQ), jnp.float32)) for _ in range(heads)))
    ot = jnp.concatenate([acc[h][0] / acc[h][1] for h in range(heads)], axis=0)
    o_ref[...] = ot.T.astype(jnp.bfloat16)
    lse_ref[...] = jnp.concatenate([tops[h] + jnp.log(acc[h][1]) for h in range(heads)] + [jnp.zeros((8 - heads, TQ), jnp.float32)], axis=0)


def attend_forward(ranges, seg, q, k, v):
    n, width = q.shape
    heads = width // HEAD
    whole = pl.BlockSpec(memory_space=pltpu.VMEM)
    return pl.pallas_call(
        functools.partial(fwd_kernel, n, heads),
        grid_spec=pltpu.PrefetchScalarGridSpec(
            num_scalar_prefetch=1,
            grid=(n // TQ,),
            in_specs=[whole, pl.BlockSpec((TQ, width), lambda t, s: (t, 0)), whole, whole],
            out_specs=[pl.BlockSpec((TQ, width), lambda t, s: (t, 0)), pl.BlockSpec((8, TQ), lambda t, s: (0, t))],
            scratch_shapes=[pltpu.VMEM((width, n), jnp.bfloat16), pltpu.VMEM((n, 128), jnp.float32), pltpu.VMEM((heads, n, TQ), jnp.float32)],
        ),
        out_shape=[jax.ShapeDtypeStruct((n, width), jnp.bfloat16), jax.ShapeDtypeStruct((8, n), jnp.float32)],
        compiler_params=pltpu.CompilerParams(vmem_limit_bytes=VMEM_BYTES),
        cost_estimate=pl.CostEstimate(flops=4 * heads * n * n * HEAD, bytes_accessed=8 * n * width, transcendentals=heads * n * n // 2),
        name="attend_forward",
    )(ranges, seg, q, k, v)


def bwd_kernel(n, heads, ranges, segv_ref, q_ref, k_ref, v_ref, o_ref, do_ref, lse_ref, dq_ref, dk_ref, dv_ref, kt, cols, dk_acc, dv_acc):
    tile = pl.program_id(0)
    width = heads * HEAD

    @pl.when(tile == 0)
    def _():
        seg_columns(segv_ref, cols, n)
        for t in range(n // TK):
            kt[:, t * TK:(t + 1) * TK] = k_ref[t * TK:(t + 1) * TK, :].astype(jnp.float32).T.astype(jnp.bfloat16)
        dk_acc[...] = jnp.zeros_like(dk_acc)
        dv_acc[...] = jnp.zeros_like(dv_acc)

    q0 = pl.multiple_of(tile * TQ, TQ)
    masks = head_masks(width, heads)
    q = q_ref[...] * jnp.bfloat16(HEAD ** -0.5)
    do = do_ref[...]
    qm = [jnp.where(m, q, jnp.bfloat16(0)) for m in masks]
    dm = [jnp.where(m, do, jnp.bfloat16(0)) for m in masks]
    seg_row = segv_ref[0:1, pl.ds(q0, TQ)].astype(jnp.float32)
    prod = do.astype(jnp.float32) * o_ref[...].astype(jnp.float32)
    high = prod.astype(jnp.bfloat16)
    rest = (prod - high.astype(jnp.float32)).astype(jnp.bfloat16)
    row = lax.broadcasted_iota(jnp.int32, (16, width), 0)
    lane = lax.broadcasted_iota(jnp.int32, (16, width), 1)
    pick = jnp.where(lane // HEAD == row, 1.0, 0.0).astype(jnp.bfloat16)
    delta = lax.dot_general(pick, high, NT, preferred_element_type=jnp.float32) + lax.dot_general(pick, rest, NT, preferred_element_type=jnp.float32)
    lse = lse_ref[...]

    def body(k0, size, acc):
        keys = k_ref[pl.ds(k0, size), :]
        vals = v_ref[pl.ds(k0, size), :]
        col = cols[pl.ds(k0, size), :]
        same = jnp.concatenate([col] * (TQ // 128), axis=1) == seg_row
        out = []
        dks = jnp.zeros((size, width), jnp.float32)
        dvs = jnp.zeros((size, width), jnp.float32)
        for h in range(heads):
            s = lax.dot_general(keys, qm[h], NT, preferred_element_type=jnp.float32)
            p = jnp.where(same, jnp.exp(s - lse[h:h + 1, :]), 0.0)
            dp = lax.dot_general(vals, dm[h], NT, preferred_element_type=jnp.float32)
            ds = (p * (dp - delta[h:h + 1, :])).astype(jnp.bfloat16)
            dvs = dvs + lax.dot_general(p.astype(jnp.bfloat16), dm[h], NN, preferred_element_type=jnp.float32)
            dks = dks + lax.dot_general(ds, qm[h], NN, preferred_element_type=jnp.float32)
            out.append(acc[h] + lax.dot_general(kt[h * HEAD:(h + 1) * HEAD, pl.ds(k0, size)], ds, NN, preferred_element_type=jnp.float32))
        dk_acc[pl.ds(k0, size), :] += dks
        dv_acc[pl.ds(k0, size), :] += dvs
        return tuple(out)

    acc = over_blocks(ranges, tile, body, tuple(jnp.zeros((HEAD, TQ), jnp.float32) for _ in range(heads)))
    dq_ref[...] = (jnp.concatenate(acc, axis=0).T * HEAD ** -0.5).astype(jnp.bfloat16)

    @pl.when(tile == n // TQ - 1)
    def _():
        dk_ref[...] = dk_acc[...].astype(jnp.bfloat16)
        dv_ref[...] = dv_acc[...].astype(jnp.bfloat16)


def attend_backward(ranges, seg, q, k, v, o, do, lse):
    n, width = q.shape
    heads = width // HEAD
    whole = pl.BlockSpec(memory_space=pltpu.VMEM)
    rows = pl.BlockSpec((TQ, width), lambda t, s: (t, 0))
    return pl.pallas_call(
        functools.partial(bwd_kernel, n, heads),
        grid_spec=pltpu.PrefetchScalarGridSpec(
            num_scalar_prefetch=1,
            grid=(n // TQ,),
            in_specs=[whole, rows, whole, whole, rows, rows, pl.BlockSpec((8, TQ), lambda t, s: (0, t))],
            out_specs=[rows, whole, whole],
            scratch_shapes=[pltpu.VMEM((width, n), jnp.bfloat16), pltpu.VMEM((n, 128), jnp.float32), pltpu.VMEM((n, width), jnp.float32), pltpu.VMEM((n, width), jnp.float32)],
        ),
        out_shape=[jax.ShapeDtypeStruct((n, width), jnp.bfloat16)] * 3,
        compiler_params=pltpu.CompilerParams(vmem_limit_bytes=VMEM_BYTES),
        cost_estimate=pl.CostEstimate(flops=10 * heads * n * n * HEAD, bytes_accessed=16 * n * width, transcendentals=heads * n * n // 2),
        name="attend_backward",
    )(ranges, seg, q, k, v, o, do, lse)


MESH_ID = pl.DeviceIdType.MESH
PARTS = 4
VMEM_BYTES = 60 << 20
MLP_CHUNKS = 6
QKV_CHUNKS = 3


def remote(src, dst, send, recv, device):
    return pltpu.make_async_remote_copy(
        src_ref=src, dst_ref=dst, send_sem=send, recv_sem=recv, device_id=device, device_id_type=MESH_ID
    )


def greet(devices):
    barrier = pltpu.get_barrier_semaphore()
    for device in devices:
        pl.semaphore_signal(barrier, inc=1, device_id=device, device_id_type=MESH_ID)
    pl.semaphore_wait(barrier, len(devices))


def norm_unit(values):
    average = jnp.mean(values, axis=-1, keepdims=True)
    centered = values - average
    variance = jnp.mean(centered * centered, axis=-1, keepdims=True)
    inverse = lax.rsqrt(variance + epsilon)
    return centered * inverse, inverse


def sum_stages(rows, chunks, dp_count):
    stages = dp_count.bit_length() - 1
    return stages if dp_count == 1 << stages and rows % (16 * chunks * dp_count) == 0 else 0


def sum_scratch(rows, width, chunks, stages):
    dma = pltpu.SemaphoreType.DMA
    return [
        pltpu.VMEM((rows, width), jnp.bfloat16), pltpu.VMEM((rows, width), jnp.bfloat16),
        dma((chunks, max(1, 2 * stages))), dma((chunks, max(1, 2 * stages))),
    ]


def left_bit(k):
    return k % 2


def packed(k, chunks):
    return k // 2 if k % 2 == 0 else (chunks + 1) // 2 + k // 2


def sum_steps(stages, chunks, acc, came, send, recv, out, half=False):
    dp, mp = lax.axis_index("dp"), lax.axis_index("mp")
    chunk = acc.shape[0] // chunks

    def bit(s):
        return lax.rem(dp // (1 << s), 2)

    def held(k, s):
        start = k * chunk
        for j in range(s):
            start = start + bit(j) * (chunk >> (j + 1))
        return start

    def span(start, size):
        return pl.ds(pl.multiple_of(start, 16), size)

    def placed(k, start):
        if not half:
            return start
        return packed(k, chunks) * (chunk // 2) + bit(1 - left_bit(k)) * (chunk // 4) + start - held(k, 2)

    def halve(k, s):
        size = chunk >> (s + 1)
        return remote(
            acc.at[span(held(k, s) + (1 - bit(s)) * size, size)],
            came.at[span(k * chunk + chunk - (chunk >> s), size)],
            send.at[k, s], recv.at[k, s], (dp ^ (1 << s), mp),
        )

    def double(k, s, mine=True):
        if half and s == 1:
            s = 1 - left_bit(k)
            place = bit(s) if mine else 1 - bit(s)
            rows = out.at[span(packed(k, chunks) * (chunk // 2) + place * (chunk // 4), chunk // 4)]
            return remote(rows, rows, send.at[k, stages + 1], recv.at[k, stages + 1], (dp ^ (1 << s), mp))
        size = chunk >> (s + 1)
        start = held(k, s + 1) if mine else held(k, s) + (1 - bit(s)) * size
        rows = out.at[span(placed(k, start), size)]
        return remote(rows, rows, send.at[k, stages + s], recv.at[k, stages + s], (dp ^ (1 << s), mp))

    final = 1 if half else 0

    def step(k, i):
        if i == 0:
            halve(k, 0).start()
        elif i <= stages:
            halve(k, i - 1).wait_recv()
            size = chunk >> i
            rows = span(held(k, i), size)
            total = acc[rows, :].astype(jnp.float32) + came[span(k * chunk + chunk - (chunk >> (i - 1)), size), :].astype(jnp.float32)
            if i < stages:
                acc[rows, :] = total.astype(jnp.bfloat16)
                halve(k, i).start()
            else:
                out[span(placed(k, held(k, i)), size), :] = total.astype(jnp.bfloat16)
                double(k, stages - 1).start()
        elif 2 * stages - i >= final:
            s = 2 * stages - i
            double(k, s, False).wait_recv()
            if s > final:
                double(k, s - 1).start()

    def drain():
        for k in range(chunks):
            for s in range(stages):
                halve(k, s).wait_send()
                if s >= final:
                    double(k, s).wait_send()

    return step, drain


def columns_of(row):
    return jnp.concatenate(
        [jnp.broadcast_to(row[:, t * 128:(t + 1) * 128], (128, 128)).T for t in range(row.shape[1] // 128)], axis=0
    )


def project_kernel(
    dp_count, tokens_hbm, gain_hbm, w_hbm, cot_ref, owner_hbm, seg_hbm, rows_hbm, q_hbm, k_hbm, v_hbm, grad_hbm, place_hbm, ranges_ref,
    tokens_ref, gain_ref, w_ref, owner_ref, seg_ref, rows_ref, q_ref, k_ref, v_ref, grad_ref, place_ref, load_sem, store_sem, out_sem, returned_ref, across_send, across_recv, pair_send, pair_recv, pass_send, pass_recv, slot_send, slot_recv, self_sem,
):
    load_tokens, load_gain, load_w, load_owner, load_seg = loads = local_copies(
        ((tokens_hbm, tokens_ref), (gain_hbm, gain_ref), (w_hbm, w_ref), (owner_hbm, owner_ref), (seg_hbm, seg_ref)), load_sem
    )
    for load in loads:
        load.start()
    stores = local_copies(
        ((q_ref, q_hbm), (k_ref, k_hbm), (v_ref, v_hbm), (place_ref, place_hbm), (grad_ref, grad_hbm)), out_sem
    )
    dp, mp = lax.axis_index("dp"), lax.axis_index("mp")
    pair, across, far = mp ^ 1, mp ^ 2, mp ^ 3
    own = tokens_ref.shape[0]
    part = own // PARTS
    greet([(dp, pair), (dp, across)] + [(lax.rem(dp + k, dp_count), mp) for k in range(1, dp_count)])

    def spot(owner, c, size):
        return pl.ds(pl.multiple_of(owner * own + c * size, size), size)

    def gather_copy(c, owner, device, send, recv):
        rows = rows_ref.at[spot(owner, c, part)]
        return remote(rows, rows, send.at[c], recv.at[c], device)

    def slot_copy(k):
        other = lax.rem(dp + k, dp_count)
        return remote(cot_ref.at[other], returned_ref.at[dp], slot_send.at[k], slot_recv.at[k], (other, mp))

    def store(i, owner):
        rows = pl.ds(pl.multiple_of(owner * own, own), own)
        return pltpu.make_async_copy(rows_ref.at[rows], rows_hbm.at[rows], store_sem.at[i])

    for k in range(1, dp_count):
        slot_copy(k).start()
    self_copy = pltpu.make_async_copy(cot_ref.at[dp], returned_ref.at[dp], self_sem)
    self_copy.start()
    load_tokens.wait()
    load_gain.wait()
    for c in range(PARTS):
        values = tokens_ref[c * part:(c + 1) * part, :].astype(jnp.float32)
        unit, _ = norm_unit(values)
        rows_ref[spot(mp, c, part), :] = (unit * gain_ref[...].reshape(1, -1)).astype(jnp.bfloat16)
        gather_copy(c, mp, (dp, across), across_send, across_recv).start()
        gather_copy(c, mp, (dp, pair), pair_send, pair_recv).start()
    def product(owner, half):
        where = spot(owner, half, own // 2)
        rows = rows_ref[where, :]
        for p, out in enumerate((q_ref, k_ref, v_ref)):
            out[where, :] = lax.dot_general(rows, w_ref[p], NT, preferred_element_type=jnp.float32).astype(jnp.bfloat16)

    def both(owner):
        def step(half, _):
            product(owner, half)
            return 0
        lax.fori_loop(0, 2, step, 0)

    load_w.wait()
    load_owner.wait()
    load_seg.wait()
    both(mp)
    ranges_ref[...] = key_ranges(seg_ref[...], ranges_ref.shape[0])
    store(0, mp).start()
    capacity = cot_ref.shape[1]
    owner_row = owner_ref[...].astype(jnp.float32)
    owner_col = columns_of(owner_row)
    earlier = lax.broadcasted_iota(jnp.int32, (own, own), 0) < lax.broadcasted_iota(jnp.int32, (own, own), 1)
    same = jnp.concatenate([owner_col] * (own // 128), axis=1) == owner_row
    rank_row = jnp.sum(jnp.where(same & earlier, 1.0, 0.0), axis=0, keepdims=True)
    slot_row = owner_row * capacity + rank_row
    slots = place_ref.shape[0]
    place_ref[...] = jnp.where(
        lax.broadcasted_iota(jnp.int32, (slots, own), 0).astype(jnp.float32) == slot_row, 1.0, 0.0
    ).astype(jnp.bfloat16)
    stores[3].start()
    for c in range(PARTS):
        gather_copy(c, pair, (dp, pair), pair_send, pair_recv).wait_recv()
    both(pair)
    store(1, pair).start()
    for half in range(2):
        for c in range(half * PARTS // 2, (half + 1) * PARTS // 2):
            gather_copy(c, across, (dp, across), across_send, across_recv).wait_recv()
            gather_copy(c, across, (dp, pair), pass_send, pass_recv).start()
        product(across, half)
    store(2, across).start()
    for half in range(2):
        for c in range(half * PARTS // 2, (half + 1) * PARTS // 2):
            gather_copy(c, far, (dp, pair), pass_send, pass_recv).wait_recv()
        product(far, half)
    store(3, far).start()
    for out in stores[:3]:
        out.start()
    for c in range(PARTS):
        gather_copy(c, mp, (dp, across), across_send, across_recv).wait_send()
        gather_copy(c, mp, (dp, pair), pair_send, pair_recv).wait_send()
        gather_copy(c, across, (dp, pair), pass_send, pass_recv).wait_send()
    self_copy.wait()
    for k in range(1, dp_count):
        slot_copy(k).wait_send()
        other = lax.rem(dp + dp_count - k, dp_count)
        remote(cot_ref.at[dp], returned_ref.at[other], slot_send.at[k], slot_recv.at[k], (other, mp)).wait_recv()
    for i, owner in enumerate((mp, pair, across, far)):
        store(i, owner).wait()
    if capacity % 16 == 0:
        back = returned_ref[...].reshape(slots, cot_ref.shape[2])
        grad_ref[...] = lax.dot_general(place_ref[...], back, TN, preferred_element_type=jnp.float32).astype(jnp.bfloat16)
    else:
        rank_col = columns_of(rank_row)[:, :capacity]
        lane = lax.broadcasted_iota(jnp.int32, (own, capacity), 1).astype(jnp.float32)

        def take(d, total):
            pick = (owner_col[:, :capacity] == d.astype(jnp.float32)) & (rank_col == lane)
            pick = jnp.where(pick, 1.0, 0.0).astype(jnp.bfloat16)
            return total + jnp.dot(pick, returned_ref[d], preferred_element_type=jnp.float32)
        grad_ref[...] = lax.fori_loop(0, dp_count, take, jnp.zeros(grad_ref.shape, jnp.float32)).astype(jnp.bfloat16)
    stores[4].start()
    for out in stores:
        out.wait()


def project(tokens, gain, w_qkv, cot, owners, seg):
    own, width = tokens.shape
    dp_count = cot.shape[0]
    total = own * 4
    cols = w_qkv.shape[1]
    vmem = pl.BlockSpec(memory_space=pltpu.VMEM)
    hbm = pl.BlockSpec(memory_space=pltpu.HBM)
    dma = pltpu.SemaphoreType.DMA
    return pl.pallas_call(
        functools.partial(project_kernel, dp_count),
        out_shape=[jax.ShapeDtypeStruct((total, width), jnp.bfloat16)]
        + [jax.ShapeDtypeStruct((total, cols), jnp.bfloat16)] * 3
        + [jax.ShapeDtypeStruct((own, width), jnp.bfloat16), jax.ShapeDtypeStruct((dp_count * cot.shape[1], own), jnp.bfloat16)]
        + [jax.ShapeDtypeStruct((seg.shape[1] // TQ, 128), jnp.int32)],
        in_specs=[hbm] * 6,
        out_specs=[hbm] * 6 + [vmem],
        scratch_shapes=[pltpu.VMEM(one.shape, one.dtype) for one in (tokens, gain, w_qkv, owners, seg)]
        + [pltpu.VMEM((total, width), jnp.bfloat16)] + [pltpu.VMEM((total, cols), jnp.bfloat16)] * 3
        + [pltpu.VMEM((own, width), jnp.bfloat16), pltpu.VMEM((dp_count * cot.shape[1], own), jnp.bfloat16)]
        + [dma((5,)), dma((4,)), dma((5,)), pltpu.VMEM(cot.shape, cot.dtype)] + [dma((PARTS,))] * 6 + [dma((dp_count,))] * 2 + [dma],
        compiler_params=pltpu.CompilerParams(collective_id=1, has_side_effects=True, vmem_limit_bytes=VMEM_BYTES),
        cost_estimate=pl.CostEstimate(flops=6 * total * width * cols, bytes_accessed=10 * total * width, transcendentals=0),
        name="project",
    )(tokens, gain, w_qkv, cot, owners, seg)


def gelu_and_slope(values):
    cumulative = 0.5 * (1.0 + lax.erf(values * 0.7071067811865476))
    density = jnp.exp(-0.5 * values * values) * 0.3989422804014327
    return values * cumulative, cumulative + values * density


def middle_kernel(
    stages, merged_hbm, w_out_hbm, tokens_hbm, gain_hbm, w_up_hbm, w_down_hbm, grad_own_hbm, grad_across_hbm, place_hbm,
    back_rows_hbm, grad_merged_hbm, grad_residual_hbm, outgoing_hbm, first_hbm, second_hbm, gain_part_hbm, d_out_hbm,
    merged_ref, w_out_ref, tokens_ref, gain_ref, gain_part_ref, d_out_ref, w_up_ref, w_down_ref, grad_own_ref, grad_across_ref, place_ref,
    back_rows_ref, grad_merged_ref, grad_residual_ref, outgoing_ref, d_mlp_ref, load_sem, store_sem,
    mlp_rows, grad_rows, active, grad_pre, residual, mine, bufs,
    sum_send, sum_recv, row_send, row_recv, grad_send, grad_recv, self_sem, acc, came, dp_send, dp_recv,
):
    first_rows = first_hbm.shape[0]
    loads = local_copies(
        (
            (merged_hbm, merged_ref), (w_out_hbm, w_out_ref), (tokens_hbm, tokens_ref), (grad_own_hbm, grad_own_ref),
            (grad_across_hbm, grad_across_ref), (w_up_hbm, w_up_ref), (w_down_hbm, w_down_ref), (place_hbm, place_ref),
            (gain_hbm, gain_ref),
        ),
        load_sem,
    )
    for load in loads:
        load.start()
    stores = local_copies(
        (
            (back_rows_ref, back_rows_hbm), (grad_merged_ref, grad_merged_hbm), (grad_residual_ref, grad_residual_hbm),
            (outgoing_ref, outgoing_hbm), (d_mlp_ref.at[0:first_rows], first_hbm), (d_mlp_ref.at[first_rows:], second_hbm),
            (gain_part_ref, gain_part_hbm), (d_out_ref, d_out_hbm),
        ),
        store_sem,
    )
    low, full = jnp.bfloat16, jnp.float32
    dp, mp = lax.axis_index("dp"), lax.axis_index("mp")
    pair, across, far = mp ^ 1, mp ^ 2, mp ^ 3
    own, width = tokens_ref.shape
    part = own // PARTS
    to_pair, to_across = (dp, pair), (dp, across)
    greet([to_pair, to_across] + [(dp ^ (1 << j), mp) for j in range(stages)])
    add_step, add_drain = sum_steps(stages, MLP_CHUNKS, acc, came, dp_send, dp_recv, d_mlp_ref, half=True)
    target = acc if stages else d_mlp_ref

    def spot(owner, c=None):
        if c is None:
            return pl.ds(pl.multiple_of(owner * own, own), own)
        return pl.ds(pl.multiple_of(owner * own + c * part, part), part)

    def piece(c):
        return pl.ds(pl.multiple_of(c * part, part), part)

    def grad_copy(i, owner, src):
        return remote(src, grad_rows.at[spot(owner)], grad_send.at[i], grad_recv.at[i], to_pair)

    grad_loads = [
        pltpu.make_async_copy(grad_own_ref, grad_rows.at[spot(mp)], self_sem.at[0]),
        pltpu.make_async_copy(grad_across_ref, grad_rows.at[spot(across)], self_sem.at[1]),
    ]

    FAR, ACROSS, PAIR = 0, 1, 2

    def sum_copy(which, kind, c):
        src, dst = bufs.at[which, 0, kind, piece(c)], bufs.at[which, 1, kind, piece(c)]
        return remote(src, dst, sum_send.at[which, kind, c], sum_recv.at[which, kind, c], to_across if kind == ACROSS else to_pair)

    def arrived(which, kind, c):
        sum_copy(which, kind, c).wait_recv()
        return bufs[which, 1, kind, piece(c), :].astype(full)

    def ship(which, kind, c, values):
        bufs[which, 0, kind, piece(c), :] = values.astype(low)
        sum_copy(which, kind, c).start()

    def row_copy(which, kind, c, owner, ref):
        rows = ref.at[spot(owner, c)]
        return remote(rows, rows, row_send.at[which, kind, c], row_recv.at[which, kind, c], to_across if kind == 0 else to_pair)

    def each(count, body):
        def step(i, _):
            body(i)
            return 0
        lax.fori_loop(0, count, step, 0)

    def out_part(owner):
        return jnp.dot(merged_ref[spot(owner), :], w_out_ref[...], preferred_element_type=full)

    loads[0].wait()
    loads[1].wait()
    bufs[0, 0, FAR] = out_part(far).astype(low)
    each(PARTS, lambda c: sum_copy(0, FAR, c).start())
    mine[0] = out_part(across)

    def pass_across(c):
        ship(0, ACROSS, c, mine[0, piece(c), :] + arrived(0, FAR, c))
    each(PARTS, pass_across)
    bufs[0, 0, PAIR] = out_part(pair).astype(low)
    each(PARTS, lambda c: sum_copy(0, PAIR, c).start())
    for load in loads[2:5]:
        load.wait()
    for copy in grad_loads:
        copy.start()
    grad_copy(0, mp, grad_own_ref).start()
    grad_copy(1, across, grad_across_ref).start()
    mine[0] = out_part(mp) + tokens_ref[...].astype(full)
    for copy in grad_loads:
        copy.wait()
    grad_copy(0, pair, grad_own_ref).wait_recv()
    grad_copy(1, far, grad_across_ref).wait_recv()

    for load in loads[5:]:
        load.wait()
    blocks = w_up_ref.shape[1] // 256
    both = 2 * part

    def mlp(first, second, c):
        rows = jnp.concatenate([mlp_rows[spot(first, c), :], mlp_rows[spot(second, c), :]], axis=0)
        grads = jnp.concatenate([grad_rows[spot(first, c), :], grad_rows[spot(second, c), :]], axis=0)

        def block(b):
            cols = pl.ds(pl.multiple_of(b * 256, 256), 256)
            pre = jnp.dot(rows, w_up_ref[:, cols], preferred_element_type=full)
            value, slope = gelu_and_slope(pre)
            value = value.astype(low)
            active[spot(first, c), cols] = value[:part]
            active[spot(second, c), cols] = value[part:]
            back = (jnp.dot(grads, w_down_ref[:, cols], preferred_element_type=full) * slope).astype(low)
            grad_pre[spot(first, c), cols] = back[:part]
            grad_pre[spot(second, c), cols] = back[part:]
        each(blocks, block)
        back = jnp.concatenate([grad_pre[spot(first, c), :], grad_pre[spot(second, c), :]], axis=0)
        return lax.dot_general(back, w_up_ref[...], NT, preferred_element_type=full)

    def near(c):
        values = mine[0, piece(c), :] + arrived(0, PAIR, c) + arrived(0, ACROSS, c)
        residual[piece(c), :] = values
        unit, _ = norm_unit(values)
        mlp_rows[spot(mp, c), :] = (unit * gain_ref[...].reshape(1, -1)).astype(low)
        row_copy(0, 0, c, mp, mlp_rows).start()
        row_copy(0, 1, c, mp, mlp_rows).start()
        row_copy(0, 1, c, pair, mlp_rows).wait_recv()
        got = mlp(mp, pair, c)
        mine[1, piece(c), :] = got[:part]
        ship(1, PAIR, c, got[part:])
    each(PARTS, near)

    def distant(c):
        row_copy(0, 0, c, across, mlp_rows).wait_recv()
        row_copy(0, 2, c, across, mlp_rows).start()
        row_copy(0, 2, c, far, mlp_rows).wait_recv()
        got = mlp(far, across, c)
        ship(1, FAR, c, got[:part])
        ship(1, ACROSS, c, got[part:] + arrived(1, FAR, c))
    each(PARTS, distant)

    size = width // MLP_CHUNKS
    for b in range(3):
        cols = slice(b * 256, (b + 1) * 256)
        up = lax.dot_general(mlp_rows[:, cols], grad_pre[...], TN, preferred_element_type=full)
        gain_col = jnp.sum(up * w_up_ref[cols, :].astype(full), axis=1, keepdims=True)
        gain_part_ref[:, cols] = jnp.broadcast_to(gain_col, (256, 128)).T[0:8] / gain_ref[cols].reshape(1, -1)
        up = up.astype(low)
        down = lax.dot_general(grad_rows[:, cols], active[...], TN, preferred_element_type=full).astype(low)
        for j in range(256 // size):
            k = b * (256 // size) + j
            target[2 * k * size:(2 * k + 1) * size, :] = up[j * size:(j + 1) * size]
            target[(2 * k + 1) * size:(2 * k + 2) * size, :] = down[j * size:(j + 1) * size]
            if stages:
                add_step(k, 0)

    def add(*steps):
        if stages:
            for k, i in steps:
                add_step(k, i)

    def down_part(owner):
        return lax.dot_general(active[spot(owner), :], w_down_ref[...], NT, preferred_element_type=full)

    bufs[2, 0, FAR] = down_part(far).astype(low)
    each(PARTS, lambda c: sum_copy(2, FAR, c).start())
    bufs[2, 0, PAIR] = down_part(pair).astype(low)
    each(PARTS, lambda c: sum_copy(2, PAIR, c).start())

    def back_norm(c):
        grad = mine[1, piece(c), :] + arrived(1, PAIR, c) + arrived(1, ACROSS, c)
        unit, inverse = norm_unit(residual[piece(c), :])
        scaled = grad * gain_ref[...].reshape(1, -1)
        first_mean = jnp.mean(scaled, axis=-1, keepdims=True)
        second_mean = jnp.mean(scaled * unit, axis=-1, keepdims=True)
        total = inverse * (scaled - first_mean - unit * second_mean) + grad_own_ref[piece(c), :].astype(full)
        grad_residual_ref[piece(c), :] = total
        back_rows_ref[spot(mp, c), :] = total.astype(low)
        row_copy(1, 0, c, mp, back_rows_ref).start()
        row_copy(1, 1, c, mp, back_rows_ref).start()
    def tick(t):
        add(*[(t - i, i) for i in range(1, 2 * stages + 1) if 0 <= t - i < MLP_CHUNKS])

    each(2, back_norm)
    tick(1)
    each(1, lambda c: back_norm(c + 2))
    tick(2)
    each(1, lambda c: back_norm(c + 3))

    mine[1] = down_part(across)

    def pass_output(c):
        ship(2, ACROSS, c, mine[1, piece(c), :] + arrived(2, FAR, c))
    each(PARTS, pass_output)
    tick(3)
    mine[0] = residual[...] + down_part(mp)

    def merged_part(owner):
        grad_merged_ref[spot(owner), :] = lax.dot_general(
            back_rows_ref[spot(owner), :], w_out_ref[...], NT, preferred_element_type=full
        ).astype(low)

    merged_part(mp)
    each(PARTS, lambda c: row_copy(1, 1, c, pair, back_rows_ref).wait_recv())
    merged_part(pair)

    def hand_on(c):
        row_copy(1, 0, c, across, back_rows_ref).wait_recv()
        row_copy(1, 2, c, across, back_rows_ref).start()
    for c in range(PARTS):
        each(1, lambda i: hand_on(i + c))
        tick(4 + c)
    tick(8)
    merged_part(across)
    each(PARTS, lambda c: row_copy(1, 2, c, far, back_rows_ref).wait_recv())
    tick(9)
    merged_part(far)
    stores[0].start()
    stores[1].start()
    stores[2].start()
    d_out_ref[...] = lax.dot_general(merged_ref[...], back_rows_ref[...], TN, preferred_element_type=full).astype(low)
    stores[6].start()
    stores[7].start()

    tick(10)

    def finish(c):
        mine[0, piece(c), :] = mine[0, piece(c), :] + arrived(2, PAIR, c) + arrived(2, ACROSS, c)
    for c in range(PARTS):
        each(1, lambda i: finish(i + c))
    stores[4].start()
    stores[5].start()
    outgoing_ref[...] = jnp.dot(place_ref[...], mine[0].astype(low), preferred_element_type=full).astype(low)
    stores[3].start()
    if stages:
        add_drain()
    for store in stores:
        store.wait()

    def drain(c):
        for which in range(3):
            for kind in range(3):
                sum_copy(which, kind, c).wait_send()
        for which, ref in ((0, mlp_rows), (1, back_rows_ref)):
            row_copy(which, 0, c, mp, ref).wait_send()
            row_copy(which, 1, c, mp, ref).wait_send()
            row_copy(which, 2, c, across, ref).wait_send()
    each(PARTS, drain)
    grad_copy(0, mp, grad_own_ref).wait_send()
    grad_copy(1, across, grad_across_ref).wait_send()


def middle(dp_count, merged, w_out, tokens, gain, w_up, w_down, grad_own, grad_across, place):
    stages = sum_stages(2 * w_up.shape[0], MLP_CHUNKS, dp_count)
    d_rows = w_up.shape[0] * (1 if stages else 2)
    total, cols = merged.shape
    own, width = tokens.shape
    hidden = w_up.shape[1]
    slots = place.shape[0]
    low, full = jnp.bfloat16, jnp.float32
    vmem = pl.BlockSpec(memory_space=pltpu.VMEM)
    hbm = pl.BlockSpec(memory_space=pl.ANY)
    dma = pltpu.SemaphoreType.DMA
    shape, room = jax.ShapeDtypeStruct, pltpu.VMEM
    return pl.pallas_call(
        functools.partial(middle_kernel, stages),
        out_shape=[
            shape((total, width), low), shape((total, cols), low), shape((own, width), full), shape((slots, width), low),
            shape((d_rows // 2, hidden), low), shape((d_rows // 2, hidden), low), shape((8, width), full), shape((cols, width), low),
        ],
        in_specs=[hbm] * 9,
        out_specs=[hbm] * 8,
        scratch_shapes=[
            room((total, cols), low), room(w_out.shape, low), room((own, width), low), room(gain.shape, full),
            room((8, width), full), room((cols, width), low), room(w_up.shape, low),
            room(w_down.shape, low), room((own, width), low), room((own, width), low), room(place.shape, low),
            room((total, width), low), room((total, cols), low), room((own, width), full), room((slots, width), low),
            room((d_rows, hidden), low), dma((9,)), dma((8,)),
            room((total, width), low), room((total, width), low),
            room((total, hidden), low), room((total, hidden), low),
            room((own, width), full), room((2, own, width), full),
            room((3, 2, 3, own, width), low),
            dma((3, 3, PARTS)), dma((3, 3, PARTS)), dma((2, 3, PARTS)), dma((2, 3, PARTS)), dma((2,)), dma((2,)), dma((2,)),
        ]
        + sum_scratch(2 * width, hidden, MLP_CHUNKS, stages),
        compiler_params=pltpu.CompilerParams(collective_id=2, has_side_effects=True, vmem_limit_bytes=VMEM_BYTES),
        cost_estimate=pl.CostEstimate(flops=16 * total * width * hidden, bytes_accessed=20 * total * width, transcendentals=0),
        name="middle",
    )(merged, w_out, tokens, gain, w_up, w_down, grad_own, grad_across, place)


def direct_fits(rows, chunks, dp_count):
    return dp_count % 2 == 0 and rows % (16 * chunks * dp_count) == 0


def direct_steps(dp_count, chunks, acc, came, send, recv, out, out_hbm, keep_sem):
    dp, mp = lax.axis_index("dp"), lax.axis_index("mp")
    chunk = acc.shape[0] // chunks
    group = dp_count // 2
    half, slot = chunk // 2, chunk // dp_count
    y, z = lax.rem(dp, 2), dp // 2
    beside = (dp + 1 - 2 * y, mp)
    others = sorted(range(1, group), key=lambda j: -min(j, group - j))

    def span(start, size):
        return pl.ds(pl.multiple_of(start, 16), size)

    def low(k, side, g=0):
        return k * chunk + side * half + g * slot

    def member(j):
        return lax.rem(z + j, group)

    def slot_of(k, j):
        return span(k * chunk + half + (j - 1) * slot, slot)

    def halve(k):
        return remote(acc.at[span(low(k, 1 - y), half)], came.at[span(k * chunk, half)], send.at[k, 0], recv.at[k, 0], beside)

    def scatter(k, j):
        piece = acc.at[span(low(k, y, member(j)), slot)]
        return remote(piece, came.at[slot_of(k, j)], send.at[k, j], recv.at[k, j], (y + 2 * member(j), mp))

    def gather(k, j, mine=True):
        rows = out.at[span(low(k, y, z if mine else member(group - j)), slot)]
        return remote(rows, rows, send.at[k, group + j - 1], recv.at[k, group + j - 1], (y + 2 * member(j), mp))

    def double(k, mine=True):
        rows = span(low(k, y if mine else 1 - y), half)
        return remote(out.at[rows], out_hbm.at[rows], send.at[k, 2 * group - 1], recv.at[k, 2 * group - 1], beside)

    def keep(k):
        rows = span(low(k, y), half)
        return pltpu.make_async_copy(out.at[rows], out_hbm.at[rows], keep_sem.at[k])

    def step(k, i):
        if i == 0:
            halve(k).start()
        elif i == 1:
            halve(k).wait_recv()
            rows = span(low(k, y), half)
            total = acc[rows, :].astype(jnp.float32) + came[span(k * chunk, half), :].astype(jnp.float32)
            acc[rows, :] = total.astype(jnp.bfloat16)
            for j in others:
                scatter(k, j).start()
        elif i == 2:
            rows = span(low(k, y, z), slot)
            total = acc[rows, :].astype(jnp.float32)
            for j in others:
                scatter(k, j).wait_recv()
                total = total + came[slot_of(k, j), :].astype(jnp.float32)
            out[rows, :] = total.astype(jnp.bfloat16)
            for j in others:
                gather(k, j).start()
        elif i == 3:
            for j in others:
                gather(k, j, False).wait_recv()
            double(k).start()
            keep(k).start()
        else:
            double(k, False).wait_recv()

    def drain():
        for k in range(chunks):
            halve(k).wait_send()
            for j in others:
                scatter(k, j).wait_send()
                gather(k, j).wait_send()
            double(k).wait_send()
            keep(k).wait()

    return step, drain


def last_kernel(
    dp_count, fits, dq_hbm, dk_hbm, dv_hbm, w_hbm, rows_hbm, grad_residual_hbm, tokens_hbm, gain_hbm, gain_part_hbm, d_out_hbm,
    grad_tokens_hbm, d_sum_hbm, gains_hbm,
    dq_ref, dk_ref, dv_ref, w_ref, rows_ref, grad_residual_ref, tokens_ref, gain_ref, gain_part_ref, d_out_ref,
    grad_tokens_ref, gains_ref, load_sem, store_sem, mine, bufs, gain_dp, gain_mp,
    sum_send, sum_recv, dp_gain_send, dp_gain_recv, mp_gain_send, mp_gain_recv, acc, came, out, dp_send, dp_recv, keep_sem,
):
    loads = local_copies(
        (
            (dq_hbm, dq_ref), (rows_hbm, rows_ref), (w_hbm, w_ref), (d_out_hbm, d_out_ref), (dk_hbm, dk_ref), (dv_hbm, dv_ref),
            (gain_hbm, gain_ref), (gain_part_hbm, gain_part_ref), (grad_residual_hbm, grad_residual_ref), (tokens_hbm, tokens_ref),
        ),
        load_sem,
    )
    for load in loads:
        load.start()
    store_tokens, store_gains = local_copies(((grad_tokens_ref, grad_tokens_hbm), (gains_ref, gains_hbm)), store_sem)
    low, full = jnp.bfloat16, jnp.float32
    dp, mp = lax.axis_index("dp"), lax.axis_index("mp")
    pair, across, far = mp ^ 1, mp ^ 2, mp ^ 3
    own, width = tokens_ref.shape
    part = own // PARTS
    cols = dq_ref.shape[1]
    to_pair, to_across = (dp, pair), (dp, across)
    greet([to_pair, to_across, (dp, far)] + [(lax.rem(dp + k, dp_count), mp) for k in range(1, dp_count)])
    add_step, add_drain = direct_steps(dp_count, QKV_CHUNKS, acc, came, dp_send, dp_recv, out, d_sum_hbm, keep_sem)
    FAR, ACROSS, PAIR = 0, 1, 2

    def add(*steps):
        if fits:
            for k, i in steps:
                add_step(k, i)

    def piece(c):
        return pl.ds(pl.multiple_of(c * part, part), part)

    def each(count, body):
        def step(i, _):
            body(i)
            return 0
        lax.fori_loop(0, count, step, 0)

    def sum_copy(kind, c):
        src, dst = bufs.at[0, kind, piece(c)], bufs.at[1, kind, piece(c)]
        return remote(src, dst, sum_send.at[kind, c], sum_recv.at[kind, c], to_across if kind == ACROSS else to_pair)

    def arrived(kind, c):
        sum_copy(kind, c).wait_recv()
        return bufs[1, kind, piece(c), :].astype(full)

    def in_part(owner):
        where = pl.ds(pl.multiple_of(owner * own, own), own)
        total = jnp.dot(dq_ref[where, :], w_ref[0], preferred_element_type=full)
        total = total + jnp.dot(dk_ref[where, :], w_ref[1], preferred_element_type=full)
        return total + jnp.dot(dv_ref[where, :], w_ref[2], preferred_element_type=full)

    def weight_grad(p, ref):
        grad = lax.dot_general(ref[...], rows_ref[...], TN, preferred_element_type=full)
        acc[(p + 1) * cols:(p + 2) * cols, :] = grad.astype(low)
        return jnp.sum(grad * w_ref[p].astype(full), axis=0, keepdims=True)

    for load in loads[:4]:
        load.wait()
    acc[0:cols, :] = d_out_ref[...]
    gain_row = weight_grad(0, dq_ref)
    add((0, 0))
    for load in loads[4:]:
        load.wait()
    bufs[0, FAR] = in_part(far).astype(low)
    each(PARTS, lambda c: sum_copy(FAR, c).start())
    gain_row = gain_row + weight_grad(1, dk_ref)
    add((1, 0))
    mine[...] = in_part(across)

    def pass_across(c):
        bufs[0, ACROSS, piece(c), :] = (mine[piece(c), :] + arrived(FAR, c)).astype(low)
        sum_copy(ACROSS, c).start()
    each(PARTS, pass_across)
    gain_row = gain_row + weight_grad(2, dv_ref)
    add((2, 0))

    row = lax.broadcasted_iota(jnp.int32, (8, width), 0)
    gain_dp[dp] = jnp.where(row == 0, gain_part_ref[...], jnp.where(row == 1, gain_row / gain_ref[...].reshape(1, -1), 0.0))

    def gain_over_dp(k, owner):
        return remote(gain_dp.at[owner], gain_dp.at[owner], dp_gain_send.at[k], dp_gain_recv.at[k], (lax.rem(dp + k, dp_count), mp))

    def gain_over_mp(i, owner):
        other = (pair, across, far)[i]
        return remote(gain_mp.at[owner], gain_mp.at[owner], mp_gain_send.at[i], mp_gain_recv.at[i], (dp, other))

    for k in range(1, dp_count):
        gain_over_dp(k, dp).start()

    def turn_gains():
        for k in range(1, dp_count):
            gain_over_dp(k, lax.rem(dp + dp_count - k, dp_count)).wait_recv()
        total = gain_dp[0]
        for k in range(1, dp_count):
            total = total + gain_dp[k]
        gain_mp[mp] = total
        for i in range(3):
            gain_over_mp(i, mp).start()

    def end_gains():
        for i, owner in enumerate((pair, across, far)):
            gain_over_mp(i, owner).wait_recv()
        gains_ref[...] = (gain_mp[0] + gain_mp[1]) + (gain_mp[2] + gain_mp[3])
        store_gains.start()

    bufs[0, PAIR] = in_part(pair).astype(low)
    each(PARTS, lambda c: sum_copy(PAIR, c).start())
    mine[...] = in_part(mp)

    def back_norm(c):
        grad = mine[piece(c), :] + arrived(PAIR, c) + arrived(ACROSS, c)
        unit, inverse = norm_unit(tokens_ref[piece(c), :].astype(full))
        scaled = grad * gain_ref[...].reshape(1, -1)
        first_mean = jnp.mean(scaled, axis=-1, keepdims=True)
        second_mean = jnp.mean(scaled * unit, axis=-1, keepdims=True)
        total = inverse * (scaled - first_mean - unit * second_mean) + grad_residual_ref[piece(c), :]
        grad_tokens_ref[piece(c), :] = total.astype(low)

    def norm(c):
        each(1, lambda i: back_norm(i + c))

    add((0, 1))
    norm(0)
    add((1, 1), (0, 2))
    norm(1)
    add((2, 1), (1, 2), (0, 3))
    norm(2)
    turn_gains()
    add((2, 2), (1, 3))
    norm(3)
    store_tokens.start()
    add((0, 4), (2, 3))
    end_gains()
    add((1, 4), (2, 4))
    if fits:
        add_drain()
    else:
        whole = pltpu.make_async_copy(acc, d_sum_hbm, keep_sem.at[0])
        whole.start()
        whole.wait()
    for k in range(1, dp_count):
        gain_over_dp(k, dp).wait_send()
    for i in range(3):
        gain_over_mp(i, mp).wait_send()

    def drain(c):
        for kind in range(3):
            sum_copy(kind, c).wait_send()
    each(PARTS, drain)
    store_tokens.wait()
    store_gains.wait()


def last(dp_count, dq, dk, dv, w_qkv, rows, grad_residual, tokens, gain, gain_part, d_out):
    own, width = tokens.shape
    cols = dq.shape[1]
    d_rows = 4 * cols
    fits = direct_fits(d_rows, QKV_CHUNKS, dp_count)
    low, full = jnp.bfloat16, jnp.float32
    hbm = pl.BlockSpec(memory_space=pl.ANY)
    dma = pltpu.SemaphoreType.DMA
    shape, room = jax.ShapeDtypeStruct, pltpu.VMEM
    operands = (dq, dk, dv, w_qkv, rows, grad_residual, tokens, gain, gain_part, d_out)
    grad_tokens, d_sum, gains = pl.pallas_call(
        functools.partial(last_kernel, dp_count, fits),
        out_shape=[shape((own, width), low), shape((d_rows, width), low), shape((8, width), full)],
        in_specs=[hbm] * 10,
        out_specs=[hbm] * 3,
        scratch_shapes=[room(one.shape, one.dtype) for one in operands]
        + [
            room((own, width), low), room((8, width), full), dma((10,)), dma((2,)),
            room((own, width), full), room((2, 3, own, width), low), room((dp_count, 8, width), full), room((4, 8, width), full),
            dma((3, PARTS)), dma((3, PARTS)), dma((dp_count,)), dma((dp_count,)), dma((3,)), dma((3,)),
            room((d_rows, width), low), room((d_rows, width), low), room((d_rows, width), low),
            dma((QKV_CHUNKS, dp_count)), dma((QKV_CHUNKS, dp_count)), dma((QKV_CHUNKS,)),
        ],
        compiler_params=pltpu.CompilerParams(collective_id=3, has_side_effects=True, vmem_limit_bytes=VMEM_BYTES),
        cost_estimate=pl.CostEstimate(flops=12 * 4 * own * width * cols, bytes_accessed=20 * own * width, transcendentals=0),
        name="last",
    )(*operands)
    return grad_tokens, d_sum if fits else lax.psum(d_sum, "dp"), gains


def finish_kernel(
    first_ref, first_came_ref, second_ref, second_came_ref, attn_ref, qkv_ref, gains_ref, tokens_hbm, relaid_hbm,
    up_ref, down_ref, attn_out_ref, qkv_out_ref, gain_attn_ref, gain_mlp_ref, tokens_out_hbm, relaid_out_hbm, tokens_ref, relaid_ref, load_sem, store_sem,
):
    loads = local_copies(((tokens_hbm, tokens_ref), (relaid_hbm, relaid_ref)), load_sem)
    stores = local_copies(((tokens_ref, tokens_out_hbm), (relaid_ref, relaid_out_hbm)), store_sem)

    @pl.when(pl.program_id(0) == 0)
    def _():
        for load in loads:
            load.start()

    @pl.when(pl.program_id(0) == 1)
    def _():
        for load, store in zip(loads, stores):
            load.wait()
            store.start()

    full = jnp.float32
    dp = lax.axis_index("dp")
    size = first_ref.shape[0]
    mine, came = first_ref[...].astype(full), first_came_ref[...].astype(full)
    even = lax.rem(dp, 2) == 0
    up_ref[0:size, :] = jnp.where(even, mine, came)
    down_ref[0:size, :] = jnp.where(even, came, mine)
    mine, came = second_ref[...].astype(full), second_came_ref[...].astype(full)
    even = lax.rem(dp // 2, 2) == 0
    low, high = jnp.where(even, mine, came), jnp.where(even, came, mine)
    half = size // 2
    up_ref[size:size + half, :] = low[:half]
    up_ref[size + half:, :] = high[:half]
    down_ref[size:size + half, :] = low[half:]
    down_ref[size + half:, :] = high[half:]
    attn_out_ref[...] = attn_ref[...].astype(full)
    qkv_out_ref[...] = qkv_ref[...].astype(full)
    gain_mlp_ref[...] = gains_ref[0]
    gain_attn_ref[...] = gains_ref[1]

    @pl.when(pl.program_id(0) == pl.num_programs(0) - 1)
    def _():
        for store in stores:
            store.wait()


def finish(first, first_came, second, second_came, weight_sum, gains, grad_tokens, relaid):
    steps = MLP_CHUNKS // 2
    size = first.shape[0] // steps
    rows, width = weight_sum.shape
    cols = rows // 4
    full = jnp.float32
    hbm = pl.BlockSpec(memory_space=pl.ANY)
    vmem = pl.BlockSpec(memory_space=pltpu.VMEM)
    shape = jax.ShapeDtypeStruct

    def block(count, ahead=0):
        return pl.BlockSpec((count, width), lambda i: (i + ahead, 0))

    return pl.pallas_call(
        finish_kernel,
        grid=(steps,),
        out_shape=[
            shape((2 * steps * size, width), full), shape((2 * steps * size, width), full), shape((cols, width), full),
            shape((3 * cols, width), full), shape((width,), full), shape((width,), full), shape(grad_tokens.shape, grad_tokens.dtype), shape(relaid.shape, relaid.dtype),
        ],
        in_specs=[block(size)] * 4 + [block(cols // 3), block(cols, 1), vmem, hbm, hbm],
        out_specs=[block(2 * size)] * 2 + [block(cols // 3), block(cols), vmem, vmem, hbm, hbm],
        scratch_shapes=[pltpu.VMEM(one.shape, one.dtype) for one in (grad_tokens, relaid)]
        + [pltpu.SemaphoreType.DMA((2,)), pltpu.SemaphoreType.DMA((2,))],
        compiler_params=pltpu.CompilerParams(vmem_limit_bytes=VMEM_BYTES),
        cost_estimate=pl.CostEstimate(flops=0, bytes_accessed=14 * rows * width, transcendentals=0),
        name="finish",
    )(first, first_came, second, second_came, weight_sum, weight_sum, gains, grad_tokens, relaid)


def local(
    tokens, segment_ids, gene_owner, w_qkv, w_attn_out, w_up, w_down, gain_attn, gain_mlp, cotangent
):
    width = tokens.shape[1]
    dp_count = lax.axis_size("dp")
    capacity = cotangent.shape[0] // dp_count
    low, full = jnp.bfloat16, jnp.float32
    w_rows = jnp.swapaxes(w_qkv, 1, 2)
    attn_in, *projected, grad_block, place, ranges = project(
        tokens, gain_attn, w_rows, cotangent.reshape(dp_count, capacity, width), gene_owner.reshape(1, -1), segment_ids
    )
    grad_across = lax.ppermute(grad_block, "mp", [(i, i ^ 2) for i in range(lax.axis_size("mp"))])
    merged, log_sums = attend_forward(ranges, segment_ids, *projected)
    residual_rows, grad_merged, grad_residual, outgoing, first, second, gain_part, d_out = middle(
        dp_count, merged, w_attn_out, tokens, gain_mlp, w_up, w_down, grad_block, grad_across, place
    )
    cols = w_qkv.shape[2]
    whole = sum_stages(2 * width, MLP_CHUNKS, dp_count) == 0
    if not whole:
        first_came = lax.ppermute(first, "dp", [(i, i ^ 1) for i in range(dp_count)])
        second_came = lax.ppermute(second, "dp", [(i, i ^ 2) for i in range(dp_count)])
        gain_part, first_came, second_came = lax.optimization_barrier((gain_part, first_came, second_came))
    relaid = lax.all_to_all(
        outgoing.reshape(dp_count, capacity, width), "dp", split_axis=0, concat_axis=0, tiled=True
    ).reshape(dp_count * capacity, width)
    grad_proj = attend_backward(ranges, segment_ids, *projected, merged, grad_merged, log_sums)
    grad_tokens, weight_sum, gains = last(
        dp_count, *grad_proj, w_rows, attn_in, grad_residual, tokens, gain_attn, gain_part, d_out
    )
    if whole:
        d_sum = lax.psum(jnp.concatenate([first, second]), "dp").reshape(MLP_CHUNKS, 2, -1, width).astype(full)
        up_sum, down_sum = (d_sum[:, i].reshape(-1, width) for i in range(2))
        attn_sum, qkv_sum = weight_sum[:cols].astype(full), weight_sum[cols:].astype(full)
        gain_one, gain_two = gains[1], gains[0]
    else:
        up_sum, down_sum, attn_sum, qkv_sum, gain_one, gain_two, grad_tokens, relaid = finish(
            first, first_came, second, second_came, weight_sum, gains, grad_tokens, relaid
        )
    qkv_sum = qkv_sum.reshape(3, cols, width)
    return (
        relaid,
        grad_tokens,
        jnp.swapaxes(qkv_sum, 1, 2),
        attn_sum,
        up_sum,
        down_sum,
        gain_one,
        gain_two,
    )


def solution(mesh):
    placed = (
        P(("dp", "mp"), None),
        P("dp", None),
        P(("dp", "mp"), None),
        P(None, None, "mp"),
        P("mp", None),
        P(None, "mp"),
        P(None, "mp"),
        P(),
        P(),
        P(("dp", "mp"), None),
    )
    return jax.shard_map(
        local,
        mesh=mesh,
        in_specs=placed,
        out_specs=(
            P(("dp", "mp"), None),
            P(("dp", "mp"), None),
            P(None, None, "mp"),
            P("mp", None),
            P(None, "mp"),
            P(None, "mp"),
            P(),
            P(),
        ),
        check_vma=False,
    )
```

```python
import functools
import jax
import jax.numpy as jnp
from jax import lax
from jax.experimental import pallas as pl
from jax.experimental.pallas import tpu as pltpu
from jax.sharding import PartitionSpec as P

HEAD = 64
TQ = 256
TK = 256
NT = (((1,), (1,)), ((), ()))
NN = (((1,), (0,)), ((), ()))
TN = (((0,), (0,)), ((), ()))
MASKED = -1e30
TALL = HEAD + 16
epsilon = 1e-05


def local_copies(pairs, sems):
    return [pltpu.make_async_copy(src, dst, sems.at[i]) for i, (src, dst) in enumerate(pairs)]


def key_ranges(seg, tiles):
    n = seg.shape[1]
    lane = lax.broadcasted_iota(jnp.int32, (tiles, n), 1)
    row = lax.broadcasted_iota(jnp.int32, (tiles, n), 0)
    ids = jnp.broadcast_to(seg.astype(jnp.float32), (tiles, n))

    def total(mask, values):
        return jnp.sum(jnp.where(mask, values, 0.0), axis=1, keepdims=True)

    first = total(lane == row * TQ, ids)
    last = total(lane == row * TQ + TQ - 1, ids)
    start = jnp.floor(total(ids < first, 1.0) * (1.0 / TK))
    end = jnp.floor((total(ids <= last, 1.0) + (TK - 1.0)) * (1.0 / TK))
    lane = lax.broadcasted_iota(jnp.int32, (tiles, 128), 1)
    return jnp.where(lane == 0, start, jnp.where(lane == 1, end, 0.0)).astype(jnp.int32)


def over_blocks(ranges, tile, body, state):
    lo, hi = ranges[tile, 0], ranges[tile, 1]
    pairs = (hi - lo) // 2
    state = lax.fori_loop(
        0, pairs, lambda i, one: body(pl.multiple_of((lo + 2 * i) * TK, TK), 2 * TK, one), state
    )
    return lax.fori_loop(lo + 2 * pairs, hi, lambda i, one: body(pl.multiple_of(i * TK, TK), TK, one), state)


def head_masks(width, heads):
    lane = lax.broadcasted_iota(jnp.int32, (1, width), 1)
    return [(lane // HEAD == h) for h in range(heads)]


def seg_columns(segv_ref, cols, n):
    for t in range(n // 128):
        row = segv_ref[0:1, t * 128:(t + 1) * 128].astype(jnp.float32)
        cols[t * 128:(t + 1) * 128, :] = jnp.broadcast_to(row, (128, 128)).T


def fwd_kernel(n, heads, ranges, segv_ref, q_ref, k_ref, v_ref, o_ref, lse_ref, vt, cols, scores):
    tile = pl.program_id(0)
    width = heads * HEAD

    @pl.when(tile == 0)
    def _():
        seg_columns(segv_ref, cols, n)
        for t in range(n // TK):
            turned = v_ref[t * TK:(t + 1) * TK, :].astype(jnp.float32).T.astype(jnp.bfloat16)
            for h in range(heads):
                vt[h * TALL:h * TALL + HEAD, t * TK:(t + 1) * TK] = turned[h * HEAD:(h + 1) * HEAD]
                vt[h * TALL + HEAD:(h + 1) * TALL, t * TK:(t + 1) * TK] = jnp.ones((TALL - HEAD, TK), jnp.bfloat16)

    q0 = pl.multiple_of(tile * TQ, TQ)
    q = q_ref[...] * jnp.bfloat16(HEAD ** -0.5)
    masks = head_masks(width, heads)
    qm = [jnp.where(m, q, jnp.bfloat16(0)) for m in masks]
    seg_row = segv_ref[0:1, pl.ds(q0, TQ)].astype(jnp.float32)

    def first(k0, size, tops):
        keys = k_ref[pl.ds(k0, size), :]
        col = cols[pl.ds(k0, size), :]
        same = jnp.concatenate([col] * (TQ // 128), axis=1) == seg_row
        out = []
        for h in range(heads):
            s = lax.dot_general(keys, qm[h], NT, preferred_element_type=jnp.float32)
            s = jnp.where(same, s, MASKED)
            scores[h, pl.ds(k0, size), :] = s
            out.append(jnp.maximum(tops[h], jnp.max(s, axis=0, keepdims=True)))
        return tuple(out)

    tops = over_blocks(ranges, tile, first, tuple(jnp.full((1, TQ), MASKED, jnp.float32) for _ in range(heads)))

    def second(k0, size, acc):
        out = []
        for h in range(heads):
            p = jnp.exp(scores[h, pl.ds(k0, size), :] - tops[h]).astype(jnp.bfloat16)
            out.append(acc[h] + jnp.dot(vt[h * TALL:(h + 1) * TALL, pl.ds(k0, size)], p, preferred_element_type=jnp.float32))
        return tuple(out)

    acc = over_blocks(ranges, tile, second, tuple(jnp.zeros((TALL, TQ), jnp.float32) for _ in range(heads)))
    totals = [one[HEAD:HEAD + 1] for one in acc]
    ot = jnp.concatenate([acc[h][:HEAD] / totals[h] for h in range(heads)], axis=0)
    o_ref[...] = ot.T.astype(jnp.bfloat16)
    lse_ref[...] = jnp.concatenate(
        [tops[h] + jnp.log(totals[h]) for h in range(heads)] + [jnp.zeros((8 - heads, TQ), jnp.float32)], axis=0
    )


def attend_forward(ranges, seg, q, k, v):
    n, width = q.shape
    heads = width // HEAD
    whole = pl.BlockSpec(memory_space=pltpu.VMEM)
    return pl.pallas_call(
        functools.partial(fwd_kernel, n, heads),
        grid_spec=pltpu.PrefetchScalarGridSpec(
            num_scalar_prefetch=1,
            grid=(n // TQ,),
            in_specs=[whole, pl.BlockSpec((TQ, width), lambda t, s: (t, 0)), whole, whole],
            out_specs=[pl.BlockSpec((TQ, width), lambda t, s: (t, 0)), pl.BlockSpec((8, TQ), lambda t, s: (0, t))],
            scratch_shapes=[pltpu.VMEM((heads * TALL, n), jnp.bfloat16), pltpu.VMEM((n, 128), jnp.float32), pltpu.VMEM((heads, n, TQ), jnp.float32)],
        ),
        out_shape=[jax.ShapeDtypeStruct((n, width), jnp.bfloat16), jax.ShapeDtypeStruct((8, n), jnp.float32)],
        compiler_params=pltpu.CompilerParams(vmem_limit_bytes=VMEM_BYTES),
        cost_estimate=pl.CostEstimate(flops=4 * heads * n * n * HEAD, bytes_accessed=8 * n * width, transcendentals=heads * n * n // 2),
        name="attend_forward",
    )(ranges, seg, q, k, v)


def bwd_kernel(
    n, heads, ranges, segv_ref, q_ref, k_ref, v_ref, o_ref, do_ref, lse_ref, dq_ref, dk_ref, dv_ref,
    kt, kh, vh, cols, dk_acc, dv_acc,
):
    tile = pl.program_id(0)

    def head_cols(h):
        return slice(h * HEAD, (h + 1) * HEAD)

    @pl.when(tile == 0)
    def _():
        dk_acc[...] = jnp.zeros_like(dk_acc)
        dv_acc[...] = jnp.zeros_like(dv_acc)
        seg_columns(segv_ref, cols, n)
        for h in range(heads):
            kh[h] = k_ref[:, head_cols(h)]
            vh[h] = v_ref[:, head_cols(h)]
        for t in range(n // TK):
            kt[:, t * TK:(t + 1) * TK] = k_ref[t * TK:(t + 1) * TK, :].astype(jnp.float32).T.astype(jnp.bfloat16)

    q0 = pl.multiple_of(tile * TQ, TQ)
    q = q_ref[...] * jnp.bfloat16(HEAD ** -0.5)
    do = do_ref[...]
    seg_row = segv_ref[0:1, pl.ds(q0, TQ)].astype(jnp.float32)
    do_wide = do.astype(jnp.float32)
    products = (do_wide * o_ref[...].astype(jnp.float32)).T
    q_turned = q.astype(jnp.float32).T.astype(jnp.bfloat16)
    do_turned = do_wide.T.astype(jnp.bfloat16)
    lse = lse_ref[...]
    deltas = [jnp.sum(products[head_cols(h)], axis=0, keepdims=True) for h in range(heads)]
    q_heads = [q[:, head_cols(h)] for h in range(heads)]
    do_heads = [do[:, head_cols(h)] for h in range(heads)]

    def body(k0, size, acc):
        where = pl.ds(k0, size)
        same = jnp.concatenate([cols[where, :]] * (TQ // 128), axis=1) == seg_row
        out = []
        for h in range(heads):
            s = jnp.dot(kh[h, where, :], q_turned[head_cols(h)], preferred_element_type=jnp.float32)
            p = jnp.where(same, jnp.exp(s - lse[h:h + 1, :]), 0.0)
            dp = jnp.dot(vh[h, where, :], do_turned[head_cols(h)], preferred_element_type=jnp.float32)
            ds = (p * (dp - deltas[h])).astype(jnp.bfloat16)
            dv_acc[h, where, :] += jnp.dot(p.astype(jnp.bfloat16), do_heads[h], preferred_element_type=jnp.float32)
            dk_acc[h, where, :] += jnp.dot(ds, q_heads[h], preferred_element_type=jnp.float32)
            out.append(acc[h] + jnp.dot(kt[head_cols(h), where], ds, preferred_element_type=jnp.float32))
        return tuple(out)

    acc = over_blocks(ranges, tile, body, tuple(jnp.zeros((HEAD, TQ), jnp.float32) for _ in range(heads)))
    dq_ref[...] = (jnp.concatenate(acc, axis=0).T * HEAD ** -0.5).astype(jnp.bfloat16)

    @pl.when(tile == n // TQ - 1)
    def _():
        for h in range(heads):
            dk_ref[:, head_cols(h)] = dk_acc[h].astype(jnp.bfloat16)
            dv_ref[:, head_cols(h)] = dv_acc[h].astype(jnp.bfloat16)


def attend_backward(ranges, seg, q, k, v, o, do, lse):
    n, width = q.shape
    heads = width // HEAD
    whole = pl.BlockSpec(memory_space=pltpu.VMEM)
    rows = pl.BlockSpec((TQ, width), lambda t, s: (t, 0))
    return pl.pallas_call(
        functools.partial(bwd_kernel, n, heads),
        grid_spec=pltpu.PrefetchScalarGridSpec(
            num_scalar_prefetch=1,
            grid=(n // TQ,),
            in_specs=[whole, rows, whole, whole, rows, rows, pl.BlockSpec((8, TQ), lambda t, s: (0, t))],
            out_specs=[rows, whole, whole],
            scratch_shapes=[pltpu.VMEM((width, n), jnp.bfloat16)] + [pltpu.VMEM((heads, n, HEAD), jnp.bfloat16)] * 2
            + [pltpu.VMEM((n, 128), jnp.float32)] + [pltpu.VMEM((heads, n, HEAD), jnp.float32)] * 2,
        ),
        out_shape=[jax.ShapeDtypeStruct((n, width), jnp.bfloat16)] * 3,
        compiler_params=pltpu.CompilerParams(vmem_limit_bytes=VMEM_BYTES),
        cost_estimate=pl.CostEstimate(flops=10 * heads * n * n * HEAD, bytes_accessed=16 * n * width, transcendentals=heads * n * n // 2),
        name="attend_backward",
    )(ranges, seg, q, k, v, o, do, lse)


MESH_ID = pl.DeviceIdType.MESH
PARTS = 4
VMEM_BYTES = 60 << 20
MLP_CHUNKS = 6
QKV_CHUNKS = (128,) * 6


def remote(src, dst, send, recv, device):
    return pltpu.make_async_remote_copy(
        src_ref=src, dst_ref=dst, send_sem=send, recv_sem=recv, device_id=device, device_id_type=MESH_ID
    )


def greet(devices):
    barrier = pltpu.get_barrier_semaphore()
    for device in devices:
        pl.semaphore_signal(barrier, inc=1, device_id=device, device_id_type=MESH_ID)
    pl.semaphore_wait(barrier, len(devices))


def norm_unit(values):
    average = jnp.mean(values, axis=-1, keepdims=True)
    centered = values - average
    variance = jnp.mean(centered * centered, axis=-1, keepdims=True)
    inverse = lax.rsqrt(variance + epsilon)
    return centered * inverse, inverse


def sum_stages(rows, chunks, dp_count):
    stages = dp_count.bit_length() - 1
    return stages if dp_count == 1 << stages and rows % (16 * chunks * dp_count) == 0 else 0


def sum_scratch(rows, width, chunks, stages):
    dma = pltpu.SemaphoreType.DMA
    return [
        pltpu.VMEM((rows, width), jnp.bfloat16), pltpu.VMEM((rows, width), jnp.bfloat16),
        dma((chunks, max(1, 2 * stages))), dma((chunks, max(1, 2 * stages))),
    ]


def left_bit(k):
    return k % 2


def packed(k, chunks):
    return k // 2 if k % 2 == 0 else (chunks + 1) // 2 + k // 2


def sum_steps(stages, chunks, acc, came, send, recv, out, half=False):
    dp, mp = lax.axis_index("dp"), lax.axis_index("mp")
    chunk = acc.shape[0] // chunks

    def bit(s):
        return lax.rem(dp // (1 << s), 2)

    def held(k, s):
        start = k * chunk
        for j in range(s):
            start = start + bit(j) * (chunk >> (j + 1))
        return start

    def span(start, size):
        return pl.ds(pl.multiple_of(start, 16), size)

    def placed(k, start):
        if not half:
            return start
        return packed(k, chunks) * (chunk // 2) + bit(1 - left_bit(k)) * (chunk // 4) + start - held(k, 2)

    def halve(k, s):
        size = chunk >> (s + 1)
        return remote(
            acc.at[span(held(k, s) + (1 - bit(s)) * size, size)],
            came.at[span(k * chunk + chunk - (chunk >> s), size)],
            send.at[k, s], recv.at[k, s], (dp ^ (1 << s), mp),
        )

    def double(k, s, mine=True):
        if half and s == 1:
            s = 1 - left_bit(k)
            place = bit(s) if mine else 1 - bit(s)
            rows = out.at[span(packed(k, chunks) * (chunk // 2) + place * (chunk // 4), chunk // 4)]
            return remote(rows, rows, send.at[k, stages + 1], recv.at[k, stages + 1], (dp ^ (1 << s), mp))
        size = chunk >> (s + 1)
        start = held(k, s + 1) if mine else held(k, s) + (1 - bit(s)) * size
        rows = out.at[span(placed(k, start), size)]
        return remote(rows, rows, send.at[k, stages + s], recv.at[k, stages + s], (dp ^ (1 << s), mp))

    final = 1 if half else 0

    def step(k, i):
        if i == 0:
            halve(k, 0).start()
        elif i <= stages:
            halve(k, i - 1).wait_recv()
            size = chunk >> i
            rows = span(held(k, i), size)
            total = acc[rows, :].astype(jnp.float32) + came[span(k * chunk + chunk - (chunk >> (i - 1)), size), :].astype(jnp.float32)
            if i < stages:
                acc[rows, :] = total.astype(jnp.bfloat16)
                halve(k, i).start()
            else:
                out[span(placed(k, held(k, i)), size), :] = total.astype(jnp.bfloat16)
                double(k, stages - 1).start()
        elif 2 * stages - i >= final:
            s = 2 * stages - i
            double(k, s, False).wait_recv()
            if s > final:
                double(k, s - 1).start()

    def drain():
        for k in range(chunks):
            for s in range(stages):
                halve(k, s).wait_send()
                if s >= final:
                    double(k, s).wait_send()

    return step, drain


def columns_of(row):
    return jnp.concatenate(
        [jnp.broadcast_to(row[:, t * 128:(t + 1) * 128], (128, 128)).T for t in range(row.shape[1] // 128)], axis=0
    )


def project_kernel(
    dp_count, tokens_hbm, gain_hbm, w_hbm, cot_ref, owner_hbm, seg_hbm, rows_hbm, q_hbm, k_hbm, v_hbm, grad_hbm, place_hbm, ranges_ref,
    tokens_ref, gain_ref, w_ref, owner_ref, seg_ref, rows_ref, q_ref, k_ref, v_ref, grad_ref, place_ref, load_sem, store_sem, out_sem, returned_ref, across_send, across_recv, pair_send, pair_recv, pass_send, pass_recv, slot_send, slot_recv, self_sem,
):
    load_tokens, load_gain, load_w, load_owner, load_seg = loads = local_copies(
        ((tokens_hbm, tokens_ref), (gain_hbm, gain_ref), (w_hbm, w_ref), (owner_hbm, owner_ref), (seg_hbm, seg_ref)), load_sem
    )
    for load in loads:
        load.start()
    stores = local_copies(
        ((q_ref, q_hbm), (k_ref, k_hbm), (v_ref, v_hbm), (place_ref, place_hbm), (grad_ref, grad_hbm)), out_sem
    )
    dp, mp = lax.axis_index("dp"), lax.axis_index("mp")
    pair, across, far = mp ^ 1, mp ^ 2, mp ^ 3
    own = tokens_ref.shape[0]
    part = own // PARTS
    greet([(dp, pair), (dp, across)] + [(lax.rem(dp + k, dp_count), mp) for k in range(1, dp_count)])

    def spot(owner, c, size):
        return pl.ds(pl.multiple_of(owner * own + c * size, size), size)

    def gather_copy(c, owner, device, send, recv):
        rows = rows_ref.at[spot(owner, c, part)]
        return remote(rows, rows, send.at[c], recv.at[c], device)

    def slot_copy(k):
        other = lax.rem(dp + k, dp_count)
        return remote(cot_ref.at[other], returned_ref.at[dp], slot_send.at[k], slot_recv.at[k], (other, mp))

    def store(i, owner):
        rows = pl.ds(pl.multiple_of(owner * own, own), own)
        return pltpu.make_async_copy(rows_ref.at[rows], rows_hbm.at[rows], store_sem.at[i])

    for k in sorted(range(1, dp_count), key=lambda k: -min(k, dp_count - k)):
        slot_copy(k).start()
    self_copy = pltpu.make_async_copy(cot_ref.at[dp], returned_ref.at[dp], self_sem)
    self_copy.start()
    load_tokens.wait()
    load_gain.wait()
    for c in range(PARTS):
        values = tokens_ref[c * part:(c + 1) * part, :].astype(jnp.float32)
        unit, _ = norm_unit(values)
        rows_ref[spot(mp, c, part), :] = (unit * gain_ref[...].reshape(1, -1)).astype(jnp.bfloat16)
        gather_copy(c, mp, (dp, across), across_send, across_recv).start()
        gather_copy(c, mp, (dp, pair), pair_send, pair_recv).start()
    def product(owner, half):
        where = spot(owner, half, own // 2)
        rows = rows_ref[where, :]
        for p, out in enumerate((q_ref, k_ref, v_ref)):
            out[where, :] = lax.dot_general(rows, w_ref[p], NT, preferred_element_type=jnp.float32).astype(jnp.bfloat16)

    def both(owner):
        def step(half, _):
            product(owner, half)
            return 0
        lax.fori_loop(0, 2, step, 0)

    load_w.wait()
    load_owner.wait()
    load_seg.wait()
    both(mp)
    ranges_ref[...] = key_ranges(seg_ref[...], ranges_ref.shape[0])
    store(0, mp).start()
    capacity = cot_ref.shape[1]
    owner_row = owner_ref[...].astype(jnp.float32)
    owner_col = columns_of(owner_row)
    earlier = lax.broadcasted_iota(jnp.int32, (own, own), 0) < lax.broadcasted_iota(jnp.int32, (own, own), 1)
    same = jnp.concatenate([owner_col] * (own // 128), axis=1) == owner_row
    rank_row = jnp.sum(jnp.where(same & earlier, 1.0, 0.0), axis=0, keepdims=True)
    slot_row = owner_row * capacity + rank_row
    slots = place_ref.shape[0]
    place_ref[...] = jnp.where(
        lax.broadcasted_iota(jnp.int32, (slots, own), 0).astype(jnp.float32) == slot_row, 1.0, 0.0
    ).astype(jnp.bfloat16)
    stores[3].start()
    for c in range(PARTS):
        gather_copy(c, pair, (dp, pair), pair_send, pair_recv).wait_recv()
    both(pair)
    store(1, pair).start()
    for half in range(2):
        for c in range(half * PARTS // 2, (half + 1) * PARTS // 2):
            gather_copy(c, across, (dp, across), across_send, across_recv).wait_recv()
            gather_copy(c, across, (dp, pair), pass_send, pass_recv).start()
        product(across, half)
    store(2, across).start()
    for half in range(2):
        for c in range(half * PARTS // 2, (half + 1) * PARTS // 2):
            gather_copy(c, far, (dp, pair), pass_send, pass_recv).wait_recv()
        product(far, half)
    store(3, far).start()
    for out in stores[:3]:
        out.start()
    for c in range(PARTS):
        gather_copy(c, mp, (dp, across), across_send, across_recv).wait_send()
        gather_copy(c, mp, (dp, pair), pair_send, pair_recv).wait_send()
        gather_copy(c, across, (dp, pair), pass_send, pass_recv).wait_send()
    self_copy.wait()
    for k in range(1, dp_count):
        slot_copy(k).wait_send()
        other = lax.rem(dp + dp_count - k, dp_count)
        remote(cot_ref.at[dp], returned_ref.at[other], slot_send.at[k], slot_recv.at[k], (other, mp)).wait_recv()
    for i, owner in enumerate((mp, pair, across, far)):
        store(i, owner).wait()
    if capacity % 16 == 0:
        back = returned_ref[...].reshape(slots, cot_ref.shape[2])
        grad_ref[...] = lax.dot_general(place_ref[...], back, TN, preferred_element_type=jnp.float32).astype(jnp.bfloat16)
    else:
        rank_col = columns_of(rank_row)[:, :capacity]
        lane = lax.broadcasted_iota(jnp.int32, (own, capacity), 1).astype(jnp.float32)

        def take(d, total):
            pick = (owner_col[:, :capacity] == d.astype(jnp.float32)) & (rank_col == lane)
            pick = jnp.where(pick, 1.0, 0.0).astype(jnp.bfloat16)
            return total + jnp.dot(pick, returned_ref[d], preferred_element_type=jnp.float32)
        grad_ref[...] = lax.fori_loop(0, dp_count, take, jnp.zeros(grad_ref.shape, jnp.float32)).astype(jnp.bfloat16)
    stores[4].start()
    for out in stores:
        out.wait()


def project(tokens, gain, w_qkv, cot, owners, seg):
    own, width = tokens.shape
    dp_count = cot.shape[0]
    total = own * 4
    cols = w_qkv.shape[1]
    vmem = pl.BlockSpec(memory_space=pltpu.VMEM)
    hbm = pl.BlockSpec(memory_space=pltpu.HBM)
    dma = pltpu.SemaphoreType.DMA
    return pl.pallas_call(
        functools.partial(project_kernel, dp_count),
        out_shape=[jax.ShapeDtypeStruct((total, width), jnp.bfloat16)]
        + [jax.ShapeDtypeStruct((total, cols), jnp.bfloat16)] * 3
        + [jax.ShapeDtypeStruct((own, width), jnp.bfloat16), jax.ShapeDtypeStruct((dp_count * cot.shape[1], own), jnp.bfloat16)]
        + [jax.ShapeDtypeStruct((seg.shape[1] // TQ, 128), jnp.int32)],
        in_specs=[hbm] * 6,
        out_specs=[hbm] * 6 + [vmem],
        scratch_shapes=[pltpu.VMEM(one.shape, one.dtype) for one in (tokens, gain, w_qkv, owners, seg)]
        + [pltpu.VMEM((total, width), jnp.bfloat16)] + [pltpu.VMEM((total, cols), jnp.bfloat16)] * 3
        + [pltpu.VMEM((own, width), jnp.bfloat16), pltpu.VMEM((dp_count * cot.shape[1], own), jnp.bfloat16)]
        + [dma((5,)), dma((4,)), dma((5,)), pltpu.VMEM(cot.shape, cot.dtype)] + [dma((PARTS,))] * 6 + [dma((dp_count,))] * 2 + [dma],
        compiler_params=pltpu.CompilerParams(collective_id=1, has_side_effects=True, vmem_limit_bytes=VMEM_BYTES),
        cost_estimate=pl.CostEstimate(flops=6 * total * width * cols, bytes_accessed=10 * total * width, transcendentals=0),
        name="project",
    )(tokens, gain, w_qkv, cot, owners, seg)


def gelu_and_slope(values):
    cumulative = 0.5 * (1.0 + lax.erf(values * 0.7071067811865476))
    density = jnp.exp(-0.5 * values * values) * 0.3989422804014327
    return values * cumulative, cumulative + values * density


def middle_kernel(
    stages, merged_hbm, w_out_hbm, tokens_hbm, gain_hbm, w_up_hbm, w_down_hbm, grad_own_hbm, grad_across_hbm, place_hbm,
    back_rows_hbm, grad_merged_hbm, grad_residual_hbm, outgoing_hbm, first_hbm, second_hbm, gain_part_hbm, d_out_hbm,
    merged_ref, w_out_ref, tokens_ref, gain_ref, gain_part_ref, d_out_ref, w_up_ref, w_down_ref, grad_own_ref, grad_across_ref, place_ref,
    back_rows_ref, grad_merged_ref, grad_residual_ref, outgoing_ref, d_mlp_ref, load_sem, store_sem,
    mlp_rows, grad_rows, active, grad_pre, residual, mine, bufs,
    sum_send, sum_recv, row_send, row_recv, grad_send, grad_recv, self_sem, acc, came, dp_send, dp_recv,
):
    first_rows = first_hbm.shape[0]
    loads = local_copies(
        (
            (merged_hbm, merged_ref), (w_out_hbm, w_out_ref), (tokens_hbm, tokens_ref), (grad_own_hbm, grad_own_ref),
            (grad_across_hbm, grad_across_ref), (w_up_hbm, w_up_ref), (w_down_hbm, w_down_ref), (place_hbm, place_ref),
            (gain_hbm, gain_ref),
        ),
        load_sem,
    )
    for load in loads:
        load.start()
    stores = local_copies(
        (
            (back_rows_ref, back_rows_hbm), (grad_merged_ref, grad_merged_hbm), (grad_residual_ref, grad_residual_hbm),
            (outgoing_ref, outgoing_hbm), (d_mlp_ref.at[0:first_rows], first_hbm), (d_mlp_ref.at[first_rows:], second_hbm),
            (gain_part_ref, gain_part_hbm), (d_out_ref, d_out_hbm),
        ),
        store_sem,
    )
    low, full = jnp.bfloat16, jnp.float32
    dp, mp = lax.axis_index("dp"), lax.axis_index("mp")
    pair, across, far = mp ^ 1, mp ^ 2, mp ^ 3
    own, width = tokens_ref.shape
    part = own // PARTS
    to_pair, to_across = (dp, pair), (dp, across)
    greet([to_pair, to_across] + [(dp ^ (1 << j), mp) for j in range(stages)])
    add_step, add_drain = sum_steps(stages, MLP_CHUNKS, acc, came, dp_send, dp_recv, d_mlp_ref, half=True)
    target = acc if stages else d_mlp_ref

    def spot(owner, c=None):
        if c is None:
            return pl.ds(pl.multiple_of(owner * own, own), own)
        return pl.ds(pl.multiple_of(owner * own + c * part, part), part)

    def piece(c):
        return pl.ds(pl.multiple_of(c * part, part), part)

    def grad_copy(i, owner, src):
        return remote(src, grad_rows.at[spot(owner)], grad_send.at[i], grad_recv.at[i], to_pair)

    grad_loads = [
        pltpu.make_async_copy(grad_own_ref, grad_rows.at[spot(mp)], self_sem.at[0]),
        pltpu.make_async_copy(grad_across_ref, grad_rows.at[spot(across)], self_sem.at[1]),
    ]

    FAR, ACROSS, PAIR = 0, 1, 2

    def sum_copy(which, kind, c):
        src, dst = bufs.at[which, 0, kind, piece(c)], bufs.at[which, 1, kind, piece(c)]
        return remote(src, dst, sum_send.at[which, kind, c], sum_recv.at[which, kind, c], to_across if kind == ACROSS else to_pair)

    def arrived(which, kind, c):
        sum_copy(which, kind, c).wait_recv()
        return bufs[which, 1, kind, piece(c), :].astype(full)

    def ship(which, kind, c, values):
        bufs[which, 0, kind, piece(c), :] = values.astype(low)
        sum_copy(which, kind, c).start()

    def row_copy(which, kind, c, owner, ref):
        rows = ref.at[spot(owner, c)]
        return remote(rows, rows, row_send.at[which, kind, c], row_recv.at[which, kind, c], to_across if kind == 0 else to_pair)

    def each(count, body):
        def step(i, _):
            body(i)
            return 0
        lax.fori_loop(0, count, step, 0)

    def out_part(owner):
        return jnp.dot(merged_ref[spot(owner), :], w_out_ref[...], preferred_element_type=full)

    loads[0].wait()
    loads[1].wait()
    bufs[0, 0, FAR] = out_part(far).astype(low)
    each(PARTS, lambda c: sum_copy(0, FAR, c).start())
    mine[0] = out_part(across)

    def pass_across(c):
        ship(0, ACROSS, c, mine[0, piece(c), :] + arrived(0, FAR, c))
    each(PARTS, pass_across)
    bufs[0, 0, PAIR] = out_part(pair).astype(low)
    each(PARTS, lambda c: sum_copy(0, PAIR, c).start())
    for load in loads[2:5]:
        load.wait()
    for copy in grad_loads:
        copy.start()
    grad_copy(0, mp, grad_own_ref).start()
    grad_copy(1, across, grad_across_ref).start()
    mine[0] = out_part(mp) + tokens_ref[...].astype(full)
    for copy in grad_loads:
        copy.wait()
    grad_copy(0, pair, grad_own_ref).wait_recv()
    grad_copy(1, far, grad_across_ref).wait_recv()

    for load in loads[5:]:
        load.wait()
    blocks = w_up_ref.shape[1] // 256
    both = 2 * part

    def mlp(first, second, c):
        rows = jnp.concatenate([mlp_rows[spot(first, c), :], mlp_rows[spot(second, c), :]], axis=0)
        grads = jnp.concatenate([grad_rows[spot(first, c), :], grad_rows[spot(second, c), :]], axis=0)

        def block(b):
            cols = pl.ds(pl.multiple_of(b * 256, 256), 256)
            pre = jnp.dot(rows, w_up_ref[:, cols], preferred_element_type=full)
            value, slope = gelu_and_slope(pre)
            value = value.astype(low)
            active[spot(first, c), cols] = value[:part]
            active[spot(second, c), cols] = value[part:]
            back = (jnp.dot(grads, w_down_ref[:, cols], preferred_element_type=full) * slope).astype(low)
            grad_pre[spot(first, c), cols] = back[:part]
            grad_pre[spot(second, c), cols] = back[part:]
        each(blocks, block)
        back = jnp.concatenate([grad_pre[spot(first, c), :], grad_pre[spot(second, c), :]], axis=0)
        return lax.dot_general(back, w_up_ref[...], NT, preferred_element_type=full)

    def near(c):
        values = mine[0, piece(c), :] + arrived(0, PAIR, c) + arrived(0, ACROSS, c)
        residual[piece(c), :] = values
        unit, _ = norm_unit(values)
        mlp_rows[spot(mp, c), :] = (unit * gain_ref[...].reshape(1, -1)).astype(low)
        row_copy(0, 0, c, mp, mlp_rows).start()
        row_copy(0, 1, c, mp, mlp_rows).start()
        row_copy(0, 1, c, pair, mlp_rows).wait_recv()
        got = mlp(mp, pair, c)
        mine[1, piece(c), :] = got[:part]
        ship(1, PAIR, c, got[part:])
    each(PARTS, near)

    def distant(c):
        row_copy(0, 0, c, across, mlp_rows).wait_recv()
        row_copy(0, 2, c, across, mlp_rows).start()
        row_copy(0, 2, c, far, mlp_rows).wait_recv()
        got = mlp(far, across, c)
        ship(1, FAR, c, got[:part])
        ship(1, ACROSS, c, got[part:] + arrived(1, FAR, c))
    each(PARTS, distant)

    size = width // MLP_CHUNKS
    for b in range(3):
        cols = slice(b * 256, (b + 1) * 256)
        up = lax.dot_general(mlp_rows[:, cols], grad_pre[...], TN, preferred_element_type=full)
        gain_col = jnp.sum(up * w_up_ref[cols, :].astype(full), axis=1, keepdims=True)
        gain_part_ref[:, cols] = jnp.broadcast_to(gain_col, (256, 128)).T[0:8] / gain_ref[cols].reshape(1, -1)
        up = up.astype(low)
        down = lax.dot_general(grad_rows[:, cols], active[...], TN, preferred_element_type=full).astype(low)
        for j in range(256 // size):
            k = b * (256 // size) + j
            target[2 * k * size:(2 * k + 1) * size, :] = up[j * size:(j + 1) * size]
            target[(2 * k + 1) * size:(2 * k + 2) * size, :] = down[j * size:(j + 1) * size]
            if stages:
                add_step(k, 0)

    def add(*steps):
        if stages:
            for k, i in steps:
                add_step(k, i)

    def down_part(owner):
        return lax.dot_general(active[spot(owner), :], w_down_ref[...], NT, preferred_element_type=full)

    bufs[2, 0, FAR] = down_part(far).astype(low)
    each(PARTS, lambda c: sum_copy(2, FAR, c).start())
    bufs[2, 0, PAIR] = down_part(pair).astype(low)
    each(PARTS, lambda c: sum_copy(2, PAIR, c).start())

    def back_norm(c):
        grad = mine[1, piece(c), :] + arrived(1, PAIR, c) + arrived(1, ACROSS, c)
        unit, inverse = norm_unit(residual[piece(c), :])
        scaled = grad * gain_ref[...].reshape(1, -1)
        first_mean = jnp.mean(scaled, axis=-1, keepdims=True)
        second_mean = jnp.mean(scaled * unit, axis=-1, keepdims=True)
        total = inverse * (scaled - first_mean - unit * second_mean) + grad_own_ref[piece(c), :].astype(full)
        grad_residual_ref[piece(c), :] = total
        back_rows_ref[spot(mp, c), :] = total.astype(low)
        row_copy(1, 0, c, mp, back_rows_ref).start()
        row_copy(1, 1, c, mp, back_rows_ref).start()
    def tick(t):
        add(*[(t - i, i) for i in range(1, 2 * stages + 1) if 0 <= t - i < MLP_CHUNKS])

    each(2, back_norm)
    tick(1)
    each(1, lambda c: back_norm(c + 2))
    tick(2)
    each(1, lambda c: back_norm(c + 3))

    mine[1] = down_part(across)

    def pass_output(c):
        ship(2, ACROSS, c, mine[1, piece(c), :] + arrived(2, FAR, c))
    each(PARTS, pass_output)
    tick(3)
    mine[0] = residual[...] + down_part(mp)

    def merged_part(owner):
        grad_merged_ref[spot(owner), :] = lax.dot_general(
            back_rows_ref[spot(owner), :], w_out_ref[...], NT, preferred_element_type=full
        ).astype(low)

    merged_part(mp)
    each(PARTS, lambda c: row_copy(1, 1, c, pair, back_rows_ref).wait_recv())
    merged_part(pair)

    def hand_on(c):
        row_copy(1, 0, c, across, back_rows_ref).wait_recv()
        row_copy(1, 2, c, across, back_rows_ref).start()
    for c in range(PARTS):
        each(1, lambda i: hand_on(i + c))
        tick(4 + c)
    tick(8)
    merged_part(across)
    each(PARTS, lambda c: row_copy(1, 2, c, far, back_rows_ref).wait_recv())
    tick(9)
    merged_part(far)
    stores[0].start()
    stores[1].start()
    stores[2].start()
    d_out_ref[...] = lax.dot_general(merged_ref[...], back_rows_ref[...], TN, preferred_element_type=full).astype(low)
    stores[6].start()
    stores[7].start()

    tick(10)

    def finish(c):
        mine[0, piece(c), :] = mine[0, piece(c), :] + arrived(2, PAIR, c) + arrived(2, ACROSS, c)
    for c in range(PARTS):
        each(1, lambda i: finish(i + c))
    stores[4].start()
    stores[5].start()
    outgoing_ref[...] = jnp.dot(place_ref[...], mine[0].astype(low), preferred_element_type=full).astype(low)
    stores[3].start()
    if stages:
        add_drain()
    for store in stores:
        store.wait()

    def drain(c):
        for which in range(3):
            for kind in range(3):
                sum_copy(which, kind, c).wait_send()
        for which, ref in ((0, mlp_rows), (1, back_rows_ref)):
            row_copy(which, 0, c, mp, ref).wait_send()
            row_copy(which, 1, c, mp, ref).wait_send()
            row_copy(which, 2, c, across, ref).wait_send()
    each(PARTS, drain)
    grad_copy(0, mp, grad_own_ref).wait_send()
    grad_copy(1, across, grad_across_ref).wait_send()


def middle(dp_count, merged, w_out, tokens, gain, w_up, w_down, grad_own, grad_across, place):
    stages = sum_stages(2 * w_up.shape[0], MLP_CHUNKS, dp_count)
    d_rows = w_up.shape[0] * (1 if stages else 2)
    total, cols = merged.shape
    own, width = tokens.shape
    hidden = w_up.shape[1]
    slots = place.shape[0]
    low, full = jnp.bfloat16, jnp.float32
    vmem = pl.BlockSpec(memory_space=pltpu.VMEM)
    hbm = pl.BlockSpec(memory_space=pl.ANY)
    dma = pltpu.SemaphoreType.DMA
    shape, room = jax.ShapeDtypeStruct, pltpu.VMEM
    return pl.pallas_call(
        functools.partial(middle_kernel, stages),
        out_shape=[
            shape((total, width), low), shape((total, cols), low), shape((own, width), full), shape((slots, width), low),
            shape((d_rows // 2, hidden), low), shape((d_rows // 2, hidden), low), shape((8, width), full), shape((cols, width), low),
        ],
        in_specs=[hbm] * 9,
        out_specs=[hbm] * 8,
        scratch_shapes=[
            room((total, cols), low), room(w_out.shape, low), room((own, width), low), room(gain.shape, full),
            room((8, width), full), room((cols, width), low), room(w_up.shape, low),
            room(w_down.shape, low), room((own, width), low), room((own, width), low), room(place.shape, low),
            room((total, width), low), room((total, cols), low), room((own, width), full), room((slots, width), low),
            room((d_rows, hidden), low), dma((9,)), dma((8,)),
            room((total, width), low), room((total, width), low),
            room((total, hidden), low), room((total, hidden), low),
            room((own, width), full), room((2, own, width), full),
            room((3, 2, 3, own, width), low),
            dma((3, 3, PARTS)), dma((3, 3, PARTS)), dma((2, 3, PARTS)), dma((2, 3, PARTS)), dma((2,)), dma((2,)), dma((2,)),
        ]
        + sum_scratch(2 * width, hidden, MLP_CHUNKS, stages),
        compiler_params=pltpu.CompilerParams(collective_id=2, has_side_effects=True, vmem_limit_bytes=VMEM_BYTES),
        cost_estimate=pl.CostEstimate(flops=16 * total * width * hidden, bytes_accessed=20 * total * width, transcendentals=0),
        name="middle",
    )(merged, w_out, tokens, gain, w_up, w_down, grad_own, grad_across, place)


def direct_fits(rows, chunks, dp_count):
    return dp_count % 2 == 0 and rows == sum(chunks) and all(one % (16 * dp_count) == 0 for one in chunks)


def direct_steps(dp_count, chunks, acc, came, send, recv, out, out_hbm, keep_sem):
    dp, mp = lax.axis_index("dp"), lax.axis_index("mp")
    group = dp_count // 2
    starts = [sum(chunks[:k]) for k in range(len(chunks))]
    halves = [one // 2 for one in chunks]
    slots = [one // dp_count for one in chunks]
    y, z = lax.rem(dp, 2), dp // 2
    beside = (dp + 1 - 2 * y, mp)
    others = sorted(range(1, group), key=lambda j: -min(j, group - j))

    def span(start, size):
        return pl.ds(pl.multiple_of(start, 16), size)

    def low(k, side, g=0):
        return starts[k] + side * halves[k] + g * slots[k]

    def member(j):
        return lax.rem(z + j, group)

    def slot_of(k, j):
        return span(starts[k] + halves[k] + (j - 1) * slots[k], slots[k])

    def halve(k):
        return remote(acc.at[span(low(k, 1 - y), halves[k])], came.at[span(starts[k], halves[k])], send.at[k, 0], recv.at[k, 0], beside)

    def scatter(k, j):
        piece = acc.at[span(low(k, y, member(j)), slots[k])]
        return remote(piece, came.at[slot_of(k, j)], send.at[k, j], recv.at[k, j], (y + 2 * member(j), mp))

    def gather(k, j, mine=True):
        rows = out.at[span(low(k, y, z if mine else member(group - j)), slots[k])]
        return remote(rows, rows, send.at[k, group + j - 1], recv.at[k, group + j - 1], (y + 2 * member(j), mp))

    def double(k, mine=True):
        rows = span(low(k, y if mine else 1 - y), halves[k])
        return remote(out.at[rows], out_hbm.at[rows], send.at[k, 2 * group - 1], recv.at[k, 2 * group - 1], beside)

    def keep(k):
        rows = span(low(k, y), halves[k])
        return pltpu.make_async_copy(out.at[rows], out_hbm.at[rows], keep_sem.at[k])

    def step(k, i):
        if i == 0:
            halve(k).start()
        elif i == 1:
            halve(k).wait_recv()
            rows = span(low(k, y), halves[k])
            total = acc[rows, :].astype(jnp.float32) + came[span(starts[k], halves[k]), :].astype(jnp.float32)
            acc[rows, :] = total.astype(jnp.bfloat16)
            for j in others:
                scatter(k, j).start()
        elif i == 2:
            rows = span(low(k, y, z), slots[k])
            total = acc[rows, :].astype(jnp.float32)
            for j in others:
                scatter(k, j).wait_recv()
                total = total + came[slot_of(k, j), :].astype(jnp.float32)
            out[rows, :] = total.astype(jnp.bfloat16)
            for j in others:
                gather(k, j).start()
        elif i == 3:
            for j in others:
                gather(k, j, False).wait_recv()
            double(k).start()
            keep(k).start()
        else:
            double(k, False).wait_recv()

    def drain():
        for k in range(len(chunks)):
            halve(k).wait_send()
            for j in others:
                scatter(k, j).wait_send()
                gather(k, j).wait_send()
            double(k).wait_send()
            keep(k).wait()

    return step, drain


def last_kernel(
    dp_count, fits, dq_hbm, dk_hbm, dv_hbm, w_hbm, rows_hbm, grad_residual_hbm, tokens_hbm, gain_hbm, gain_part_hbm, d_out_hbm,
    grad_tokens_hbm, d_sum_hbm, gains_hbm,
    dq_ref, dk_ref, dv_ref, w_ref, rows_ref, grad_residual_ref, tokens_ref, gain_ref, gain_part_ref, d_out_ref,
    grad_tokens_ref, gains_ref, load_sem, store_sem, mine, bufs, gain_dp, gain_mp,
    sum_send, sum_recv, dp_gain_send, dp_gain_recv, mp_gain_send, mp_gain_recv, acc, came, out, dp_send, dp_recv, keep_sem,
):
    loads = local_copies(
        (
            (d_out_hbm, d_out_ref), (dq_hbm, dq_ref), (rows_hbm, rows_ref), (w_hbm, w_ref), (dk_hbm, dk_ref), (dv_hbm, dv_ref),
            (gain_hbm, gain_ref), (gain_part_hbm, gain_part_ref), (grad_residual_hbm, grad_residual_ref), (tokens_hbm, tokens_ref),
        ),
        load_sem,
    )
    for load in loads:
        load.start()
    store_tokens, store_gains = local_copies(((grad_tokens_ref, grad_tokens_hbm), (gains_ref, gains_hbm)), store_sem)
    low, full = jnp.bfloat16, jnp.float32
    dp, mp = lax.axis_index("dp"), lax.axis_index("mp")
    pair, across, far = mp ^ 1, mp ^ 2, mp ^ 3
    own, width = tokens_ref.shape
    part = own // PARTS
    cols = dq_ref.shape[1]
    to_pair, to_across = (dp, pair), (dp, across)
    greet([to_pair, to_across, (dp, far)] + [(lax.rem(dp + k, dp_count), mp) for k in range(1, dp_count)])
    add_step, add_drain = direct_steps(dp_count, QKV_CHUNKS, acc, came, dp_send, dp_recv, out, d_sum_hbm, keep_sem)
    FAR, ACROSS, PAIR = 0, 1, 2

    def add(*steps):
        if fits:
            for k, i in steps:
                add_step(k, i)

    def piece(c):
        return pl.ds(pl.multiple_of(c * part, part), part)

    def each(count, body):
        def step(i, _):
            body(i)
            return 0
        lax.fori_loop(0, count, step, 0)

    def sum_copy(kind, c):
        src, dst = bufs.at[0, kind, piece(c)], bufs.at[1, kind, piece(c)]
        return remote(src, dst, sum_send.at[kind, c], sum_recv.at[kind, c], to_across if kind == ACROSS else to_pair)

    def arrived(kind, c):
        sum_copy(kind, c).wait_recv()
        return bufs[1, kind, piece(c), :].astype(full)

    def in_part(owner):
        where = pl.ds(pl.multiple_of(owner * own, own), own)
        total = jnp.dot(dq_ref[where, :], w_ref[0], preferred_element_type=full)
        total = total + jnp.dot(dk_ref[where, :], w_ref[1], preferred_element_type=full)
        return total + jnp.dot(dv_ref[where, :], w_ref[2], preferred_element_type=full)

    ends = [sum(QKV_CHUNKS[:k + 1]) for k in range(len(QKV_CHUNKS))]

    def ready(low_row, high_row):
        add(*[(k, 0) for k, end in enumerate(ends) if low_row < end <= high_row])

    def weight_grad(p, ref):
        grad = lax.dot_general(ref[...], rows_ref[...], TN, preferred_element_type=full)
        acc[(p + 1) * cols:(p + 2) * cols, :] = grad.astype(low)
        ready((p + 1) * cols, (p + 2) * cols)
        return jnp.sum(grad * w_ref[p].astype(full), axis=0, keepdims=True)

    count = len(QKV_CHUNKS)

    def tick(t):
        add(*[(t - i, i) for i in range(1, 5) if 0 <= t - i < count])

    loads[0].wait()
    acc[0:cols, :] = d_out_ref[...]
    ready(0, cols)
    for load in loads[1:4]:
        load.wait()
    gain_row = weight_grad(0, dq_ref)
    for load in loads[4:]:
        load.wait()
    bufs[0, FAR] = in_part(far).astype(low)
    each(PARTS, lambda c: sum_copy(FAR, c).start())
    tick(1)
    gain_row = gain_row + weight_grad(1, dk_ref)
    mine[...] = in_part(across)

    def pass_across(c):
        bufs[0, ACROSS, piece(c), :] = (mine[piece(c), :] + arrived(FAR, c)).astype(low)
        sum_copy(ACROSS, c).start()
    each(PARTS, pass_across)
    tick(2)
    gain_row = gain_row + weight_grad(2, dv_ref)
    tick(3)

    row = lax.broadcasted_iota(jnp.int32, (8, width), 0)
    gain_dp[dp] = jnp.where(row == 0, gain_part_ref[...], jnp.where(row == 1, gain_row / gain_ref[...].reshape(1, -1), 0.0))

    def gain_over_dp(k, owner):
        return remote(gain_dp.at[owner], gain_dp.at[owner], dp_gain_send.at[k], dp_gain_recv.at[k], (lax.rem(dp + k, dp_count), mp))

    def gain_over_mp(i, owner):
        other = (pair, across, far)[i]
        return remote(gain_mp.at[owner], gain_mp.at[owner], mp_gain_send.at[i], mp_gain_recv.at[i], (dp, other))

    for k in range(1, dp_count):
        gain_over_dp(k, dp).start()

    def turn_gains():
        for k in range(1, dp_count):
            gain_over_dp(k, lax.rem(dp + dp_count - k, dp_count)).wait_recv()
        total = gain_dp[0]
        for k in range(1, dp_count):
            total = total + gain_dp[k]
        gain_mp[mp] = total
        for i in range(3):
            gain_over_mp(i, mp).start()

    def end_gains():
        for i, owner in enumerate((pair, across, far)):
            gain_over_mp(i, owner).wait_recv()
        gains_ref[...] = (gain_mp[0] + gain_mp[1]) + (gain_mp[2] + gain_mp[3])
        store_gains.start()

    bufs[0, PAIR] = in_part(pair).astype(low)
    each(PARTS, lambda c: sum_copy(PAIR, c).start())
    mine[...] = in_part(mp)

    def back_norm(c):
        grad = mine[piece(c), :] + arrived(PAIR, c) + arrived(ACROSS, c)
        unit, inverse = norm_unit(tokens_ref[piece(c), :].astype(full))
        scaled = grad * gain_ref[...].reshape(1, -1)
        first_mean = jnp.mean(scaled, axis=-1, keepdims=True)
        second_mean = jnp.mean(scaled * unit, axis=-1, keepdims=True)
        total = inverse * (scaled - first_mean - unit * second_mean) + grad_residual_ref[piece(c), :]
        grad_tokens_ref[piece(c), :] = total.astype(low)

    def norm(c):
        each(1, lambda i: back_norm(i + c))

    for t in range(4, max(count + 4, 5 + PARTS)):
        tick(t)
        if t < 4 + PARTS:
            norm(t - 4)
        if t == 5:
            turn_gains()
        if t == 4 + PARTS:
            store_tokens.start()
            end_gains()
    if fits:
        add_drain()
    else:
        whole = pltpu.make_async_copy(acc, d_sum_hbm, keep_sem.at[0])
        whole.start()
        whole.wait()
    for k in range(1, dp_count):
        gain_over_dp(k, dp).wait_send()
    for i in range(3):
        gain_over_mp(i, mp).wait_send()

    def drain(c):
        for kind in range(3):
            sum_copy(kind, c).wait_send()
    each(PARTS, drain)
    store_tokens.wait()
    store_gains.wait()


def last(dp_count, dq, dk, dv, w_qkv, rows, grad_residual, tokens, gain, gain_part, d_out):
    own, width = tokens.shape
    cols = dq.shape[1]
    d_rows = 4 * cols
    fits = direct_fits(d_rows, QKV_CHUNKS, dp_count)
    low, full = jnp.bfloat16, jnp.float32
    hbm = pl.BlockSpec(memory_space=pl.ANY)
    dma = pltpu.SemaphoreType.DMA
    shape, room = jax.ShapeDtypeStruct, pltpu.VMEM
    operands = (dq, dk, dv, w_qkv, rows, grad_residual, tokens, gain, gain_part, d_out)
    grad_tokens, d_sum, gains = pl.pallas_call(
        functools.partial(last_kernel, dp_count, fits),
        out_shape=[shape((own, width), low), shape((d_rows, width), low), shape((8, width), full)],
        in_specs=[hbm] * 10,
        out_specs=[hbm] * 3,
        scratch_shapes=[room(one.shape, one.dtype) for one in operands]
        + [
            room((own, width), low), room((8, width), full), dma((10,)), dma((2,)),
            room((own, width), full), room((2, 3, own, width), low), room((dp_count, 8, width), full), room((4, 8, width), full),
            dma((3, PARTS)), dma((3, PARTS)), dma((dp_count,)), dma((dp_count,)), dma((3,)), dma((3,)),
            room((d_rows, width), low), room((d_rows, width), low), room((d_rows, width), low),
            dma((len(QKV_CHUNKS), dp_count)), dma((len(QKV_CHUNKS), dp_count)), dma((len(QKV_CHUNKS),)),
        ],
        compiler_params=pltpu.CompilerParams(collective_id=3, has_side_effects=True, vmem_limit_bytes=VMEM_BYTES),
        cost_estimate=pl.CostEstimate(flops=12 * 4 * own * width * cols, bytes_accessed=20 * own * width, transcendentals=0),
        name="last",
    )(*operands)
    return grad_tokens, d_sum if fits else lax.psum(d_sum, "dp"), gains


def finish_kernel(
    first_ref, first_came_ref, second_ref, second_came_ref, attn_ref, qkv_ref, gains_ref, tokens_hbm, relaid_hbm,
    up_ref, down_ref, attn_out_ref, qkv_out_ref, gain_attn_ref, gain_mlp_ref, tokens_out_hbm, relaid_out_hbm, tokens_ref, relaid_ref, load_sem, store_sem,
):
    loads = local_copies(((tokens_hbm, tokens_ref), (relaid_hbm, relaid_ref)), load_sem)
    stores = local_copies(((tokens_ref, tokens_out_hbm), (relaid_ref, relaid_out_hbm)), store_sem)

    @pl.when(pl.program_id(0) == 0)
    def _():
        for load in loads:
            load.start()

    @pl.when(pl.program_id(0) == 1)
    def _():
        for load, store in zip(loads, stores):
            load.wait()
            store.start()

    full = jnp.float32
    dp = lax.axis_index("dp")
    size = first_ref.shape[0]
    mine, came = first_ref[...].astype(full), first_came_ref[...].astype(full)
    even = lax.rem(dp, 2) == 0
    up_ref[0:size, :] = jnp.where(even, mine, came)
    down_ref[0:size, :] = jnp.where(even, came, mine)
    mine, came = second_ref[...].astype(full), second_came_ref[...].astype(full)
    even = lax.rem(dp // 2, 2) == 0
    low, high = jnp.where(even, mine, came), jnp.where(even, came, mine)
    half = size // 2
    up_ref[size:size + half, :] = low[:half]
    up_ref[size + half:, :] = high[:half]
    down_ref[size:size + half, :] = low[half:]
    down_ref[size + half:, :] = high[half:]
    attn_out_ref[...] = attn_ref[...].astype(full)
    qkv_out_ref[...] = qkv_ref[...].astype(full)
    gain_mlp_ref[...] = gains_ref[0]
    gain_attn_ref[...] = gains_ref[1]

    @pl.when(pl.program_id(0) == pl.num_programs(0) - 1)
    def _():
        for store in stores:
            store.wait()


def finish(first, first_came, second, second_came, weight_sum, gains, grad_tokens, relaid):
    steps = MLP_CHUNKS // 2
    size = first.shape[0] // steps
    rows, width = weight_sum.shape
    cols = rows // 4
    full = jnp.float32
    hbm = pl.BlockSpec(memory_space=pl.ANY)
    vmem = pl.BlockSpec(memory_space=pltpu.VMEM)
    shape = jax.ShapeDtypeStruct

    def block(count, ahead=0):
        return pl.BlockSpec((count, width), lambda i: (i + ahead, 0))

    return pl.pallas_call(
        finish_kernel,
        grid=(steps,),
        out_shape=[
            shape((2 * steps * size, width), full), shape((2 * steps * size, width), full), shape((cols, width), full),
            shape((3 * cols, width), full), shape((width,), full), shape((width,), full), shape(grad_tokens.shape, grad_tokens.dtype), shape(relaid.shape, relaid.dtype),
        ],
        in_specs=[block(size)] * 4 + [block(cols // 3), block(cols, 1), vmem, hbm, hbm],
        out_specs=[block(2 * size)] * 2 + [block(cols // 3), block(cols), vmem, vmem, hbm, hbm],
        scratch_shapes=[pltpu.VMEM(one.shape, one.dtype) for one in (grad_tokens, relaid)]
        + [pltpu.SemaphoreType.DMA((2,)), pltpu.SemaphoreType.DMA((2,))],
        compiler_params=pltpu.CompilerParams(vmem_limit_bytes=VMEM_BYTES),
        cost_estimate=pl.CostEstimate(flops=0, bytes_accessed=14 * rows * width, transcendentals=0),
        name="finish",
    )(first, first_came, second, second_came, weight_sum, weight_sum, gains, grad_tokens, relaid)


def local(
    tokens, segment_ids, gene_owner, w_qkv, w_attn_out, w_up, w_down, gain_attn, gain_mlp, cotangent
):
    width = tokens.shape[1]
    dp_count = lax.axis_size("dp")
    capacity = cotangent.shape[0] // dp_count
    low, full = jnp.bfloat16, jnp.float32
    w_rows = jnp.swapaxes(w_qkv, 1, 2)
    attn_in, *projected, grad_block, place, ranges = project(
        tokens, gain_attn, w_rows, cotangent.reshape(dp_count, capacity, width), gene_owner.reshape(1, -1), segment_ids
    )
    grad_across = lax.ppermute(grad_block, "mp", [(i, i ^ 2) for i in range(lax.axis_size("mp"))])
    merged, log_sums = attend_forward(ranges, segment_ids, *projected)
    residual_rows, grad_merged, grad_residual, outgoing, first, second, gain_part, d_out = middle(
        dp_count, merged, w_attn_out, tokens, gain_mlp, w_up, w_down, grad_block, grad_across, place
    )
    cols = w_qkv.shape[2]
    whole = sum_stages(2 * width, MLP_CHUNKS, dp_count) == 0
    if not whole:
        first_came = lax.ppermute(first, "dp", [(i, i ^ 1) for i in range(dp_count)])
        second_came = lax.ppermute(second, "dp", [(i, i ^ 2) for i in range(dp_count)])
        gain_part, first_came, second_came = lax.optimization_barrier((gain_part, first_came, second_came))
    relaid = lax.all_to_all(
        outgoing.reshape(dp_count, capacity, width), "dp", split_axis=0, concat_axis=0, tiled=True
    ).reshape(dp_count * capacity, width)
    grad_proj = attend_backward(ranges, segment_ids, *projected, merged, grad_merged, log_sums)
    grad_tokens, weight_sum, gains = last(
        dp_count, *grad_proj, w_rows, attn_in, grad_residual, tokens, gain_attn, gain_part, d_out
    )
    if whole:
        d_sum = lax.psum(jnp.concatenate([first, second]), "dp").reshape(MLP_CHUNKS, 2, -1, width).astype(full)
        up_sum, down_sum = (d_sum[:, i].reshape(-1, width) for i in range(2))
        attn_sum, qkv_sum = weight_sum[:cols].astype(full), weight_sum[cols:].astype(full)
        gain_one, gain_two = gains[1], gains[0]
    else:
        up_sum, down_sum, attn_sum, qkv_sum, gain_one, gain_two, grad_tokens, relaid = finish(
            first, first_came, second, second_came, weight_sum, gains, grad_tokens, relaid
        )
    qkv_sum = qkv_sum.reshape(3, cols, width)
    return (
        relaid,
        grad_tokens,
        jnp.swapaxes(qkv_sum, 1, 2),
        attn_sum,
        up_sum,
        down_sum,
        gain_one,
        gain_two,
    )


def solution(mesh):
    placed = (
        P(("dp", "mp"), None),
        P("dp", None),
        P(("dp", "mp"), None),
        P(None, None, "mp"),
        P("mp", None),
        P(None, "mp"),
        P(None, "mp"),
        P(),
        P(),
        P(("dp", "mp"), None),
    )
    return jax.shard_map(
        local,
        mesh=mesh,
        in_specs=placed,
        out_specs=(
            P(("dp", "mp"), None),
            P(("dp", "mp"), None),
            P(None, None, "mp"),
            P("mp", None),
            P(None, "mp"),
            P(None, "mp"),
            P(),
            P(),
        ),
        check_vma=False,
    )
```

```python
import functools
import jax
import jax.numpy as jnp
from jax import lax
from jax.experimental import pallas as pl
from jax.experimental.pallas import tpu as pltpu
from jax.sharding import PartitionSpec as P

HEAD = 64
TQ = 256
TK = 256
NT = (((1,), (1,)), ((), ()))
NN = (((1,), (0,)), ((), ()))
TN = (((0,), (0,)), ((), ()))
MASKED = -1e30
TALL = HEAD + 16
epsilon = 1e-05


def local_copies(pairs, sems):
    return [pltpu.make_async_copy(src, dst, sems.at[i]) for i, (src, dst) in enumerate(pairs)]


def key_ranges(seg, tiles):
    n = seg.shape[1]
    lane = lax.broadcasted_iota(jnp.int32, (tiles, n), 1)
    row = lax.broadcasted_iota(jnp.int32, (tiles, n), 0)
    ids = jnp.broadcast_to(seg.astype(jnp.float32), (tiles, n))

    def total(mask, values):
        return jnp.sum(jnp.where(mask, values, 0.0), axis=1, keepdims=True)

    first = total(lane == row * TQ, ids)
    last = total(lane == row * TQ + TQ - 1, ids)
    start = jnp.floor(total(ids < first, 1.0) * (1.0 / TK))
    end = jnp.floor((total(ids <= last, 1.0) + (TK - 1.0)) * (1.0 / TK))
    lane = lax.broadcasted_iota(jnp.int32, (tiles, 128), 1)
    return jnp.where(lane == 0, start, jnp.where(lane == 1, end, 0.0)).astype(jnp.int32)


def over_blocks(ranges, tile, body, state):
    lo, hi = ranges[tile, 0], ranges[tile, 1]
    pairs = (hi - lo) // 2
    state = lax.fori_loop(
        0, pairs, lambda i, one: body(pl.multiple_of((lo + 2 * i) * TK, TK), 2 * TK, one), state
    )
    return lax.fori_loop(lo + 2 * pairs, hi, lambda i, one: body(pl.multiple_of(i * TK, TK), TK, one), state)


def head_masks(width, heads):
    lane = lax.broadcasted_iota(jnp.int32, (1, width), 1)
    return [(lane // HEAD == h) for h in range(heads)]


def seg_columns(segv_ref, cols, n):
    for t in range(n // 128):
        row = segv_ref[0:1, t * 128:(t + 1) * 128].astype(jnp.float32)
        cols[t * 128:(t + 1) * 128, :] = jnp.broadcast_to(row, (128, 128)).T


def fwd_kernel(n, heads, ranges, segv_ref, q_ref, k_ref, v_ref, o_ref, lse_ref, vt, cols, scores):
    tile = pl.program_id(0)
    width = heads * HEAD

    @pl.when(tile == 0)
    def _():
        seg_columns(segv_ref, cols, n)
        for t in range(n // TK):
            turned = v_ref[t * TK:(t + 1) * TK, :].astype(jnp.float32).T.astype(jnp.bfloat16)
            for h in range(heads):
                vt[h * TALL:h * TALL + HEAD, t * TK:(t + 1) * TK] = turned[h * HEAD:(h + 1) * HEAD]
                vt[h * TALL + HEAD:(h + 1) * TALL, t * TK:(t + 1) * TK] = jnp.ones((TALL - HEAD, TK), jnp.bfloat16)

    q0 = pl.multiple_of(tile * TQ, TQ)
    q = q_ref[...] * jnp.bfloat16(HEAD ** -0.5)
    masks = head_masks(width, heads)
    qm = [jnp.where(m, q, jnp.bfloat16(0)) for m in masks]
    seg_row = segv_ref[0:1, pl.ds(q0, TQ)].astype(jnp.float32)

    def first(k0, size, tops):
        keys = k_ref[pl.ds(k0, size), :]
        col = cols[pl.ds(k0, size), :]
        same = jnp.concatenate([col] * (TQ // 128), axis=1) == seg_row
        out = []
        for h in range(heads):
            s = lax.dot_general(keys, qm[h], NT, preferred_element_type=jnp.float32)
            s = jnp.where(same, s, MASKED)
            scores[h, pl.ds(k0, size), :] = s
            out.append(jnp.maximum(tops[h], jnp.max(s, axis=0, keepdims=True)))
        return tuple(out)

    tops = over_blocks(ranges, tile, first, tuple(jnp.full((1, TQ), MASKED, jnp.float32) for _ in range(heads)))

    def second(k0, size, acc):
        out = []
        for h in range(heads):
            p = jnp.exp(scores[h, pl.ds(k0, size), :] - tops[h]).astype(jnp.bfloat16)
            out.append(acc[h] + jnp.dot(vt[h * TALL:(h + 1) * TALL, pl.ds(k0, size)], p, preferred_element_type=jnp.float32))
        return tuple(out)

    acc = over_blocks(ranges, tile, second, tuple(jnp.zeros((TALL, TQ), jnp.float32) for _ in range(heads)))
    totals = [one[HEAD:HEAD + 1] for one in acc]
    ot = jnp.concatenate([acc[h][:HEAD] / totals[h] for h in range(heads)], axis=0)
    o_ref[...] = ot.T.astype(jnp.bfloat16)
    lse_ref[...] = jnp.concatenate(
        [tops[h] + jnp.log(totals[h]) for h in range(heads)] + [jnp.zeros((8 - heads, TQ), jnp.float32)], axis=0
    )


def attend_forward(ranges, seg, q, k, v):
    n, width = q.shape
    heads = width // HEAD
    whole = pl.BlockSpec(memory_space=pltpu.VMEM)
    return pl.pallas_call(
        functools.partial(fwd_kernel, n, heads),
        grid_spec=pltpu.PrefetchScalarGridSpec(
            num_scalar_prefetch=1,
            grid=(n // TQ,),
            in_specs=[whole, pl.BlockSpec((TQ, width), lambda t, s: (t, 0)), whole, whole],
            out_specs=[pl.BlockSpec((TQ, width), lambda t, s: (t, 0)), pl.BlockSpec((8, TQ), lambda t, s: (0, t))],
            scratch_shapes=[pltpu.VMEM((heads * TALL, n), jnp.bfloat16), pltpu.VMEM((n, 128), jnp.float32), pltpu.VMEM((heads, n, TQ), jnp.float32)],
        ),
        out_shape=[jax.ShapeDtypeStruct((n, width), jnp.bfloat16), jax.ShapeDtypeStruct((8, n), jnp.float32)],
        compiler_params=pltpu.CompilerParams(vmem_limit_bytes=VMEM_BYTES),
        cost_estimate=pl.CostEstimate(flops=4 * heads * n * n * HEAD, bytes_accessed=8 * n * width, transcendentals=heads * n * n // 2),
        name="attend_forward",
    )(ranges, seg, q, k, v)


def bwd_kernel(
    n, heads, ranges, segv_ref, q_ref, k_ref, v_ref, o_ref, do_ref, lse_ref, dq_ref, dk_ref, dv_ref,
    kt, kh, vh, cols, dk_acc, dv_acc,
):
    tile = pl.program_id(0)

    def head_cols(h):
        return slice(h * HEAD, (h + 1) * HEAD)

    @pl.when(tile == 0)
    def _():
        dk_acc[...] = jnp.zeros_like(dk_acc)
        dv_acc[...] = jnp.zeros_like(dv_acc)
        seg_columns(segv_ref, cols, n)
        for h in range(heads):
            kh[h] = k_ref[:, head_cols(h)]
            vh[h] = v_ref[:, head_cols(h)]
        for t in range(n // TK):
            kt[:, t * TK:(t + 1) * TK] = k_ref[t * TK:(t + 1) * TK, :].astype(jnp.float32).T.astype(jnp.bfloat16)

    q0 = pl.multiple_of(tile * TQ, TQ)
    q = q_ref[...] * jnp.bfloat16(HEAD ** -0.5)
    do = do_ref[...]
    seg_row = segv_ref[0:1, pl.ds(q0, TQ)].astype(jnp.float32)
    do_wide = do.astype(jnp.float32)
    products = (do_wide * o_ref[...].astype(jnp.float32)).T
    q_turned = q.astype(jnp.float32).T.astype(jnp.bfloat16)
    do_turned = do_wide.T.astype(jnp.bfloat16)
    lse = lse_ref[...]
    deltas = [jnp.sum(products[head_cols(h)], axis=0, keepdims=True) for h in range(heads)]
    q_heads = [q[:, head_cols(h)] for h in range(heads)]
    do_heads = [do[:, head_cols(h)] for h in range(heads)]

    def body(k0, size, acc):
        where = pl.ds(k0, size)
        same = jnp.concatenate([cols[where, :]] * (TQ // 128), axis=1) == seg_row
        out = []
        for h in range(heads):
            s = jnp.dot(kh[h, where, :], q_turned[head_cols(h)], preferred_element_type=jnp.float32)
            p = jnp.where(same, jnp.exp(s - lse[h:h + 1, :]), 0.0)
            dp = jnp.dot(vh[h, where, :], do_turned[head_cols(h)], preferred_element_type=jnp.float32)
            ds = (p * (dp - deltas[h])).astype(jnp.bfloat16)
            dv_acc[h, where, :] += jnp.dot(p.astype(jnp.bfloat16), do_heads[h], preferred_element_type=jnp.float32)
            dk_acc[h, where, :] += jnp.dot(ds, q_heads[h], preferred_element_type=jnp.float32)
            out.append(acc[h] + jnp.dot(kt[head_cols(h), where], ds, preferred_element_type=jnp.float32))
        return tuple(out)

    acc = over_blocks(ranges, tile, body, tuple(jnp.zeros((HEAD, TQ), jnp.float32) for _ in range(heads)))
    dq_ref[...] = (jnp.concatenate(acc, axis=0).T * HEAD ** -0.5).astype(jnp.bfloat16)

    @pl.when(tile == n // TQ - 1)
    def _():
        for h in range(heads):
            dk_ref[:, head_cols(h)] = dk_acc[h].astype(jnp.bfloat16)
            dv_ref[:, head_cols(h)] = dv_acc[h].astype(jnp.bfloat16)


def attend_backward(ranges, seg, q, k, v, o, do, lse):
    n, width = q.shape
    heads = width // HEAD
    whole = pl.BlockSpec(memory_space=pltpu.VMEM)
    rows = pl.BlockSpec((TQ, width), lambda t, s: (t, 0))
    return pl.pallas_call(
        functools.partial(bwd_kernel, n, heads),
        grid_spec=pltpu.PrefetchScalarGridSpec(
            num_scalar_prefetch=1,
            grid=(n // TQ,),
            in_specs=[whole, rows, whole, whole, rows, rows, pl.BlockSpec((8, TQ), lambda t, s: (0, t))],
            out_specs=[rows, whole, whole],
            scratch_shapes=[pltpu.VMEM((width, n), jnp.bfloat16)] + [pltpu.VMEM((heads, n, HEAD), jnp.bfloat16)] * 2
            + [pltpu.VMEM((n, 128), jnp.float32)] + [pltpu.VMEM((heads, n, HEAD), jnp.float32)] * 2,
        ),
        out_shape=[jax.ShapeDtypeStruct((n, width), jnp.bfloat16)] * 3,
        compiler_params=pltpu.CompilerParams(vmem_limit_bytes=VMEM_BYTES),
        cost_estimate=pl.CostEstimate(flops=10 * heads * n * n * HEAD, bytes_accessed=16 * n * width, transcendentals=heads * n * n // 2),
        name="attend_backward",
    )(ranges, seg, q, k, v, o, do, lse)


MESH_ID = pl.DeviceIdType.MESH
PARTS = 4
VMEM_BYTES = 60 << 20
MLP_CHUNKS = 6
QKV_CHUNKS = (128, 128, 256, 256)


def remote(src, dst, send, recv, device):
    return pltpu.make_async_remote_copy(
        src_ref=src, dst_ref=dst, send_sem=send, recv_sem=recv, device_id=device, device_id_type=MESH_ID
    )


def greet(devices):
    barrier = pltpu.get_barrier_semaphore()
    for device in devices:
        pl.semaphore_signal(barrier, inc=1, device_id=device, device_id_type=MESH_ID)
    pl.semaphore_wait(barrier, len(devices))


def norm_unit(values):
    average = jnp.mean(values, axis=-1, keepdims=True)
    centered = values - average
    variance = jnp.mean(centered * centered, axis=-1, keepdims=True)
    inverse = lax.rsqrt(variance + epsilon)
    return centered * inverse, inverse


def sum_stages(rows, chunks, dp_count):
    stages = dp_count.bit_length() - 1
    return stages if dp_count == 1 << stages and rows % (16 * chunks * dp_count) == 0 else 0


def sum_scratch(rows, width, chunks, stages):
    dma = pltpu.SemaphoreType.DMA
    return [
        pltpu.VMEM((rows, width), jnp.bfloat16), pltpu.VMEM((rows, width), jnp.bfloat16),
        dma((chunks, max(1, 2 * stages))), dma((chunks, max(1, 2 * stages))),
    ]


def left_bit(k):
    return k % 2


def packed(k, chunks):
    return k // 2 if k % 2 == 0 else (chunks + 1) // 2 + k // 2


def sum_steps(stages, chunks, acc, came, send, recv, out, half=False):
    dp, mp = lax.axis_index("dp"), lax.axis_index("mp")
    chunk = acc.shape[0] // chunks

    def bit(s):
        return lax.rem(dp // (1 << s), 2)

    def held(k, s):
        start = k * chunk
        for j in range(s):
            start = start + bit(j) * (chunk >> (j + 1))
        return start

    def span(start, size):
        return pl.ds(pl.multiple_of(start, 16), size)

    def placed(k, start):
        if not half:
            return start
        return packed(k, chunks) * (chunk // 2) + bit(1 - left_bit(k)) * (chunk // 4) + start - held(k, 2)

    def halve(k, s):
        size = chunk >> (s + 1)
        return remote(
            acc.at[span(held(k, s) + (1 - bit(s)) * size, size)],
            came.at[span(k * chunk + chunk - (chunk >> s), size)],
            send.at[k, s], recv.at[k, s], (dp ^ (1 << s), mp),
        )

    def double(k, s, mine=True):
        if half and s == 1:
            s = 1 - left_bit(k)
            place = bit(s) if mine else 1 - bit(s)
            rows = out.at[span(packed(k, chunks) * (chunk // 2) + place * (chunk // 4), chunk // 4)]
            return remote(rows, rows, send.at[k, stages + 1], recv.at[k, stages + 1], (dp ^ (1 << s), mp))
        size = chunk >> (s + 1)
        start = held(k, s + 1) if mine else held(k, s) + (1 - bit(s)) * size
        rows = out.at[span(placed(k, start), size)]
        return remote(rows, rows, send.at[k, stages + s], recv.at[k, stages + s], (dp ^ (1 << s), mp))

    final = 1 if half else 0

    def step(k, i):
        if i == 0:
            halve(k, 0).start()
        elif i <= stages:
            halve(k, i - 1).wait_recv()
            size = chunk >> i
            rows = span(held(k, i), size)
            total = acc[rows, :].astype(jnp.float32) + came[span(k * chunk + chunk - (chunk >> (i - 1)), size), :].astype(jnp.float32)
            if i < stages:
                acc[rows, :] = total.astype(jnp.bfloat16)
                halve(k, i).start()
            else:
                out[span(placed(k, held(k, i)), size), :] = total.astype(jnp.bfloat16)
                double(k, stages - 1).start()
        elif 2 * stages - i >= final:
            s = 2 * stages - i
            double(k, s, False).wait_recv()
            if s > final:
                double(k, s - 1).start()

    def drain():
        for k in range(chunks):
            for s in range(stages):
                halve(k, s).wait_send()
                if s >= final:
                    double(k, s).wait_send()

    return step, drain


def columns_of(row):
    return jnp.concatenate(
        [jnp.broadcast_to(row[:, t * 128:(t + 1) * 128], (128, 128)).T for t in range(row.shape[1] // 128)], axis=0
    )


def project_kernel(
    dp_count, tokens_hbm, gain_hbm, w_hbm, cot_ref, owner_hbm, seg_hbm, rows_hbm, q_hbm, k_hbm, v_hbm, grad_hbm, place_hbm, ranges_ref,
    tokens_ref, gain_ref, w_ref, owner_ref, seg_ref, rows_ref, q_ref, k_ref, v_ref, grad_ref, place_ref, load_sem, store_sem, out_sem, returned_ref, across_send, across_recv, pair_send, pair_recv, pass_send, pass_recv, slot_send, slot_recv, self_sem,
):
    load_tokens, load_gain, load_w, load_owner, load_seg = loads = local_copies(
        ((tokens_hbm, tokens_ref), (gain_hbm, gain_ref), (w_hbm, w_ref), (owner_hbm, owner_ref), (seg_hbm, seg_ref)), load_sem
    )
    for load in loads:
        load.start()
    stores = local_copies(
        ((q_ref, q_hbm), (k_ref, k_hbm), (v_ref, v_hbm), (place_ref, place_hbm), (grad_ref, grad_hbm)), out_sem
    )
    dp, mp = lax.axis_index("dp"), lax.axis_index("mp")
    pair, across, far = mp ^ 1, mp ^ 2, mp ^ 3
    own = tokens_ref.shape[0]
    part = own // PARTS
    greet([(dp, pair), (dp, across)] + [(lax.rem(dp + k, dp_count), mp) for k in range(1, dp_count)])

    def spot(owner, c, size):
        return pl.ds(pl.multiple_of(owner * own + c * size, size), size)

    def gather_copy(c, owner, device, send, recv):
        rows = rows_ref.at[spot(owner, c, part)]
        return remote(rows, rows, send.at[c], recv.at[c], device)

    def slot_copy(k):
        other = lax.rem(dp + k, dp_count)
        return remote(cot_ref.at[other], returned_ref.at[dp], slot_send.at[k], slot_recv.at[k], (other, mp))

    def store(i, owner):
        rows = pl.ds(pl.multiple_of(owner * own, own), own)
        return pltpu.make_async_copy(rows_ref.at[rows], rows_hbm.at[rows], store_sem.at[i])

    for k in sorted(range(1, dp_count), key=lambda k: -min(k, dp_count - k)):
        slot_copy(k).start()
    self_copy = pltpu.make_async_copy(cot_ref.at[dp], returned_ref.at[dp], self_sem)
    self_copy.start()
    load_tokens.wait()
    load_gain.wait()
    for c in range(PARTS):
        values = tokens_ref[c * part:(c + 1) * part, :].astype(jnp.float32)
        unit, _ = norm_unit(values)
        rows_ref[spot(mp, c, part), :] = (unit * gain_ref[...].reshape(1, -1)).astype(jnp.bfloat16)
        gather_copy(c, mp, (dp, across), across_send, across_recv).start()
        gather_copy(c, mp, (dp, pair), pair_send, pair_recv).start()
    def product(owner, half):
        where = spot(owner, half, own // 2)
        rows = rows_ref[where, :]
        for p, out in enumerate((q_ref, k_ref, v_ref)):
            out[where, :] = lax.dot_general(rows, w_ref[p], NT, preferred_element_type=jnp.float32).astype(jnp.bfloat16)

    def both(owner):
        def step(half, _):
            product(owner, half)
            return 0
        lax.fori_loop(0, 2, step, 0)

    load_w.wait()
    load_owner.wait()
    load_seg.wait()
    both(mp)
    ranges_ref[...] = key_ranges(seg_ref[...], ranges_ref.shape[0])
    store(0, mp).start()
    capacity = cot_ref.shape[1]
    owner_row = owner_ref[...].astype(jnp.float32)
    owner_col = columns_of(owner_row)
    earlier = lax.broadcasted_iota(jnp.int32, (own, own), 0) < lax.broadcasted_iota(jnp.int32, (own, own), 1)
    same = jnp.concatenate([owner_col] * (own // 128), axis=1) == owner_row
    rank_row = jnp.sum(jnp.where(same & earlier, 1.0, 0.0), axis=0, keepdims=True)
    slot_row = owner_row * capacity + rank_row
    slots = place_ref.shape[0]
    place_ref[...] = jnp.where(
        lax.broadcasted_iota(jnp.int32, (slots, own), 0).astype(jnp.float32) == slot_row, 1.0, 0.0
    ).astype(jnp.bfloat16)
    stores[3].start()
    for c in range(PARTS):
        gather_copy(c, pair, (dp, pair), pair_send, pair_recv).wait_recv()
    both(pair)
    store(1, pair).start()
    for half in range(2):
        for c in range(half * PARTS // 2, (half + 1) * PARTS // 2):
            gather_copy(c, across, (dp, across), across_send, across_recv).wait_recv()
            gather_copy(c, across, (dp, pair), pass_send, pass_recv).start()
        product(across, half)
    store(2, across).start()
    for half in range(2):
        for c in range(half * PARTS // 2, (half + 1) * PARTS // 2):
            gather_copy(c, far, (dp, pair), pass_send, pass_recv).wait_recv()
        product(far, half)
    store(3, far).start()
    for out in stores[:3]:
        out.start()
    for c in range(PARTS):
        gather_copy(c, mp, (dp, across), across_send, across_recv).wait_send()
        gather_copy(c, mp, (dp, pair), pair_send, pair_recv).wait_send()
        gather_copy(c, across, (dp, pair), pass_send, pass_recv).wait_send()
    self_copy.wait()
    for k in range(1, dp_count):
        slot_copy(k).wait_send()
        other = lax.rem(dp + dp_count - k, dp_count)
        remote(cot_ref.at[dp], returned_ref.at[other], slot_send.at[k], slot_recv.at[k], (other, mp)).wait_recv()
    for i, owner in enumerate((mp, pair, across, far)):
        store(i, owner).wait()
    if capacity % 16 == 0:
        back = returned_ref[...].reshape(slots, cot_ref.shape[2])
        grad_ref[...] = lax.dot_general(place_ref[...], back, TN, preferred_element_type=jnp.float32).astype(jnp.bfloat16)
    else:
        rank_col = columns_of(rank_row)[:, :capacity]
        lane = lax.broadcasted_iota(jnp.int32, (own, capacity), 1).astype(jnp.float32)

        def take(d, total):
            pick = (owner_col[:, :capacity] == d.astype(jnp.float32)) & (rank_col == lane)
            pick = jnp.where(pick, 1.0, 0.0).astype(jnp.bfloat16)
            return total + jnp.dot(pick, returned_ref[d], preferred_element_type=jnp.float32)
        grad_ref[...] = lax.fori_loop(0, dp_count, take, jnp.zeros(grad_ref.shape, jnp.float32)).astype(jnp.bfloat16)
    stores[4].start()
    for out in stores:
        out.wait()


def project(tokens, gain, w_qkv, cot, owners, seg):
    own, width = tokens.shape
    dp_count = cot.shape[0]
    total = own * 4
    cols = w_qkv.shape[1]
    vmem = pl.BlockSpec(memory_space=pltpu.VMEM)
    hbm = pl.BlockSpec(memory_space=pltpu.HBM)
    dma = pltpu.SemaphoreType.DMA
    return pl.pallas_call(
        functools.partial(project_kernel, dp_count),
        out_shape=[jax.ShapeDtypeStruct((total, width), jnp.bfloat16)]
        + [jax.ShapeDtypeStruct((total, cols), jnp.bfloat16)] * 3
        + [jax.ShapeDtypeStruct((own, width), jnp.bfloat16), jax.ShapeDtypeStruct((dp_count * cot.shape[1], own), jnp.bfloat16)]
        + [jax.ShapeDtypeStruct((seg.shape[1] // TQ, 128), jnp.int32)],
        in_specs=[hbm] * 6,
        out_specs=[hbm] * 6 + [vmem],
        scratch_shapes=[pltpu.VMEM(one.shape, one.dtype) for one in (tokens, gain, w_qkv, owners, seg)]
        + [pltpu.VMEM((total, width), jnp.bfloat16)] + [pltpu.VMEM((total, cols), jnp.bfloat16)] * 3
        + [pltpu.VMEM((own, width), jnp.bfloat16), pltpu.VMEM((dp_count * cot.shape[1], own), jnp.bfloat16)]
        + [dma((5,)), dma((4,)), dma((5,)), pltpu.VMEM(cot.shape, cot.dtype)] + [dma((PARTS,))] * 6 + [dma((dp_count,))] * 2 + [dma],
        compiler_params=pltpu.CompilerParams(collective_id=1, has_side_effects=True, vmem_limit_bytes=VMEM_BYTES),
        cost_estimate=pl.CostEstimate(flops=6 * total * width * cols, bytes_accessed=10 * total * width, transcendentals=0),
        name="project",
    )(tokens, gain, w_qkv, cot, owners, seg)


def gelu_and_slope(values):
    cumulative = 0.5 * (1.0 + lax.erf(values * 0.7071067811865476))
    density = jnp.exp(-0.5 * values * values) * 0.3989422804014327
    return values * cumulative, cumulative + values * density


def middle_kernel(
    stages, merged_hbm, w_out_hbm, tokens_hbm, gain_hbm, w_up_hbm, w_down_hbm, grad_own_hbm, grad_across_hbm, place_hbm,
    back_rows_hbm, grad_merged_hbm, grad_residual_hbm, outgoing_hbm, first_hbm, second_hbm, gain_part_hbm, d_out_hbm,
    merged_ref, w_out_ref, tokens_ref, gain_ref, gain_part_ref, d_out_ref, w_up_ref, w_down_ref, grad_own_ref, grad_across_ref, place_ref,
    back_rows_ref, grad_merged_ref, grad_residual_ref, outgoing_ref, d_mlp_ref, load_sem, store_sem,
    mlp_rows, grad_rows, active, grad_pre, residual, mine, bufs,
    sum_send, sum_recv, row_send, row_recv, grad_send, grad_recv, self_sem, acc, came, dp_send, dp_recv,
):
    first_rows = first_hbm.shape[0]
    loads = local_copies(
        (
            (merged_hbm, merged_ref), (w_out_hbm, w_out_ref), (tokens_hbm, tokens_ref), (grad_own_hbm, grad_own_ref),
            (grad_across_hbm, grad_across_ref), (w_up_hbm, w_up_ref), (w_down_hbm, w_down_ref), (place_hbm, place_ref),
            (gain_hbm, gain_ref),
        ),
        load_sem,
    )
    for load in loads:
        load.start()
    stores = local_copies(
        (
            (back_rows_ref, back_rows_hbm), (grad_merged_ref, grad_merged_hbm), (grad_residual_ref, grad_residual_hbm),
            (outgoing_ref, outgoing_hbm), (d_mlp_ref.at[0:first_rows], first_hbm), (d_mlp_ref.at[first_rows:], second_hbm),
            (gain_part_ref, gain_part_hbm), (d_out_ref, d_out_hbm),
        ),
        store_sem,
    )
    low, full = jnp.bfloat16, jnp.float32
    dp, mp = lax.axis_index("dp"), lax.axis_index("mp")
    pair, across, far = mp ^ 1, mp ^ 2, mp ^ 3
    own, width = tokens_ref.shape
    part = own // PARTS
    to_pair, to_across = (dp, pair), (dp, across)
    greet([to_pair, to_across] + [(dp ^ (1 << j), mp) for j in range(stages)])
    add_step, add_drain = sum_steps(stages, MLP_CHUNKS, acc, came, dp_send, dp_recv, d_mlp_ref, half=True)
    target = acc if stages else d_mlp_ref

    def spot(owner, c=None):
        if c is None:
            return pl.ds(pl.multiple_of(owner * own, own), own)
        return pl.ds(pl.multiple_of(owner * own + c * part, part), part)

    def piece(c):
        return pl.ds(pl.multiple_of(c * part, part), part)

    def grad_copy(i, owner, src):
        return remote(src, grad_rows.at[spot(owner)], grad_send.at[i], grad_recv.at[i], to_pair)

    grad_loads = [
        pltpu.make_async_copy(grad_own_ref, grad_rows.at[spot(mp)], self_sem.at[0]),
        pltpu.make_async_copy(grad_across_ref, grad_rows.at[spot(across)], self_sem.at[1]),
    ]

    FAR, ACROSS, PAIR = 0, 1, 2

    def sum_copy(which, kind, c):
        src, dst = bufs.at[which, 0, kind, piece(c)], bufs.at[which, 1, kind, piece(c)]
        return remote(src, dst, sum_send.at[which, kind, c], sum_recv.at[which, kind, c], to_across if kind == ACROSS else to_pair)

    def arrived(which, kind, c):
        sum_copy(which, kind, c).wait_recv()
        return bufs[which, 1, kind, piece(c), :].astype(full)

    def ship(which, kind, c, values):
        bufs[which, 0, kind, piece(c), :] = values.astype(low)
        sum_copy(which, kind, c).start()

    def row_copy(which, kind, c, owner, ref):
        rows = ref.at[spot(owner, c)]
        return remote(rows, rows, row_send.at[which, kind, c], row_recv.at[which, kind, c], to_across if kind == 0 else to_pair)

    def each(count, body):
        def step(i, _):
            body(i)
            return 0
        lax.fori_loop(0, count, step, 0)

    def out_part(owner):
        return jnp.dot(merged_ref[spot(owner), :], w_out_ref[...], preferred_element_type=full)

    loads[0].wait()
    loads[1].wait()
    bufs[0, 0, FAR] = out_part(far).astype(low)
    each(PARTS, lambda c: sum_copy(0, FAR, c).start())
    mine[0] = out_part(across)

    def pass_across(c):
        ship(0, ACROSS, c, mine[0, piece(c), :] + arrived(0, FAR, c))
    each(PARTS, pass_across)
    bufs[0, 0, PAIR] = out_part(pair).astype(low)
    each(PARTS, lambda c: sum_copy(0, PAIR, c).start())
    for load in loads[2:5]:
        load.wait()
    for copy in grad_loads:
        copy.start()
    grad_copy(0, mp, grad_own_ref).start()
    grad_copy(1, across, grad_across_ref).start()
    mine[0] = out_part(mp) + tokens_ref[...].astype(full)
    for copy in grad_loads:
        copy.wait()
    grad_copy(0, pair, grad_own_ref).wait_recv()
    grad_copy(1, far, grad_across_ref).wait_recv()

    for load in loads[5:]:
        load.wait()
    blocks = w_up_ref.shape[1] // 256
    both = 2 * part

    def mlp(first, second, c):
        rows = jnp.concatenate([mlp_rows[spot(first, c), :], mlp_rows[spot(second, c), :]], axis=0)
        grads = jnp.concatenate([grad_rows[spot(first, c), :], grad_rows[spot(second, c), :]], axis=0)

        def block(b):
            cols = pl.ds(pl.multiple_of(b * 256, 256), 256)
            pre = jnp.dot(rows, w_up_ref[:, cols], preferred_element_type=full)
            value, slope = gelu_and_slope(pre)
            value = value.astype(low)
            active[spot(first, c), cols] = value[:part]
            active[spot(second, c), cols] = value[part:]
            back = (jnp.dot(grads, w_down_ref[:, cols], preferred_element_type=full) * slope).astype(low)
            grad_pre[spot(first, c), cols] = back[:part]
            grad_pre[spot(second, c), cols] = back[part:]
        each(blocks, block)
        back = jnp.concatenate([grad_pre[spot(first, c), :], grad_pre[spot(second, c), :]], axis=0)
        return lax.dot_general(back, w_up_ref[...], NT, preferred_element_type=full)

    def near(c):
        values = mine[0, piece(c), :] + arrived(0, PAIR, c) + arrived(0, ACROSS, c)
        residual[piece(c), :] = values
        unit, _ = norm_unit(values)
        mlp_rows[spot(mp, c), :] = (unit * gain_ref[...].reshape(1, -1)).astype(low)
        row_copy(0, 0, c, mp, mlp_rows).start()
        row_copy(0, 1, c, mp, mlp_rows).start()
        row_copy(0, 1, c, pair, mlp_rows).wait_recv()
        got = mlp(mp, pair, c)
        mine[1, piece(c), :] = got[:part]
        ship(1, PAIR, c, got[part:])
    each(PARTS, near)

    def distant(c):
        row_copy(0, 0, c, across, mlp_rows).wait_recv()
        row_copy(0, 2, c, across, mlp_rows).start()
        row_copy(0, 2, c, far, mlp_rows).wait_recv()
        got = mlp(far, across, c)
        ship(1, FAR, c, got[:part])
        ship(1, ACROSS, c, got[part:] + arrived(1, FAR, c))
    each(PARTS, distant)

    size = width // MLP_CHUNKS
    for b in range(3):
        cols = slice(b * 256, (b + 1) * 256)
        up = lax.dot_general(mlp_rows[:, cols], grad_pre[...], TN, preferred_element_type=full)
        gain_col = jnp.sum(up * w_up_ref[cols, :].astype(full), axis=1, keepdims=True)
        gain_part_ref[:, cols] = jnp.broadcast_to(gain_col, (256, 128)).T[0:8] / gain_ref[cols].reshape(1, -1)
        up = up.astype(low)
        down = lax.dot_general(grad_rows[:, cols], active[...], TN, preferred_element_type=full).astype(low)
        for j in range(256 // size):
            k = b * (256 // size) + j
            target[2 * k * size:(2 * k + 1) * size, :] = up[j * size:(j + 1) * size]
            target[(2 * k + 1) * size:(2 * k + 2) * size, :] = down[j * size:(j + 1) * size]
            if stages:
                add_step(k, 0)

    def add(*steps):
        if stages:
            for k, i in steps:
                add_step(k, i)

    def down_part(owner):
        return lax.dot_general(active[spot(owner), :], w_down_ref[...], NT, preferred_element_type=full)

    bufs[2, 0, FAR] = down_part(far).astype(low)
    each(PARTS, lambda c: sum_copy(2, FAR, c).start())
    bufs[2, 0, PAIR] = down_part(pair).astype(low)
    each(PARTS, lambda c: sum_copy(2, PAIR, c).start())

    def back_norm(c):
        grad = mine[1, piece(c), :] + arrived(1, PAIR, c) + arrived(1, ACROSS, c)
        unit, inverse = norm_unit(residual[piece(c), :])
        scaled = grad * gain_ref[...].reshape(1, -1)
        first_mean = jnp.mean(scaled, axis=-1, keepdims=True)
        second_mean = jnp.mean(scaled * unit, axis=-1, keepdims=True)
        total = inverse * (scaled - first_mean - unit * second_mean) + grad_own_ref[piece(c), :].astype(full)
        grad_residual_ref[piece(c), :] = total
        back_rows_ref[spot(mp, c), :] = total.astype(low)
        row_copy(1, 0, c, mp, back_rows_ref).start()
        row_copy(1, 1, c, mp, back_rows_ref).start()
    def tick(t):
        add(*[(t - i, i) for i in range(1, 2 * stages + 1) if 0 <= t - i < MLP_CHUNKS])

    each(2, back_norm)
    tick(1)
    each(1, lambda c: back_norm(c + 2))
    tick(2)
    each(1, lambda c: back_norm(c + 3))

    mine[1] = down_part(across)

    def pass_output(c):
        ship(2, ACROSS, c, mine[1, piece(c), :] + arrived(2, FAR, c))
    each(PARTS, pass_output)
    tick(3)
    mine[0] = residual[...] + down_part(mp)

    def merged_part(owner):
        grad_merged_ref[spot(owner), :] = lax.dot_general(
            back_rows_ref[spot(owner), :], w_out_ref[...], NT, preferred_element_type=full
        ).astype(low)

    merged_part(mp)
    each(PARTS, lambda c: row_copy(1, 1, c, pair, back_rows_ref).wait_recv())
    merged_part(pair)

    def hand_on(c):
        row_copy(1, 0, c, across, back_rows_ref).wait_recv()
        row_copy(1, 2, c, across, back_rows_ref).start()
    for c in range(PARTS):
        each(1, lambda i: hand_on(i + c))
        tick(4 + c)
    tick(8)
    merged_part(across)
    each(PARTS, lambda c: row_copy(1, 2, c, far, back_rows_ref).wait_recv())
    tick(9)
    merged_part(far)
    stores[0].start()
    stores[1].start()
    stores[2].start()
    d_out_ref[...] = lax.dot_general(merged_ref[...], back_rows_ref[...], TN, preferred_element_type=full).astype(low)
    stores[6].start()
    stores[7].start()

    tick(10)

    def finish(c):
        mine[0, piece(c), :] = mine[0, piece(c), :] + arrived(2, PAIR, c) + arrived(2, ACROSS, c)
    for c in range(PARTS):
        each(1, lambda i: finish(i + c))
    stores[4].start()
    stores[5].start()
    outgoing_ref[...] = jnp.dot(place_ref[...], mine[0].astype(low), preferred_element_type=full).astype(low)
    stores[3].start()
    if stages:
        add_drain()
    for store in stores:
        store.wait()

    def drain(c):
        for which in range(3):
            for kind in range(3):
                sum_copy(which, kind, c).wait_send()
        for which, ref in ((0, mlp_rows), (1, back_rows_ref)):
            row_copy(which, 0, c, mp, ref).wait_send()
            row_copy(which, 1, c, mp, ref).wait_send()
            row_copy(which, 2, c, across, ref).wait_send()
    each(PARTS, drain)
    grad_copy(0, mp, grad_own_ref).wait_send()
    grad_copy(1, across, grad_across_ref).wait_send()


def middle(dp_count, merged, w_out, tokens, gain, w_up, w_down, grad_own, grad_across, place):
    stages = sum_stages(2 * w_up.shape[0], MLP_CHUNKS, dp_count)
    d_rows = w_up.shape[0] * (1 if stages else 2)
    total, cols = merged.shape
    own, width = tokens.shape
    hidden = w_up.shape[1]
    slots = place.shape[0]
    low, full = jnp.bfloat16, jnp.float32
    vmem = pl.BlockSpec(memory_space=pltpu.VMEM)
    hbm = pl.BlockSpec(memory_space=pl.ANY)
    dma = pltpu.SemaphoreType.DMA
    shape, room = jax.ShapeDtypeStruct, pltpu.VMEM
    return pl.pallas_call(
        functools.partial(middle_kernel, stages),
        out_shape=[
            shape((total, width), low), shape((total, cols), low), shape((own, width), full), shape((slots, width), low),
            shape((d_rows // 2, hidden), low), shape((d_rows // 2, hidden), low), shape((8, width), full), shape((cols, width), low),
        ],
        in_specs=[hbm] * 9,
        out_specs=[hbm] * 8,
        scratch_shapes=[
            room((total, cols), low), room(w_out.shape, low), room((own, width), low), room(gain.shape, full),
            room((8, width), full), room((cols, width), low), room(w_up.shape, low),
            room(w_down.shape, low), room((own, width), low), room((own, width), low), room(place.shape, low),
            room((total, width), low), room((total, cols), low), room((own, width), full), room((slots, width), low),
            room((d_rows, hidden), low), dma((9,)), dma((8,)),
            room((total, width), low), room((total, width), low),
            room((total, hidden), low), room((total, hidden), low),
            room((own, width), full), room((2, own, width), full),
            room((3, 2, 3, own, width), low),
            dma((3, 3, PARTS)), dma((3, 3, PARTS)), dma((2, 3, PARTS)), dma((2, 3, PARTS)), dma((2,)), dma((2,)), dma((2,)),
        ]
        + sum_scratch(2 * width, hidden, MLP_CHUNKS, stages),
        compiler_params=pltpu.CompilerParams(collective_id=2, has_side_effects=True, vmem_limit_bytes=VMEM_BYTES),
        cost_estimate=pl.CostEstimate(flops=16 * total * width * hidden, bytes_accessed=20 * total * width, transcendentals=0),
        name="middle",
    )(merged, w_out, tokens, gain, w_up, w_down, grad_own, grad_across, place)


def direct_fits(rows, chunks, dp_count):
    return dp_count == 8 and rows == sum(chunks) and all(one % (16 * dp_count) == 0 for one in chunks)


def direct_steps(dp_count, chunks, acc, came, send, recv, out, out_hbm, keep_sem):
    dp, mp = lax.axis_index("dp"), lax.axis_index("mp")
    group = dp_count // 2
    starts = [sum(chunks[:k]) for k in range(len(chunks))]
    halves = [one // 2 for one in chunks]
    slots = [one // dp_count for one in chunks]
    y, z = lax.rem(dp, 2), dp // 2
    beside = (dp + 1 - 2 * y, mp)
    others = sorted(range(1, group), key=lambda j: -min(j, group - j))

    def span(start, size):
        return pl.ds(pl.multiple_of(start, 16), size)

    def low(k, side, g=0):
        return starts[k] + side * halves[k] + g * slots[k]

    def member(j):
        return lax.rem(z + j, group)

    first, second = lax.rem(z, 2), lax.rem(z // 2, 2)

    def piece_of(member_z):
        return 2 * lax.rem(member_z, 2) + lax.rem(member_z // 2, 2)

    def halve(k):
        return remote(acc.at[span(low(k, 1 - y), halves[k])], came.at[span(starts[k], halves[k])], send.at[k, 0], recv.at[k, 0], beside)

    def split(k):
        rows = span(low(k, y, 2 * (1 - first)), 2 * slots[k])
        here = span(starts[k] + halves[k], 2 * slots[k])
        return remote(acc.at[rows], came.at[here], send.at[k, 1], recv.at[k, 1], (dp + 2 - 4 * first, mp))

    def split_again(k):
        rows = span(low(k, y, 2 * first + 1 - second), slots[k])
        here = span(starts[k] + halves[k] + 2 * slots[k], slots[k])
        return remote(acc.at[rows], came.at[here], send.at[k, 2], recv.at[k, 2], (dp + 4 - 8 * second, mp))

    def gather(k, j, mine=True):
        rows = out.at[span(low(k, y, piece_of(z if mine else member(group - j))), slots[k])]
        return remote(rows, rows, send.at[k, group + j - 1], recv.at[k, group + j - 1], (y + 2 * member(j), mp))

    def double(k, mine=True):
        rows = span(low(k, y if mine else 1 - y), halves[k])
        return remote(out.at[rows], out_hbm.at[rows], send.at[k, 2 * group - 1], recv.at[k, 2 * group - 1], beside)

    def keep(k):
        rows = span(low(k, y), halves[k])
        return pltpu.make_async_copy(out.at[rows], out_hbm.at[rows], keep_sem.at[k])

    def step(k, i):
        if i == 0:
            halve(k).start()
        elif i == 1:
            halve(k).wait_recv()
            rows = span(low(k, y), halves[k])
            total = acc[rows, :].astype(jnp.float32) + came[span(starts[k], halves[k]), :].astype(jnp.float32)
            acc[rows, :] = total.astype(jnp.bfloat16)
            split(k).start()
        elif i == 2:
            split(k).wait_recv()
            rows = span(low(k, y, 2 * first), 2 * slots[k])
            here = span(starts[k] + halves[k], 2 * slots[k])
            acc[rows, :] = (acc[rows, :].astype(jnp.float32) + came[here, :].astype(jnp.float32)).astype(jnp.bfloat16)
            split_again(k).start()
        elif i == 3:
            split_again(k).wait_recv()
            rows = span(low(k, y, 2 * first + second), slots[k])
            here = span(starts[k] + halves[k] + 2 * slots[k], slots[k])
            out[rows, :] = (acc[rows, :].astype(jnp.float32) + came[here, :].astype(jnp.float32)).astype(jnp.bfloat16)
            for j in others:
                gather(k, j).start()
        elif i == 4:
            for j in others:
                gather(k, j, False).wait_recv()
            double(k).start()
            keep(k).start()
        else:
            double(k, False).wait_recv()

    def drain():
        for k in range(len(chunks)):
            halve(k).wait_send()
            split(k).wait_send()
            split_again(k).wait_send()
            for j in others:
                gather(k, j).wait_send()
            double(k).wait_send()
            keep(k).wait()

    return step, drain


def last_kernel(
    dp_count, fits, dq_hbm, dk_hbm, dv_hbm, w_hbm, rows_hbm, grad_residual_hbm, tokens_hbm, gain_hbm, gain_part_hbm, d_out_hbm,
    grad_tokens_hbm, d_sum_hbm, gains_hbm,
    dq_ref, dk_ref, dv_ref, w_ref, rows_ref, grad_residual_ref, tokens_ref, gain_ref, gain_part_ref, d_out_ref,
    grad_tokens_ref, gains_ref, load_sem, store_sem, mine, bufs, gain_dp, gain_mp,
    sum_send, sum_recv, dp_gain_send, dp_gain_recv, mp_gain_send, mp_gain_recv, acc, came, out, dp_send, dp_recv, keep_sem,
):
    loads = local_copies(
        (
            (d_out_hbm, d_out_ref), (dq_hbm, dq_ref), (rows_hbm, rows_ref), (w_hbm, w_ref), (dk_hbm, dk_ref), (dv_hbm, dv_ref),
            (gain_hbm, gain_ref), (gain_part_hbm, gain_part_ref), (grad_residual_hbm, grad_residual_ref), (tokens_hbm, tokens_ref),
        ),
        load_sem,
    )
    for load in loads:
        load.start()
    store_tokens, store_gains = local_copies(((grad_tokens_ref, grad_tokens_hbm), (gains_ref, gains_hbm)), store_sem)
    low, full = jnp.bfloat16, jnp.float32
    dp, mp = lax.axis_index("dp"), lax.axis_index("mp")
    pair, across, far = mp ^ 1, mp ^ 2, mp ^ 3
    own, width = tokens_ref.shape
    part = own // PARTS
    cols = dq_ref.shape[1]
    to_pair, to_across = (dp, pair), (dp, across)
    greet([to_pair, to_across, (dp, far)] + [(lax.rem(dp + k, dp_count), mp) for k in range(1, dp_count)])
    add_step, add_drain = direct_steps(dp_count, QKV_CHUNKS, acc, came, dp_send, dp_recv, out, d_sum_hbm, keep_sem)
    FAR, ACROSS, PAIR = 0, 1, 2

    def add(*steps):
        if fits:
            for k, i in steps:
                add_step(k, i)

    def piece(c):
        return pl.ds(pl.multiple_of(c * part, part), part)

    def each(count, body):
        def step(i, _):
            body(i)
            return 0
        lax.fori_loop(0, count, step, 0)

    def sum_copy(kind, c):
        src, dst = bufs.at[0, kind, piece(c)], bufs.at[1, kind, piece(c)]
        return remote(src, dst, sum_send.at[kind, c], sum_recv.at[kind, c], to_across if kind == ACROSS else to_pair)

    def arrived(kind, c):
        sum_copy(kind, c).wait_recv()
        return bufs[1, kind, piece(c), :].astype(full)

    def in_part(owner):
        where = pl.ds(pl.multiple_of(owner * own, own), own)
        total = jnp.dot(dq_ref[where, :], w_ref[0], preferred_element_type=full)
        total = total + jnp.dot(dk_ref[where, :], w_ref[1], preferred_element_type=full)
        return total + jnp.dot(dv_ref[where, :], w_ref[2], preferred_element_type=full)

    ends = [sum(QKV_CHUNKS[:k + 1]) for k in range(len(QKV_CHUNKS))]

    def ready(low_row, high_row):
        add(*[(k, 0) for k, end in enumerate(ends) if low_row < end <= high_row])

    def weight_grad(p, ref):
        grad = lax.dot_general(ref[...], rows_ref[...], TN, preferred_element_type=full)
        acc[(p + 1) * cols:(p + 2) * cols, :] = grad.astype(low)
        ready((p + 1) * cols, (p + 2) * cols)
        return jnp.sum(grad * w_ref[p].astype(full), axis=0, keepdims=True)

    count = len(QKV_CHUNKS)

    def tick(t):
        add(*[(t - i, i) for i in range(1, 6) if 0 <= t - i < count])

    loads[0].wait()
    acc[0:cols, :] = d_out_ref[...]
    ready(0, cols)
    for load in loads[1:4]:
        load.wait()
    gain_row = weight_grad(0, dq_ref)
    for load in loads[4:]:
        load.wait()
    bufs[0, FAR] = in_part(far).astype(low)
    each(PARTS, lambda c: sum_copy(FAR, c).start())
    tick(1)
    gain_row = gain_row + weight_grad(1, dk_ref)
    mine[...] = in_part(across)

    def pass_across(c):
        bufs[0, ACROSS, piece(c), :] = (mine[piece(c), :] + arrived(FAR, c)).astype(low)
        sum_copy(ACROSS, c).start()
    each(PARTS, pass_across)
    tick(2)
    gain_row = gain_row + weight_grad(2, dv_ref)
    tick(3)

    row = lax.broadcasted_iota(jnp.int32, (8, width), 0)
    gain_dp[dp] = jnp.where(row == 0, gain_part_ref[...], jnp.where(row == 1, gain_row / gain_ref[...].reshape(1, -1), 0.0))

    def gain_over_dp(k, owner):
        return remote(gain_dp.at[owner], gain_dp.at[owner], dp_gain_send.at[k], dp_gain_recv.at[k], (lax.rem(dp + k, dp_count), mp))

    def gain_over_mp(i, owner):
        other = (pair, across, far)[i]
        return remote(gain_mp.at[owner], gain_mp.at[owner], mp_gain_send.at[i], mp_gain_recv.at[i], (dp, other))

    for k in range(1, dp_count):
        gain_over_dp(k, dp).start()

    def turn_gains():
        for k in range(1, dp_count):
            gain_over_dp(k, lax.rem(dp + dp_count - k, dp_count)).wait_recv()
        total = gain_dp[0]
        for k in range(1, dp_count):
            total = total + gain_dp[k]
        gain_mp[mp] = total
        for i in range(3):
            gain_over_mp(i, mp).start()

    def end_gains():
        for i, owner in enumerate((pair, across, far)):
            gain_over_mp(i, owner).wait_recv()
        gains_ref[...] = (gain_mp[0] + gain_mp[1]) + (gain_mp[2] + gain_mp[3])
        store_gains.start()

    bufs[0, PAIR] = in_part(pair).astype(low)
    each(PARTS, lambda c: sum_copy(PAIR, c).start())
    mine[...] = in_part(mp)

    def back_norm(c):
        grad = mine[piece(c), :] + arrived(PAIR, c) + arrived(ACROSS, c)
        unit, inverse = norm_unit(tokens_ref[piece(c), :].astype(full))
        scaled = grad * gain_ref[...].reshape(1, -1)
        first_mean = jnp.mean(scaled, axis=-1, keepdims=True)
        second_mean = jnp.mean(scaled * unit, axis=-1, keepdims=True)
        total = inverse * (scaled - first_mean - unit * second_mean) + grad_residual_ref[piece(c), :]
        grad_tokens_ref[piece(c), :] = total.astype(low)

    def norm(c):
        each(1, lambda i: back_norm(i + c))

    for t in range(4, max(count + 5, 5 + PARTS)):
        tick(t)
        if t < 4 + PARTS:
            norm(t - 4)
        if t == 5:
            turn_gains()
        if t == 4 + PARTS:
            store_tokens.start()
            end_gains()
    if fits:
        add_drain()
    else:
        whole = pltpu.make_async_copy(acc, d_sum_hbm, keep_sem.at[0])
        whole.start()
        whole.wait()
    for k in range(1, dp_count):
        gain_over_dp(k, dp).wait_send()
    for i in range(3):
        gain_over_mp(i, mp).wait_send()

    def drain(c):
        for kind in range(3):
            sum_copy(kind, c).wait_send()
    each(PARTS, drain)
    store_tokens.wait()
    store_gains.wait()


def last(dp_count, dq, dk, dv, w_qkv, rows, grad_residual, tokens, gain, gain_part, d_out):
    own, width = tokens.shape
    cols = dq.shape[1]
    d_rows = 4 * cols
    fits = direct_fits(d_rows, QKV_CHUNKS, dp_count)
    low, full = jnp.bfloat16, jnp.float32
    hbm = pl.BlockSpec(memory_space=pl.ANY)
    dma = pltpu.SemaphoreType.DMA
    shape, room = jax.ShapeDtypeStruct, pltpu.VMEM
    operands = (dq, dk, dv, w_qkv, rows, grad_residual, tokens, gain, gain_part, d_out)
    grad_tokens, d_sum, gains = pl.pallas_call(
        functools.partial(last_kernel, dp_count, fits),
        out_shape=[shape((own, width), low), shape((d_rows, width), low), shape((8, width), full)],
        in_specs=[hbm] * 10,
        out_specs=[hbm] * 3,
        scratch_shapes=[room(one.shape, one.dtype) for one in operands]
        + [
            room((own, width), low), room((8, width), full), dma((10,)), dma((2,)),
            room((own, width), full), room((2, 3, own, width), low), room((dp_count, 8, width), full), room((4, 8, width), full),
            dma((3, PARTS)), dma((3, PARTS)), dma((dp_count,)), dma((dp_count,)), dma((3,)), dma((3,)),
            room((d_rows, width), low), room((d_rows, width), low), room((d_rows, width), low),
            dma((len(QKV_CHUNKS), dp_count)), dma((len(QKV_CHUNKS), dp_count)), dma((len(QKV_CHUNKS),)),
        ],
        compiler_params=pltpu.CompilerParams(collective_id=3, has_side_effects=True, vmem_limit_bytes=VMEM_BYTES),
        cost_estimate=pl.CostEstimate(flops=12 * 4 * own * width * cols, bytes_accessed=20 * own * width, transcendentals=0),
        name="last",
    )(*operands)
    return grad_tokens, d_sum if fits else lax.psum(d_sum, "dp"), gains


def finish_kernel(
    first_ref, first_came_ref, second_ref, second_came_ref, attn_ref, qkv_ref, gains_ref, tokens_hbm, relaid_hbm,
    up_ref, down_ref, attn_out_ref, qkv_out_ref, gain_attn_ref, gain_mlp_ref, tokens_out_hbm, relaid_out_hbm, tokens_ref, relaid_ref, load_sem, store_sem,
):
    loads = local_copies(((tokens_hbm, tokens_ref), (relaid_hbm, relaid_ref)), load_sem)
    stores = local_copies(((tokens_ref, tokens_out_hbm), (relaid_ref, relaid_out_hbm)), store_sem)

    @pl.when(pl.program_id(0) == 0)
    def _():
        for load in loads:
            load.start()

    @pl.when(pl.program_id(0) == 1)
    def _():
        for load, store in zip(loads, stores):
            load.wait()
            store.start()

    full = jnp.float32
    dp = lax.axis_index("dp")
    size = first_ref.shape[0]
    mine, came = first_ref[...].astype(full), first_came_ref[...].astype(full)
    even = lax.rem(dp, 2) == 0
    up_ref[0:size, :] = jnp.where(even, mine, came)
    down_ref[0:size, :] = jnp.where(even, came, mine)
    mine, came = second_ref[...].astype(full), second_came_ref[...].astype(full)
    even = lax.rem(dp // 2, 2) == 0
    low, high = jnp.where(even, mine, came), jnp.where(even, came, mine)
    half = size // 2
    up_ref[size:size + half, :] = low[:half]
    up_ref[size + half:, :] = high[:half]
    down_ref[size:size + half, :] = low[half:]
    down_ref[size + half:, :] = high[half:]
    attn_out_ref[...] = attn_ref[...].astype(full)
    qkv_out_ref[...] = qkv_ref[...].astype(full)
    gain_mlp_ref[...] = gains_ref[0]
    gain_attn_ref[...] = gains_ref[1]

    @pl.when(pl.program_id(0) == pl.num_programs(0) - 1)
    def _():
        for store in stores:
            store.wait()


def finish(first, first_came, second, second_came, weight_sum, gains, grad_tokens, relaid):
    steps = MLP_CHUNKS // 2
    size = first.shape[0] // steps
    rows, width = weight_sum.shape
    cols = rows // 4
    full = jnp.float32
    hbm = pl.BlockSpec(memory_space=pl.ANY)
    vmem = pl.BlockSpec(memory_space=pltpu.VMEM)
    shape = jax.ShapeDtypeStruct

    def block(count, ahead=0):
        return pl.BlockSpec((count, width), lambda i: (i + ahead, 0))

    return pl.pallas_call(
        finish_kernel,
        grid=(steps,),
        out_shape=[
            shape((2 * steps * size, width), full), shape((2 * steps * size, width), full), shape((cols, width), full),
            shape((3 * cols, width), full), shape((width,), full), shape((width,), full), shape(grad_tokens.shape, grad_tokens.dtype), shape(relaid.shape, relaid.dtype),
        ],
        in_specs=[block(size)] * 4 + [block(cols // 3), block(cols, 1), vmem, hbm, hbm],
        out_specs=[block(2 * size)] * 2 + [block(cols // 3), block(cols), vmem, vmem, hbm, hbm],
        scratch_shapes=[pltpu.VMEM(one.shape, one.dtype) for one in (grad_tokens, relaid)]
        + [pltpu.SemaphoreType.DMA((2,)), pltpu.SemaphoreType.DMA((2,))],
        compiler_params=pltpu.CompilerParams(vmem_limit_bytes=VMEM_BYTES - (6 << 20)),
        cost_estimate=pl.CostEstimate(flops=0, bytes_accessed=14 * rows * width, transcendentals=0),
        name="finish",
    )(first, first_came, second, second_came, weight_sum, weight_sum, gains, grad_tokens, relaid)


def local(
    tokens, segment_ids, gene_owner, w_qkv, w_attn_out, w_up, w_down, gain_attn, gain_mlp, cotangent
):
    width = tokens.shape[1]
    dp_count = lax.axis_size("dp")
    capacity = cotangent.shape[0] // dp_count
    low, full = jnp.bfloat16, jnp.float32
    w_rows = jnp.swapaxes(w_qkv, 1, 2)
    attn_in, *projected, grad_block, place, ranges = project(
        tokens, gain_attn, w_rows, cotangent.reshape(dp_count, capacity, width), gene_owner.reshape(1, -1), segment_ids
    )
    grad_across = lax.ppermute(grad_block, "mp", [(i, i ^ 2) for i in range(lax.axis_size("mp"))])
    merged, log_sums = attend_forward(ranges, segment_ids, *projected)
    residual_rows, grad_merged, grad_residual, outgoing, first, second, gain_part, d_out = middle(
        dp_count, merged, w_attn_out, tokens, gain_mlp, w_up, w_down, grad_block, grad_across, place
    )
    cols = w_qkv.shape[2]
    whole = sum_stages(2 * width, MLP_CHUNKS, dp_count) == 0
    if not whole:
        first_came = lax.ppermute(first, "dp", [(i, i ^ 1) for i in range(dp_count)])
        second_came = lax.ppermute(second, "dp", [(i, i ^ 2) for i in range(dp_count)])
        gain_part, first_came, second_came = lax.optimization_barrier((gain_part, first_came, second_came))
    relaid = lax.all_to_all(
        outgoing.reshape(dp_count, capacity, width), "dp", split_axis=0, concat_axis=0, tiled=True
    ).reshape(dp_count * capacity, width)
    grad_proj = attend_backward(ranges, segment_ids, *projected, merged, grad_merged, log_sums)
    grad_tokens, weight_sum, gains = last(
        dp_count, *grad_proj, w_rows, attn_in, grad_residual, tokens, gain_attn, gain_part, d_out
    )
    if whole:
        d_sum = lax.psum(jnp.concatenate([first, second]), "dp").reshape(MLP_CHUNKS, 2, -1, width).astype(full)
        up_sum, down_sum = (d_sum[:, i].reshape(-1, width) for i in range(2))
        attn_sum, qkv_sum = weight_sum[:cols].astype(full), weight_sum[cols:].astype(full)
        gain_one, gain_two = gains[1], gains[0]
    else:
        up_sum, down_sum, attn_sum, qkv_sum, gain_one, gain_two, grad_tokens, relaid = finish(
            first, first_came, second, second_came, weight_sum, gains, grad_tokens, relaid
        )
    qkv_sum = qkv_sum.reshape(3, cols, width)
    return (
        relaid,
        grad_tokens,
        jnp.swapaxes(qkv_sum, 1, 2),
        attn_sum,
        up_sum,
        down_sum,
        gain_one,
        gain_two,
    )


def solution(mesh):
    placed = (
        P(("dp", "mp"), None),
        P("dp", None),
        P(("dp", "mp"), None),
        P(None, None, "mp"),
        P("mp", None),
        P(None, "mp"),
        P(None, "mp"),
        P(),
        P(),
        P(("dp", "mp"), None),
    )
    return jax.shard_map(
        local,
        mesh=mesh,
        in_specs=placed,
        out_specs=(
            P(("dp", "mp"), None),
            P(("dp", "mp"), None),
            P(None, None, "mp"),
            P("mp", None),
            P(None, "mp"),
            P(None, "mp"),
            P(),
            P(),
        ),
        check_vma=False,
    )
```
